32 devices in a mesh: ex: 4 (over x, core), ey: 8 (over z, y).
Axes of the slice: x: 2, y: 2, z: 4, core: 2. Of those that a mesh axis runs over, the one named last changes fastest.
Arguments:
- source: float32 [8, 8, 8, 4, 1024], P(None, None, None, 'ex', 'ey'), may hold values from -4 to 4
- point_base: int32 [3, 32], P(None, ('ex', 'ey')), may hold values from 0 to 62, as said below
- point_offset: float32 [3, 32], P(None, ('ex', 'ey')), may hold values from -0.5 to 0.5
- point_force: float32 [3, 32], P(None, ('ex', 'ey')), may hold values from -4 to 4
Outputs:
- pressure: float32 [8, 8, 8, 4, 1024], P(None, None, None, 'ex', 'ey')
- forces: float32 [3, 8, 8, 8, 4, 1024], P(None, None, None, None, 'ex', 'ey')
The draws below stay inside these ranges and needn't reach their ends.
Inputs may be any that keep to these rules, and one draw needn't show every extreme that they name: `point_base`: row 0 is the turbine's element index along the first dimension, the same for all points of a turbine; the first turbine has 0 and the last 2. Rows 1 and 2 lie within 6 of their turbine's hub, between 0 and 14, resp. 0 and 62; the first point sits at 14 in row 1 and 62 in row 2.
All inputs are finite; a program needn't handle non-finite values.
Results may differ from the reference program's by a relative error of at most 0.00027.
Values sent between devices are 32-bit elements; how exact they have to be, the bound alone decides.
No kernel may reach another device: no remote copies, remote signals or barrier semaphores. Data moves between devices by JAX's collectives and lax.ppermute only.
A program may use at most 128 MiB of HBM per device.

```python
import math
import jax
import jax.numpy as jnp
import numpy as np
from jax import lax

NODES = 8
EZ = 64
TURBINES = 4
CG_STEPS = 4
CYCLES = 2
NE1 = 4
NE2 = 16
NPTS = 32
RADIUS = 6


def draw_source(key, part):
    dims_all = (NODES, NODES, NODES, NE1, NE2 * EZ)
    return jax.random.truncated_normal(key, -4.0, 4.0, dims_all, jnp.float32)


def draw_point_base(key, part):
    key_hub_y, key_hub_z, key_span_y, key_span_z = jax.random.split(key, 4)
    turbine = jnp.arange(NPTS, dtype=jnp.int32) % TURBINES
    hub_x = turbine * (NE1 - 2) // (TURBINES - 1)
    hub_y = jax.random.randint(key_hub_y, (TURBINES,), RADIUS, NE2 - 1 - RADIUS)
    hub_z = jax.random.randint(key_hub_z, (TURBINES,), RADIUS, EZ - 1 - RADIUS)
    hub_y = hub_y.at[0].set(NE2 - 2 - RADIUS)
    hub_z = hub_z.at[0].set(EZ - 2 - RADIUS)
    span_y = jax.random.randint(key_span_y, (NPTS,), -RADIUS, RADIUS + 1)
    span_z = jax.random.randint(key_span_z, (NPTS,), -RADIUS, RADIUS + 1)
    span_y = span_y.at[0].set(RADIUS)
    span_z = span_z.at[0].set(RADIUS)
    return jnp.stack([hub_x, hub_y[turbine] + span_y, hub_z[turbine] + span_z], 0).astype(jnp.int32)


def steps_of(stream_key, shape, cuts, least, top_value):
    factor_of = 1.0
    for dim, shards_of in cuts:
        heights = jax.random.uniform(jax.random.fold_in(jax.random.fold_in(stream_key, 6), dim), (shards_of,), jnp.float32, least / len(cuts), top_value / len(cuts))
        factor_of = factor_of * jnp.repeat(jnp.exp(heights), shape[dim] // shards_of).reshape((-1,) + (1,) * (len(shape) - 1 - dim))
    return factor_of


def normal_values(key, dims, scale, bound, pieces=(), kind=jnp.bfloat16):
    loudness = steps_of(key, dims, pieces, -0.22, 0.18) if pieces else 1.0
    result = jax.random.normal(key, dims, jnp.float32) * scale * loudness
    return jnp.minimum(jnp.maximum(result, -bound), bound).astype(kind)


def setup_inputs(seed: int = 0) -> dict:
    key_of = jax.random.split(jax.random.key(seed), 5)
    source = draw_source(jax.random.fold_in(key_of[4], 71), 0)
    point_base = draw_point_base(jax.random.fold_in(key_of[4], 71), 0)
    point_offset = jnp.clip(jax.random.uniform(key_of[2], (3, NPTS), jnp.float32, -0.5, 0.5) * steps_of(key_of[2], (3, NPTS), ((1, 32),), -0.4, 0.0), -0.5, 0.5)
    point_force = normal_values(key_of[3], (3, NPTS), 1.0, 4.0, ((1, 32),), jnp.float32)
    return dict(source=source, point_base=point_base, point_offset=point_offset, point_force=point_force)


GLL_POINTS = np.array([-1.0, -0.8717401485096066, -0.5917001814331423, -0.2092992179024789, 0.2092992179024789, 0.5917001814331423, 0.8717401485096066, 1.0])
WIDTH_EPS = 0.35
GAUSS_NORM = 1.0 / (math.pi ** 1.5 * WIDTH_EPS ** 3)
CHEB_LOW = 1.5
CHEB_HIGH = 12.0
HIGHEST = lax.Precision.HIGHEST


def build_tables():
    points = GLL_POINTS
    degree = len(points) - 1
    previous = points * 0.0 + 1.0
    current = points.copy()
    for k in range(1, degree):
        following = ((2 * k + 1) * points * current - k * previous) / (k + 1)
        previous = current
        current = following
    legendre = current
    derivative = np.zeros((degree + 1, degree + 1))
    for i in range(degree + 1):
        for j in range(degree + 1):
            if i != j:
                derivative[i, j] = legendre[i] / (legendre[j] * (points[i] - points[j]))
    derivative[0, 0] = -degree * (degree + 1) / 4.0
    derivative[degree, degree] = degree * (degree + 1) / 4.0
    weights = 2.0 / (degree * (degree + 1) * legendre ** 2)
    interp = np.stack([(1.0 - points) / 2.0, (1.0 + points) / 2.0], axis=1)
    stiff_one = derivative.T @ (weights[:, None] * derivative)
    stiff_two = interp.T @ stiff_one @ interp
    mass_two = interp.T @ (weights[:, None] * interp)
    coarse_matrix = 0.5 * (np.kron(np.kron(stiff_two, mass_two), mass_two) + np.kron(np.kron(mass_two, stiff_two), mass_two) + np.kron(np.kron(mass_two, mass_two), stiff_two))
    stiff_diag = (weights[:, None] * derivative ** 2).sum(axis=0)
    return (jnp.asarray(derivative, jnp.float32), jnp.asarray(weights, jnp.float32), jnp.asarray(interp, jnp.float32), jnp.asarray(coarse_matrix, jnp.float32), jnp.asarray(stiff_diag, jnp.float32))


def edge_flags(size_n, first, elem_count, total):
    node_index = jnp.arange(size_n, dtype=jnp.int32)[:, None]
    elem_index = first + jnp.arange(elem_count, dtype=jnp.int32)[None, :]
    outer = ((node_index == 0) & (elem_index == 0)) | ((node_index == size_n - 1) & (elem_index == total - 1))
    interior = jnp.where(outer, jnp.float32(0.0), jnp.float32(1.0))
    owner_flag = jnp.where((node_index == 0) & (elem_index > 0), jnp.float32(0.0), jnp.float32(1.0))
    return interior, owner_flag


def tensor_flags(flag_x, flag_y, flag_z):
    combined = flag_x[:, None, None, :, None, None] * flag_y[None, :, None, None, :, None] * flag_z[None, None, :, None, None, :]
    dims_all = combined.shape
    return combined.reshape(dims_all[0], dims_all[1], dims_all[2], dims_all[3], dims_all[4] * dims_all[5])


def assemble_side(grid_vals, node_dim, elem_dim, fetcher):
    last_node = grid_vals.shape[node_dim] - 1
    elem_count = grid_vals.shape[elem_dim]
    lower_face = lax.index_in_dim(grid_vals, 0, node_dim, keepdims=False)
    upper_face = lax.index_in_dim(grid_vals, last_node, node_dim, keepdims=False)
    paired = jnp.stack([lower_face, upper_face], 0)
    if fetcher is None:
        widths = [(0, 0)] * paired.ndim
        widths[elem_dim] = (1, 1)
        extended = jnp.pad(paired, widths)
    else:
        extended = fetcher(paired)
    from_below = lax.slice_in_dim(extended[1], 0, elem_count, axis=elem_dim - 1)
    from_above = lax.slice_in_dim(extended[0], 2, elem_count + 2, axis=elem_dim - 1)
    middle = lax.slice_in_dim(grid_vals, 1, last_node, axis=node_dim)
    return jnp.concatenate([jnp.expand_dims(lower_face + from_below, node_dim), middle, jnp.expand_dims(upper_face + from_above, node_dim)], node_dim)


def assemble(grid_vals, slab_width, fetch_x, fetch_y):
    dims_all = grid_vals.shape
    blocks = grid_vals.reshape(dims_all[0], dims_all[1], dims_all[2], dims_all[3], dims_all[4] // slab_width, slab_width)
    blocks = assemble_side(blocks, 0, 3, fetch_x)
    blocks = assemble_side(blocks, 1, 4, fetch_y)
    blocks = assemble_side(blocks, 2, 5, None)
    return blocks.reshape(dims_all)


def stiffness(grid_vals, derivative, half_weights):
    grad_x = jnp.einsum('ai,ijklm->ajklm', derivative, grid_vals, precision=HIGHEST)
    grad_y = jnp.einsum('aj,ijklm->iaklm', derivative, grid_vals, precision=HIGHEST)
    grad_z = jnp.einsum('ak,ijklm->ijalm', derivative, grid_vals, precision=HIGHEST)
    return (jnp.einsum('ai,ajklm->ijklm', derivative, half_weights * grad_x, precision=HIGHEST) + jnp.einsum('aj,iaklm->ijklm', derivative, half_weights * grad_y, precision=HIGHEST) + jnp.einsum('ak,ijalm->ijklm', derivative, half_weights * grad_z, precision=HIGHEST))


def weak_divergence(forces, derivative, tensor_weights):
    return 0.25 * (jnp.einsum('ai,ajklm->ijklm', derivative, tensor_weights * forces[0], precision=HIGHEST) + jnp.einsum('aj,iaklm->ijklm', derivative, tensor_weights * forces[1], precision=HIGHEST) + jnp.einsum('ak,ijalm->ijklm', derivative, tensor_weights * forces[2], precision=HIGHEST))


def restrict(grid_vals, interp):
    return jnp.einsum('ia,jb,kc,ijklm->abclm', interp, interp, interp, grid_vals, precision=HIGHEST)


def prolong(vertex_vals, interp):
    return jnp.einsum('ia,jb,kc,abclm->ijklm', interp, interp, interp, vertex_vals, precision=HIGHEST)


def coarse_apply(vertex_vals, coarse_matrix):
    dims_all = vertex_vals.shape
    flattened = vertex_vals.reshape(8, dims_all[3] * dims_all[4])
    return jnp.dot(coarse_matrix, flattened, precision=HIGHEST).reshape(dims_all)


def gauss_factor(position, base_elem, first, elem_count):
    points = jnp.asarray(GLL_POINTS, jnp.float32)
    elem_index = first + jnp.arange(elem_count, dtype=jnp.int32)
    coords = elem_index.astype(jnp.float32)[None, :] + 0.5 * (1.0 + points)[:, None]
    distance = coords[None, :, :] - position[:, None, None]
    node_index = jnp.arange(8, dtype=jnp.int32)[None, :, None]
    elem_grid = elem_index[None, None, :]
    base_grid = base_elem[:, None, None]
    inside = (elem_grid == base_grid) | (elem_grid == base_grid + 1) | ((elem_grid == base_grid - 1) & (node_index == 7)) | ((elem_grid == base_grid + 2) & (node_index == 0))
    return jnp.where(inside, jnp.exp(-(distance * distance) / (WIDTH_EPS * WIDTH_EPS)), jnp.float32(0.0))


def spread_forces(base_elem, offset, force, first_x, count_x, first_y, count_y, depth):
    position = base_elem.astype(jnp.float32) + 1.0 + offset
    factor_x = gauss_factor(position[0], base_elem[0], first_x, count_x)
    factor_y = gauss_factor(position[1], base_elem[1], first_y, count_y)
    factor_z = gauss_factor(position[2], base_elem[2], 0, depth)
    spread = jnp.einsum('cp,pie,pjf,pkg->cijkefg', GAUSS_NORM * force, factor_x, factor_y, factor_z, precision=HIGHEST)
    return spread.reshape(3, 8, 8, 8, count_x, count_y * depth)


def chebyshev_pass(solution, residual, operate, inverse_diag, need_residual):
    theta_mid = 0.5 * (CHEB_HIGH + CHEB_LOW)
    delta_half = 0.5 * (CHEB_HIGH - CHEB_LOW)
    rho_first = delta_half / theta_mid
    rho_second = 1.0 / (2.0 * theta_mid / delta_half - rho_first)
    update = inverse_diag * residual / theta_mid
    solution = solution + update
    residual = residual - operate(update)
    update = rho_second * rho_first * update + (2.0 * rho_second / delta_half) * inverse_diag * residual
    solution = solution + update
    if need_residual:
        residual = residual - operate(update)
    return solution, residual


def coarse_cg_classic(right_side, operate, owner_flag, reduce_curv, reduce_norm):
    solution = jnp.zeros_like(right_side)
    residual = right_side
    direction = right_side
    norm_now = reduce_norm(jnp.sum(owner_flag * residual * residual))
    for step in range(CG_STEPS):
        image = operate(direction)
        alpha = norm_now / reduce_curv(jnp.sum(owner_flag * direction * image))
        solution = solution + alpha * direction
        residual = residual - alpha * image
        norm_next = reduce_norm(jnp.sum(owner_flag * residual * residual))
        direction = residual + (norm_next / norm_now) * direction
        norm_now = norm_next
    return solution


def vcycle(solution, right_side, operate, inverse_diag, own_fine, mask_fine, interp, solve_coarse):
    residual = right_side - operate(solution)
    solution, residual = chebyshev_pass(solution, residual, operate, inverse_diag, True)
    correction = solve_coarse(restrict(own_fine * residual, interp))
    solution = solution + mask_fine * prolong(correction, interp)
    residual = right_side - operate(solution)
    solution, residual = chebyshev_pass(solution, residual, operate, inverse_diag, False)
    return solution


def reference(source, point_base, point_offset, point_force):
    derivative, weights, interp, coarse_matrix, stiff_diag = build_tables()
    tensor_weights = (weights[:, None, None] * weights[None, :, None] * weights[None, None, :])[:, :, :, None, None]
    half_weights = 0.5 * tensor_weights
    kept_x, own_x = edge_flags(8, 0, NE1, NE1)
    kept_y, own_y = edge_flags(8, 0, NE2, NE2)
    kept_z, own_z = edge_flags(8, 0, EZ, EZ)
    mask_fine = tensor_flags(kept_x, kept_y, kept_z)
    own_fine = tensor_flags(own_x, own_y, own_z)
    vkept_x, vown_x = edge_flags(2, 0, NE1, NE1)
    vkept_y, vown_y = edge_flags(2, 0, NE2, NE2)
    vkept_z, vown_z = edge_flags(2, 0, EZ, EZ)
    mask_vertex = tensor_flags(vkept_x, vkept_y, vkept_z)
    own_vertex = tensor_flags(vown_x, vown_y, vown_z)
    forces = spread_forces(point_base, point_offset, point_force, 0, NE1, 0, NE2, EZ)
    right_side = mask_fine * assemble(source + weak_divergence(forces, derivative, tensor_weights), EZ, None, None)
    diag_local = 0.5 * (stiff_diag[:, None, None] * weights[None, :, None] * weights[None, None, :] + weights[:, None, None] * stiff_diag[None, :, None] * weights[None, None, :] + weights[:, None, None] * weights[None, :, None] * stiff_diag[None, None, :])
    diagonal = assemble(jnp.broadcast_to(diag_local[:, :, :, None, None], source.shape), EZ, None, None)
    inverse_diag = mask_fine / diagonal

    def operate(grid_vals):
        return mask_fine * assemble(stiffness(grid_vals, derivative, half_weights), EZ, None, None)

    def operate_coarse(vertex_vals):
        return mask_vertex * assemble(coarse_apply(vertex_vals, coarse_matrix), EZ, None, None)

    def plain_sum(value):
        return value

    def solve_coarse(local_load):
        assembled = mask_vertex * assemble(local_load, EZ, None, None)
        return coarse_cg_classic(assembled, operate_coarse, own_vertex, plain_sum, plain_sum)

    solution = jnp.zeros_like(source)
    for cycle in range(CYCLES):
        solution = vcycle(solution, right_side, operate, inverse_diag, own_fine, mask_fine, interp, solve_coarse)
    return solution, forces
```

```python
import functools
import math

import jax
import jax.numpy as jnp
import numpy as np
from jax import lax
from jax.experimental import pallas as pl
from jax.experimental.pallas import tpu as pltpu
from jax.sharding import PartitionSpec as P

EZ = 64
CG_STEPS = 4
CYCLES = 2
N = 8
GLL_POINTS = np.array(
    [
        -1.0,
        -0.8717401485096066,
        -0.5917001814331423,
        -0.2092992179024789,
        0.2092992179024789,
        0.5917001814331423,
        0.8717401485096066,
        1.0,
    ]
)
WIDTH_EPS = 0.35
GAUSS_NORM = 1.0 / (math.pi**1.5 * WIDTH_EPS**3)
CHEB_LOW = 1.5
CHEB_HIGH = 12.0
THETA = 0.5 * (CHEB_HIGH + CHEB_LOW)
DELTA = 0.5 * (CHEB_HIGH - CHEB_LOW)
RHO_FIRST = DELTA / THETA
RHO_SECOND = 1.0 / (2.0 * THETA / DELTA - RHO_FIRST)
HIGHEST = lax.Precision.HIGHEST
F32 = jnp.float32
BF16 = jnp.bfloat16
PAD = 128
FACE = N * N


def build_tables():
    points = GLL_POINTS
    degree = len(points) - 1
    previous = points * 0.0 + 1.0
    current = points.copy()
    for k in range(1, degree):
        following = ((2 * k + 1) * points * current - k * previous) / (k + 1)
        previous = current
        current = following
    derivative = np.zeros((degree + 1, degree + 1))
    for i in range(degree + 1):
        for j in range(degree + 1):
            if i != j:
                derivative[i, j] = current[i] / (current[j] * (points[i] - points[j]))
    derivative[0, 0] = -degree * (degree + 1) / 4.0
    derivative[degree, degree] = degree * (degree + 1) / 4.0
    weights = 2.0 / (degree * (degree + 1) * current**2)
    interp = np.stack([(1.0 - points) / 2.0, (1.0 + points) / 2.0], axis=1)
    stiff_one = derivative.T @ (weights[:, None] * derivative)
    return derivative, weights, interp, stiff_one


def kron3(a, b, c):
    return np.kron(np.kron(a, b), c)


class Layout:
    def __init__(self, mesh_x, mesh_y, tiles_x, tiles_y):
        self.mesh_x, self.mesh_y = mesh_x, mesh_y
        self.num_x, self.num_y = tiles_x * mesh_x, tiles_y * mesh_y
        self.tiles_y = tiles_y
        self.joint = EZ % (2 * mesh_x * mesh_y) == 0
        self.axis = ("ex", "ey") if self.joint else "ey"
        self.slabs = mesh_x * mesh_y if self.joint else mesh_y
        self.depth = EZ // self.slabs
        self.width = self.num_x * self.num_y * self.depth
        self.step_y = self.depth
        self.step_x = self.depth * self.num_y
        self.order = self._order()
        self.slab_of = np.argsort(self.order)

    def _order(self):
        snake = []
        if self.joint and self.mesh_x % 2 == 0 and self.mesh_y % 2 == 0:
            cols = [(x, y) for x in range(self.mesh_x // 2) for y in ((0, 1) if x % 2 == 0 else (1, 0))]
            high = self.mesh_y // 2
            for n, (x, y) in enumerate(cols):
                for z in range(high) if n % 2 == 0 else range(high - 1, -1, -1):
                    for core in range(2):
                        snake.append((x * 2 + core) * self.mesh_y + z * 2 + y)
        elif not self.joint and self.mesh_y % 8 == 0:
            for n in range(self.mesh_y // 8):
                row = list(range(8 * n, 8 * n + 8))
                snake += row if n % 2 == 0 else row[::-1]
        else:
            snake = list(range(self.slabs))
        return np.array(snake)

    def swaps(self, first):
        pairs = []
        for s in range(first, self.slabs - 1, 2):
            a, b = int(self.order[s]), int(self.order[s + 1])
            pairs += [(a, b), (b, a)]
        return pairs

    def pack_matrices(self):
        rows = self.slabs * self.tiles_y * self.depth
        lanes = self.tiles_y * EZ
        out = np.zeros((3, rows, lanes))
        for d in range(self.slabs):
            slab = int(self.slab_of[d])
            for e2 in range(self.tiles_y):
                for e3 in range(self.depth):
                    row = (d * self.tiles_y + e2) * self.depth + e3
                    z = slab * self.depth + e3
                    out[0, row, e2 * EZ + z] = 1
                    if e3 == 0 and z > 0:
                        out[1, row, e2 * EZ + z - 1] = 1
                    if e3 == self.depth - 1 and z < EZ - 1:
                        out[2, row, e2 * EZ + z + 1] = 1
        return out


def split(x):
    high = x.astype(BF16)
    return high, (x - high.astype(F32)).astype(BF16)


def times3(high, low, x):
    xh, xl = split(x)
    dot = functools.partial(jnp.dot, preferred_element_type=F32)
    return dot(high, xh) + dot(high, xl) + dot(low, xh)


def dot_exact(a, b, dims):
    return lax.dot_general(a, b, (dims, ((), ())), precision=HIGHEST, preferred_element_type=F32)


def roll(x, shift, axis):
    size = x.shape[axis]
    return pltpu.roll(x, shift % size, axis)


def lane_parts(lay, shape):
    lane = lax.broadcasted_iota(jnp.int32, shape, len(shape) - 1)
    part_z = lane & (lay.depth - 1)
    part_y = lax.shift_right_logical(lane, int(math.log2(lay.step_y))) & (lay.num_y - 1)
    part_x = lax.shift_right_logical(lane, int(math.log2(lay.step_x)))
    return part_x, part_y, part_z


def get_rows(ref, k):
    if ref.shape[1] == 128:
        return ref[pl.ds(k, FACE, stride=N), :]
    return jnp.concatenate([ref[pl.ds(n * N + k, 1), :] for n in range(FACE)], 0)


def set_rows(ref, k, value):
    if ref.shape[1] == 128:
        ref[pl.ds(k, FACE, stride=N), :] = value
    else:
        for n in range(FACE):
            ref[pl.ds(n * N + k, 1), :] = value[n : n + 1]


def assemble(lay, g_ref, s_ref, halo):
    _, _, part_z = lane_parts(lay, halo.shape)
    s_ref[...] = g_ref[...]
    low = get_rows(g_ref, 0)
    high = get_rows(g_ref, N - 1)
    set_rows(s_ref, 0, low + jnp.where(part_z == 0, halo, roll(high, 1, 1)))
    set_rows(s_ref, N - 1, high + jnp.where(part_z == lay.depth - 1, halo, roll(low, -1, 1)))
    last = N - 1
    for j in range(N):
        a, b = pl.ds(j * N, N), pl.ds((last * N + j) * N, N)
        low, high = s_ref[a, :], s_ref[b, :]
        s_ref[a, :] = low + roll(high, lay.step_x, 1)
        s_ref[b, :] = high + roll(low, -lay.step_x, 1)
    for i in range(N):
        a, b = pl.ds(i * N * N, N), pl.ds((i * N + last) * N, N)
        low, high = s_ref[a, :], s_ref[b, :]
        s_ref[a, :] = low + roll(high, lay.step_y, 1)
        s_ref[b, :] = high + roll(low, -lay.step_y, 1)


def store_faces(lay, g_ref, face_ref):
    low = get_rows(g_ref, 0)
    high = get_rows(g_ref, N - 1)
    _, _, part_z = lane_parts(lay, low.shape)
    face_ref[...] = jnp.where(part_z == 0, low, high)


def halo_of(lay, slab_ref, core_ref, chip_ref):
    odd = (slab_ref[0] & 1) == 1
    core, chip = core_ref[...], chip_ref[...]
    below = jnp.where(odd, core, chip)
    above = jnp.where(odd, chip, core)
    _, _, part_z = lane_parts(lay, core.shape)
    return jnp.where(part_z == 0, roll(below, 1 - lay.depth, 1), roll(above, lay.depth - 1, 1))


def pack_kernel(lay, source_ref, perm_ref, points_ref, out_ref):
    nt = ((1,), (1,))
    body = dot_exact(perm_ref[0], source_ref[...], nt)
    below = dot_exact(perm_ref[1], get_rows(source_ref, N - 1), nt)
    above = dot_exact(perm_ref[2], get_rows(source_ref, 0), nt)
    block = lay.tiles_y * lay.depth
    tail = jnp.concatenate([below + above, jnp.broadcast_to(points_ref[...], below.shape)], 1)
    for d in range(lay.slabs):
        part = slice(d * block, (d + 1) * block)
        out_ref[d, :, : N**3] = body[part]
        out_ref[d, :, N**3 :] = tail[part]


def gauss(elem, base, position, half_nodes):
    node = lax.broadcasted_iota(jnp.int32, elem.shape, 0)
    elem = elem.astype(F32)
    away = elem + half_nodes - position
    inside = (
        (elem == base)
        | (elem == base + 1.0)
        | ((elem == base - 1.0) & (node == N - 1))
        | ((elem == base + 2.0) & (node == 0))
    )
    return jnp.where(inside, jnp.exp(-(away * away) / (WIDTH_EPS * WIDTH_EPS)), 0.0)


def right_side(lay, num_points, slab_ref, points_ref, nodes_ref, dcols_ref, g_ref, halo_ref):
    shape = (N, lay.width)
    part_x, part_y, part_z = lane_parts(lay, shape)
    first_z = slab_ref[0] * lay.depth
    elem_z = first_z + part_z
    elem_halo = jnp.where(part_z == 0, first_z - 1, first_z + lay.depth)

    def weighted(elem, base, position):
        plain = nodes_ref[1] * gauss(elem, base, position, nodes_ref[0])
        deriv = dcols_ref[0] * plain[0:1]
        for a in range(1, N):
            deriv = deriv + dcols_ref[a] * plain[a : a + 1]
        return plain, deriv

    def one(p, _):
        base = [points_ref[p, d] for d in range(3)]
        position = [points_ref[p, d] + 1.0 + points_ref[p, 3 + d] for d in range(3)]
        force = [points_ref[p, 6 + d] * (0.25 * GAUSS_NORM) for d in range(3)]
        first = first_z.astype(F32)

        @pl.when((base[2] + 2.0 >= first - 1.0) & (base[2] - 1.0 <= first + lay.depth))
        def _():
            x0, x1 = weighted(part_x, base[0], position[0])
            y0, y1 = weighted(part_y, base[1], position[1])
            z0, z1 = weighted(elem_z, base[2], position[2])
            h0, h1 = weighted(elem_halo, base[2], position[2])
            pick = part_z[0:1] == 0
            h0 = jnp.where(pick, h0[N - 1 : N], h0[0:1])
            h1 = jnp.where(pick, h1[N - 1 : N], h1[0:1])
            x1 = force[0] * x1
            fz1 = force[2] * z1
            fz0 = force[1] * z0
            for j in range(N):
                first_part = y0[j : j + 1] * z0
                other_part = y1[j : j + 1] * fz0 + y0[j : j + 1] * fz1
                for i in range(N):
                    rows = pl.ds((i * N + j) * N, N)
                    g_ref[rows, :] += x1[i : i + 1] * first_part + x0[i : i + 1] * other_part
            first_part = y0 * h0
            other_part = y1 * (force[1] * h0) + y0 * (force[2] * h1)
            for i in range(N):
                rows = pl.ds(i * N, N)
                halo_ref[rows, :] += x1[i : i + 1] * first_part + x0[i : i + 1] * other_part

        return 0

    lax.fori_loop(0, num_points, one, 0)


def inverse_diagonal(lay, slab_ref, factor_ref, dinv_ref):
    shape = (N, lay.width)
    part_x, part_y, part_z = lane_parts(lay, shape)
    part_z = slab_ref[0] * lay.depth + part_z
    node = lax.broadcasted_iota(jnp.int32, shape, 0)

    def share(low, high):
        return (
            jnp.where(low, 0.0, 0.5),
            jnp.where(high, 0.0, 0.5),
        )

    low_z, high_z = share(part_z == 0, part_z == EZ - 1)
    along_z = jnp.where(node == 0, low_z, jnp.where(node == N - 1, high_z, 1.0))
    along_x = dict(zip((0, N - 1), share(part_x == 0, part_x == lay.num_x - 1)))
    along_y = dict(zip((0, N - 1), share(part_y == 0, part_y == lay.num_y - 1)))
    for i in range(N):
        for j in range(N):
            rows = pl.ds((i * N + j) * N, N)
            value = factor_ref[rows, :] * along_z
            if i in along_x:
                value = value * along_x[i]
            if j in along_y:
                value = value * along_y[j]
            dinv_ref[rows, :] = value


def first_kernel(
    lay,
    num_points,
    slab_ref,
    points_ref,
    recv_ref,
    nodes_ref,
    dcols_ref,
    factor_ref,
    high_ref,
    low_ref,
    g_ref,
    x_ref,
    dinv_ref,
    face_ref,
    s_ref,
    halo_ref,
    flat_ref,
):
    count, block = recv_ref.shape[0], recv_ref.shape[1]
    for d in range(count):
        flat_ref[pl.ds(d * block, block), :] = recv_ref[d]
    g_ref[...] = flat_ref[:, : N**3].T
    halo_ref[...] = flat_ref[:, N**3 :].T[:FACE]
    inverse_diagonal(lay, slab_ref, factor_ref, dinv_ref)
    right_side(lay, num_points, slab_ref, points_ref, nodes_ref, dcols_ref, g_ref, halo_ref)
    assemble(lay, g_ref, s_ref, halo_ref[...])
    update = (1.0 / THETA) * dinv_ref[...] * s_ref[...]
    x_ref[...] = update
    g_ref[...] = g_ref[...] - times3(high_ref[...], low_ref[...], update)
    store_faces(lay, g_ref, face_ref)


def step_kernel(
    lay,
    coef_old,
    coef_new,
    kind,
    slab_ref,
    core_ref,
    chip_ref,
    g_ref,
    x_ref,
    *refs,
):
    refs = list(refs)
    u_ref = refs.pop(0) if coef_old else None
    dinv_ref = refs.pop(0)
    if kind != "last":
        high_ref, low_ref = refs.pop(0), refs.pop(0)
    if kind == "restrict":
        interp_ref = refs.pop(0)
    if kind == "last":
        out_ref, s_ref = refs
    elif kind == "restrict":
        g_out, x_out, send_ref, s_ref = refs
    else:
        g_out, x_out, u_out, face_ref, s_ref = refs
    assemble(lay, g_ref, s_ref, halo_of(lay, slab_ref, core_ref, chip_ref))
    update = coef_new * dinv_ref[...] * s_ref[...]
    if coef_old:
        update = update + coef_old * u_ref[...]
    if kind == "last":
        total = (x_ref[...] + update).T
        count, block = out_ref.shape[0], out_ref.shape[1]
        for d in range(count):
            out_ref[d] = total[d * block : (d + 1) * block]
        return
    x_out[...] = x_ref[...] + update
    g_out[...] = g_ref[...] - times3(high_ref[...], low_ref[...], update)
    if kind == "restrict":
        inner = jnp.where(dinv_ref[...] != 0.0, g_out[...], 0.0)
        load = dot_exact(interp_ref[...], inner, ((0,), (0,)))
        rows = [load[n : n + 1] for n in range(N)]
        rows = [rows[n] + roll(rows[4 + n], lay.step_x, 1) for n in range(4)]
        rows = [rows[n] + roll(rows[2 + n], lay.step_y, 1) for n in range(2)]
        for d in range(send_ref.shape[0]):
            send_ref[d, 0:1] = rows[0]
            send_ref[d, 1:2] = rows[1]
    else:
        u_out[...] = update
        store_faces(lay, g_out, face_ref)


def coarse_kernel(
    lay,
    mass,
    stiff,
    slab_ref,
    loads_ref,
    g_ref,
    x_ref,
    interp_ref,
    image_ref,
    g_out,
    x_out,
    face_ref,
    first_ref,
    second_ref,
):
    for s in range(lay.slabs):
        d = int(lay.order[s])
        first_ref[pl.ds(s, 1), :] = loads_ref[d, 0:1]
        second_ref[pl.ds(s, 1), :] = loads_ref[d, 1:2]
    shape = (lay.slabs, lay.width)
    part_x, part_y, part_z = lane_parts(lay, shape)
    row = lax.broadcasted_iota(jnp.int32, shape, 0)
    keep = ((part_x > 0) & (part_y > 0) & ((part_z > 0) | (row > 0))).astype(F32)
    bottom, top = part_z == 0, part_z == lay.depth - 1

    def below(v):
        return jnp.where(bottom, roll(roll(v, 1, 0), 1 - lay.depth, 1), roll(v, 1, 1))

    def above(v):
        return jnp.where(top, roll(roll(v, -1, 0), lay.depth - 1, 1), roll(v, -1, 1))

    def neighbours(v, step):
        return roll(v, step, 1) + roll(v, -step, 1)

    def mix(pair, v, around):
        return (2.0 * pair[0]) * v + pair[1] * around

    def operate(v):
        around = below(v) + above(v)
        mass_z, stiff_z = mix(mass, v, around), mix(stiff, v, around)
        around = neighbours(mass_z, lay.step_y)
        both = mix(mass, mass_z, around)
        rest = mix(stiff, mass_z, around) + mix(mass, stiff_z, neighbours(stiff_z, lay.step_y))
        out = mix(stiff, both, neighbours(both, lay.step_x)) + mix(
            mass, rest, neighbours(rest, lay.step_x)
        )
        return (0.5 * keep) * out

    def inner(a, b):
        return jnp.sum(jnp.sum(a * b, axis=1, keepdims=True), axis=0, keepdims=True)

    residual = keep * (first_ref[...] + below(second_ref[...]))
    direction = residual
    total = jnp.zeros(shape, F32)
    norm = inner(residual, residual)
    for step in range(CG_STEPS):
        image = operate(direction)
        alpha = norm / inner(direction, image)
        total = total + alpha * direction
        if step + 1 < CG_STEPS:
            residual = residual - alpha * image
            following = inner(residual, residual)
            direction = residual + (following / norm) * direction
            norm = following
    first_ref[...] = total
    second_ref[...] = above(total)
    mine = pl.ds(slab_ref[0], 1)
    rows = [first_ref[mine, :], second_ref[mine, :]]
    rows = rows + [roll(r, -lay.step_y, 1) for r in rows]
    rows = rows + [roll(r, -lay.step_x, 1) for r in rows]
    corner = lax.broadcasted_iota(jnp.int32, (N, lay.width), 0)
    local = jnp.broadcast_to(rows[0], (N, lay.width))
    for n in range(1, N):
        local = jnp.where(corner == n, rows[n], local)
    plain = ((1,), (0,))
    x_out[...] = x_ref[...] + dot_exact(interp_ref[...], local, plain)
    g_out[...] = g_ref[...] - dot_exact(image_ref[...], local, plain)
    store_faces(lay, g_out, face_ref)


def unpack_kernel(recv_ref, perm_ref, out_ref, flat_ref):
    count, block = recv_ref.shape[0], recv_ref.shape[1]
    for d in range(count):
        flat_ref[pl.ds(d * block, block), :] = recv_ref[d]
    out_ref[...] = dot_exact(flat_ref[...], perm_ref[0], ((0,), (0,)))


def forces_kernel(tiles_y, num_points, place_ref, points_ref, nodes_ref, out_ref):
    width = tiles_y * EZ
    shape = (N, width)
    lane = lax.broadcasted_iota(jnp.int32, shape, 1)
    first_x, first_y = place_ref[0], place_ref[1]
    elem_x = jnp.broadcast_to(first_x, shape)
    elem_y = first_y + lax.shift_right_logical(lane, int(math.log2(EZ)))
    elem_z = lane & (EZ - 1)
    out_ref[...] = jnp.zeros(out_ref.shape, F32)

    def one(p, _):
        base = [points_ref[p, d] for d in range(3)]
        position = [points_ref[p, d] + 1.0 + points_ref[p, 3 + d] for d in range(3)]
        force = [points_ref[p, 6 + d] * GAUSS_NORM for d in range(3)]
        low_x, low_y = first_x.astype(F32), first_y.astype(F32)

        @pl.when(
            (base[0] + 2.0 >= low_x)
            & (base[0] - 1.0 <= low_x)
            & (base[1] + 2.0 >= low_y)
            & (base[1] - 1.0 <= low_y + (tiles_y - 1))
        )
        def _():
            x = gauss(elem_x, base[0], position[0], nodes_ref[0])
            y = gauss(elem_y, base[1], position[1], nodes_ref[0])
            z = gauss(elem_z, base[2], position[2], nodes_ref[0])
            for j in range(N):
                plane = y[j : j + 1] * z
                for i in range(N):
                    value = x[i : i + 1] * plane
                    rows = pl.ds((i * N + j) * N, N)
                    for c in range(3):
                        out_ref[c, rows, :] += force[c] * value

        return 0

    lax.fori_loop(0, num_points, one, 0)


def call(kernel, outs, inputs, scratch=(), smem=0):
    specs = [
        pl.BlockSpec(memory_space=pltpu.SMEM if n < smem else pltpu.VMEM) for n in range(len(inputs))
    ]
    shapes = [jax.ShapeDtypeStruct(s, F32) for s in outs]
    result = pl.pallas_call(
        kernel,
        out_shape=shapes,
        in_specs=specs,
        out_specs=[pl.BlockSpec(memory_space=pltpu.VMEM)] * len(shapes),
        scratch_shapes=[pltpu.VMEM(s, F32) for s in scratch],
        compiler_params=pltpu.CompilerParams(vmem_limit_bytes=40 * 1024 * 1024),
    )(*inputs)
    return result


def shards(source, point_base, point_offset, point_force):
    tiles_x, tiles_y = source.shape[3], source.shape[4] // EZ
    lay = Layout(lax.axis_size("ex"), lax.axis_size("ey"), tiles_x, tiles_y)
    devices = lay.mesh_x * lay.mesh_y
    derivative, weights, interp, stiff_one = build_tables()
    width, fields = lay.width, (N**3, lay.width)

    diag_w = np.diag(weights)
    full = 0.5 * (
        kron3(stiff_one, diag_w, diag_w)
        + kron3(diag_w, stiff_one, diag_w)
        + kron3(diag_w, diag_w, stiff_one)
    )
    full_high = full.astype(BF16)
    full_low = (full - full_high.astype(np.float64)).astype(BF16)
    interp3 = kron3(interp, interp, interp)
    image3 = full @ interp3
    ratio = (weights[:, None] * derivative**2).sum(axis=0) / weights
    diag = 0.5 * (ratio[:, None, None] + ratio[None, :, None] + ratio[None, None, :])
    diag = diag * weights[:, None, None] * weights[None, :, None] * weights[None, None, :]
    factor = np.broadcast_to(1.0 / diag.reshape(N**3, 1), fields)
    nodes = np.stack([0.5 * (1.0 + GLL_POINTS), weights])
    nodes_wide = np.broadcast_to(nodes[:, :, None], (2, N, width))
    nodes_local = np.broadcast_to(nodes[:, :, None], (2, N, tiles_y * EZ))
    dcols = np.broadcast_to(derivative[:, :, None], (N, N, width))
    mass = interp.T @ diag_w @ interp
    stiff = interp.T @ stiff_one @ interp
    perms = jnp.asarray(lay.pack_matrices(), F32)
    high, low = jnp.asarray(full_high), jnp.asarray(full_low)
    interp3, image3 = jnp.asarray(interp3, F32), jnp.asarray(image3, F32)
    factor, nodes_wide, nodes_local, dcols = (
        jnp.asarray(t, F32) for t in (factor, nodes_wide, nodes_local, dcols)
    )

    slab = jnp.asarray(lay.slab_of, jnp.int32)[lax.axis_index(lay.axis)].reshape(1)
    place = jnp.stack([lax.axis_index("ex") * tiles_x, lax.axis_index("ey") * tiles_y]).astype(
        jnp.int32
    )

    local_points = point_base.shape[1]
    packed = jnp.concatenate([point_base.astype(F32), point_offset, point_force], 0)
    packed = packed.T.reshape(1, local_points * 9)
    packed = jnp.pad(packed, ((0, 0), (0, PAD - FACE - packed.shape[1])))
    block = lay.tiles_y * lay.depth
    (send,) = call(
        functools.partial(pack_kernel, lay),
        [(lay.slabs, block, N**3 + PAD)],
        [source.reshape(N**3, tiles_y * EZ), perms, packed],
    )
    recv = lax.all_to_all(send, lay.axis, 0, 0)
    if not lay.joint:
        recv = lax.all_gather(recv, "ex", axis=0, tiled=True)
    points = recv[:, 0, N**3 + FACE : N**3 + FACE + 9 * local_points]
    points = points.reshape(devices * local_points, 9)
    num_points = devices * local_points

    (forces,) = call(
        functools.partial(forces_kernel, tiles_y, num_points),
        [(3, N**3, tiles_y * EZ)],
        [place, points, nodes_local],
        smem=2,
    )

    def swap(face):
        return (
            lax.ppermute(face, lay.axis, lay.swaps(0)),
            lax.ppermute(face, lay.axis, lay.swaps(1)),
        )

    face_shape = (FACE, width)
    g, x, dinv, face = call(
        functools.partial(first_kernel, lay, num_points),
        [fields, fields, fields, face_shape],
        [slab, points, recv, nodes_wide, dcols, factor, high, low],
        [fields, face_shape, (width, N**3 + PAD)],
        smem=2,
    )
    u = x
    first = (0.0, 1.0 / THETA)
    second = (RHO_SECOND * RHO_FIRST, 2.0 * RHO_SECOND / DELTA)

    def step(coefs, kind, face, g, x, u):
        inputs = [slab, *swap(face), g, x]
        if coefs[0]:
            inputs.append(u)
        inputs.append(dinv)
        if kind != "last":
            inputs += [high, low]
        if kind == "restrict":
            inputs.append(interp3)
            outs = [fields, fields, (lay.slabs, 2, width)]
        elif kind == "last":
            outs = [(lay.mesh_x * lay.mesh_y, block, N**3)]
        else:
            outs = [fields, fields, fields, face_shape]
        return call(
            functools.partial(step_kernel, lay, *coefs, kind), outs, inputs, [fields], smem=1
        )

    for cycle in range(CYCLES):
        if cycle > 0:
            g, x, u, face = step(first, "plain", face, g, x, u)
        g, x, loads = step(second, "restrict", face, g, x, u)
        loads = lax.all_to_all(loads, lay.axis, 0, 0)
        g, x, face = call(
            functools.partial(coarse_kernel, lay, (mass[0, 0], mass[0, 1]), (stiff[0, 0], stiff[0, 1])),
            [fields, fields, face_shape],
            [slab, loads, g, x, interp3, image3],
            [(lay.slabs, width)] * 2,
            smem=1,
        )
        g, x, u, face = step(first, "plain", face, g, x, u)
        if cycle + 1 < CYCLES:
            g, x, u, face = step(second, "plain", face, g, x, u)
    (out,) = step(second, "last", face, g, x, u)
    if not lay.joint:
        out = lax.dynamic_slice_in_dim(out, lax.axis_index("ex") * lay.mesh_y, lay.mesh_y, 0)
    out = lax.all_to_all(out, lay.axis, 0, 0)
    (pressure,) = call(
        unpack_kernel,
        [(N**3, tiles_y * EZ)],
        [out, perms],
        [(lay.slabs * block, N**3)],
    )
    return (
        pressure.reshape(source.shape),
        forces.reshape((3, *source.shape)),
    )


def solution(mesh):
    in_specs = (
        P(None, None, None, "ex", "ey"),
        P(None, ("ex", "ey")),
        P(None, ("ex", "ey")),
        P(None, ("ex", "ey")),
    )
    out_specs = (P(None, None, None, "ex", "ey"), P(None, None, None, None, "ex", "ey"))
    return jax.shard_map(shards, mesh=mesh, in_specs=in_specs, out_specs=out_specs, check_vma=False)
```

```python
import functools
import math

import jax
import jax.numpy as jnp
import numpy as np
from jax import lax
from jax.experimental import pallas as pl
from jax.experimental.pallas import tpu as pltpu
from jax.sharding import PartitionSpec as P

EZ = 64
CG_STEPS = 4
CYCLES = 2
N = 8
GLL_POINTS = np.array(
    [
        -1.0,
        -0.8717401485096066,
        -0.5917001814331423,
        -0.2092992179024789,
        0.2092992179024789,
        0.5917001814331423,
        0.8717401485096066,
        1.0,
    ]
)
WIDTH_EPS = 0.35
GAUSS_NORM = 1.0 / (math.pi**1.5 * WIDTH_EPS**3)
CHEB_LOW = 1.5
CHEB_HIGH = 12.0
THETA = 0.5 * (CHEB_HIGH + CHEB_LOW)
DELTA = 0.5 * (CHEB_HIGH - CHEB_LOW)
RHO_FIRST = DELTA / THETA
RHO_SECOND = 1.0 / (2.0 * THETA / DELTA - RHO_FIRST)
HIGHEST = lax.Precision.HIGHEST
F32 = jnp.float32
BF16 = jnp.bfloat16
FACE = N * N


def build_tables():
    points = GLL_POINTS
    degree = len(points) - 1
    previous = points * 0.0 + 1.0
    current = points.copy()
    for k in range(1, degree):
        following = ((2 * k + 1) * points * current - k * previous) / (k + 1)
        previous = current
        current = following
    derivative = np.zeros((degree + 1, degree + 1))
    for i in range(degree + 1):
        for j in range(degree + 1):
            if i != j:
                derivative[i, j] = current[i] / (current[j] * (points[i] - points[j]))
    derivative[0, 0] = -degree * (degree + 1) / 4.0
    derivative[degree, degree] = degree * (degree + 1) / 4.0
    weights = 2.0 / (degree * (degree + 1) * current**2)
    interp = np.stack([(1.0 - points) / 2.0, (1.0 + points) / 2.0], axis=1)
    stiff_one = derivative.T @ (weights[:, None] * derivative)
    return derivative, weights, interp, stiff_one


def kron3(a, b, c):
    return np.kron(np.kron(a, b), c)


def log2(n):
    return int(n).bit_length() - 1


class Layout:
    def __init__(self, mesh_x, mesh_y, tiles_x, tiles_y):
        self.mesh_x, self.mesh_y = mesh_x, mesh_y
        self.num_x, self.num_y = tiles_x * mesh_x, tiles_y * mesh_y
        self.tiles_y = tiles_y
        self.joint = EZ % (2 * mesh_x * mesh_y) == 0
        self.axis = ("ex", "ey") if self.joint else "ey"
        self.slabs = mesh_x * mesh_y if self.joint else mesh_y
        self.depth = EZ // self.slabs
        assert self.depth == 2 and tiles_x == 1
        self.width = self.num_x * self.num_y * self.depth
        self.step_y = self.depth
        self.step_x = self.depth * self.num_y
        self.block = tiles_y * self.depth
        slab_of = [self.slab_at(d) for d in range(self.slabs)]
        self.order = [slab_of.index(s) for s in range(self.slabs)]

    def slab_at(self, d):
        if self.joint and self.mesh_x % 2 == 0 and self.mesh_y % 2 == 0:
            high = self.mesh_y // 2
            y = d & 1
            z = (d >> 1) & (high - 1)
            core = (d >> log2(self.mesh_y)) & 1
            x = d >> (log2(self.mesh_y) + 1)
            turn = y ^ (x & 1)
            return ((x * 2 + turn) * high + (z ^ (turn * (high - 1)))) * 2 + core
        if not self.joint and self.mesh_y % 8 == 0:
            return d ^ (((d >> 3) & 1) * 7)
        return d

    def swaps(self, first):
        pairs = []
        for s in range(first, self.slabs - 1, 2):
            a, b = self.order[s], self.order[s + 1]
            pairs += [(a, b), (b, a)]
        return pairs

    def permutation(self):
        shape = (self.slabs * self.block, self.tiles_y * EZ)
        row = lax.broadcasted_iota(jnp.int32, shape, 0)
        lane = lax.broadcasted_iota(jnp.int32, shape, 1)
        slab = self.slab_at(row >> log2(self.block))
        e2 = (row >> 1) & (self.tiles_y - 1)
        return (lane == e2 * EZ + slab * self.depth + (row & 1)).astype(F32)


def split(x):
    high = x.astype(BF16)
    return high, (x - high.astype(F32)).astype(BF16)


def times3(high, low, x):
    xh, xl = split(x)
    dot = functools.partial(jnp.dot, preferred_element_type=F32)
    return dot(high, xh) + dot(high, xl) + dot(low, xh)


def dot_exact(a, b, dims):
    return lax.dot_general(a, b, (dims, ((), ())), precision=HIGHEST, preferred_element_type=F32)


def roll(x, shift, axis):
    size = x.shape[axis]
    return pltpu.roll(x, shift % size, axis)


def lane_parts(lay, shape):
    lane = lax.broadcasted_iota(jnp.int32, shape, len(shape) - 1)
    part_z = lane & (lay.depth - 1)
    part_y = lax.shift_right_logical(lane, log2(lay.step_y)) & (lay.num_y - 1)
    part_x = lax.shift_right_logical(lane, log2(lay.step_x))
    return part_x, part_y, part_z


def get_rows(ref, k):
    if ref.shape[1] == 128:
        return ref[pl.ds(k, FACE, stride=N), :]
    return jnp.concatenate([ref[pl.ds(n * N + k, 1), :] for n in range(FACE)], 0)


def set_rows(ref, k, value):
    if ref.shape[1] == 128:
        ref[pl.ds(k, FACE, stride=N), :] = value
    else:
        for n in range(FACE):
            ref[pl.ds(n * N + k, 1), :] = value[n : n + 1]


def assemble_xy(lay, s_ref):
    last = N - 1
    for j in range(N):
        a, b = pl.ds(j * N, N), pl.ds((last * N + j) * N, N)
        low, high = s_ref[a, :], s_ref[b, :]
        s_ref[a, :] = low + roll(high, lay.step_x, 1)
        s_ref[b, :] = high + roll(low, -lay.step_x, 1)
    for i in range(N):
        a, b = pl.ds(i * N * N, N), pl.ds((i * N + last) * N, N)
        low, high = s_ref[a, :], s_ref[b, :]
        s_ref[a, :] = low + roll(high, lay.step_y, 1)
        s_ref[b, :] = high + roll(low, -lay.step_y, 1)


def assemble(lay, g_ref, s_ref, halo):
    _, _, part_z = lane_parts(lay, halo.shape)
    s_ref[...] = g_ref[...]
    low = get_rows(g_ref, 0)
    high = get_rows(g_ref, N - 1)
    set_rows(s_ref, 0, low + jnp.where(part_z == 0, halo, roll(high, 1, 1)))
    set_rows(s_ref, N - 1, high + jnp.where(part_z == lay.depth - 1, halo, roll(low, -1, 1)))
    assemble_xy(lay, s_ref)


def store_faces(lay, g_ref, face_ref):
    low = get_rows(g_ref, 0)
    high = get_rows(g_ref, N - 1)
    _, _, part_z = lane_parts(lay, low.shape)
    face_ref[...] = jnp.where(part_z == 0, low, high)


def halo_of(lay, slab_ref, core_ref, chip_ref):
    odd = (slab_ref[0] & 1) == 1
    core, chip = core_ref[...], chip_ref[...]
    below = jnp.where(odd, core, chip)
    above = jnp.where(odd, chip, core)
    _, _, part_z = lane_parts(lay, core.shape)
    return jnp.where(part_z == 0, roll(below, 1 - lay.depth, 1), roll(above, lay.depth - 1, 1))


def assemble_both(lay, g_ref, h_ref, s_ref, sh_ref):
    low, high = get_rows(g_ref, 0), get_rows(g_ref, N - 1)
    out_low, out_high = get_rows(h_ref, 0), get_rows(h_ref, N - 1)
    _, _, part_z = lane_parts(lay, low.shape)
    bottom = part_z == 0
    s_ref[...] = g_ref[...]
    sh_ref[...] = h_ref[...]
    set_rows(s_ref, 0, low + jnp.where(bottom, out_high, roll(high, 1, 1)))
    set_rows(s_ref, N - 1, high + jnp.where(bottom, roll(low, -1, 1), out_low))
    set_rows(sh_ref, N - 1, out_high + jnp.where(bottom, low, 0.0))
    set_rows(sh_ref, 0, out_low + jnp.where(bottom, 0.0, high))
    assemble_xy(lay, s_ref)
    assemble_xy(lay, sh_ref)


def send_layers(lay, slab_ref, g_ref, s_ref, core_ref, chip_ref):
    low, high = get_rows(g_ref, 0), get_rows(g_ref, N - 1)
    _, _, part_z = lane_parts(lay, low.shape)
    s_ref[...] = g_ref[...]
    set_rows(s_ref, N - 1, jnp.where(part_z == 0, high + roll(low, -1, 1), high))
    set_rows(s_ref, 0, jnp.where(part_z == 0, low, low + roll(high, 1, 1)))
    half = N**3 // 2
    a, b = s_ref[:half, :], s_ref[half:, :]
    _, _, part_z = lane_parts(lay, a.shape)
    bottom = part_z == 0
    first = jnp.where(bottom, a, roll(b, 1, 1))
    second = jnp.where(bottom, roll(a, -1, 1), b)
    odd = (slab_ref[0] & 1) == 1
    core_ref[...] = jnp.where(odd, first, second)
    chip_ref[...] = jnp.where(odd, second, first)


def receive_layers(lay, slab_ref, core_ref, chip_ref, h_ref):
    odd = (slab_ref[0] & 1) == 1
    core, chip = core_ref[...], chip_ref[...]
    below, above = jnp.where(odd, core, chip), jnp.where(odd, chip, core)
    _, _, part_z = lane_parts(lay, core.shape)
    bottom = part_z == 0
    half = N**3 // 2
    h_ref[:half, :] = jnp.where(bottom, below, roll(above, 1, 1))
    h_ref[half:, :] = jnp.where(bottom, roll(below, -1, 1), above)


def pack_kernel(lay, base_ref, offset_ref, force_ref, source_ref, out_ref, s_ref):
    s_ref[...] = source_ref[...]
    mean = 0.5 * (get_rows(source_ref, N - 1) + roll(get_rows(source_ref, 0), -1, 1))
    set_rows(s_ref, N - 1, mean)
    set_rows(s_ref, 0, roll(mean, 1, 1))
    body = dot_exact(lay.permutation(), s_ref[...], ((1,), (1,)))
    shape = (lay.block, N**3)
    lane = lax.broadcasted_iota(jnp.int32, shape, 1)
    points = jnp.zeros(shape, F32)
    for p in range(base_ref.shape[1]):
        values = [base_ref[d, p].astype(F32) for d in range(3)]
        values += [ref[d, p] for ref in (offset_ref, force_ref) for d in range(3)]
        for n, value in enumerate(values):
            points = jnp.where(lane == (p * 9 + n) * N, value, points)
    row = lax.broadcasted_iota(jnp.int32, shape, 0)
    used = (row == 1) & ((lane & (N - 1)) == 0)
    for d in range(lay.slabs):
        out_ref[d] = jnp.where(used, points, body[d * lay.block : (d + 1) * lay.block])


def gauss(elem, base, position, half_nodes):
    node = lax.broadcasted_iota(jnp.int32, elem.shape, 0)
    elem = elem.astype(F32)
    away = elem + half_nodes - position
    inside = (
        (elem == base)
        | (elem == base + 1.0)
        | ((elem == base - 1.0) & (node == N - 1))
        | ((elem == base + 2.0) & (node == 0))
    )
    return jnp.where(inside, jnp.exp(-(away * away) / (WIDTH_EPS * WIDTH_EPS)), 0.0)


def right_side(lay, num_points, slab_ref, points_ref, nodes_ref, dcols_ref, g_ref, halo_ref):
    shape = (N, lay.width)
    part_x, part_y, part_z = lane_parts(lay, shape)
    first_z = slab_ref[0] * lay.depth
    elem_z = first_z + part_z
    elem_halo = jnp.where(part_z == 0, first_z - 1, first_z + lay.depth)

    def weighted(elem, base, position):
        plain = nodes_ref[1] * gauss(elem, base, position, nodes_ref[0])
        deriv = dcols_ref[0] * plain[0:1]
        for a in range(1, N):
            deriv = deriv + dcols_ref[a] * plain[a : a + 1]
        return plain, deriv

    def one(p, _):
        base = [points_ref[p, d] for d in range(3)]
        position = [points_ref[p, d] + 1.0 + points_ref[p, 3 + d] for d in range(3)]
        force = [points_ref[p, 6 + d] * (0.25 * GAUSS_NORM) for d in range(3)]
        first = first_z.astype(F32)

        @pl.when((base[2] + 2.0 >= first - 1.0) & (base[2] - 1.0 <= first + lay.depth))
        def _():
            x0, x1 = weighted(part_x, base[0], position[0])
            y0, y1 = weighted(part_y, base[1], position[1])
            z0, z1 = weighted(elem_z, base[2], position[2])
            h0, h1 = weighted(elem_halo, base[2], position[2])
            pick = part_z[0:1] == 0
            h0 = jnp.where(pick, h0[N - 1 : N], h0[0:1])
            h1 = jnp.where(pick, h1[N - 1 : N], h1[0:1])
            x1 = force[0] * x1
            fz1 = force[2] * z1
            fz0 = force[1] * z0
            for j in range(N):
                first_part = y0[j : j + 1] * z0
                other_part = y1[j : j + 1] * fz0 + y0[j : j + 1] * fz1
                for i in range(N):
                    rows = pl.ds((i * N + j) * N, N)
                    g_ref[rows, :] += x1[i : i + 1] * first_part + x0[i : i + 1] * other_part
            first_part = y0 * h0
            other_part = y1 * (force[1] * h0) + y0 * (force[2] * h1)
            for i in range(N):
                rows = pl.ds(i * N, N)
                halo_ref[rows, :] += x1[i : i + 1] * first_part + x0[i : i + 1] * other_part

        return 0

    lax.fori_loop(0, num_points, one, 0)


def inverse_diagonal(lay, slab_ref, factor_ref, dinv_ref, outer):
    shape = (N, lay.width)
    part_x, part_y, part_z = lane_parts(lay, shape)
    first = slab_ref[0] * lay.depth
    part_z = jnp.where(part_z == 0, first - 1, first + lay.depth) if outer else first + part_z
    node = lax.broadcasted_iota(jnp.int32, shape, 0)

    def share(low, high):
        return (
            jnp.where(low, 0.0, 0.5),
            jnp.where(high, 0.0, 0.5),
        )

    low_z, high_z = share(part_z == 0, part_z == EZ - 1)
    along_z = jnp.where(node == 0, low_z, jnp.where(node == N - 1, high_z, 1.0))
    if outer:
        along_z = jnp.where((part_z < 0) | (part_z >= EZ), 0.0, along_z)
    along_x = dict(zip((0, N - 1), share(part_x == 0, part_x == lay.num_x - 1)))
    along_y = dict(zip((0, N - 1), share(part_y == 0, part_y == lay.num_y - 1)))
    for i in range(N):
        for j in range(N):
            rows = pl.ds((i * N + j) * N, N)
            value = factor_ref[rows, :] * along_z
            if i in along_x:
                value = value * along_x[i]
            if j in along_y:
                value = value * along_y[j]
            dinv_ref[rows, :] = value


def diagonal_kernel(lay, slab_ref, factor_ref, dinv_ref, outer_ref):
    inverse_diagonal(lay, slab_ref, factor_ref, dinv_ref, False)
    inverse_diagonal(lay, slab_ref, factor_ref, outer_ref, True)


def first_kernel(
    lay,
    num_points,
    slab_ref,
    points_ref,
    recv_ref,
    nodes_ref,
    dcols_ref,
    dinv_ref,
    high_ref,
    low_ref,
    g_ref,
    x_ref,
    face_ref,
    s_ref,
    halo_ref,
    flat_ref,
):
    count, block = recv_ref.shape[0], recv_ref.shape[1]
    for d in range(count):
        flat_ref[pl.ds(d * block, block), :] = recv_ref[d]
    g_ref[...] = flat_ref[...].T
    low, high = get_rows(g_ref, 0), get_rows(g_ref, N - 1)
    _, _, part_z = lane_parts(lay, low.shape)
    set_rows(g_ref, 0, jnp.where(part_z == 0, low, roll(high, 1, 1)))
    halo_ref[...] = jnp.where(part_z == 0, low, high)
    right_side(lay, num_points, slab_ref, points_ref, nodes_ref, dcols_ref, g_ref, halo_ref)
    assemble(lay, g_ref, s_ref, halo_ref[...])
    update = (1.0 / THETA) * dinv_ref[...] * s_ref[...]
    x_ref[...] = update
    g_ref[...] = g_ref[...] - times3(high_ref[...], low_ref[...], update)
    store_faces(lay, g_ref, face_ref)


def restriction(lay, g_ref, dinv_ref, interp_ref, send_ref):
    inner = jnp.where(dinv_ref[...] != 0.0, g_ref[...], 0.0)
    load = dot_exact(interp_ref[...], inner, ((0,), (0,)))
    rows = [load[n : n + 1] for n in range(N)]
    rows = [rows[n] + roll(rows[4 + n], lay.step_x, 1) for n in range(4)]
    rows = [rows[n] + roll(rows[2 + n], lay.step_y, 1) for n in range(2)]
    for d in range(send_ref.shape[0]):
        send_ref[d, 0:1] = rows[0]
        send_ref[d, 1:2] = rows[1]


OLD = RHO_SECOND * RHO_FIRST
NEW = 2.0 * RHO_SECOND / DELTA


def second_kernel(
    lay,
    slab_ref,
    core_ref,
    chip_ref,
    g_ref,
    x_ref,
    dinv_ref,
    high_ref,
    low_ref,
    interp_ref,
    g_out,
    x_out,
    send_ref,
    core_out,
    chip_out,
    s_ref,
):
    assemble(lay, g_ref, s_ref, halo_of(lay, slab_ref, core_ref, chip_ref))
    update = OLD * x_ref[...] + NEW * dinv_ref[...] * s_ref[...]
    x_out[...] = x_ref[...] + update
    g_out[...] = g_ref[...] - times3(high_ref[...], low_ref[...], update)
    restriction(lay, g_out, dinv_ref, interp_ref, send_ref)
    send_layers(lay, slab_ref, g_out, s_ref, core_out, chip_out)


def solve_coarse(lay, mass, stiff, loads_ref, first_ref, second_ref):
    for s in range(lay.slabs):
        d = lay.order[s]
        first_ref[pl.ds(s, 1), :] = loads_ref[d, 0:1]
        second_ref[pl.ds(s, 1), :] = loads_ref[d, 1:2]
    shape = (lay.slabs, lay.width)
    part_x, part_y, part_z = lane_parts(lay, shape)
    row = lax.broadcasted_iota(jnp.int32, shape, 0)
    keep = ((part_x > 0) & (part_y > 0) & ((part_z > 0) | (row > 0))).astype(F32)
    bottom = part_z == 0

    def below(v):
        return jnp.where(bottom, roll(roll(v, 1, 0), -1, 1), roll(v, 1, 1))

    def above(v):
        return jnp.where(bottom, roll(v, -1, 1), roll(roll(v, -1, 0), 1, 1))

    def neighbours(v, step):
        return roll(v, step, 1) + roll(v, -step, 1)

    def mix(pair, v, around):
        return (2.0 * pair[0]) * v + pair[1] * around

    def operate(v):
        around = below(v) + above(v)
        mass_z, stiff_z = mix(mass, v, around), mix(stiff, v, around)
        around = neighbours(mass_z, lay.step_y)
        both = mix(mass, mass_z, around)
        rest = mix(stiff, mass_z, around) + mix(mass, stiff_z, neighbours(stiff_z, lay.step_y))
        out = mix(stiff, both, neighbours(both, lay.step_x)) + mix(
            mass, rest, neighbours(rest, lay.step_x)
        )
        return (0.5 * keep) * out

    def inner(a, b):
        return jnp.sum(jnp.sum(a * b, axis=1, keepdims=True), axis=0, keepdims=True)

    here = pl.ds(0, lay.slabs)
    residual = keep * (first_ref[here, :] + below(second_ref[here, :]))
    direction = residual
    total = jnp.zeros(shape, F32)
    norm = inner(residual, residual)
    for step in range(CG_STEPS):
        image = operate(direction)
        alpha = norm / inner(direction, image)
        total = total + alpha * direction
        if step + 1 < CG_STEPS:
            residual = residual - alpha * image
            following = inner(residual, residual)
            direction = residual + (following / norm) * direction
            norm = following
    here = pl.ds(N, lay.slabs)
    for ref, value in ((first_ref, total), (second_ref, above(total))):
        ref[...] = jnp.zeros(ref.shape, F32)
        ref[here, :] = value


def corners(lay, low, high):
    rows = [low, high]
    rows = rows + [roll(r, -lay.step_y, 1) for r in rows]
    rows = rows + [roll(r, -lay.step_x, 1) for r in rows]
    corner = lax.broadcasted_iota(jnp.int32, (N, lay.width), 0)
    local = jnp.broadcast_to(rows[0], (N, lay.width))
    for n in range(1, N):
        local = jnp.where(corner == n, rows[n], local)
    return local


def prolong_coarse(lay, slab_ref, first_ref, second_ref, interp_ref, image_ref, edge_ref, g_ref, h_ref, x_ref):
    mine = slab_ref[0] + N
    _, _, part_z = lane_parts(lay, (1, lay.width))
    bottom = part_z == 0
    own, outer, far = [], [], []
    for ref in (first_ref, second_ref):
        before, here, after = (ref[pl.ds(mine + shift, 1), :] for shift in (-1, 0, 1))
        own.append(here)
        outer.append(jnp.where(bottom, roll(before, -1, 1), roll(after, 1, 1)))
        far.append(jnp.where(bottom, before, after))
    plain = ((1,), (0,))
    local = corners(lay, *own)
    x_ref[...] += dot_exact(interp_ref[...], local, plain)
    g_ref[...] -= dot_exact(image_ref[...], local, plain)
    h_ref[...] -= dot_exact(image_ref[...], corners(lay, *outer), plain)
    edge = dot_exact(edge_ref[...], corners(lay, *far), plain)
    low, high = get_rows(h_ref, 0), get_rows(h_ref, N - 1)
    set_rows(h_ref, 0, low - jnp.where(bottom, edge[FACE:], 0.0))
    set_rows(h_ref, N - 1, high - jnp.where(bottom, 0.0, edge[:FACE]))


def pair_kernel(lay, coarse, kind, slab_ref, core_ref, chip_ref, g_ref, x_ref, dinv_ref, outer_ref, *refs):
    refs = list(refs)
    high_ref, low_ref, edge_high_ref, edge_low_ref = (refs.pop(0) for _ in range(4))
    if coarse:
        loads_ref, image_ref, image_edge_ref = (refs.pop(0) for _ in range(3))
    if coarse or kind == "restrict":
        interp_ref = refs.pop(0)
    if kind == "last":
        out_ref = refs.pop(0)
    else:
        g_out, x_out = refs.pop(0), refs.pop(0)
        if kind == "restrict":
            send_ref = refs.pop(0)
        core_out, chip_out = refs.pop(0), refs.pop(0)
    s_ref, sh_ref, h_ref = (refs.pop(0) for _ in range(3))
    if kind == "last":
        g_out, x_out = refs.pop(0), refs.pop(0)

    g_out[...] = g_ref[...]
    x_out[...] = x_ref[...]
    receive_layers(lay, slab_ref, core_ref, chip_ref, h_ref)
    if coarse:
        first_ref, second_ref = refs
        solve_coarse(lay, *coarse, loads_ref, first_ref, second_ref)
        prolong_coarse(
            lay, slab_ref, first_ref, second_ref, interp_ref, image_ref, image_edge_ref, g_out, h_ref, x_out
        )
    assemble_both(lay, g_out, h_ref, s_ref, sh_ref)
    update = (1.0 / THETA) * dinv_ref[...] * s_ref[...]
    outer = (1.0 / THETA) * outer_ref[...] * sh_ref[...]
    high, low = high_ref[...], low_ref[...]
    edge = times3(edge_high_ref[...], edge_low_ref[...], outer)
    _, _, part_z = lane_parts(lay, (FACE, lay.width))
    near = jnp.where(
        part_z == 0, get_rows(h_ref, N - 1) - edge[FACE:], get_rows(h_ref, 0) - edge[:FACE]
    )
    g_out[...] -= times3(high, low, update)
    assemble(lay, g_out, s_ref, near)
    following = OLD * update + NEW * dinv_ref[...] * s_ref[...]
    if kind == "last":
        total = (x_out[...] + (update + following)).T
        count, block = out_ref.shape[0], out_ref.shape[1]
        for d in range(count):
            out_ref[d] = total[d * block : (d + 1) * block]
        return
    x_out[...] += update + following
    g_out[...] -= times3(high, low, following)
    if kind == "restrict":
        restriction(lay, g_out, dinv_ref, interp_ref, send_ref)
    send_layers(lay, slab_ref, g_out, s_ref, core_out, chip_out)


def unpack_kernel(lay, recv_ref, out_ref, flat_ref):
    count, block = recv_ref.shape[0], recv_ref.shape[1]
    for d in range(count):
        flat_ref[pl.ds(d * block, block), :] = recv_ref[d]
    out_ref[...] = dot_exact(flat_ref[...], lay.permutation(), ((0,), (0,)))


def forces_kernel(tiles_y, num_points, place_ref, points_ref, nodes_ref, out_ref):
    width = tiles_y * EZ
    shape = (N, width)
    lane = lax.broadcasted_iota(jnp.int32, shape, 1)
    first_x, first_y = place_ref[0], place_ref[1]
    elem_x = jnp.broadcast_to(first_x, shape)
    elem_y = first_y + lax.shift_right_logical(lane, log2(EZ))
    elem_z = lane & (EZ - 1)
    out_ref[...] = jnp.zeros(out_ref.shape, F32)

    def one(p, _):
        base = [points_ref[p, d] for d in range(3)]
        position = [points_ref[p, d] + 1.0 + points_ref[p, 3 + d] for d in range(3)]
        force = [points_ref[p, 6 + d] * GAUSS_NORM for d in range(3)]
        low_x, low_y = first_x.astype(F32), first_y.astype(F32)

        @pl.when(
            (base[0] + 2.0 >= low_x)
            & (base[0] - 1.0 <= low_x)
            & (base[1] + 2.0 >= low_y)
            & (base[1] - 1.0 <= low_y + (tiles_y - 1))
        )
        def _():
            x = gauss(elem_x, base[0], position[0], nodes_ref[0])
            y = gauss(elem_y, base[1], position[1], nodes_ref[0])
            z = gauss(elem_z, base[2], position[2], nodes_ref[0])
            for j in range(N):
                plane = y[j : j + 1] * z
                for i in range(N):
                    value = x[i : i + 1] * plane
                    rows = pl.ds((i * N + j) * N, N)
                    for c in range(3):
                        out_ref[c, rows, :] += force[c] * value

        return 0

    lax.fori_loop(0, num_points, one, 0)


def call(kernel, outs, inputs, scratch=(), smem=0):
    specs = [
        pl.BlockSpec(memory_space=pltpu.SMEM if n < smem else pltpu.VMEM) for n in range(len(inputs))
    ]
    shapes = [jax.ShapeDtypeStruct(s, F32) for s in outs]
    result = pl.pallas_call(
        kernel,
        out_shape=shapes,
        in_specs=specs,
        out_specs=[pl.BlockSpec(memory_space=pltpu.VMEM)] * len(shapes),
        scratch_shapes=[pltpu.VMEM(s, F32) for s in scratch],
        compiler_params=pltpu.CompilerParams(vmem_limit_bytes=40 * 1024 * 1024),
    )(*inputs)
    return result


def shards(source, point_base, point_offset, point_force):
    tiles_x, tiles_y = source.shape[3], source.shape[4] // EZ
    lay = Layout(lax.axis_size("ex"), lax.axis_size("ey"), tiles_x, tiles_y)
    devices = lay.mesh_x * lay.mesh_y
    derivative, weights, interp, stiff_one = build_tables()
    width, fields = lay.width, (N**3, lay.width)

    diag_w = np.diag(weights)
    full = 0.5 * (
        kron3(stiff_one, diag_w, diag_w)
        + kron3(diag_w, stiff_one, diag_w)
        + kron3(diag_w, diag_w, stiff_one)
    )
    full_high = full.astype(BF16)
    full_low = (full - full_high.astype(np.float64)).astype(BF16)
    interp3 = kron3(interp, interp, interp)
    image3 = full @ interp3
    ratio = (weights[:, None] * derivative**2).sum(axis=0) / weights
    diag = 0.5 * (ratio[:, None, None] + ratio[None, :, None] + ratio[None, None, :])
    diag = diag * weights[:, None, None] * weights[None, :, None] * weights[None, None, :]
    factor = np.broadcast_to(1.0 / diag.reshape(N**3, 1), fields)
    nodes = np.stack([0.5 * (1.0 + GLL_POINTS), weights])
    nodes_wide = np.broadcast_to(nodes[:, :, None], (2, N, width))
    nodes_local = np.broadcast_to(nodes[:, :, None], (2, N, tiles_y * EZ))
    dcols = np.broadcast_to(derivative[:, :, None], (N, N, width))
    mass = interp.T @ diag_w @ interp
    stiff = interp.T @ stiff_one @ interp
    edge_rows = np.concatenate([np.arange(FACE) * N, np.arange(FACE) * N + N - 1])
    high, low = jnp.asarray(full_high), jnp.asarray(full_low)
    edge_high, edge_low = jnp.asarray(full_high[edge_rows]), jnp.asarray(full_low[edge_rows])
    image_edge = jnp.asarray(image3[edge_rows], F32)
    interp3, image3 = jnp.asarray(interp3, F32), jnp.asarray(image3, F32)
    factor, nodes_wide, nodes_local, dcols = (
        jnp.asarray(t, F32) for t in (factor, nodes_wide, nodes_local, dcols)
    )

    slab = lay.slab_at(lax.axis_index(lay.axis).astype(jnp.int32)).reshape(1)
    place = jnp.stack([lax.axis_index("ex") * tiles_x, lax.axis_index("ey") * tiles_y]).astype(
        jnp.int32
    )

    local_points = point_base.shape[1]
    block = lay.block
    (send,) = call(
        functools.partial(pack_kernel, lay),
        [(lay.slabs, block, N**3)],
        [point_base, point_offset, point_force, source.reshape(N**3, tiles_y * EZ)],
        [(N**3, tiles_y * EZ)],
        smem=3,
    )
    recv = lax.all_to_all(send, lay.axis, 0, 0)
    if not lay.joint:
        recv = lax.all_gather(recv, "ex", axis=0, tiled=True)
    points = recv[:, 1, : 9 * N * local_points : N]
    num_points = devices * local_points
    points = points.reshape(num_points, 9)
    dinv, outer = call(
        functools.partial(diagonal_kernel, lay), [fields, fields], [slab, factor], smem=1
    )

    (forces,) = call(
        functools.partial(forces_kernel, tiles_y, num_points),
        [(3, N**3, tiles_y * EZ)],
        [place, points, nodes_local],
        smem=2,
    )

    def swap(core, chip):
        return (
            lax.ppermute(core, lay.axis, lay.swaps(0)),
            lax.ppermute(chip, lay.axis, lay.swaps(1)),
        )

    def gather(loads):
        return lax.all_to_all(loads, lay.axis, 0, 0)

    face_shape = (FACE, width)
    layer = (N**3 // 2, width)
    loads_shape = (lay.slabs, 2, width)
    g, x, face = call(
        functools.partial(first_kernel, lay, num_points),
        [fields, fields, face_shape],
        [slab, points, recv, nodes_wide, dcols, dinv, high, low],
        [fields, face_shape, (width, N**3)],
        smem=2,
    )
    g, x, loads, core, chip = call(
        functools.partial(second_kernel, lay),
        [fields, fields, loads_shape, layer, layer],
        [slab, *swap(face, face), g, x, dinv, high, low, interp3],
        [fields],
        smem=1,
    )
    coarse = ((mass[0, 0], mass[0, 1]), (stiff[0, 0], stiff[0, 1]))
    stiffness = [high, low, edge_high, edge_low]

    for cycle in range(CYCLES):
        core, chip = swap(core, chip)
        last = cycle + 1 == CYCLES
        outs = [fields, fields, layer, layer]
        scratch = [fields, fields, fields]
        if last:
            outs = [(lay.mesh_x * lay.mesh_y, block, N**3)]
            scratch += [fields, fields]
        outs = call(
            functools.partial(pair_kernel, lay, coarse, "last" if last else "plain"),
            outs,
            [slab, core, chip, g, x, dinv, outer, *stiffness, gather(loads), image3, image_edge, interp3],
            scratch + [(lay.slabs + 2 * N, width)] * 2,
            smem=1,
        )
        if last:
            break
        g, x, core, chip = outs
        g, x, loads, core, chip = call(
            functools.partial(pair_kernel, lay, None, "restrict"),
            [fields, fields, loads_shape, layer, layer],
            [slab, *swap(core, chip), g, x, dinv, outer, *stiffness, interp3],
            [fields, fields, fields],
            smem=1,
        )
    (out,) = outs
    if not lay.joint:
        out = lax.dynamic_slice_in_dim(out, lax.axis_index("ex") * lay.mesh_y, lay.mesh_y, 0)
    out = lax.all_to_all(out, lay.axis, 0, 0)
    (pressure,) = call(
        functools.partial(unpack_kernel, lay),
        [(N**3, tiles_y * EZ)],
        [out],
        [(lay.slabs * block, N**3)],
    )
    return (
        pressure.reshape(source.shape),
        forces.reshape((3, *source.shape)),
    )


def solution(mesh):
    in_specs = (
        P(None, None, None, "ex", "ey"),
        P(None, ("ex", "ey")),
        P(None, ("ex", "ey")),
        P(None, ("ex", "ey")),
    )
    out_specs = (P(None, None, None, "ex", "ey"), P(None, None, None, None, "ex", "ey"))
    return jax.shard_map(shards, mesh=mesh, in_specs=in_specs, out_specs=out_specs, check_vma=False)
```

```python
import functools
import math

import jax
import jax.numpy as jnp
import numpy as np
from jax import lax
from jax.experimental import pallas as pl
from jax.experimental.pallas import tpu as pltpu
from jax.sharding import PartitionSpec as P

EZ = 64
CG_STEPS = 4
CYCLES = 2
N = 8
GLL_POINTS = np.array(
    [
        -1.0,
        -0.8717401485096066,
        -0.5917001814331423,
        -0.2092992179024789,
        0.2092992179024789,
        0.5917001814331423,
        0.8717401485096066,
        1.0,
    ]
)
WIDTH_EPS = 0.35
GAUSS_NORM = 1.0 / (math.pi**1.5 * WIDTH_EPS**3)
CHEB_LOW = 1.5
CHEB_HIGH = 12.0
THETA = 0.5 * (CHEB_HIGH + CHEB_LOW)
DELTA = 0.5 * (CHEB_HIGH - CHEB_LOW)
RHO_FIRST = DELTA / THETA
RHO_SECOND = 1.0 / (2.0 * THETA / DELTA - RHO_FIRST)
F32 = jnp.float32
BF16 = jnp.bfloat16
FACE = N * N


def build_tables():
    points = GLL_POINTS
    degree = len(points) - 1
    previous = points * 0.0 + 1.0
    current = points.copy()
    for k in range(1, degree):
        following = ((2 * k + 1) * points * current - k * previous) / (k + 1)
        previous = current
        current = following
    derivative = np.zeros((degree + 1, degree + 1))
    for i in range(degree + 1):
        for j in range(degree + 1):
            if i != j:
                derivative[i, j] = current[i] / (current[j] * (points[i] - points[j]))
    derivative[0, 0] = -degree * (degree + 1) / 4.0
    derivative[degree, degree] = degree * (degree + 1) / 4.0
    weights = 2.0 / (degree * (degree + 1) * current**2)
    interp = np.stack([(1.0 - points) / 2.0, (1.0 + points) / 2.0], axis=1)
    stiff_one = derivative.T @ (weights[:, None] * derivative)
    return derivative, weights, interp, stiff_one


def kron3(a, b, c):
    return np.kron(np.kron(a, b), c)


def log2(n):
    return int(n).bit_length() - 1


class Layout:
    def __init__(self, mesh_x, mesh_y, tiles_x, tiles_y):
        self.mesh_x, self.mesh_y = mesh_x, mesh_y
        self.num_x, self.num_y = tiles_x * mesh_x, tiles_y * mesh_y
        self.tiles_y = tiles_y
        self.joint = EZ % (2 * mesh_x * mesh_y) == 0
        self.axis = ("ex", "ey") if self.joint else "ey"
        self.slabs = mesh_x * mesh_y if self.joint else mesh_y
        self.depth = EZ // self.slabs
        assert self.depth == 2 and tiles_x == 1
        self.width = self.num_x * self.num_y * self.depth
        self.step_y = self.depth
        self.step_x = self.depth * self.num_y
        self.block = tiles_y * self.depth
        slab_of = [self.slab_at(d) for d in range(self.slabs)]
        self.order = [slab_of.index(s) for s in range(self.slabs)]

    def slab_at(self, d):
        if self.joint and self.mesh_x % 2 == 0 and self.mesh_y % 2 == 0:
            high = self.mesh_y // 2
            y = d & 1
            z = (d >> 1) & (high - 1)
            core = (d >> log2(self.mesh_y)) & 1
            x = d >> (log2(self.mesh_y) + 1)
            turn = y ^ (x & 1)
            return ((x * 2 + turn) * high + (z ^ (turn * (high - 1)))) * 2 + core
        if not self.joint and self.mesh_y % 8 == 0:
            return d ^ (((d >> 3) & 1) * 7)
        return d

    def swaps(self, first):
        pairs = []
        for s in range(first, self.slabs, 2):
            a, b = self.order[s], self.order[(s + 1) % self.slabs]
            pairs += [(a, b), (b, a)]
        return pairs


def split(x):
    high = x.astype(BF16)
    return high, (x - high.astype(F32)).astype(BF16)


def times3(high, low, x):
    xh, xl = split(x)
    dot = functools.partial(jnp.dot, preferred_element_type=F32)
    return dot(high, xh) + dot(high, xl) + dot(low, xh)


def split_table(x):
    high = x.astype(BF16)
    return high, (x - high.astype(np.float64)).astype(BF16)


def stacked_table(x):
    high, low = split_table(x)
    return np.concatenate([high, high, low, low], 1)


def stacked(x):
    high = x.astype(BF16).astype(F32)
    low = x - high
    return jnp.concatenate([high, low, high, low], 0).astype(BF16)


def roll(x, shift, axis):
    size = x.shape[axis]
    return pltpu.roll(x, shift % size, axis)


def lane_parts(lay, shape):
    lane = lax.broadcasted_iota(jnp.int32, shape, len(shape) - 1)
    part_z = lane & (lay.depth - 1)
    part_y = lax.shift_right_logical(lane, log2(lay.step_y)) & (lay.num_y - 1)
    part_x = lax.shift_right_logical(lane, log2(lay.step_x))
    return part_x, part_y, part_z


def get_rows(ref, k):
    if ref.shape[1] == 128:
        return ref[pl.ds(k, FACE, stride=N), :]
    return jnp.concatenate([ref[pl.ds(n * N + k, 1), :] for n in range(FACE)], 0)


def set_rows(ref, k, value):
    if ref.shape[1] == 128:
        ref[pl.ds(k, FACE, stride=N), :] = value
    else:
        for n in range(FACE):
            ref[pl.ds(n * N + k, 1), :] = value[n : n + 1]


def assemble_xy(lay, s_ref):
    last = N - 1
    for j in range(N):
        a, b = pl.ds(j * N, N), pl.ds((last * N + j) * N, N)
        low, high = s_ref[a, :], s_ref[b, :]
        s_ref[a, :] = low + roll(high, lay.step_x, 1)
        s_ref[b, :] = high + roll(low, -lay.step_x, 1)
    for i in range(N):
        a, b = pl.ds(i * N * N, N), pl.ds((i * N + last) * N, N)
        low, high = s_ref[a, :], s_ref[b, :]
        s_ref[a, :] = low + roll(high, lay.step_y, 1)
        s_ref[b, :] = high + roll(low, -lay.step_y, 1)


def assemble(lay, g_ref, s_ref, halo):
    _, _, part_z = lane_parts(lay, halo.shape)
    s_ref[...] = g_ref[...]
    low = get_rows(g_ref, 0)
    high = get_rows(g_ref, N - 1)
    set_rows(s_ref, 0, low + jnp.where(part_z == 0, halo, roll(high, 1, 1)))
    set_rows(s_ref, N - 1, high + jnp.where(part_z == lay.depth - 1, halo, roll(low, -1, 1)))
    assemble_xy(lay, s_ref)


def store_faces(lay, g_ref, face_ref):
    low = get_rows(g_ref, 0)
    high = get_rows(g_ref, N - 1)
    _, _, part_z = lane_parts(lay, low.shape)
    face_ref[...] = jnp.where(part_z == 0, low, high)


def halo_of(lay, slab_ref, core_ref, chip_ref):
    odd = (slab_ref[0] & 1) == 1
    core, chip = core_ref[...], chip_ref[...]
    below = jnp.where(odd, core, chip)
    above = jnp.where(odd, chip, core)
    _, _, part_z = lane_parts(lay, core.shape)
    return jnp.where(part_z == 0, roll(below, 1 - lay.depth, 1), roll(above, lay.depth - 1, 1))


def assemble_both(lay, g_ref, h_ref, s_ref, sh_ref):
    low, high = get_rows(g_ref, 0), get_rows(g_ref, N - 1)
    out_low, out_high = get_rows(h_ref, 0), get_rows(h_ref, N - 1)
    _, _, part_z = lane_parts(lay, low.shape)
    bottom = part_z == 0
    s_ref[...] = g_ref[...]
    sh_ref[...] = h_ref[...]
    set_rows(s_ref, 0, low + jnp.where(bottom, out_high, roll(high, 1, 1)))
    set_rows(s_ref, N - 1, high + jnp.where(bottom, roll(low, -1, 1), out_low))
    set_rows(sh_ref, N - 1, out_high + jnp.where(bottom, low, 0.0))
    set_rows(sh_ref, 0, out_low + jnp.where(bottom, 0.0, high))
    assemble_xy(lay, s_ref)
    assemble_xy(lay, sh_ref)


def send_layers(lay, slab_ref, g_ref, s_ref, core_ref, chip_ref):
    low, high = get_rows(g_ref, 0), get_rows(g_ref, N - 1)
    _, _, part_z = lane_parts(lay, low.shape)
    s_ref[...] = g_ref[...]
    set_rows(s_ref, N - 1, jnp.where(part_z == 0, high + roll(low, -1, 1), high))
    set_rows(s_ref, 0, jnp.where(part_z == 0, low, low + roll(high, 1, 1)))
    half = N**3 // 2
    a, b = s_ref[:half, :], s_ref[half:, :]
    _, _, part_z = lane_parts(lay, a.shape)
    bottom = part_z == 0
    first = jnp.where(bottom, a, roll(b, 1, 1))
    second = jnp.where(bottom, roll(a, -1, 1), b)
    odd = (slab_ref[0] & 1) == 1
    core_ref[...] = jnp.where(odd, first, second)
    chip_ref[...] = jnp.where(odd, second, first)


def receive_layers(lay, slab_ref, core_ref, chip_ref, h_ref):
    odd = (slab_ref[0] & 1) == 1
    core, chip = core_ref[...], chip_ref[...]
    below, above = jnp.where(odd, core, chip), jnp.where(odd, chip, core)
    _, _, part_z = lane_parts(lay, core.shape)
    bottom = part_z == 0
    half = N**3 // 2
    h_ref[:half, :] = jnp.where(bottom, below, roll(above, 1, 1))
    h_ref[half:, :] = jnp.where(bottom, roll(below, -1, 1), above)


def pack_kernel(
    lay,
    base_ref,
    offset_ref,
    force_ref,
    source_ref,
    out_ref,
    base_buf,
    offset_buf,
    force_buf,
    field_ref,
    flat_ref,
    sems,
):
    pairs = (
        (source_ref, field_ref),
        (base_ref, base_buf),
        (offset_ref, offset_buf),
        (force_ref, force_buf),
    )
    copies = [pltpu.make_async_copy(a, b, sems.at[n]) for n, (a, b) in enumerate(pairs)]
    for copy in copies:
        copy.start()
    for copy in copies:
        copy.wait()
    mean = 0.5 * (get_rows(field_ref, N - 1) + roll(get_rows(field_ref, 0), -1, 1))
    set_rows(field_ref, N - 1, mean)
    set_rows(field_ref, 0, roll(mean, 1, 1))
    flat_ref[...] = field_ref[...].T
    shape = (1, N**3)
    lane = lax.broadcasted_iota(jnp.int32, shape, 1)
    points = jnp.zeros(shape, F32)
    for p in range(base_buf.shape[0]):
        for c, ref in enumerate((base_buf, offset_buf, force_buf)):
            for d in range(3):
                value = ref[p : p + 1, d : d + 1].astype(F32)
                points = jnp.where(lane == (p * 9 + c * 3 + d) * N, value, points)
    used = (lane & (N - 1)) == 0
    for d in range(lay.slabs):
        first = lay.slab_at(d) * lay.depth
        for e2 in range(lay.tiles_y):
            rows = flat_ref[pl.ds(e2 * EZ + first, lay.depth), :]
            out_ref[d, pl.ds(e2 * lay.depth, lay.depth), :] = rows
        out_ref[d, 1:2, :] = jnp.where(used, points, out_ref[d, 1:2, :])


def gauss(elem, base, position, half_nodes):
    node = lax.broadcasted_iota(jnp.int32, elem.shape, 0)
    elem = elem.astype(F32)
    away = elem + half_nodes - position
    inside = (
        (elem == base)
        | (elem == base + 1.0)
        | ((elem == base - 1.0) & (node == N - 1))
        | ((elem == base + 2.0) & (node == 0))
    )
    return jnp.where(inside, jnp.exp(-(away * away) / (WIDTH_EPS * WIDTH_EPS)), 0.0)


def right_side(lay, num_points, slab_ref, points_ref, nodes_ref, dcols_ref, g_ref, halo_ref):
    shape = (N, lay.width)
    part_x, part_y, part_z = lane_parts(lay, shape)
    first_z = slab_ref[0] * lay.depth
    elem_z = first_z + part_z
    elem_halo = jnp.where(part_z == 0, first_z - 1, first_z + lay.depth)

    def weighted(elem, base, position):
        plain = nodes_ref[1] * gauss(elem, base, position, nodes_ref[0])
        deriv = dcols_ref[0] * plain[0:1]
        for a in range(1, N):
            deriv = deriv + dcols_ref[a] * plain[a : a + 1]
        return plain, deriv

    def one(p, _):
        base = [points_ref[p, d] for d in range(3)]
        position = [points_ref[p, d] + 1.0 + points_ref[p, 3 + d] for d in range(3)]
        force = [points_ref[p, 6 + d] * (0.25 * GAUSS_NORM) for d in range(3)]
        first = first_z.astype(F32)

        @pl.when((base[2] + 2.0 >= first - 1.0) & (base[2] - 1.0 <= first + lay.depth))
        def _():
            x0, x1 = weighted(part_x, base[0], position[0])
            y0, y1 = weighted(part_y, base[1], position[1])
            z0, z1 = weighted(elem_z, base[2], position[2])
            h0, h1 = weighted(elem_halo, base[2], position[2])
            pick = part_z[0:1] == 0
            h0 = jnp.where(pick, h0[N - 1 : N], h0[0:1])
            h1 = jnp.where(pick, h1[N - 1 : N], h1[0:1])
            x1 = force[0] * x1
            fz1 = force[2] * z1
            fz0 = force[1] * z0
            for j in range(N):
                first_part = y0[j : j + 1] * z0
                other_part = y1[j : j + 1] * fz0 + y0[j : j + 1] * fz1
                for i in range(N):
                    rows = pl.ds((i * N + j) * N, N)
                    g_ref[rows, :] += x1[i : i + 1] * first_part + x0[i : i + 1] * other_part
            first_part = y0 * h0
            other_part = y1 * (force[1] * h0) + y0 * (force[2] * h1)
            for i in range(N):
                rows = pl.ds(i * N, N)
                halo_ref[rows, :] += x1[i : i + 1] * first_part + x0[i : i + 1] * other_part

        return 0

    lax.fori_loop(0, num_points, one, 0)


def inverse_diagonal(lay, slab_ref, factor_ref, dinv_ref, outer):
    shape = (N, lay.width)
    part_x, part_y, part_z = lane_parts(lay, shape)
    first = slab_ref[0] * lay.depth
    part_z = jnp.where(part_z == 0, first - 1, first + lay.depth) if outer else first + part_z
    node = lax.broadcasted_iota(jnp.int32, shape, 0)

    def share(low, high):
        return (
            jnp.where(low, 0.0, 0.5),
            jnp.where(high, 0.0, 0.5),
        )

    low_z, high_z = share(part_z == 0, part_z == EZ - 1)
    along_z = jnp.where(node == 0, low_z, jnp.where(node == N - 1, high_z, 1.0))
    if outer:
        along_z = jnp.where((part_z < 0) | (part_z >= EZ), 0.0, along_z)
    along_x = dict(zip((0, N - 1), share(part_x == 0, part_x == lay.num_x - 1)))
    along_y = dict(zip((0, N - 1), share(part_y == 0, part_y == lay.num_y - 1)))
    for i in range(N):
        for j in range(N):
            rows = pl.ds((i * N + j) * N, N)
            value = factor_ref[rows, :] * along_z
            if i in along_x:
                value = value * along_x[i]
            if j in along_y:
                value = value * along_y[j]
            dinv_ref[rows, :] = value


def diagonal_kernel(lay, slab_ref, factor_ref, dinv_ref, outer_ref):
    inverse_diagonal(lay, slab_ref, factor_ref, dinv_ref, False)
    inverse_diagonal(lay, slab_ref, factor_ref, outer_ref, True)


def first_kernel(
    lay,
    num_points,
    slab_ref,
    points_ref,
    recv_ref,
    nodes_ref,
    dcols_ref,
    dinv_ref,
    high_ref,
    low_ref,
    g_ref,
    x_ref,
    face_ref,
    s_ref,
    halo_ref,
    flat_ref,
):
    count, block = recv_ref.shape[0], recv_ref.shape[1]
    for d in range(count):
        flat_ref[pl.ds(d * block, block), :] = recv_ref[d]
    g_ref[...] = flat_ref[...].T
    low, high = get_rows(g_ref, 0), get_rows(g_ref, N - 1)
    _, _, part_z = lane_parts(lay, low.shape)
    set_rows(g_ref, 0, jnp.where(part_z == 0, low, roll(high, 1, 1)))
    halo_ref[...] = jnp.where(part_z == 0, low, high)
    right_side(lay, num_points, slab_ref, points_ref, nodes_ref, dcols_ref, g_ref, halo_ref)
    assemble(lay, g_ref, s_ref, halo_ref[...])
    update = (1.0 / THETA) * dinv_ref[...] * s_ref[...]
    x_ref[...] = update
    g_ref[...] = g_ref[...] - times3(high_ref[...], low_ref[...], update)
    store_faces(lay, g_ref, face_ref)


def restriction(lay, g_ref, dinv_ref, interp_ref, send_ref):
    inner = jnp.where(dinv_ref[...] != 0.0, g_ref[...], 0.0)
    high, low = split(inner)
    both = jnp.dot(
        interp_ref[...], jnp.concatenate([high, low], 1), preferred_element_type=F32
    )
    load = both[:N, : lay.width] + both[:N, lay.width :] + both[N:, : lay.width]
    rows = [load[n : n + 1] for n in range(N)]
    rows = [rows[n] + roll(rows[4 + n], lay.step_x, 1) for n in range(4)]
    rows = [rows[n] + roll(rows[2 + n], lay.step_y, 1) for n in range(2)]
    for d in range(send_ref.shape[0]):
        send_ref[d, 0:1] = rows[0]
        send_ref[d, 1:2] = rows[1]


OLD = RHO_SECOND * RHO_FIRST
NEW = 2.0 * RHO_SECOND / DELTA


def second_kernel(
    lay,
    slab_ref,
    core_ref,
    chip_ref,
    g_ref,
    x_ref,
    dinv_ref,
    high_ref,
    low_ref,
    interp_ref,
    g_out,
    x_out,
    send_ref,
    core_out,
    chip_out,
    s_ref,
):
    assemble(lay, g_ref, s_ref, halo_of(lay, slab_ref, core_ref, chip_ref))
    update = OLD * x_ref[...] + NEW * dinv_ref[...] * s_ref[...]
    x_out[...] = x_ref[...] + update
    g_out[...] = g_ref[...] - times3(high_ref[...], low_ref[...], update)
    restriction(lay, g_out, dinv_ref, interp_ref, send_ref)
    send_layers(lay, slab_ref, g_out, s_ref, core_out, chip_out)


def solve_coarse(lay, mass, stiff, loads_ref, first_ref, second_ref):
    for s in range(lay.slabs):
        d = lay.order[s]
        first_ref[pl.ds(s, 1), :] = loads_ref[d, 0:1]
        second_ref[pl.ds(s, 1), :] = loads_ref[d, 1:2]
    shape = (lay.slabs, lay.width)
    part_x, part_y, part_z = lane_parts(lay, shape)
    row = lax.broadcasted_iota(jnp.int32, shape, 0)
    keep = ((part_x > 0) & (part_y > 0) & ((part_z > 0) | (row > 0))).astype(F32)
    bottom = part_z == 0

    def below(v):
        return jnp.where(bottom, roll(roll(v, 1, 0), -1, 1), roll(v, 1, 1))

    def above(v):
        return jnp.where(bottom, roll(v, -1, 1), roll(roll(v, -1, 0), 1, 1))

    def neighbours(v, step):
        return roll(v, step, 1) + roll(v, -step, 1)

    def mix(pair, v, around):
        return (2.0 * pair[0]) * v + pair[1] * around

    def operate(v):
        around = below(v) + above(v)
        mass_z, stiff_z = mix(mass, v, around), mix(stiff, v, around)
        around = neighbours(mass_z, lay.step_y)
        both = mix(mass, mass_z, around)
        rest = mix(stiff, mass_z, around) + mix(mass, stiff_z, neighbours(stiff_z, lay.step_y))
        out = mix(stiff, both, neighbours(both, lay.step_x)) + mix(
            mass, rest, neighbours(rest, lay.step_x)
        )
        return (0.5 * keep) * out

    def inner(a, b):
        return jnp.sum(jnp.sum(a * b, axis=1, keepdims=True), axis=0, keepdims=True)

    here = pl.ds(0, lay.slabs)
    residual = keep * (first_ref[here, :] + below(second_ref[here, :]))
    direction = residual
    total = jnp.zeros(shape, F32)
    norm = inner(residual, residual)
    for step in range(CG_STEPS):
        image = operate(direction)
        alpha = norm / inner(direction, image)
        total = total + alpha * direction
        if step + 1 < CG_STEPS:
            residual = residual - alpha * image
            following = inner(residual, residual)
            direction = residual + (following / norm) * direction
            norm = following
    here = pl.ds(N, lay.slabs)
    for ref, value in ((first_ref, total), (second_ref, above(total))):
        ref[...] = jnp.zeros(ref.shape, F32)
        ref[here, :] = value


def corners(lay, low, high):
    rows = [low, high]
    rows = rows + [roll(r, -lay.step_y, 1) for r in rows]
    rows = rows + [roll(r, -lay.step_x, 1) for r in rows]
    corner = lax.broadcasted_iota(jnp.int32, (N, lay.width), 0)
    local = jnp.broadcast_to(rows[0], (N, lay.width))
    for n in range(1, N):
        local = jnp.where(corner == n, rows[n], local)
    return local


def prolong_coarse(lay, slab_ref, first_ref, second_ref, interp_ref, image_ref, edge_ref, g_ref, h_ref, x_ref):
    mine = slab_ref[0] + N
    _, _, part_z = lane_parts(lay, (1, lay.width))
    bottom = part_z == 0
    own, outer, far = [], [], []
    for ref in (first_ref, second_ref):
        before, here, after = (ref[pl.ds(mine + shift, 1), :] for shift in (-1, 0, 1))
        own.append(here)
        outer.append(jnp.where(bottom, roll(before, -1, 1), roll(after, 1, 1)))
        far.append(jnp.where(bottom, before, after))
    local = stacked(corners(lay, *own))
    dot = functools.partial(jnp.dot, preferred_element_type=F32)
    x_ref[...] += dot(interp_ref[...], local)
    g_ref[...] -= dot(image_ref[...], local)
    h_ref[...] -= dot(image_ref[...], stacked(corners(lay, *outer)))
    edge = dot(edge_ref[...], stacked(corners(lay, *far)))
    low, high = get_rows(h_ref, 0), get_rows(h_ref, N - 1)
    set_rows(h_ref, 0, low - jnp.where(bottom, edge[FACE:], 0.0))
    set_rows(h_ref, N - 1, high - jnp.where(bottom, 0.0, edge[:FACE]))


def pair_kernel(lay, coarse, kind, slab_ref, core_ref, chip_ref, g_ref, x_ref, dinv_ref, outer_ref, *refs):
    refs = list(refs)
    high_ref, low_ref, edge_high_ref, edge_low_ref = (refs.pop(0) for _ in range(4))
    if coarse:
        loads_ref, image_ref, image_edge_ref = (refs.pop(0) for _ in range(3))
    if coarse or kind == "restrict":
        interp_ref = refs.pop(0)
    if kind == "last":
        out_ref = refs.pop(0)
    else:
        g_out, x_out = refs.pop(0), refs.pop(0)
        if kind == "restrict":
            send_ref = refs.pop(0)
        core_out, chip_out = refs.pop(0), refs.pop(0)
    s_ref, sh_ref, h_ref = (refs.pop(0) for _ in range(3))
    if kind == "last":
        g_out, x_out = refs.pop(0), refs.pop(0)

    g_out[...] = g_ref[...]
    x_out[...] = x_ref[...]
    receive_layers(lay, slab_ref, core_ref, chip_ref, h_ref)
    if coarse:
        first_ref, second_ref = refs
        solve_coarse(lay, *coarse, loads_ref, first_ref, second_ref)
        prolong_coarse(
            lay, slab_ref, first_ref, second_ref, interp_ref, image_ref, image_edge_ref, g_out, h_ref, x_out
        )
    assemble_both(lay, g_out, h_ref, s_ref, sh_ref)
    update = (1.0 / THETA) * dinv_ref[...] * s_ref[...]
    outer = (1.0 / THETA) * outer_ref[...] * sh_ref[...]
    high, low = high_ref[...], low_ref[...]
    edge = times3(edge_high_ref[...], edge_low_ref[...], outer)
    _, _, part_z = lane_parts(lay, (FACE, lay.width))
    near = jnp.where(
        part_z == 0, get_rows(h_ref, N - 1) - edge[FACE:], get_rows(h_ref, 0) - edge[:FACE]
    )
    g_out[...] -= times3(high, low, update)
    assemble(lay, g_out, s_ref, near)
    following = OLD * update + NEW * dinv_ref[...] * s_ref[...]
    if kind == "last":
        total = (x_out[...] + (update + following)).T
        count, block = out_ref.shape[0], out_ref.shape[1]
        for d in range(count):
            out_ref[d] = total[d * block : (d + 1) * block]
        return
    x_out[...] += update + following
    g_out[...] -= times3(high, low, following)
    if kind == "restrict":
        restriction(lay, g_out, dinv_ref, interp_ref, send_ref)
    send_layers(lay, slab_ref, g_out, s_ref, core_out, chip_out)


def unpack_kernel(lay, recv_ref, out_ref, flat_ref):
    for d in range(lay.slabs):
        first = lay.slab_at(d) * lay.depth
        for e2 in range(lay.tiles_y):
            rows = recv_ref[d, pl.ds(e2 * lay.depth, lay.depth), :]
            flat_ref[pl.ds(e2 * EZ + first, lay.depth), :] = rows
    out_ref[...] = flat_ref[...].T


def forces_kernel(tiles_y, num_points, place_ref, points_ref, nodes_ref, out_ref):
    width = tiles_y * EZ
    shape = (N, width)
    lane = lax.broadcasted_iota(jnp.int32, shape, 1)
    first_x, first_y = place_ref[0], place_ref[1]
    elem_x = jnp.broadcast_to(first_x, shape)
    elem_y = first_y + lax.shift_right_logical(lane, log2(EZ))
    elem_z = lane & (EZ - 1)
    out_ref[...] = jnp.zeros(out_ref.shape, F32)

    def one(p, _):
        base = [points_ref[p, d] for d in range(3)]
        position = [points_ref[p, d] + 1.0 + points_ref[p, 3 + d] for d in range(3)]
        force = [points_ref[p, 6 + d] * GAUSS_NORM for d in range(3)]
        low_x, low_y = first_x.astype(F32), first_y.astype(F32)

        @pl.when(
            (base[0] + 2.0 >= low_x)
            & (base[0] - 1.0 <= low_x)
            & (base[1] + 2.0 >= low_y)
            & (base[1] - 1.0 <= low_y + (tiles_y - 1))
        )
        def _():
            x = gauss(elem_x, base[0], position[0], nodes_ref[0])
            y = gauss(elem_y, base[1], position[1], nodes_ref[0])
            z = gauss(elem_z, base[2], position[2], nodes_ref[0])
            for j in range(N):
                plane = y[j : j + 1] * z
                for i in range(N):
                    value = x[i : i + 1] * plane
                    rows = pl.ds((i * N + j) * N, N)
                    for c in range(3):
                        out_ref[c, rows, :] += force[c] * value

        return 0

    lax.fori_loop(0, num_points, one, 0)


def call(kernel, outs, inputs, scratch=(), smem=0, spaces=None):
    spaces = spaces or [pltpu.SMEM] * smem + [pltpu.VMEM] * (len(inputs) - smem)
    specs = [pl.BlockSpec(memory_space=space) for space in spaces]
    shapes = [jax.ShapeDtypeStruct(s, F32) for s in outs]
    result = pl.pallas_call(
        kernel,
        out_shape=shapes,
        in_specs=specs,
        out_specs=[pl.BlockSpec(memory_space=pltpu.VMEM)] * len(shapes),
        scratch_shapes=[pltpu.VMEM(s, F32) if isinstance(s, tuple) else s for s in scratch],
        compiler_params=pltpu.CompilerParams(vmem_limit_bytes=40 * 1024 * 1024),
    )(*inputs)
    return result


def shards(source, point_base, point_offset, point_force):
    tiles_x, tiles_y = source.shape[3], source.shape[4] // EZ
    lay = Layout(lax.axis_size("ex"), lax.axis_size("ey"), tiles_x, tiles_y)
    devices = lay.mesh_x * lay.mesh_y
    derivative, weights, interp, stiff_one = build_tables()
    width, fields = lay.width, (N**3, lay.width)

    diag_w = np.diag(weights)
    full = 0.5 * (
        kron3(stiff_one, diag_w, diag_w)
        + kron3(diag_w, stiff_one, diag_w)
        + kron3(diag_w, diag_w, stiff_one)
    )
    full_high, full_low = split_table(full)
    interp3 = kron3(interp, interp, interp)
    image3 = full @ interp3
    ratio = (weights[:, None] * derivative**2).sum(axis=0) / weights
    diag = 0.5 * (ratio[:, None, None] + ratio[None, :, None] + ratio[None, None, :])
    diag = diag * weights[:, None, None] * weights[None, :, None] * weights[None, None, :]
    factor = np.broadcast_to(1.0 / diag.reshape(N**3, 1), fields)
    nodes = np.stack([0.5 * (1.0 + GLL_POINTS), weights])
    nodes_wide = np.broadcast_to(nodes[:, :, None], (2, N, width))
    nodes_local = np.broadcast_to(nodes[:, :, None], (2, N, tiles_y * EZ))
    dcols = np.broadcast_to(derivative[:, :, None], (N, N, width))
    mass = interp.T @ diag_w @ interp
    stiff = interp.T @ stiff_one @ interp
    edge_rows = np.concatenate([np.arange(FACE) * N, np.arange(FACE) * N + N - 1])
    high, low = jnp.asarray(full_high), jnp.asarray(full_low)
    edge_high, edge_low = jnp.asarray(full_high[edge_rows]), jnp.asarray(full_low[edge_rows])
    restrict3 = jnp.asarray(np.concatenate(split_table(interp3.T), 0))
    prolong3, image3, image_edge = (
        jnp.asarray(stacked_table(t)) for t in (interp3, image3, image3[edge_rows])
    )
    factor, nodes_wide, nodes_local, dcols = (
        jnp.asarray(t, F32) for t in (factor, nodes_wide, nodes_local, dcols)
    )

    slab = lay.slab_at(lax.axis_index(lay.axis).astype(jnp.int32)).reshape(1)
    place = jnp.stack([lax.axis_index("ex") * tiles_x, lax.axis_index("ey") * tiles_y]).astype(
        jnp.int32
    )

    local_points = point_base.shape[1]
    block = lay.block
    (send,) = call(
        functools.partial(pack_kernel, lay),
        [(lay.slabs, block, N**3)],
        [point_base.T, point_offset.T, point_force.T, source.reshape(N**3, tiles_y * EZ)],
        [
            pltpu.VMEM((local_points, 3), jnp.int32),
            (local_points, 3),
            (local_points, 3),
            (N**3, tiles_y * EZ),
            (tiles_y * EZ, N**3),
            pltpu.SemaphoreType.DMA((4,)),
        ],
        spaces=[pl.ANY] * 4,
    )
    recv = lax.all_to_all(send, lay.axis, 0, 0)
    if not lay.joint:
        recv = lax.all_gather(recv, "ex", axis=0, tiled=True)
    points = recv[:, 1, : 9 * N * local_points : N]
    num_points = devices * local_points
    points = points.reshape(num_points, 9)
    dinv, outer = call(
        functools.partial(diagonal_kernel, lay), [fields, fields], [slab, factor], smem=1
    )

    (forces,) = call(
        functools.partial(forces_kernel, tiles_y, num_points),
        [(3, N**3, tiles_y * EZ)],
        [place, points, nodes_local],
        smem=2,
    )

    def swap(core, chip):
        return (
            lax.ppermute(core, lay.axis, lay.swaps(0)),
            lax.ppermute(chip, lay.axis, lay.swaps(1)),
        )

    def gather(loads):
        return lax.all_to_all(loads, lay.axis, 0, 0)

    face_shape = (FACE, width)
    layer = (N**3 // 2, width)
    loads_shape = (lay.slabs, 2, width)
    g, x, face = call(
        functools.partial(first_kernel, lay, num_points),
        [fields, fields, face_shape],
        [slab, points, recv, nodes_wide, dcols, dinv, high, low],
        [fields, face_shape, (width, N**3)],
        smem=2,
    )
    g, x, loads, core, chip = call(
        functools.partial(second_kernel, lay),
        [fields, fields, loads_shape, layer, layer],
        [slab, *swap(face, face), g, x, dinv, high, low, restrict3],
        [fields],
        smem=1,
    )
    coarse = ((mass[0, 0], mass[0, 1]), (stiff[0, 0], stiff[0, 1]))
    stiffness = [high, low, edge_high, edge_low]

    for cycle in range(CYCLES):
        core, chip = swap(core, chip)
        last = cycle + 1 == CYCLES
        outs = [fields, fields, layer, layer]
        scratch = [fields, fields, fields]
        if last:
            outs = [(lay.mesh_x * lay.mesh_y, block, N**3)]
            scratch += [fields, fields]
        outs = call(
            functools.partial(pair_kernel, lay, coarse, "last" if last else "plain"),
            outs,
            [slab, core, chip, g, x, dinv, outer, *stiffness, gather(loads), image3, image_edge, prolong3],
            scratch + [(lay.slabs + 2 * N, width)] * 2,
            smem=1,
        )
        if last:
            break
        g, x, core, chip = outs
        g, x, loads, core, chip = call(
            functools.partial(pair_kernel, lay, None, "restrict"),
            [fields, fields, loads_shape, layer, layer],
            [slab, *swap(core, chip), g, x, dinv, outer, *stiffness, restrict3],
            [fields, fields, fields],
            smem=1,
        )
    (out,) = outs
    if not lay.joint:
        out = lax.dynamic_slice_in_dim(out, lax.axis_index("ex") * lay.mesh_y, lay.mesh_y, 0)
    out = lax.all_to_all(out, lay.axis, 0, 0)
    (pressure,) = call(
        functools.partial(unpack_kernel, lay),
        [(N**3, tiles_y * EZ)],
        [out],
        [(lay.slabs * block, N**3)],
    )
    return (
        pressure.reshape(source.shape),
        forces.reshape((3, *source.shape)),
    )


def solution(mesh):
    in_specs = (
        P(None, None, None, "ex", "ey"),
        P(None, ("ex", "ey")),
        P(None, ("ex", "ey")),
        P(None, ("ex", "ey")),
    )
    out_specs = (P(None, None, None, "ex", "ey"), P(None, None, None, None, "ex", "ey"))
    return jax.shard_map(shards, mesh=mesh, in_specs=in_specs, out_specs=out_specs, check_vma=False)
```

```python
import functools
import math

import jax
import jax.numpy as jnp
import numpy as np
from jax import lax
from jax.experimental import pallas as pl
from jax.experimental.pallas import tpu as pltpu
from jax.sharding import PartitionSpec as P

EZ = 64
CG_STEPS = 4
CYCLES = 2
N = 8
GLL_POINTS = np.array(
    [
        -1.0,
        -0.8717401485096066,
        -0.5917001814331423,
        -0.2092992179024789,
        0.2092992179024789,
        0.5917001814331423,
        0.8717401485096066,
        1.0,
    ]
)
WIDTH_EPS = 0.35
GAUSS_NORM = 1.0 / (math.pi**1.5 * WIDTH_EPS**3)
CHEB_LOW = 1.5
CHEB_HIGH = 12.0
THETA = 0.5 * (CHEB_HIGH + CHEB_LOW)
DELTA = 0.5 * (CHEB_HIGH - CHEB_LOW)
RHO_FIRST = DELTA / THETA
RHO_SECOND = 1.0 / (2.0 * THETA / DELTA - RHO_FIRST)
F32 = jnp.float32
BF16 = jnp.bfloat16
FACE = N * N


def build_tables():
    points = GLL_POINTS
    degree = len(points) - 1
    previous = points * 0.0 + 1.0
    current = points.copy()
    for k in range(1, degree):
        following = ((2 * k + 1) * points * current - k * previous) / (k + 1)
        previous = current
        current = following
    derivative = np.zeros((degree + 1, degree + 1))
    for i in range(degree + 1):
        for j in range(degree + 1):
            if i != j:
                derivative[i, j] = current[i] / (current[j] * (points[i] - points[j]))
    derivative[0, 0] = -degree * (degree + 1) / 4.0
    derivative[degree, degree] = degree * (degree + 1) / 4.0
    weights = 2.0 / (degree * (degree + 1) * current**2)
    interp = np.stack([(1.0 - points) / 2.0, (1.0 + points) / 2.0], axis=1)
    stiff_one = derivative.T @ (weights[:, None] * derivative)
    return derivative, weights, interp, stiff_one


def kron3(a, b, c):
    return np.kron(np.kron(a, b), c)


def log2(n):
    return int(n).bit_length() - 1


class Layout:
    def __init__(self, mesh_x, mesh_y, tiles_x, tiles_y):
        self.mesh_x, self.mesh_y = mesh_x, mesh_y
        self.num_x, self.num_y = tiles_x * mesh_x, tiles_y * mesh_y
        self.tiles_y = tiles_y
        self.joint = EZ % (2 * mesh_x * mesh_y) == 0
        self.axis = ("ex", "ey") if self.joint else "ey"
        self.slabs = mesh_x * mesh_y if self.joint else mesh_y
        self.depth = EZ // self.slabs
        assert self.depth == 2 and tiles_x == 1
        self.width = self.num_x * self.num_y * self.depth
        self.step_y = self.depth
        self.step_x = self.depth * self.num_y
        self.block = tiles_y * self.depth
        slab_of = [self.slab_at(d) for d in range(self.slabs)]
        self.order = [slab_of.index(s) for s in range(self.slabs)]

    def slab_at(self, d):
        if self.joint and self.mesh_x % 2 == 0 and self.mesh_y % 2 == 0:
            high = self.mesh_y // 2
            y = d & 1
            z = (d >> 1) & (high - 1)
            core = (d >> log2(self.mesh_y)) & 1
            x = d >> (log2(self.mesh_y) + 1)
            turn = y ^ (x & 1)
            return ((x * 2 + turn) * high + (z ^ (turn * (high - 1)))) * 2 + core
        if not self.joint and self.mesh_y % 8 == 0:
            return d ^ (((d >> 3) & 1) * 7)
        return d

    def swaps(self, first):
        pairs = []
        for s in range(first, self.slabs, 2):
            a, b = self.order[s], self.order[(s + 1) % self.slabs]
            pairs += [(a, b), (b, a)]
        return pairs


def split(x):
    high = x.astype(BF16)
    return high, (x - high.astype(F32)).astype(BF16)


def times3(high, low, x):
    xh, xl = split(x)
    dot = functools.partial(jnp.dot, preferred_element_type=F32)
    return dot(high, xh) + dot(high, xl) + dot(low, xh)


def split_table(x):
    high = x.astype(BF16)
    return high, (x - high.astype(np.float64)).astype(BF16)


def stacked_table(x):
    high, low = split_table(x)
    return np.concatenate([high, high, low, low], 1)


def stacked(x):
    high = x.astype(BF16).astype(F32)
    low = x - high
    return jnp.concatenate([high, low, high, low], 0).astype(BF16)


def subtract_stiffness(lay, one, u_ref, g_ref, high_ref, low_ref, along_ref):
    matrix, weights = one
    dot = functools.partial(jnp.dot, preferred_element_type=F32)
    half = N // 2
    for first in (0, half):
        scaled = [
            float(weights[i]) * u_ref[pl.ds(i * FACE, FACE), :] for i in range(first, first + half)
        ]
        xh, xl = split(jnp.concatenate(scaled, 0))
        both = dot(high_ref[...], jnp.concatenate([xh, xl], 1))
        rows = pl.ds(first * FACE, half * FACE)
        g_ref[rows, :] -= both[:, : lay.width] + both[:, lay.width :] + dot(low_ref[...], xh)
    even = 0.5 * (matrix[:half, :half] + matrix[:half, :half - 1 : -1])
    odd = 0.5 * (matrix[:half, :half] - matrix[:half, :half - 1 : -1])
    for j in range(N):
        values = [u_ref[pl.ds((i * N + j) * N, N), :] for i in range(N)]
        sums = [values[i] + values[N - 1 - i] for i in range(half)]
        gaps = [values[i] - values[N - 1 - i] for i in range(half)]
        along = along_ref[pl.ds(j * N, N), :]
        for i in range(half):
            a = sum(float(even[i, q]) * sums[q] for q in range(half))
            b = sum(float(odd[i, q]) * gaps[q] for q in range(half))
            g_ref[pl.ds((i * N + j) * N, N), :] -= along * (a + b)
            g_ref[pl.ds(((N - 1 - i) * N + j) * N, N), :] -= along * (a - b)


def roll(x, shift, axis):
    size = x.shape[axis]
    return pltpu.roll(x, shift % size, axis)


def lane_parts(lay, shape):
    lane = lax.broadcasted_iota(jnp.int32, shape, len(shape) - 1)
    part_z = lane & (lay.depth - 1)
    part_y = lax.shift_right_logical(lane, log2(lay.step_y)) & (lay.num_y - 1)
    part_x = lax.shift_right_logical(lane, log2(lay.step_x))
    return part_x, part_y, part_z


def get_rows(ref, k):
    if ref.shape[1] == 128:
        return ref[pl.ds(k, FACE, stride=N), :]
    return jnp.concatenate([ref[pl.ds(n * N + k, 1), :] for n in range(FACE)], 0)


def set_rows(ref, k, value):
    if ref.shape[1] == 128:
        ref[pl.ds(k, FACE, stride=N), :] = value
    else:
        for n in range(FACE):
            ref[pl.ds(n * N + k, 1), :] = value[n : n + 1]


def assemble_xy(lay, s_ref):
    last = N - 1
    for j in range(N):
        a, b = pl.ds(j * N, N), pl.ds((last * N + j) * N, N)
        low, high = s_ref[a, :], s_ref[b, :]
        s_ref[a, :] = low + roll(high, lay.step_x, 1)
        s_ref[b, :] = high + roll(low, -lay.step_x, 1)
    for i in range(N):
        a, b = pl.ds(i * N * N, N), pl.ds((i * N + last) * N, N)
        low, high = s_ref[a, :], s_ref[b, :]
        s_ref[a, :] = low + roll(high, lay.step_y, 1)
        s_ref[b, :] = high + roll(low, -lay.step_y, 1)


def assemble(lay, g_ref, s_ref, halo):
    _, _, part_z = lane_parts(lay, halo.shape)
    s_ref[...] = g_ref[...]
    low = get_rows(g_ref, 0)
    high = get_rows(g_ref, N - 1)
    set_rows(s_ref, 0, low + jnp.where(part_z == 0, halo, roll(high, 1, 1)))
    set_rows(s_ref, N - 1, high + jnp.where(part_z == lay.depth - 1, halo, roll(low, -1, 1)))
    assemble_xy(lay, s_ref)


def store_faces(lay, g_ref, face_ref):
    low = get_rows(g_ref, 0)
    high = get_rows(g_ref, N - 1)
    _, _, part_z = lane_parts(lay, low.shape)
    face_ref[...] = jnp.where(part_z == 0, low, high)


def halo_of(lay, slab_ref, core_ref, chip_ref):
    odd = (slab_ref[0] & 1) == 1
    core, chip = core_ref[...], chip_ref[...]
    below = jnp.where(odd, core, chip)
    above = jnp.where(odd, chip, core)
    _, _, part_z = lane_parts(lay, core.shape)
    return jnp.where(part_z == 0, roll(below, 1 - lay.depth, 1), roll(above, lay.depth - 1, 1))


def assemble_both(lay, g_ref, h_ref, s_ref, sh_ref):
    low, high = get_rows(g_ref, 0), get_rows(g_ref, N - 1)
    out_low, out_high = get_rows(h_ref, 0), get_rows(h_ref, N - 1)
    _, _, part_z = lane_parts(lay, low.shape)
    bottom = part_z == 0
    s_ref[...] = g_ref[...]
    sh_ref[...] = h_ref[...]
    set_rows(s_ref, 0, low + jnp.where(bottom, out_high, roll(high, 1, 1)))
    set_rows(s_ref, N - 1, high + jnp.where(bottom, roll(low, -1, 1), out_low))
    set_rows(sh_ref, N - 1, out_high + jnp.where(bottom, low, 0.0))
    set_rows(sh_ref, 0, out_low + jnp.where(bottom, 0.0, high))
    assemble_xy(lay, s_ref)
    assemble_xy(lay, sh_ref)


def send_layers(lay, slab_ref, g_ref, s_ref, core_ref, chip_ref):
    low, high = get_rows(g_ref, 0), get_rows(g_ref, N - 1)
    _, _, part_z = lane_parts(lay, low.shape)
    s_ref[...] = g_ref[...]
    set_rows(s_ref, N - 1, jnp.where(part_z == 0, high + roll(low, -1, 1), high))
    set_rows(s_ref, 0, jnp.where(part_z == 0, low, low + roll(high, 1, 1)))
    half = N**3 // 2
    a, b = s_ref[:half, :], s_ref[half:, :]
    _, _, part_z = lane_parts(lay, a.shape)
    bottom = part_z == 0
    first = jnp.where(bottom, a, roll(b, 1, 1))
    second = jnp.where(bottom, roll(a, -1, 1), b)
    odd = (slab_ref[0] & 1) == 1
    core_ref[...] = jnp.where(odd, first, second)
    chip_ref[...] = jnp.where(odd, second, first)


def receive_layers(lay, slab_ref, core_ref, chip_ref, h_ref):
    odd = (slab_ref[0] & 1) == 1
    core, chip = core_ref[...], chip_ref[...]
    below, above = jnp.where(odd, core, chip), jnp.where(odd, chip, core)
    _, _, part_z = lane_parts(lay, core.shape)
    bottom = part_z == 0
    half = N**3 // 2
    h_ref[:half, :] = jnp.where(bottom, below, roll(above, 1, 1))
    h_ref[half:, :] = jnp.where(bottom, roll(below, -1, 1), above)


def pack_kernel(
    lay,
    base_ref,
    offset_ref,
    force_ref,
    source_ref,
    out_ref,
    base_buf,
    offset_buf,
    force_buf,
    field_ref,
    flat_ref,
    sems,
):
    pairs = (
        (source_ref, field_ref),
        (base_ref, base_buf),
        (offset_ref, offset_buf),
        (force_ref, force_buf),
    )
    copies = [pltpu.make_async_copy(a, b, sems.at[n]) for n, (a, b) in enumerate(pairs)]
    for copy in copies:
        copy.start()
    for copy in copies:
        copy.wait()
    mean = 0.5 * (get_rows(field_ref, N - 1) + roll(get_rows(field_ref, 0), -1, 1))
    set_rows(field_ref, N - 1, mean)
    set_rows(field_ref, 0, roll(mean, 1, 1))
    flat_ref[...] = field_ref[...].T
    shape = (1, N**3)
    lane = lax.broadcasted_iota(jnp.int32, shape, 1)
    points = jnp.zeros(shape, F32)
    for p in range(base_buf.shape[0]):
        for c, ref in enumerate((base_buf, offset_buf, force_buf)):
            for d in range(3):
                value = ref[p : p + 1, d : d + 1].astype(F32)
                points = jnp.where(lane == (p * 9 + c * 3 + d) * N, value, points)
    used = (lane & (N - 1)) == 0
    for d in range(lay.slabs):
        first = lay.slab_at(d) * lay.depth
        for e2 in range(lay.tiles_y):
            rows = flat_ref[pl.ds(e2 * EZ + first, lay.depth), :]
            out_ref[d, pl.ds(e2 * lay.depth, lay.depth), :] = rows
        out_ref[d, 1:2, :] = jnp.where(used, points, out_ref[d, 1:2, :])


def column(values, shape):
    node = lax.broadcasted_iota(jnp.int32, shape, 0)
    out = jnp.full(shape, float(values[0]), F32)
    for n in range(1, N):
        out = jnp.where(node == n, float(values[n]), out)
    return out


def gauss(elem, base, position, half_nodes):
    node = lax.broadcasted_iota(jnp.int32, elem.shape, 0)
    elem = elem.astype(F32)
    away = elem + half_nodes - position
    inside = (
        (elem == base)
        | (elem == base + 1.0)
        | ((elem == base - 1.0) & (node == N - 1))
        | ((elem == base + 2.0) & (node == 0))
    )
    return jnp.where(inside, jnp.exp(-(away * away) / (WIDTH_EPS * WIDTH_EPS)), 0.0)


def point_values(points_ref, row, place, scale):
    base, offset, force = (
        [points_ref[row, (place * 9 + c * 3 + d) * N] for d in range(3)] for c in range(3)
    )
    return base, [b + 1.0 + o for b, o in zip(base, offset)], [scale * f for f in force]


def for_points(points_ref, local_points, visit):
    def row_of(row, _):
        for place in range(local_points):
            visit(row, place)
        return 0

    lax.fori_loop(0, points_ref.shape[0], row_of, 0)


def right_side(lay, local_points, one, slab_ref, points_ref, g_ref, halo_ref):
    derivative, weights = one
    shape = (N, lay.width)
    part_x, part_y, part_z = lane_parts(lay, shape)
    first_z = slab_ref[0] * lay.depth
    elem_z = first_z + part_z
    elem_halo = jnp.where(part_z == 0, first_z - 1, first_z + lay.depth)
    half_nodes = column(0.5 * (1.0 + GLL_POINTS), shape)
    weight = column(weights, shape)
    columns = [column(derivative[a], shape) for a in range(N)]

    def weighted(elem, base, position):
        plain = weight * gauss(elem, base, position, half_nodes)
        terms = [columns[a] * plain[a : a + 1] for a in range(N)]
        while len(terms) > 1:
            terms = [a + b for a, b in zip(terms[::2], terms[1::2])]
        return plain, terms[0]

    def visit(p, place):
        base, position, force = point_values(points_ref, p, place, 0.25 * GAUSS_NORM)
        first = first_z.astype(F32)

        @pl.when((base[2] + 2.0 >= first - 1.0) & (base[2] - 1.0 <= first + lay.depth))
        def _():
            x0, x1 = weighted(part_x, base[0], position[0])
            y0, y1 = weighted(part_y, base[1], position[1])
            z0, z1 = weighted(elem_z, base[2], position[2])
            h0, h1 = weighted(elem_halo, base[2], position[2])
            pick = part_z[0:1] == 0
            h0 = jnp.where(pick, h0[N - 1 : N], h0[0:1])
            h1 = jnp.where(pick, h1[N - 1 : N], h1[0:1])
            x1 = force[0] * x1
            fz1 = force[2] * z1
            fz0 = force[1] * z0
            for j in range(N):
                first_part = y0[j : j + 1] * z0
                other_part = y1[j : j + 1] * fz0 + y0[j : j + 1] * fz1
                for i in range(N):
                    rows = pl.ds((i * N + j) * N, N)
                    g_ref[rows, :] += x1[i : i + 1] * first_part + x0[i : i + 1] * other_part
            first_part = y0 * h0
            other_part = y1 * (force[1] * h0) + y0 * (force[2] * h1)
            for i in range(N):
                rows = pl.ds(i * N, N)
                halo_ref[rows, :] += x1[i : i + 1] * first_part + x0[i : i + 1] * other_part

    for_points(points_ref, local_points, visit)


def inverse_diagonal(lay, slab_ref, factor_ref, dinv_ref, outer):
    shape = (N, lay.width)
    part_x, part_y, part_z = lane_parts(lay, shape)
    first = slab_ref[0] * lay.depth
    part_z = jnp.where(part_z == 0, first - 1, first + lay.depth) if outer else first + part_z
    node = lax.broadcasted_iota(jnp.int32, shape, 0)

    def share(low, high):
        return (
            jnp.where(low, 0.0, 0.5),
            jnp.where(high, 0.0, 0.5),
        )

    low_z, high_z = share(part_z == 0, part_z == EZ - 1)
    along_z = jnp.where(node == 0, low_z, jnp.where(node == N - 1, high_z, 1.0))
    if outer:
        along_z = jnp.where((part_z < 0) | (part_z >= EZ), 0.0, along_z)
    along_x = dict(zip((0, N - 1), share(part_x == 0, part_x == lay.num_x - 1)))
    along_y = dict(zip((0, N - 1), share(part_y == 0, part_y == lay.num_y - 1)))
    for i in range(N):
        for j in range(N):
            rows = pl.ds((i * N + j) * N, N)
            value = factor_ref[rows, :] * along_z
            if i in along_x:
                value = value * along_x[i]
            if j in along_y:
                value = value * along_y[j]
            dinv_ref[rows, :] = value


def diagonal_kernel(lay, slab_ref, factor_ref, dinv_ref, outer_ref):
    inverse_diagonal(lay, slab_ref, factor_ref, dinv_ref, False)
    inverse_diagonal(lay, slab_ref, factor_ref, outer_ref, True)


def first_kernel(
    lay,
    local_points,
    derivative,
    one,
    slab_ref,
    recv_ref,
    dinv_ref,
    high_ref,
    low_ref,
    along_ref,
    g_ref,
    x_ref,
    face_ref,
    points_ref,
    s_ref,
    halo_ref,
    flat_ref,
    table_ref,
    sem,
):
    count, block = recv_ref.shape[0], recv_ref.shape[1]
    for d in range(count):
        points_ref[pl.ds(d, 1), :] = recv_ref[d, 1:2, : points_ref.shape[1]]
    copy = pltpu.make_async_copy(points_ref, table_ref, sem)
    copy.start()
    for d in range(count):
        flat_ref[pl.ds(d * block, block), :] = recv_ref[d]
    g_ref[...] = flat_ref[...].T
    low, high = get_rows(g_ref, 0), get_rows(g_ref, N - 1)
    _, _, part_z = lane_parts(lay, low.shape)
    set_rows(g_ref, 0, jnp.where(part_z == 0, low, roll(high, 1, 1)))
    halo_ref[...] = jnp.where(part_z == 0, low, high)
    copy.wait()
    right_side(lay, local_points, (derivative, one[1]), slab_ref, table_ref, g_ref, halo_ref)
    assemble(lay, g_ref, s_ref, halo_ref[...])
    x_ref[...] = (1.0 / THETA) * dinv_ref[...] * s_ref[...]
    subtract_stiffness(lay, one, x_ref, g_ref, high_ref, low_ref, along_ref)
    store_faces(lay, g_ref, face_ref)


def restriction(lay, g_ref, dinv_ref, interp_ref, send_ref):
    inner = jnp.where(dinv_ref[...] != 0.0, g_ref[...], 0.0)
    high, low = split(inner)
    both = jnp.dot(
        interp_ref[...], jnp.concatenate([high, low], 1), preferred_element_type=F32
    )
    load = both[:N, : lay.width] + both[:N, lay.width :] + both[N:, : lay.width]
    rows = [load[n : n + 1] for n in range(N)]
    rows = [rows[n] + roll(rows[4 + n], lay.step_x, 1) for n in range(4)]
    rows = [rows[n] + roll(rows[2 + n], lay.step_y, 1) for n in range(2)]
    for d in range(send_ref.shape[0]):
        send_ref[d, 0:1] = rows[0]
        send_ref[d, 1:2] = rows[1]


OLD = RHO_SECOND * RHO_FIRST
NEW = 2.0 * RHO_SECOND / DELTA


def second_kernel(
    lay,
    one,
    slab_ref,
    core_ref,
    chip_ref,
    g_ref,
    x_ref,
    dinv_ref,
    high_ref,
    low_ref,
    along_ref,
    interp_ref,
    g_out,
    x_out,
    send_ref,
    core_out,
    chip_out,
    s_ref,
    u_ref,
):
    assemble(lay, g_ref, s_ref, halo_of(lay, slab_ref, core_ref, chip_ref))
    update = OLD * x_ref[...] + NEW * dinv_ref[...] * s_ref[...]
    u_ref[...] = update
    x_out[...] = x_ref[...] + update
    g_out[...] = g_ref[...]
    subtract_stiffness(lay, one, u_ref, g_out, high_ref, low_ref, along_ref)
    restriction(lay, g_out, dinv_ref, interp_ref, send_ref)
    send_layers(lay, slab_ref, g_out, s_ref, core_out, chip_out)


def solve_coarse(lay, mass, stiff, loads_ref, first_ref, second_ref):
    for s in range(lay.slabs):
        d = lay.order[s]
        first_ref[pl.ds(s, 1), :] = loads_ref[d, 0:1]
        second_ref[pl.ds(s, 1), :] = loads_ref[d, 1:2]
    shape = (lay.slabs, lay.width)
    part_x, part_y, part_z = lane_parts(lay, shape)
    row = lax.broadcasted_iota(jnp.int32, shape, 0)
    keep = ((part_x > 0) & (part_y > 0) & ((part_z > 0) | (row > 0))).astype(F32)
    bottom = part_z == 0

    def below(v):
        return jnp.where(bottom, roll(roll(v, 1, 0), -1, 1), roll(v, 1, 1))

    def around_z(v):
        return jnp.where(bottom, roll(v + roll(v, 1, 0), -1, 1), roll(v + roll(v, -1, 0), 1, 1))

    def above(v):
        return jnp.where(bottom, roll(v, -1, 1), roll(roll(v, -1, 0), 1, 1))

    def neighbours(v, step):
        return roll(v, step, 1) + roll(v, -step, 1)

    def mix(pair, v, around):
        return (2.0 * pair[0]) * v + pair[1] * around

    def operate(v):
        around = around_z(v)
        mass_z, stiff_z = mix(mass, v, around), mix(stiff, v, around)
        around = neighbours(mass_z, lay.step_y)
        both = mix(mass, mass_z, around)
        rest = mix(stiff, mass_z, around) + mix(mass, stiff_z, neighbours(stiff_z, lay.step_y))
        out = mix(stiff, both, neighbours(both, lay.step_x)) + mix(
            mass, rest, neighbours(rest, lay.step_x)
        )
        return (0.5 * keep) * out

    def inner(a, b):
        return jnp.sum(jnp.sum(a * b, axis=1, keepdims=True), axis=0, keepdims=True)

    here = pl.ds(0, lay.slabs)
    residual = keep * (first_ref[here, :] + below(second_ref[here, :]))
    image = operate(residual)
    total = jnp.zeros(shape, F32)
    for step in range(CG_STEPS):
        last = step + 1 == CG_STEPS
        norm, curv = inner(residual, residual), inner(image, residual)
        if not last:
            second = operate(image)
        if step == 0:
            alpha = norm / curv
            direction, moved = residual, image
            if not last:
                moved_image = second
        else:
            beta = norm / norm_old
            alpha = norm / (curv - beta * norm / alpha)
            direction = residual + beta * direction
            if not last:
                moved, moved_image = image + beta * moved, second + beta * moved_image
        norm_old = norm
        total = total + alpha * direction
        if not last:
            residual, image = residual - alpha * moved, image - alpha * moved_image
    here = pl.ds(N, lay.slabs)
    for ref, value in ((first_ref, total), (second_ref, above(total))):
        ref[...] = jnp.zeros(ref.shape, F32)
        ref[here, :] = value


def corners(lay, low, high):
    rows = [low, high]
    rows = rows + [roll(r, -lay.step_y, 1) for r in rows]
    rows = rows + [roll(r, -lay.step_x, 1) for r in rows]
    corner = lax.broadcasted_iota(jnp.int32, (N, lay.width), 0)
    local = jnp.broadcast_to(rows[0], (N, lay.width))
    for n in range(1, N):
        local = jnp.where(corner == n, rows[n], local)
    return local


def prolong_coarse(lay, slab_ref, first_ref, second_ref, interp_ref, image_ref, edge_ref, g_ref, h_ref, x_ref):
    mine = slab_ref[0] + N
    _, _, part_z = lane_parts(lay, (1, lay.width))
    bottom = part_z == 0
    own, outer, far = [], [], []
    for ref in (first_ref, second_ref):
        before, here, after = (ref[pl.ds(mine + shift, 1), :] for shift in (-1, 0, 1))
        own.append(here)
        outer.append(jnp.where(bottom, roll(before, -1, 1), roll(after, 1, 1)))
        far.append(jnp.where(bottom, before, after))
    local = stacked(corners(lay, *own))
    dot = functools.partial(jnp.dot, preferred_element_type=F32)
    x_ref[...] += dot(interp_ref[...], local)
    g_ref[...] -= dot(image_ref[...], local)
    h_ref[...] -= dot(image_ref[...], stacked(corners(lay, *outer)))
    edge = dot(edge_ref[...], stacked(corners(lay, *far)))
    low, high = get_rows(h_ref, 0), get_rows(h_ref, N - 1)
    set_rows(h_ref, 0, low - jnp.where(bottom, edge[FACE:], 0.0))
    set_rows(h_ref, N - 1, high - jnp.where(bottom, 0.0, edge[:FACE]))


def pair_kernel(lay, one, coarse, kind, slab_ref, core_ref, chip_ref, g_ref, x_ref, dinv_ref, outer_ref, *refs):
    refs = list(refs)
    high_ref, low_ref, along_ref, edge_high_ref, edge_low_ref = (refs.pop(0) for _ in range(5))
    if coarse:
        loads_ref, image_ref, image_edge_ref = (refs.pop(0) for _ in range(3))
    if coarse or kind == "restrict":
        interp_ref = refs.pop(0)
    if kind == "last":
        out_ref = refs.pop(0)
    else:
        g_out, x_out = refs.pop(0), refs.pop(0)
        if kind == "restrict":
            send_ref = refs.pop(0)
        core_out, chip_out = refs.pop(0), refs.pop(0)
    s_ref, sh_ref, h_ref, u_ref = (refs.pop(0) for _ in range(4))
    if kind == "last":
        g_out, x_out = refs.pop(0), refs.pop(0)

    g_out[...] = g_ref[...]
    x_out[...] = x_ref[...]
    receive_layers(lay, slab_ref, core_ref, chip_ref, h_ref)
    if coarse:
        first_ref, second_ref = refs
        solve_coarse(lay, *coarse, loads_ref, first_ref, second_ref)
        prolong_coarse(
            lay, slab_ref, first_ref, second_ref, interp_ref, image_ref, image_edge_ref, g_out, h_ref, x_out
        )
    assemble_both(lay, g_out, h_ref, s_ref, sh_ref)
    update = (1.0 / THETA) * dinv_ref[...] * s_ref[...]
    u_ref[...] = update
    outer = (1.0 / THETA) * outer_ref[...] * sh_ref[...]
    edge = times3(edge_high_ref[...], edge_low_ref[...], outer)
    _, _, part_z = lane_parts(lay, (FACE, lay.width))
    near = jnp.where(
        part_z == 0, get_rows(h_ref, N - 1) - edge[FACE:], get_rows(h_ref, 0) - edge[:FACE]
    )
    subtract_stiffness(lay, one, u_ref, g_out, high_ref, low_ref, along_ref)
    assemble(lay, g_out, s_ref, near)
    update = u_ref[...]
    following = OLD * update + NEW * dinv_ref[...] * s_ref[...]
    if kind == "last":
        total = (x_out[...] + (update + following)).T
        count, block = out_ref.shape[0], out_ref.shape[1]
        for d in range(count):
            out_ref[d] = total[d * block : (d + 1) * block]
        return
    x_out[...] += update + following
    u_ref[...] = following
    subtract_stiffness(lay, one, u_ref, g_out, high_ref, low_ref, along_ref)
    if kind == "restrict":
        restriction(lay, g_out, dinv_ref, interp_ref, send_ref)
    send_layers(lay, slab_ref, g_out, s_ref, core_out, chip_out)


def unpack_kernel(lay, recv_ref, out_ref, flat_ref):
    for d in range(lay.slabs):
        first = lay.slab_at(d) * lay.depth
        for e2 in range(lay.tiles_y):
            rows = recv_ref[d, pl.ds(e2 * lay.depth, lay.depth), :]
            flat_ref[pl.ds(e2 * EZ + first, lay.depth), :] = rows
    out_ref[...] = flat_ref[...].T


def forces_kernel(tiles_y, local_points, place_ref, points_ref, out_ref):
    shape = (N, tiles_y * EZ)
    lane = lax.broadcasted_iota(jnp.int32, shape, 1)
    first_x, first_y = place_ref[0], place_ref[1]
    elem_x = jnp.broadcast_to(first_x, shape)
    elem_y = first_y + lax.shift_right_logical(lane, log2(EZ))
    elem_z = lane & (EZ - 1)
    half_nodes = column(0.5 * (1.0 + GLL_POINTS), shape)
    out_ref[...] = jnp.zeros(out_ref.shape, F32)

    def visit(p, place):
        base, position, force = point_values(points_ref, p, place, GAUSS_NORM)
        low_x, low_y = first_x.astype(F32), first_y.astype(F32)

        @pl.when(
            (base[0] + 2.0 >= low_x)
            & (base[0] - 1.0 <= low_x)
            & (base[1] + 2.0 >= low_y)
            & (base[1] - 1.0 <= low_y + (tiles_y - 1))
        )
        def _():
            x = gauss(elem_x, base[0], position[0], half_nodes)
            y = gauss(elem_y, base[1], position[1], half_nodes)
            z = gauss(elem_z, base[2], position[2], half_nodes)
            for j in range(N):
                plane = y[j : j + 1] * z
                for i in range(N):
                    value = x[i : i + 1] * plane
                    rows = pl.ds((i * N + j) * N, N)
                    for c in range(3):
                        out_ref[c, rows, :] += force[c] * value

    for_points(points_ref, local_points, visit)


def call(kernel, outs, inputs, scratch=(), smem=0, spaces=None):
    spaces = spaces or [pltpu.SMEM] * smem + [pltpu.VMEM] * (len(inputs) - smem)
    specs = [pl.BlockSpec(memory_space=space) for space in spaces]
    shapes = [jax.ShapeDtypeStruct(s, F32) for s in outs]
    result = pl.pallas_call(
        kernel,
        out_shape=shapes,
        in_specs=specs,
        out_specs=[pl.BlockSpec(memory_space=pltpu.VMEM)] * len(shapes),
        scratch_shapes=[pltpu.VMEM(s, F32) if isinstance(s, tuple) else s for s in scratch],
        compiler_params=pltpu.CompilerParams(vmem_limit_bytes=40 * 1024 * 1024),
    )(*inputs)
    return result


def shards(source, point_base, point_offset, point_force):
    tiles_x, tiles_y = source.shape[3], source.shape[4] // EZ
    lay = Layout(lax.axis_size("ex"), lax.axis_size("ey"), tiles_x, tiles_y)
    devices = lay.mesh_x * lay.mesh_y
    derivative, weights, interp, stiff_one = build_tables()
    width, fields = lay.width, (N**3, lay.width)

    diag_w = np.diag(weights)
    full = 0.5 * (
        kron3(stiff_one, diag_w, diag_w)
        + kron3(diag_w, stiff_one, diag_w)
        + kron3(diag_w, diag_w, stiff_one)
    )
    edge_rows = np.concatenate([np.arange(FACE) * N, np.arange(FACE) * N + N - 1])
    plane = 0.5 * (np.kron(stiff_one, diag_w) + np.kron(diag_w, stiff_one))
    high, low = (jnp.asarray(t) for t in split_table(np.kron(np.eye(N // 2), plane)))
    along = np.broadcast_to(0.5 * np.kron(weights, weights)[:, None], (FACE, width))
    along = jnp.asarray(along, F32)
    edge_high, edge_low = (jnp.asarray(t) for t in split_table(full[edge_rows]))
    one = (stiff_one, weights)
    interp3 = kron3(interp, interp, interp)
    image3 = full @ interp3
    ratio = (weights[:, None] * derivative**2).sum(axis=0) / weights
    diag = 0.5 * (ratio[:, None, None] + ratio[None, :, None] + ratio[None, None, :])
    diag = diag * weights[:, None, None] * weights[None, :, None] * weights[None, None, :]
    factor = np.broadcast_to(1.0 / diag.reshape(N**3, 1), fields)
    mass = interp.T @ diag_w @ interp
    stiff = interp.T @ stiff_one @ interp
    restrict3 = jnp.asarray(np.concatenate(split_table(interp3.T), 0))
    prolong3, image3, image_edge = (
        jnp.asarray(stacked_table(t)) for t in (interp3, image3, image3[edge_rows])
    )
    factor = jnp.asarray(factor, F32)

    slab = lay.slab_at(lax.axis_index(lay.axis).astype(jnp.int32)).reshape(1)
    place = jnp.stack([lax.axis_index("ex") * tiles_x, lax.axis_index("ey") * tiles_y]).astype(
        jnp.int32
    )

    local_points = point_base.shape[1]
    block = lay.block
    (send,) = call(
        functools.partial(pack_kernel, lay),
        [(lay.slabs, block, N**3)],
        [point_base.T, point_offset.T, point_force.T, source.reshape(N**3, tiles_y * EZ)],
        [
            pltpu.VMEM((local_points, 3), jnp.int32),
            (local_points, 3),
            (local_points, 3),
            (N**3, tiles_y * EZ),
            (tiles_y * EZ, N**3),
            pltpu.SemaphoreType.DMA((4,)),
        ],
        spaces=[pltpu.HBM] * 4,
    )
    recv = lax.all_to_all(send, lay.axis, 0, 0)
    if not lay.joint:
        recv = lax.all_gather(recv, "ex", axis=0, tiled=True)
    dinv, outer = call(
        functools.partial(diagonal_kernel, lay), [fields, fields], [slab, factor], smem=1
    )

    def swap(core, chip):
        return (
            lax.ppermute(core, lay.axis, lay.swaps(0)),
            lax.ppermute(chip, lay.axis, lay.swaps(1)),
        )

    def gather(loads):
        return lax.all_to_all(loads, lay.axis, 0, 0)

    face_shape = (FACE, width)
    layer = (N**3 // 2, width)
    loads_shape = (lay.slabs, 2, width)
    table = (devices, -(-9 * N * local_points // 128) * 128)
    g, x, face, points = call(
        functools.partial(first_kernel, lay, local_points, derivative, one),
        [fields, fields, face_shape, table],
        [slab, recv, dinv, high, low, along],
        [fields, face_shape, (width, N**3), pltpu.SMEM(table, F32), pltpu.SemaphoreType.DMA],
        smem=1,
    )
    (forces,) = call(
        functools.partial(forces_kernel, tiles_y, local_points),
        [(3, N**3, tiles_y * EZ)],
        [place, points],
        smem=2,
    )
    g, x, loads, core, chip = call(
        functools.partial(second_kernel, lay, one),
        [fields, fields, loads_shape, layer, layer],
        [slab, *swap(face, face), g, x, dinv, high, low, along, restrict3],
        [fields, fields],
        smem=1,
    )
    coarse = ((mass[0, 0], mass[0, 1]), (stiff[0, 0], stiff[0, 1]))
    stiffness = [high, low, along, edge_high, edge_low]

    for cycle in range(CYCLES):
        core, chip = swap(core, chip)
        last = cycle + 1 == CYCLES
        outs = [fields, fields, layer, layer]
        scratch = [fields] * 4
        if last:
            outs = [(lay.mesh_x * lay.mesh_y, block, N**3)]
            scratch += [fields, fields]
        outs = call(
            functools.partial(pair_kernel, lay, one, coarse, "last" if last else "plain"),
            outs,
            [slab, core, chip, g, x, dinv, outer, *stiffness, gather(loads), image3, image_edge, prolong3],
            scratch + [(lay.slabs + 2 * N, width)] * 2,
            smem=1,
        )
        if last:
            break
        g, x, core, chip = outs
        g, x, loads, core, chip = call(
            functools.partial(pair_kernel, lay, one, None, "restrict"),
            [fields, fields, loads_shape, layer, layer],
            [slab, *swap(core, chip), g, x, dinv, outer, *stiffness, restrict3],
            [fields] * 4,
            smem=1,
        )
    (out,) = outs
    if not lay.joint:
        out = lax.dynamic_slice_in_dim(out, lax.axis_index("ex") * lay.mesh_y, lay.mesh_y, 0)
    out = lax.all_to_all(out, lay.axis, 0, 0)
    (pressure,) = call(
        functools.partial(unpack_kernel, lay),
        [(N**3, tiles_y * EZ)],
        [out],
        [(lay.slabs * block, N**3)],
    )
    return (
        pressure.reshape(source.shape),
        forces.reshape((3, *source.shape)),
    )


def solution(mesh):
    in_specs = (
        P(None, None, None, "ex", "ey"),
        P(None, ("ex", "ey")),
        P(None, ("ex", "ey")),
        P(None, ("ex", "ey")),
    )
    out_specs = (P(None, None, None, "ex", "ey"), P(None, None, None, None, "ex", "ey"))
    return jax.shard_map(shards, mesh=mesh, in_specs=in_specs, out_specs=out_specs, check_vma=False)
```

```python
import functools
import math

import jax
import jax.numpy as jnp
import numpy as np
from jax import lax
from jax.experimental import pallas as pl
from jax.experimental.pallas import tpu as pltpu
from jax.sharding import PartitionSpec as P

EZ = 64
CG_STEPS = 4
CYCLES = 2
N = 8
GLL_POINTS = np.array(
    [
        -1.0,
        -0.8717401485096066,
        -0.5917001814331423,
        -0.2092992179024789,
        0.2092992179024789,
        0.5917001814331423,
        0.8717401485096066,
        1.0,
    ]
)
WIDTH_EPS = 0.35
GAUSS_NORM = 1.0 / (math.pi**1.5 * WIDTH_EPS**3)
CHEB_LOW = 1.5
CHEB_HIGH = 12.0
THETA = 0.5 * (CHEB_HIGH + CHEB_LOW)
DELTA = 0.5 * (CHEB_HIGH - CHEB_LOW)
RHO_FIRST = DELTA / THETA
RHO_SECOND = 1.0 / (2.0 * THETA / DELTA - RHO_FIRST)
F32 = jnp.float32
BF16 = jnp.bfloat16
FACE = N * N


def build_tables():
    points = GLL_POINTS
    degree = len(points) - 1
    previous = points * 0.0 + 1.0
    current = points.copy()
    for k in range(1, degree):
        following = ((2 * k + 1) * points * current - k * previous) / (k + 1)
        previous = current
        current = following
    derivative = np.zeros((degree + 1, degree + 1))
    for i in range(degree + 1):
        for j in range(degree + 1):
            if i != j:
                derivative[i, j] = current[i] / (current[j] * (points[i] - points[j]))
    derivative[0, 0] = -degree * (degree + 1) / 4.0
    derivative[degree, degree] = degree * (degree + 1) / 4.0
    weights = 2.0 / (degree * (degree + 1) * current**2)
    interp = np.stack([(1.0 - points) / 2.0, (1.0 + points) / 2.0], axis=1)
    stiff_one = derivative.T @ (weights[:, None] * derivative)
    return derivative, weights, interp, stiff_one


def kron3(a, b, c):
    return np.kron(np.kron(a, b), c)


def log2(n):
    return int(n).bit_length() - 1


class Layout:
    def __init__(self, mesh_x, mesh_y, tiles_x, tiles_y):
        self.mesh_x, self.mesh_y = mesh_x, mesh_y
        self.num_x, self.num_y = tiles_x * mesh_x, tiles_y * mesh_y
        self.tiles_y = tiles_y
        self.joint = EZ % (2 * mesh_x * mesh_y) == 0
        self.axis = ("ex", "ey") if self.joint else "ey"
        self.slabs = mesh_x * mesh_y if self.joint else mesh_y
        self.depth = EZ // self.slabs
        assert self.depth == 2 and tiles_x == 1
        self.width = self.num_x * self.num_y * self.depth
        self.step_y = self.depth
        self.step_x = self.depth * self.num_y
        self.block = tiles_y * self.depth
        slab_of = [self.slab_at(d) for d in range(self.slabs)]
        self.order = [slab_of.index(s) for s in range(self.slabs)]

    def slab_at(self, d):
        if self.joint and self.mesh_x % 2 == 0 and self.mesh_y % 2 == 0:
            high = self.mesh_y // 2
            y = d & 1
            z = (d >> 1) & (high - 1)
            core = (d >> log2(self.mesh_y)) & 1
            x = d >> (log2(self.mesh_y) + 1)
            turn = y ^ (x & 1)
            return ((x * 2 + turn) * high + (z ^ (turn * (high - 1)))) * 2 + core
        if not self.joint and self.mesh_y % 8 == 0:
            return d ^ (((d >> 3) & 1) * 7)
        return d

    def slab(self):
        d = lax.axis_index("ey")
        return self.slab_at(lax.axis_index("ex") * self.mesh_y + d if self.joint else d)

    def swaps(self, first):
        pairs = []
        for s in range(first, self.slabs, 2):
            a, b = self.order[s], self.order[(s + 1) % self.slabs]
            pairs += [(a, b), (b, a)]
        return pairs


def split(x):
    high = x.astype(BF16)
    return high, (x - high.astype(F32)).astype(BF16)


def times3(high, low, x):
    xh, xl = split(x)
    dot = functools.partial(jnp.dot, preferred_element_type=F32)
    return dot(high, xh) + dot(high, xl) + dot(low, xh)


def split_table(x):
    high = x.astype(BF16)
    return high, (x - high.astype(np.float64)).astype(BF16)


def stacked_table(x):
    high, low = split_table(x)
    return np.concatenate([high, high, low, low], 1)


def stacked(x):
    high = x.astype(BF16).astype(F32)
    low = x - high
    return jnp.concatenate([high, low, high, low], 0).astype(BF16)


def subtract_stiffness(lay, one, u_ref, g_ref, high_ref, low_ref, along_ref):
    matrix, weights = one
    dot = functools.partial(jnp.dot, preferred_element_type=F32)
    half = N // 2
    for first in (0, half):
        scaled = [
            float(weights[i]) * u_ref[pl.ds(i * FACE, FACE), :] for i in range(first, first + half)
        ]
        xh, xl = split(jnp.concatenate(scaled, 0))
        both = dot(high_ref[...], jnp.concatenate([xh, xl], 1))
        rows = pl.ds(first * FACE, half * FACE)
        g_ref[rows, :] -= both[:, : lay.width] + both[:, lay.width :] + dot(low_ref[...], xh)
    even = 0.5 * (matrix[:half, :half] + matrix[:half, :half - 1 : -1])
    odd = 0.5 * (matrix[:half, :half] - matrix[:half, :half - 1 : -1])
    for j in range(N):
        values = [u_ref[pl.ds((i * N + j) * N, N), :] for i in range(N)]
        sums = [values[i] + values[N - 1 - i] for i in range(half)]
        gaps = [values[i] - values[N - 1 - i] for i in range(half)]
        along = along_ref[pl.ds(j * N, N), :]
        for i in range(half):
            a = sum(float(even[i, q]) * sums[q] for q in range(half))
            b = sum(float(odd[i, q]) * gaps[q] for q in range(half))
            g_ref[pl.ds((i * N + j) * N, N), :] -= along * (a + b)
            g_ref[pl.ds(((N - 1 - i) * N + j) * N, N), :] -= along * (a - b)


def roll(x, shift, axis):
    size = x.shape[axis]
    return pltpu.roll(x, shift % size, axis)


def lane_parts(lay, shape):
    lane = lax.broadcasted_iota(jnp.int32, shape, len(shape) - 1)
    part_z = lane & (lay.depth - 1)
    part_y = lax.shift_right_logical(lane, log2(lay.step_y)) & (lay.num_y - 1)
    part_x = lax.shift_right_logical(lane, log2(lay.step_x))
    return part_x, part_y, part_z


def get_rows(ref, k):
    if ref.shape[1] == 128:
        return ref[pl.ds(k, FACE, stride=N), :]
    return jnp.concatenate([ref[pl.ds(n * N + k, 1), :] for n in range(FACE)], 0)


def set_rows(ref, k, value):
    if ref.shape[1] == 128:
        ref[pl.ds(k, FACE, stride=N), :] = value
    else:
        for n in range(FACE):
            ref[pl.ds(n * N + k, 1), :] = value[n : n + 1]


def assemble_xy(lay, s_ref):
    last = N - 1
    for j in range(N):
        a, b = pl.ds(j * N, N), pl.ds((last * N + j) * N, N)
        low, high = s_ref[a, :], s_ref[b, :]
        s_ref[a, :] = low + roll(high, lay.step_x, 1)
        s_ref[b, :] = high + roll(low, -lay.step_x, 1)
    for i in range(N):
        a, b = pl.ds(i * N * N, N), pl.ds((i * N + last) * N, N)
        low, high = s_ref[a, :], s_ref[b, :]
        s_ref[a, :] = low + roll(high, lay.step_y, 1)
        s_ref[b, :] = high + roll(low, -lay.step_y, 1)


def assemble(lay, g_ref, s_ref, halo):
    _, _, part_z = lane_parts(lay, halo.shape)
    s_ref[...] = g_ref[...]
    low = get_rows(g_ref, 0)
    high = get_rows(g_ref, N - 1)
    set_rows(s_ref, 0, low + jnp.where(part_z == 0, halo, roll(high, 1, 1)))
    set_rows(s_ref, N - 1, high + jnp.where(part_z == lay.depth - 1, halo, roll(low, -1, 1)))
    assemble_xy(lay, s_ref)


def store_faces(lay, g_ref, face_ref):
    low = get_rows(g_ref, 0)
    high = get_rows(g_ref, N - 1)
    _, _, part_z = lane_parts(lay, low.shape)
    face_ref[...] = jnp.where(part_z == 0, low, high)


def halo_of(lay, core_ref, chip_ref):
    odd = (lay.slab() & 1) == 1
    core, chip = core_ref[...], chip_ref[...]
    below = jnp.where(odd, core, chip)
    above = jnp.where(odd, chip, core)
    _, _, part_z = lane_parts(lay, core.shape)
    return jnp.where(part_z == 0, roll(below, 1 - lay.depth, 1), roll(above, lay.depth - 1, 1))


def assemble_both(lay, g_ref, h_ref, s_ref, sh_ref):
    low, high = get_rows(g_ref, 0), get_rows(g_ref, N - 1)
    out_low, out_high = get_rows(h_ref, 0), get_rows(h_ref, N - 1)
    _, _, part_z = lane_parts(lay, low.shape)
    bottom = part_z == 0
    s_ref[...] = g_ref[...]
    sh_ref[...] = h_ref[...]
    set_rows(s_ref, 0, low + jnp.where(bottom, out_high, roll(high, 1, 1)))
    set_rows(s_ref, N - 1, high + jnp.where(bottom, roll(low, -1, 1), out_low))
    set_rows(sh_ref, N - 1, out_high + jnp.where(bottom, low, 0.0))
    set_rows(sh_ref, 0, out_low + jnp.where(bottom, 0.0, high))
    assemble_xy(lay, s_ref)
    assemble_xy(lay, sh_ref)


def send_layers(lay, g_ref, s_ref, core_ref, chip_ref):
    low, high = get_rows(g_ref, 0), get_rows(g_ref, N - 1)
    _, _, part_z = lane_parts(lay, low.shape)
    s_ref[...] = g_ref[...]
    set_rows(s_ref, N - 1, jnp.where(part_z == 0, high + roll(low, -1, 1), high))
    set_rows(s_ref, 0, jnp.where(part_z == 0, low, low + roll(high, 1, 1)))
    half = N**3 // 2
    a, b = s_ref[:half, :], s_ref[half:, :]
    _, _, part_z = lane_parts(lay, a.shape)
    bottom = part_z == 0
    first = jnp.where(bottom, a, roll(b, 1, 1))
    second = jnp.where(bottom, roll(a, -1, 1), b)
    odd = (lay.slab() & 1) == 1
    core_ref[...] = jnp.where(odd, first, second)
    chip_ref[...] = jnp.where(odd, second, first)


def receive_layers(lay, core_ref, chip_ref, h_ref):
    odd = (lay.slab() & 1) == 1
    core, chip = core_ref[...], chip_ref[...]
    below, above = jnp.where(odd, core, chip), jnp.where(odd, chip, core)
    _, _, part_z = lane_parts(lay, core.shape)
    bottom = part_z == 0
    half = N**3 // 2
    h_ref[:half, :] = jnp.where(bottom, below, roll(above, 1, 1))
    h_ref[half:, :] = jnp.where(bottom, roll(below, -1, 1), above)


def pack_kernel(
    lay,
    base_ref,
    offset_ref,
    force_ref,
    source_ref,
    out_ref,
    base_buf,
    offset_buf,
    force_buf,
    field_ref,
    flat_ref,
    sems,
):
    pairs = (
        (source_ref, field_ref),
        (base_ref, base_buf),
        (offset_ref, offset_buf),
        (force_ref, force_buf),
    )
    copies = [pltpu.make_async_copy(a, b, sems.at[n]) for n, (a, b) in enumerate(pairs)]
    for copy in copies:
        copy.start()
    for copy in copies:
        copy.wait()
    mean = 0.5 * (get_rows(field_ref, N - 1) + roll(get_rows(field_ref, 0), -1, 1))
    set_rows(field_ref, N - 1, mean)
    set_rows(field_ref, 0, roll(mean, 1, 1))
    flat_ref[...] = field_ref[...].T
    shape = (1, N**3)
    lane = lax.broadcasted_iota(jnp.int32, shape, 1)
    points = jnp.zeros(shape, F32)
    for p in range(base_buf.shape[0]):
        for c, ref in enumerate((base_buf, offset_buf, force_buf)):
            for d in range(3):
                value = ref[p : p + 1, d : d + 1].astype(F32)
                points = jnp.where(lane == (p * 9 + c * 3 + d) * N, value, points)
    used = (lane & (N - 1)) == 0
    for d in range(lay.slabs):
        first = lay.slab_at(d) * lay.depth
        for e2 in range(lay.tiles_y):
            rows = flat_ref[pl.ds(e2 * EZ + first, lay.depth), :]
            out_ref[d, pl.ds(e2 * lay.depth, lay.depth), :] = rows
        out_ref[d, 1:2, :] = jnp.where(used, points, out_ref[d, 1:2, :])


def column(values, shape):
    node = lax.broadcasted_iota(jnp.int32, shape, 0)
    out = jnp.full(shape, float(values[0]), F32)
    for n in range(1, N):
        out = jnp.where(node == n, float(values[n]), out)
    return out


def gauss(elem, base, position, half_nodes):
    node = lax.broadcasted_iota(jnp.int32, elem.shape, 0)
    elem = elem.astype(F32)
    away = elem + half_nodes - position
    inside = (
        (elem == base)
        | (elem == base + 1.0)
        | ((elem == base - 1.0) & (node == N - 1))
        | ((elem == base + 2.0) & (node == 0))
    )
    return jnp.where(inside, jnp.exp(-(away * away) / (WIDTH_EPS * WIDTH_EPS)), 0.0)


def point_values(points_ref, row, place, scale):
    base, offset, force = (
        [points_ref[row, (place * 9 + c * 3 + d) * N] for d in range(3)] for c in range(3)
    )
    return base, [b + 1.0 + o for b, o in zip(base, offset)], [scale * f for f in force]


def for_points(points_ref, local_points, visit):
    def row_of(row, _):
        for place in range(local_points):
            visit(row, place)
        return 0

    lax.fori_loop(0, points_ref.shape[0], row_of, 0)


def right_side(lay, local_points, one, points_ref, g_ref, halo_ref):
    derivative, weights = one
    shape = (N, lay.width)
    part_x, part_y, part_z = lane_parts(lay, shape)
    first_z = lay.slab() * lay.depth
    elem_z = first_z + part_z
    elem_halo = jnp.where(part_z == 0, first_z - 1, first_z + lay.depth)
    half_nodes = column(0.5 * (1.0 + GLL_POINTS), shape)
    weight = column(weights, shape)
    columns = [column(derivative[a], shape) for a in range(N)]

    def weighted(elem, base, position):
        plain = weight * gauss(elem, base, position, half_nodes)
        terms = [columns[a] * plain[a : a + 1] for a in range(N)]
        while len(terms) > 1:
            terms = [a + b for a, b in zip(terms[::2], terms[1::2])]
        return plain, terms[0]

    def visit(p, place):
        base, position, force = point_values(points_ref, p, place, 0.25 * GAUSS_NORM)
        first = first_z.astype(F32)

        @pl.when((base[2] + 2.0 >= first - 1.0) & (base[2] - 1.0 <= first + lay.depth))
        def _():
            x0, x1 = weighted(part_x, base[0], position[0])
            y0, y1 = weighted(part_y, base[1], position[1])
            z0, z1 = weighted(elem_z, base[2], position[2])
            h0, h1 = weighted(elem_halo, base[2], position[2])
            pick = part_z[0:1] == 0
            h0 = jnp.where(pick, h0[N - 1 : N], h0[0:1])
            h1 = jnp.where(pick, h1[N - 1 : N], h1[0:1])
            x1 = force[0] * x1
            fz1 = force[2] * z1
            fz0 = force[1] * z0
            for j in range(N):
                first_part = y0[j : j + 1] * z0
                other_part = y1[j : j + 1] * fz0 + y0[j : j + 1] * fz1
                for i in range(N):
                    rows = pl.ds((i * N + j) * N, N)
                    g_ref[rows, :] += x1[i : i + 1] * first_part + x0[i : i + 1] * other_part
            first_part = y0 * h0
            other_part = y1 * (force[1] * h0) + y0 * (force[2] * h1)
            for i in range(N):
                rows = pl.ds(i * N, N)
                halo_ref[rows, :] += x1[i : i + 1] * first_part + x0[i : i + 1] * other_part

    for_points(points_ref, local_points, visit)


def inverse_diagonal(lay, factor, dinv_ref, outer):
    shape = (N, lay.width)
    part_x, part_y, part_z = lane_parts(lay, shape)
    first = lay.slab() * lay.depth
    part_z = jnp.where(part_z == 0, first - 1, first + lay.depth) if outer else first + part_z
    node = lax.broadcasted_iota(jnp.int32, shape, 0)

    def share(low, high):
        return (
            jnp.where(low, 0.0, 0.5),
            jnp.where(high, 0.0, 0.5),
        )

    low_z, high_z = share(part_z == 0, part_z == EZ - 1)
    along_z = jnp.where(node == 0, low_z, jnp.where(node == N - 1, high_z, 1.0))
    if outer:
        along_z = jnp.where((part_z < 0) | (part_z >= EZ), 0.0, along_z)
    along_x = dict(zip((0, N - 1), share(part_x == 0, part_x == lay.num_x - 1)))
    along_y = dict(zip((0, N - 1), share(part_y == 0, part_y == lay.num_y - 1)))
    tables = {}
    for i in range(N // 2):
        for j in range(i + 1):
            tables[i, j] = tables[j, i] = column(factor[i, j], shape) * along_z
    for i in range(N):
        for j in range(N):
            rows = pl.ds((i * N + j) * N, N)
            value = tables[min(i, N - 1 - i), min(j, N - 1 - j)]
            if i in along_x:
                value = value * along_x[i]
            if j in along_y:
                value = value * along_y[j]
            dinv_ref[rows, :] = value


def first_kernel(
    lay,
    local_points,
    derivative,
    one,
    factor,
    recv_ref,
    high_ref,
    low_ref,
    along_ref,
    g_ref,
    x_ref,
    dinv_ref,
    outer_ref,
    face_ref,
    points_ref,
    s_ref,
    halo_ref,
    flat_ref,
    table_ref,
    sem,
):
    count, block = recv_ref.shape[0], recv_ref.shape[1]
    for d in range(count):
        points_ref[pl.ds(d, 1), :] = recv_ref[d, 1:2, : points_ref.shape[1]]
    copy = pltpu.make_async_copy(points_ref, table_ref, sem)
    copy.start()
    for d in range(count):
        flat_ref[pl.ds(d * block, block), :] = recv_ref[d]
    g_ref[...] = flat_ref[...].T
    low, high = get_rows(g_ref, 0), get_rows(g_ref, N - 1)
    _, _, part_z = lane_parts(lay, low.shape)
    set_rows(g_ref, 0, jnp.where(part_z == 0, low, roll(high, 1, 1)))
    halo_ref[...] = jnp.where(part_z == 0, low, high)
    inverse_diagonal(lay, factor, dinv_ref, False)
    inverse_diagonal(lay, factor, outer_ref, True)
    copy.wait()
    right_side(lay, local_points, (derivative, one[1]), table_ref, g_ref, halo_ref)
    assemble(lay, g_ref, s_ref, halo_ref[...])
    x_ref[...] = (1.0 / THETA) * dinv_ref[...] * s_ref[...]
    subtract_stiffness(lay, one, x_ref, g_ref, high_ref, low_ref, along_ref)
    store_faces(lay, g_ref, face_ref)


def restriction(lay, g_ref, dinv_ref, interp_ref, send_ref):
    inner = jnp.where(dinv_ref[...] != 0.0, g_ref[...], 0.0)
    high, low = split(inner)
    both = jnp.dot(
        interp_ref[...], jnp.concatenate([high, low], 1), preferred_element_type=F32
    )
    load = both[:N, : lay.width] + both[:N, lay.width :] + both[N:, : lay.width]
    rows = [load[n : n + 1] for n in range(N)]
    rows = [rows[n] + roll(rows[4 + n], lay.step_x, 1) for n in range(4)]
    rows = [rows[n] + roll(rows[2 + n], lay.step_y, 1) for n in range(2)]
    for d in range(send_ref.shape[0]):
        send_ref[d, 0:1] = rows[0]
        send_ref[d, 1:2] = rows[1]


OLD = RHO_SECOND * RHO_FIRST
NEW = 2.0 * RHO_SECOND / DELTA


def second_kernel(
    lay,
    one,
    core_ref,
    chip_ref,
    g_ref,
    x_ref,
    dinv_ref,
    high_ref,
    low_ref,
    along_ref,
    interp_ref,
    g_out,
    x_out,
    send_ref,
    core_out,
    chip_out,
    s_ref,
    u_ref,
):
    assemble(lay, g_ref, s_ref, halo_of(lay, core_ref, chip_ref))
    update = OLD * x_ref[...] + NEW * dinv_ref[...] * s_ref[...]
    u_ref[...] = update
    x_out[...] = x_ref[...] + update
    g_out[...] = g_ref[...]
    subtract_stiffness(lay, one, u_ref, g_out, high_ref, low_ref, along_ref)
    restriction(lay, g_out, dinv_ref, interp_ref, send_ref)
    send_layers(lay, g_out, s_ref, core_out, chip_out)


def solve_coarse(lay, mass, stiff, loads_ref, first_ref, second_ref):
    for s in range(lay.slabs):
        d = lay.order[s]
        first_ref[pl.ds(s, 1), :] = loads_ref[d, 0:1]
        second_ref[pl.ds(s, 1), :] = loads_ref[d, 1:2]
    shape = (lay.slabs, lay.width)
    part_x, part_y, part_z = lane_parts(lay, shape)
    row = lax.broadcasted_iota(jnp.int32, shape, 0)
    keep = ((part_x > 0) & (part_y > 0) & ((part_z > 0) | (row > 0))).astype(F32)
    bottom = part_z == 0

    def below(v):
        return jnp.where(bottom, roll(roll(v, 1, 0), -1, 1), roll(v, 1, 1))

    def around_z(v):
        return jnp.where(bottom, roll(v + roll(v, 1, 0), -1, 1), roll(v + roll(v, -1, 0), 1, 1))

    def above(v):
        return jnp.where(bottom, roll(v, -1, 1), roll(roll(v, -1, 0), 1, 1))

    def neighbours(v, step):
        return roll(v, step, 1) + roll(v, -step, 1)

    def mix(pair, v, around):
        return (2.0 * pair[0]) * v + pair[1] * around

    def operate(v):
        around = around_z(v)
        mass_z, stiff_z = mix(mass, v, around), mix(stiff, v, around)
        around = neighbours(mass_z, lay.step_y)
        both = mix(mass, mass_z, around)
        rest = mix(stiff, mass_z, around) + mix(mass, stiff_z, neighbours(stiff_z, lay.step_y))
        out = mix(stiff, both, neighbours(both, lay.step_x)) + mix(
            mass, rest, neighbours(rest, lay.step_x)
        )
        return (0.5 * keep) * out

    def inner(a, b):
        return jnp.sum(jnp.sum(a * b, axis=1, keepdims=True), axis=0, keepdims=True)

    here = pl.ds(0, lay.slabs)
    residual = keep * (first_ref[here, :] + below(second_ref[here, :]))
    image = operate(residual)
    total = jnp.zeros(shape, F32)
    for step in range(CG_STEPS):
        last = step + 1 == CG_STEPS
        norm, curv = inner(residual, residual), inner(image, residual)
        if not last:
            second = operate(image)
        if step == 0:
            alpha = norm / curv
            direction, moved = residual, image
            if not last:
                moved_image = second
        else:
            beta = norm / norm_old
            alpha = norm / (curv - beta * norm / alpha)
            direction = residual + beta * direction
            if not last:
                moved, moved_image = image + beta * moved, second + beta * moved_image
        norm_old = norm
        total = total + alpha * direction
        if not last:
            residual, image = residual - alpha * moved, image - alpha * moved_image
    here = pl.ds(N, lay.slabs)
    for ref, value in ((first_ref, total), (second_ref, above(total))):
        ref[...] = jnp.zeros(ref.shape, F32)
        ref[here, :] = value


def corners(lay, low, high):
    rows = [low, high]
    rows = rows + [roll(r, -lay.step_y, 1) for r in rows]
    rows = rows + [roll(r, -lay.step_x, 1) for r in rows]
    corner = lax.broadcasted_iota(jnp.int32, (N, lay.width), 0)
    local = jnp.broadcast_to(rows[0], (N, lay.width))
    for n in range(1, N):
        local = jnp.where(corner == n, rows[n], local)
    return local


def prolong_coarse(lay, first_ref, second_ref, interp_ref, image_ref, edge_ref, g_ref, h_ref, x_ref):
    mine = lay.slab() + N
    _, _, part_z = lane_parts(lay, (1, lay.width))
    bottom = part_z == 0
    own, outer, far = [], [], []
    for ref in (first_ref, second_ref):
        before, here, after = (ref[pl.ds(mine + shift, 1), :] for shift in (-1, 0, 1))
        own.append(here)
        outer.append(jnp.where(bottom, roll(before, -1, 1), roll(after, 1, 1)))
        far.append(jnp.where(bottom, before, after))
    local = stacked(corners(lay, *own))
    dot = functools.partial(jnp.dot, preferred_element_type=F32)
    x_ref[...] += dot(interp_ref[...], local)
    g_ref[...] -= dot(image_ref[...], local)
    h_ref[...] -= dot(image_ref[...], stacked(corners(lay, *outer)))
    edge = dot(edge_ref[...], stacked(corners(lay, *far)))
    low, high = get_rows(h_ref, 0), get_rows(h_ref, N - 1)
    set_rows(h_ref, 0, low - jnp.where(bottom, edge[FACE:], 0.0))
    set_rows(h_ref, N - 1, high - jnp.where(bottom, 0.0, edge[:FACE]))


def pair_kernel(lay, one, coarse, kind, core_ref, chip_ref, g_ref, x_ref, dinv_ref, outer_ref, *refs):
    refs = list(refs)
    high_ref, low_ref, along_ref, edge_high_ref, edge_low_ref = (refs.pop(0) for _ in range(5))
    if coarse:
        loads_ref, image_ref, image_edge_ref = (refs.pop(0) for _ in range(3))
    if coarse or kind == "restrict":
        interp_ref = refs.pop(0)
    if kind != "last":
        extra_ref = refs.pop(0)
    if kind == "last":
        out_ref = refs.pop(0)
    else:
        g_out, x_out = refs.pop(0), refs.pop(0)
        if kind == "restrict":
            send_ref = refs.pop(0)
        core_out, chip_out = refs.pop(0), refs.pop(0)
        if kind == "plain":
            points_out = refs.pop(0)
            points_out[...] = extra_ref[...]
    s_ref, sh_ref, h_ref, u_ref = (refs.pop(0) for _ in range(4))
    if kind == "last":
        g_out, x_out = refs.pop(0), refs.pop(0)

    g_out[...] = g_ref[...]
    x_out[...] = x_ref[...]
    receive_layers(lay, core_ref, chip_ref, h_ref)
    if coarse:
        first_ref, second_ref = refs
        solve_coarse(lay, *coarse, loads_ref, first_ref, second_ref)
        prolong_coarse(
            lay, first_ref, second_ref, interp_ref, image_ref, image_edge_ref, g_out, h_ref, x_out
        )
    assemble_both(lay, g_out, h_ref, s_ref, sh_ref)
    update = (1.0 / THETA) * dinv_ref[...] * s_ref[...]
    u_ref[...] = update
    outer = (1.0 / THETA) * outer_ref[...] * sh_ref[...]
    edge = times3(edge_high_ref[...], edge_low_ref[...], outer)
    _, _, part_z = lane_parts(lay, (FACE, lay.width))
    near = jnp.where(
        part_z == 0, get_rows(h_ref, N - 1) - edge[FACE:], get_rows(h_ref, 0) - edge[:FACE]
    )
    subtract_stiffness(lay, one, u_ref, g_out, high_ref, low_ref, along_ref)
    assemble(lay, g_out, s_ref, near)
    update = u_ref[...]
    following = OLD * update + NEW * dinv_ref[...] * s_ref[...]
    if kind == "last":
        total = (x_out[...] + (update + following)).T
        count, block = out_ref.shape[0], out_ref.shape[1]
        for d in range(count):
            out_ref[d] = total[d * block : (d + 1) * block]
        return
    x_out[...] += update + following
    u_ref[...] = following
    subtract_stiffness(lay, one, u_ref, g_out, high_ref, low_ref, along_ref)
    if kind == "restrict":
        restriction(lay, g_out, dinv_ref, interp_ref, send_ref)
    send_layers(lay, g_out, s_ref, core_out, chip_out)


def unpack_kernel(lay, recv_ref, out_ref, flat_ref):
    for d in range(lay.slabs):
        first = lay.slab_at(d) * lay.depth
        for e2 in range(lay.tiles_y):
            rows = recv_ref[d, pl.ds(e2 * lay.depth, lay.depth), :]
            flat_ref[pl.ds(e2 * EZ + first, lay.depth), :] = rows
    out_ref[...] = flat_ref[...].T


def forces_kernel(tiles_y, local_points, points_ref, out_ref, done_ref):
    shape = (N, tiles_y * EZ)
    lane = lax.broadcasted_iota(jnp.int32, shape, 1)
    first_x, first_y = lax.axis_index("ex"), lax.axis_index("ey") * tiles_y
    elem_x = jnp.broadcast_to(first_x, shape)
    elem_y = first_y + lax.shift_right_logical(lane, log2(EZ))
    elem_z = lane & (EZ - 1)
    half_nodes = column(0.5 * (1.0 + GLL_POINTS), shape)
    out_ref[...] = jnp.zeros(out_ref.shape, F32)
    done_ref[...] = jnp.zeros(done_ref.shape, F32)

    def visit(p, place):
        base, position, force = point_values(points_ref, p, place, GAUSS_NORM)
        low_x, low_y = first_x.astype(F32), first_y.astype(F32)

        @pl.when(
            (base[0] + 2.0 >= low_x)
            & (base[0] - 1.0 <= low_x)
            & (base[1] + 2.0 >= low_y)
            & (base[1] - 1.0 <= low_y + (tiles_y - 1))
        )
        def _():
            x = gauss(elem_x, base[0], position[0], half_nodes)
            y = gauss(elem_y, base[1], position[1], half_nodes)
            z = gauss(elem_z, base[2], position[2], half_nodes)
            for j in range(N):
                plane = y[j : j + 1] * z
                for i in range(N):
                    value = x[i : i + 1] * plane
                    rows = pl.ds((i * N + j) * N, N)
                    for c in range(3):
                        out_ref[c, rows, :] += force[c] * value

    for_points(points_ref, local_points, visit)


def call(kernel, outs, inputs, scratch=(), smem=0, spaces=None, limit=40):
    spaces = spaces or [pltpu.SMEM] * smem + [pltpu.VMEM] * (len(inputs) - smem)
    specs = [pl.BlockSpec(memory_space=space) for space in spaces]
    shapes = [jax.ShapeDtypeStruct(s, F32) for s in outs]
    result = pl.pallas_call(
        kernel,
        out_shape=shapes,
        in_specs=specs,
        out_specs=[pl.BlockSpec(memory_space=pltpu.VMEM)] * len(shapes),
        scratch_shapes=[pltpu.VMEM(s, F32) if isinstance(s, tuple) else s for s in scratch],
        compiler_params=pltpu.CompilerParams(vmem_limit_bytes=limit * 1024 * 1024),
    )(*inputs)
    return result


def shards(source, point_base, point_offset, point_force):
    tiles_x, tiles_y = source.shape[3], source.shape[4] // EZ
    lay = Layout(lax.axis_size("ex"), lax.axis_size("ey"), tiles_x, tiles_y)
    devices = lay.mesh_x * lay.mesh_y
    derivative, weights, interp, stiff_one = build_tables()
    width, fields = lay.width, (N**3, lay.width)

    diag_w = np.diag(weights)
    full = 0.5 * (
        kron3(stiff_one, diag_w, diag_w)
        + kron3(diag_w, stiff_one, diag_w)
        + kron3(diag_w, diag_w, stiff_one)
    )
    edge_rows = np.concatenate([np.arange(FACE) * N, np.arange(FACE) * N + N - 1])
    plane = 0.5 * (np.kron(stiff_one, diag_w) + np.kron(diag_w, stiff_one))
    high, low = (jnp.asarray(t) for t in split_table(np.kron(np.eye(N // 2), plane)))
    along = np.broadcast_to(0.5 * np.kron(weights, weights)[:, None], (FACE, width))
    along = jnp.asarray(along, F32)
    edge_high, edge_low = (jnp.asarray(t) for t in split_table(full[edge_rows]))
    one = (stiff_one, weights)
    interp3 = kron3(interp, interp, interp)
    image3 = full @ interp3
    ratio = (weights[:, None] * derivative**2).sum(axis=0) / weights
    diag = 0.5 * (ratio[:, None, None] + ratio[None, :, None] + ratio[None, None, :])
    diag = diag * weights[:, None, None] * weights[None, :, None] * weights[None, None, :]
    factor = 1.0 / diag
    mass = interp.T @ diag_w @ interp
    stiff = interp.T @ stiff_one @ interp
    restrict3 = jnp.asarray(np.concatenate(split_table(interp3.T), 0))
    prolong3, image3, image_edge = (
        jnp.asarray(stacked_table(t)) for t in (interp3, image3, image3[edge_rows])
    )

    local_points = point_base.shape[1]
    block = lay.block
    (send,) = call(
        functools.partial(pack_kernel, lay),
        [(lay.slabs, block, N**3)],
        [point_base.T, point_offset.T, point_force.T, source.reshape(N**3, tiles_y * EZ)],
        [
            pltpu.VMEM((local_points, 3), jnp.int32),
            (local_points, 3),
            (local_points, 3),
            (N**3, tiles_y * EZ),
            (tiles_y * EZ, N**3),
            pltpu.SemaphoreType.DMA((4,)),
        ],
        spaces=[pltpu.HBM] * 4,
        limit=60,
    )
    recv = lax.all_to_all(send, lay.axis, 0, 0)
    if not lay.joint:
        recv = lax.all_gather(recv, "ex", axis=0, tiled=True)

    def swap(core, chip):
        return (
            lax.ppermute(core, lay.axis, lay.swaps(0)),
            lax.ppermute(chip, lay.axis, lay.swaps(1)),
        )

    def gather(loads):
        return lax.all_to_all(loads, lay.axis, 0, 0)

    face_shape = (FACE, width)
    layer = (N**3 // 2, width)
    loads_shape = (lay.slabs, 2, width)
    table = (devices, -(-9 * N * local_points // 128) * 128)
    g, x, dinv, outer, face, points = call(
        functools.partial(first_kernel, lay, local_points, derivative, one, factor),
        [fields, fields, fields, fields, face_shape, table],
        [recv, high, low, along],
        [fields, face_shape, (width, N**3), pltpu.SMEM(table, F32), pltpu.SemaphoreType.DMA],
    )
    g, x, loads, core, chip = call(
        functools.partial(second_kernel, lay, one),
        [fields, fields, loads_shape, layer, layer],
        [*swap(face, face), g, x, dinv, high, low, along, restrict3],
        [fields, fields],
    )
    coarse = ((mass[0, 0], mass[0, 1]), (stiff[0, 0], stiff[0, 1]))
    stiffness = [high, low, along, edge_high, edge_low]

    for cycle in range(CYCLES):
        core, chip = swap(core, chip)
        last = cycle + 1 == CYCLES
        outs = [fields, fields, layer, layer, table]
        extra = [points]
        scratch = [fields] * 4
        if last:
            extra = []
            outs = [(lay.mesh_x * lay.mesh_y, block, N**3)]
            scratch += [fields, fields]
        outs = call(
            functools.partial(pair_kernel, lay, one, coarse, "last" if last else "plain"),
            outs,
            [core, chip, g, x, dinv, outer, *stiffness, gather(loads), image3, image_edge, prolong3, *extra],
            scratch + [(lay.slabs + 2 * N, width)] * 2,
        )
        if last:
            break
        g, x, core, chip, points = outs
        forces, done = call(
            functools.partial(forces_kernel, tiles_y, local_points),
            [(3, N**3, tiles_y * EZ), (N, 128)],
            [points],
            smem=1,
        )
        g, x, loads, core, chip = call(
            functools.partial(pair_kernel, lay, one, None, "restrict"),
            [fields, fields, loads_shape, layer, layer],
            [*swap(core, chip), g, x, dinv, outer, *stiffness, restrict3, done],
            [fields] * 4,
        )
    (out,) = outs
    if not lay.joint:
        out = lax.dynamic_slice_in_dim(out, lax.axis_index("ex") * lay.mesh_y, lay.mesh_y, 0)
    out = lax.all_to_all(out, lay.axis, 0, 0)
    (pressure,) = call(
        functools.partial(unpack_kernel, lay),
        [(N**3, tiles_y * EZ)],
        [out],
        [(lay.slabs * block, N**3)],
    )
    return (
        pressure.reshape(source.shape),
        forces.reshape((3, *source.shape)),
    )


def solution(mesh):
    in_specs = (
        P(None, None, None, "ex", "ey"),
        P(None, ("ex", "ey")),
        P(None, ("ex", "ey")),
        P(None, ("ex", "ey")),
    )
    out_specs = (P(None, None, None, "ex", "ey"), P(None, None, None, None, "ex", "ey"))
    return jax.shard_map(shards, mesh=mesh, in_specs=in_specs, out_specs=out_specs, check_vma=False)
```

```python
import functools
import math

import jax
import jax.numpy as jnp
import numpy as np
from jax import lax
from jax.experimental import pallas as pl
from jax.experimental.pallas import tpu as pltpu
from jax.sharding import PartitionSpec as P

EZ = 64
CG_STEPS = 4
CYCLES = 2
N = 8
GLL_POINTS = np.array(
    [
        -1.0,
        -0.8717401485096066,
        -0.5917001814331423,
        -0.2092992179024789,
        0.2092992179024789,
        0.5917001814331423,
        0.8717401485096066,
        1.0,
    ]
)
WIDTH_EPS = 0.35
GAUSS_NORM = 1.0 / (math.pi**1.5 * WIDTH_EPS**3)
CHEB_LOW = 1.5
CHEB_HIGH = 12.0
THETA = 0.5 * (CHEB_HIGH + CHEB_LOW)
DELTA = 0.5 * (CHEB_HIGH - CHEB_LOW)
RHO_FIRST = DELTA / THETA
RHO_SECOND = 1.0 / (2.0 * THETA / DELTA - RHO_FIRST)
F32 = jnp.float32
BF16 = jnp.bfloat16
FACE = N * N


def build_tables():
    points = GLL_POINTS
    degree = len(points) - 1
    previous = points * 0.0 + 1.0
    current = points.copy()
    for k in range(1, degree):
        following = ((2 * k + 1) * points * current - k * previous) / (k + 1)
        previous = current
        current = following
    derivative = np.zeros((degree + 1, degree + 1))
    for i in range(degree + 1):
        for j in range(degree + 1):
            if i != j:
                derivative[i, j] = current[i] / (current[j] * (points[i] - points[j]))
    derivative[0, 0] = -degree * (degree + 1) / 4.0
    derivative[degree, degree] = degree * (degree + 1) / 4.0
    weights = 2.0 / (degree * (degree + 1) * current**2)
    interp = np.stack([(1.0 - points) / 2.0, (1.0 + points) / 2.0], axis=1)
    stiff_one = derivative.T @ (weights[:, None] * derivative)
    return derivative, weights, interp, stiff_one


def kron3(a, b, c):
    return np.kron(np.kron(a, b), c)


def log2(n):
    return int(n).bit_length() - 1


class Layout:
    def __init__(self, mesh_x, mesh_y, tiles_x, tiles_y):
        self.mesh_x, self.mesh_y = mesh_x, mesh_y
        self.num_x, self.num_y = tiles_x * mesh_x, tiles_y * mesh_y
        self.tiles_y = tiles_y
        self.joint = EZ % (2 * mesh_x * mesh_y) == 0
        self.axis = ("ex", "ey") if self.joint else "ey"
        self.slabs = mesh_x * mesh_y if self.joint else mesh_y
        self.depth = EZ // self.slabs
        assert self.depth == 2 and tiles_x == 1
        self.width = self.num_x * self.num_y * self.depth
        self.step_y = self.depth
        self.step_x = self.depth * self.num_y
        self.block = tiles_y * self.depth
        slab_of = [self.slab_at(d) for d in range(self.slabs)]
        self.order = [slab_of.index(s) for s in range(self.slabs)]

    def slab_at(self, d):
        if self.joint and self.mesh_x % 2 == 0 and self.mesh_y % 2 == 0:
            high = self.mesh_y // 2
            y = d & 1
            z = (d >> 1) & (high - 1)
            core = (d >> log2(self.mesh_y)) & 1
            x = d >> (log2(self.mesh_y) + 1)
            turn = y ^ (x & 1)
            return ((x * 2 + turn) * high + (z ^ (turn * (high - 1)))) * 2 + core
        if not self.joint and self.mesh_y % 8 == 0:
            return d ^ (((d >> 3) & 1) * 7)
        return d

    def slab(self):
        d = lax.axis_index("ey")
        return self.slab_at(lax.axis_index("ex") * self.mesh_y + d if self.joint else d)

    def swaps(self, first):
        pairs = []
        for s in range(first, self.slabs, 2):
            a, b = self.order[s], self.order[(s + 1) % self.slabs]
            pairs += [(a, b), (b, a)]
        return pairs


def split(x):
    high = x.astype(BF16)
    return high, (x - high.astype(F32)).astype(BF16)


def times3(high, low, x):
    xh, xl = split(x)
    dot = functools.partial(jnp.dot, preferred_element_type=F32)
    return dot(high, xh) + dot(high, xl) + dot(low, xh)


def split_table(x):
    high = x.astype(BF16)
    return high, (x - high.astype(np.float64)).astype(BF16)


def stacked_table(x):
    high, low = split_table(x)
    return np.concatenate([high, high, low, low], 1)


def stacked(x):
    high = x.astype(BF16).astype(F32)
    low = x - high
    return jnp.concatenate([high, low, high, low], 0).astype(BF16)


def subtract_stiffness(lay, one, u_ref, g_ref, high_ref, low_ref, along_ref):
    matrix, weights = one
    dot = functools.partial(jnp.dot, preferred_element_type=F32)
    half = N // 2
    for first in (0, half):
        scaled = [
            float(weights[i]) * u_ref[pl.ds(i * FACE, FACE), :] for i in range(first, first + half)
        ]
        xh, xl = split(jnp.concatenate(scaled, 0))
        both = dot(high_ref[...], jnp.concatenate([xh, xl], 1))
        rows = pl.ds(first * FACE, half * FACE)
        g_ref[rows, :] -= both[:, : lay.width] + both[:, lay.width :] + dot(low_ref[...], xh)
    even = 0.5 * (matrix[:half, :half] + matrix[:half, :half - 1 : -1])
    odd = 0.5 * (matrix[:half, :half] - matrix[:half, :half - 1 : -1])
    for j in range(N):
        values = [u_ref[pl.ds((i * N + j) * N, N), :] for i in range(N)]
        sums = [values[i] + values[N - 1 - i] for i in range(half)]
        gaps = [values[i] - values[N - 1 - i] for i in range(half)]
        along = along_ref[pl.ds(j * N, N), :]
        for i in range(half):
            a = sum(float(even[i, q]) * sums[q] for q in range(half))
            b = sum(float(odd[i, q]) * gaps[q] for q in range(half))
            g_ref[pl.ds((i * N + j) * N, N), :] -= along * (a + b)
            g_ref[pl.ds(((N - 1 - i) * N + j) * N, N), :] -= along * (a - b)


def roll(x, shift, axis):
    size = x.shape[axis]
    return pltpu.roll(x, shift % size, axis)


def lane_parts(lay, shape):
    lane = lax.broadcasted_iota(jnp.int32, shape, len(shape) - 1)
    part_z = lane & (lay.depth - 1)
    part_y = lax.shift_right_logical(lane, log2(lay.step_y)) & (lay.num_y - 1)
    part_x = lax.shift_right_logical(lane, log2(lay.step_x))
    return part_x, part_y, part_z


def get_rows(ref, k):
    if ref.shape[1] == 128:
        return ref[pl.ds(k, FACE, stride=N), :]
    return jnp.concatenate([ref[pl.ds(n * N + k, 1), :] for n in range(FACE)], 0)


def set_rows(ref, k, value):
    if ref.shape[1] == 128:
        ref[pl.ds(k, FACE, stride=N), :] = value
    else:
        for n in range(FACE):
            ref[pl.ds(n * N + k, 1), :] = value[n : n + 1]


def assemble_xy(lay, s_ref):
    last = N - 1
    for j in range(N):
        a, b = pl.ds(j * N, N), pl.ds((last * N + j) * N, N)
        low, high = s_ref[a, :], s_ref[b, :]
        s_ref[a, :] = low + roll(high, lay.step_x, 1)
        s_ref[b, :] = high + roll(low, -lay.step_x, 1)
    for i in range(N):
        a, b = pl.ds(i * N * N, N), pl.ds((i * N + last) * N, N)
        low, high = s_ref[a, :], s_ref[b, :]
        s_ref[a, :] = low + roll(high, lay.step_y, 1)
        s_ref[b, :] = high + roll(low, -lay.step_y, 1)


def assemble(lay, g_ref, s_ref, halo):
    _, _, part_z = lane_parts(lay, halo.shape)
    s_ref[...] = g_ref[...]
    low = get_rows(g_ref, 0)
    high = get_rows(g_ref, N - 1)
    set_rows(s_ref, 0, low + jnp.where(part_z == 0, halo, roll(high, 1, 1)))
    set_rows(s_ref, N - 1, high + jnp.where(part_z == lay.depth - 1, halo, roll(low, -1, 1)))
    assemble_xy(lay, s_ref)


def store_faces(lay, g_ref, face_ref):
    low = get_rows(g_ref, 0)
    high = get_rows(g_ref, N - 1)
    _, _, part_z = lane_parts(lay, low.shape)
    face_ref[...] = jnp.where(part_z == 0, low, high)


def halo_of(lay, core_ref, chip_ref):
    odd = (lay.slab() & 1) == 1
    core, chip = core_ref[...], chip_ref[...]
    below = jnp.where(odd, core, chip)
    above = jnp.where(odd, chip, core)
    _, _, part_z = lane_parts(lay, core.shape)
    return jnp.where(part_z == 0, roll(below, 1 - lay.depth, 1), roll(above, lay.depth - 1, 1))


def assemble_both(lay, g_ref, h_ref, s_ref, sh_ref):
    low, high = get_rows(g_ref, 0), get_rows(g_ref, N - 1)
    out_low, out_high = get_rows(h_ref, 0), get_rows(h_ref, N - 1)
    _, _, part_z = lane_parts(lay, low.shape)
    bottom = part_z == 0
    s_ref[...] = g_ref[...]
    sh_ref[...] = h_ref[...]
    set_rows(s_ref, 0, low + jnp.where(bottom, out_high, roll(high, 1, 1)))
    set_rows(s_ref, N - 1, high + jnp.where(bottom, roll(low, -1, 1), out_low))
    set_rows(sh_ref, N - 1, out_high + jnp.where(bottom, low, 0.0))
    set_rows(sh_ref, 0, out_low + jnp.where(bottom, 0.0, high))
    assemble_xy(lay, s_ref)
    assemble_xy(lay, sh_ref)


def send_layers(lay, g_ref, s_ref, core_ref, chip_ref):
    low, high = get_rows(g_ref, 0), get_rows(g_ref, N - 1)
    _, _, part_z = lane_parts(lay, low.shape)
    s_ref[...] = g_ref[...]
    set_rows(s_ref, N - 1, jnp.where(part_z == 0, high + roll(low, -1, 1), high))
    set_rows(s_ref, 0, jnp.where(part_z == 0, low, low + roll(high, 1, 1)))
    half = N**3 // 2
    a, b = s_ref[:half, :], s_ref[half:, :]
    _, _, part_z = lane_parts(lay, a.shape)
    bottom = part_z == 0
    first = jnp.where(bottom, a, roll(b, 1, 1))
    second = jnp.where(bottom, roll(a, -1, 1), b)
    odd = (lay.slab() & 1) == 1
    core_ref[...] = jnp.where(odd, first, second)
    chip_ref[...] = jnp.where(odd, second, first)


def receive_layers(lay, core_ref, chip_ref, h_ref):
    odd = (lay.slab() & 1) == 1
    core, chip = core_ref[...], chip_ref[...]
    below, above = jnp.where(odd, core, chip), jnp.where(odd, chip, core)
    _, _, part_z = lane_parts(lay, core.shape)
    bottom = part_z == 0
    half = N**3 // 2
    h_ref[:half, :] = jnp.where(bottom, below, roll(above, 1, 1))
    h_ref[half:, :] = jnp.where(bottom, roll(below, -1, 1), above)


def pack_kernel(
    lay,
    base_ref,
    offset_ref,
    force_ref,
    source_ref,
    out_ref,
    base_buf,
    offset_buf,
    force_buf,
    field_ref,
    flat_ref,
    sems,
):
    pairs = (
        (source_ref, field_ref),
        (base_ref, base_buf),
        (offset_ref, offset_buf),
        (force_ref, force_buf),
    )
    copies = [pltpu.make_async_copy(a, b, sems.at[n]) for n, (a, b) in enumerate(pairs)]
    for copy in copies:
        copy.start()
    for copy in copies:
        copy.wait()
    mean = 0.5 * (get_rows(field_ref, N - 1) + roll(get_rows(field_ref, 0), -1, 1))
    set_rows(field_ref, N - 1, mean)
    set_rows(field_ref, 0, roll(mean, 1, 1))
    flat_ref[...] = field_ref[...].T
    shape = (1, N**3)
    lane = lax.broadcasted_iota(jnp.int32, shape, 1)
    points = jnp.zeros(shape, F32)
    for p in range(base_buf.shape[0]):
        for c, ref in enumerate((base_buf, offset_buf, force_buf)):
            for d in range(3):
                value = ref[p : p + 1, d : d + 1].astype(F32)
                points = jnp.where(lane == (p * 9 + c * 3 + d) * N, value, points)
    used = (lane & (N - 1)) == 0
    for d in range(lay.slabs):
        first = lay.slab_at(d) * lay.depth
        for e2 in range(lay.tiles_y):
            rows = flat_ref[pl.ds(e2 * EZ + first, lay.depth), :]
            out_ref[d, pl.ds(e2 * lay.depth, lay.depth), :] = rows
        out_ref[d, 1:2, :] = jnp.where(used, points, out_ref[d, 1:2, :])


def column(values, shape):
    node = lax.broadcasted_iota(jnp.int32, shape, 0)
    out = jnp.full(shape, float(values[0]), F32)
    for n in range(1, N):
        out = jnp.where(node == n, float(values[n]), out)
    return out


def gauss(elem, base, position, half_nodes):
    node = lax.broadcasted_iota(jnp.int32, elem.shape, 0)
    elem = elem.astype(F32)
    away = elem + half_nodes - position
    inside = (
        (elem == base)
        | (elem == base + 1.0)
        | ((elem == base - 1.0) & (node == N - 1))
        | ((elem == base + 2.0) & (node == 0))
    )
    return jnp.where(inside, jnp.exp(-(away * away) / (WIDTH_EPS * WIDTH_EPS)), 0.0)


def point_values(points_ref, row, place, scale):
    base, offset, force = (
        [points_ref[row, (place * 9 + c * 3 + d) * N] for d in range(3)] for c in range(3)
    )
    return base, [b + 1.0 + o for b, o in zip(base, offset)], [scale * f for f in force]


def for_points(points_ref, local_points, visit):
    def row_of(row, _):
        for place in range(local_points):
            visit(row, place)
        return 0

    lax.fori_loop(0, points_ref.shape[0], row_of, 0)


def right_side(lay, local_points, one, points_ref, g_ref, halo_ref):
    derivative, weights = one
    shape = (N, lay.width)
    part_x, part_y, part_z = lane_parts(lay, shape)
    first_z = lay.slab() * lay.depth
    elem_z = first_z + part_z
    elem_halo = jnp.where(part_z == 0, first_z - 1, first_z + lay.depth)
    half_nodes = column(0.5 * (1.0 + GLL_POINTS), shape)
    weight = column(weights, shape)
    columns = [column(derivative[a], shape) for a in range(N)]

    def weighted(elem, base, position):
        plain = weight * gauss(elem, base, position, half_nodes)
        terms = [columns[a] * plain[a : a + 1] for a in range(N)]
        while len(terms) > 1:
            terms = [a + b for a, b in zip(terms[::2], terms[1::2])]
        return plain, terms[0]

    def visit(p, place):
        base, position, force = point_values(points_ref, p, place, 0.25 * GAUSS_NORM)
        first = first_z.astype(F32)

        @pl.when((base[2] + 2.0 >= first - 1.0) & (base[2] - 1.0 <= first + lay.depth))
        def _():
            x0, x1 = weighted(part_x, base[0], position[0])
            y0, y1 = weighted(part_y, base[1], position[1])
            z0, z1 = weighted(elem_z, base[2], position[2])
            h0, h1 = weighted(elem_halo, base[2], position[2])
            pick = part_z[0:1] == 0
            h0 = jnp.where(pick, h0[N - 1 : N], h0[0:1])
            h1 = jnp.where(pick, h1[N - 1 : N], h1[0:1])
            x1 = force[0] * x1
            fz1 = force[2] * z1
            fz0 = force[1] * z0
            for j in range(N):
                first_part = y0[j : j + 1] * z0
                other_part = y1[j : j + 1] * fz0 + y0[j : j + 1] * fz1
                for i in range(N):
                    rows = pl.ds((i * N + j) * N, N)
                    g_ref[rows, :] += x1[i : i + 1] * first_part + x0[i : i + 1] * other_part
            first_part = y0 * h0
            other_part = y1 * (force[1] * h0) + y0 * (force[2] * h1)
            for i in range(N):
                rows = pl.ds(i * N, N)
                halo_ref[rows, :] += x1[i : i + 1] * first_part + x0[i : i + 1] * other_part

    for_points(points_ref, local_points, visit)


def inverse_diagonal(lay, factor, dinv_ref, outer):
    shape = (N, lay.width)
    part_x, part_y, part_z = lane_parts(lay, shape)
    first = lay.slab() * lay.depth
    part_z = jnp.where(part_z == 0, first - 1, first + lay.depth) if outer else first + part_z
    node = lax.broadcasted_iota(jnp.int32, shape, 0)

    def share(low, high):
        return (
            jnp.where(low, 0.0, 0.5),
            jnp.where(high, 0.0, 0.5),
        )

    low_z, high_z = share(part_z == 0, part_z == EZ - 1)
    along_z = jnp.where(node == 0, low_z, jnp.where(node == N - 1, high_z, 1.0))
    if outer:
        along_z = jnp.where((part_z < 0) | (part_z >= EZ), 0.0, along_z)
    along_x = dict(zip((0, N - 1), share(part_x == 0, part_x == lay.num_x - 1)))
    along_y = dict(zip((0, N - 1), share(part_y == 0, part_y == lay.num_y - 1)))
    tables = {}
    for i in range(N // 2):
        for j in range(i + 1):
            tables[i, j] = tables[j, i] = column(factor[i, j], shape) * along_z
    for i in range(N):
        for j in range(N):
            rows = pl.ds((i * N + j) * N, N)
            value = tables[min(i, N - 1 - i), min(j, N - 1 - j)]
            if i in along_x:
                value = value * along_x[i]
            if j in along_y:
                value = value * along_y[j]
            dinv_ref[rows, :] = value


def first_kernel(
    lay,
    local_points,
    derivative,
    one,
    factor,
    recv_ref,
    high_ref,
    low_ref,
    along_ref,
    g_ref,
    x_ref,
    dinv_ref,
    outer_ref,
    face_ref,
    points_ref,
    s_ref,
    halo_ref,
    flat_ref,
    table_ref,
    sem,
):
    count, block = recv_ref.shape[0], recv_ref.shape[1]
    for d in range(count):
        points_ref[pl.ds(d, 1), :] = recv_ref[d, 1:2, : points_ref.shape[1]]
    copy = pltpu.make_async_copy(points_ref, table_ref, sem)
    copy.start()
    for d in range(count):
        flat_ref[pl.ds(d * block, block), :] = recv_ref[d]
    g_ref[...] = flat_ref[...].T
    low, high = get_rows(g_ref, 0), get_rows(g_ref, N - 1)
    _, _, part_z = lane_parts(lay, low.shape)
    set_rows(g_ref, 0, jnp.where(part_z == 0, low, roll(high, 1, 1)))
    halo_ref[...] = jnp.where(part_z == 0, low, high)
    inverse_diagonal(lay, factor, dinv_ref, False)
    inverse_diagonal(lay, factor, outer_ref, True)
    copy.wait()
    right_side(lay, local_points, (derivative, one[1]), table_ref, g_ref, halo_ref)
    assemble(lay, g_ref, s_ref, halo_ref[...])
    x_ref[...] = (1.0 / THETA) * dinv_ref[...] * s_ref[...]
    subtract_stiffness(lay, one, x_ref, g_ref, high_ref, low_ref, along_ref)
    store_faces(lay, g_ref, face_ref)


def restriction(lay, g_ref, dinv_ref, interp_ref, send_ref):
    inner = jnp.where(dinv_ref[...] != 0.0, g_ref[...], 0.0)
    high, low = split(inner)
    both = jnp.dot(
        interp_ref[...], jnp.concatenate([high, low], 1), preferred_element_type=F32
    )
    load = both[:N, : lay.width] + both[:N, lay.width :] + both[N:, : lay.width]
    rows = [load[n : n + 1] for n in range(N)]
    rows = [rows[n] + roll(rows[4 + n], lay.step_x, 1) for n in range(4)]
    rows = [rows[n] + roll(rows[2 + n], lay.step_y, 1) for n in range(2)]
    for d in range(send_ref.shape[0]):
        send_ref[d, 0:1] = rows[0]
        send_ref[d, 1:2] = rows[1]


OLD = RHO_SECOND * RHO_FIRST
NEW = 2.0 * RHO_SECOND / DELTA


def second_kernel(
    lay,
    one,
    core_ref,
    chip_ref,
    g_ref,
    x_ref,
    dinv_ref,
    high_ref,
    low_ref,
    along_ref,
    interp_ref,
    g_out,
    x_out,
    send_ref,
    core_out,
    chip_out,
    s_ref,
    u_ref,
):
    assemble(lay, g_ref, s_ref, halo_of(lay, core_ref, chip_ref))
    update = OLD * x_ref[...] + NEW * dinv_ref[...] * s_ref[...]
    u_ref[...] = update
    x_out[...] = x_ref[...] + update
    g_out[...] = g_ref[...]
    subtract_stiffness(lay, one, u_ref, g_out, high_ref, low_ref, along_ref)
    restriction(lay, g_out, dinv_ref, interp_ref, send_ref)
    send_layers(lay, g_out, s_ref, core_out, chip_out)


def solve_coarse(lay, mass, stiff, loads_ref, first_ref, second_ref):
    for s in range(lay.slabs):
        d = lay.order[s]
        first_ref[pl.ds(s, 1), :] = loads_ref[d, 0:1]
        second_ref[pl.ds(s, 1), :] = loads_ref[d, 1:2]
    shape = (lay.slabs, lay.width)
    part_x, part_y, part_z = lane_parts(lay, shape)
    row = lax.broadcasted_iota(jnp.int32, shape, 0)
    keep = ((part_x > 0) & (part_y > 0) & ((part_z > 0) | (row > 0))).astype(F32)
    bottom = part_z == 0

    def below(v):
        return jnp.where(bottom, roll(roll(v, 1, 0), -1, 1), roll(v, 1, 1))

    def around_z(v):
        return jnp.where(bottom, roll(v + roll(v, 1, 0), -1, 1), roll(v + roll(v, -1, 0), 1, 1))

    def above(v):
        return jnp.where(bottom, roll(v, -1, 1), roll(roll(v, -1, 0), 1, 1))

    def neighbours(v, step):
        return roll(v, step, 1) + roll(v, -step, 1)

    def mix(pair, v, around):
        return (2.0 * pair[0]) * v + pair[1] * around

    def operate(v):
        around = around_z(v)
        mass_z, stiff_z = mix(mass, v, around), mix(stiff, v, around)
        around = neighbours(mass_z, lay.step_y)
        both = mix(mass, mass_z, around)
        rest = mix(stiff, mass_z, around) + mix(mass, stiff_z, neighbours(stiff_z, lay.step_y))
        out = mix(stiff, both, neighbours(both, lay.step_x)) + mix(
            mass, rest, neighbours(rest, lay.step_x)
        )
        return (0.5 * keep) * out

    def inner(a, b):
        return jnp.sum(jnp.sum(a * b, axis=1, keepdims=True), axis=0, keepdims=True)

    here = pl.ds(0, lay.slabs)
    residual = keep * (first_ref[here, :] + below(second_ref[here, :]))
    image = operate(residual)
    total = jnp.zeros(shape, F32)
    for step in range(CG_STEPS):
        last = step + 1 == CG_STEPS
        norm, curv = inner(residual, residual), inner(image, residual)
        if not last:
            second = operate(image)
        if step == 0:
            alpha = norm / curv
            direction, moved = residual, image
            if not last:
                moved_image = second
        else:
            beta = norm / norm_old
            alpha = norm / (curv - beta * norm / alpha)
            direction = residual + beta * direction
            if not last:
                moved, moved_image = image + beta * moved, second + beta * moved_image
        norm_old = norm
        total = total + alpha * direction
        if not last:
            residual, image = residual - alpha * moved, image - alpha * moved_image
    here = pl.ds(N, lay.slabs)
    for ref, value in ((first_ref, total), (second_ref, above(total))):
        ref[...] = jnp.zeros(ref.shape, F32)
        ref[here, :] = value


def corners(lay, low, high):
    rows = [low, high]
    rows = rows + [roll(r, -lay.step_y, 1) for r in rows]
    rows = rows + [roll(r, -lay.step_x, 1) for r in rows]
    corner = lax.broadcasted_iota(jnp.int32, (N, lay.width), 0)
    local = jnp.broadcast_to(rows[0], (N, lay.width))
    for n in range(1, N):
        local = jnp.where(corner == n, rows[n], local)
    return local


def prolong_coarse(lay, first_ref, second_ref, interp_ref, image_ref, edge_ref, g_ref, h_ref, x_ref):
    mine = lay.slab() + N
    _, _, part_z = lane_parts(lay, (1, lay.width))
    bottom = part_z == 0
    own, outer, far = [], [], []
    for ref in (first_ref, second_ref):
        before, here, after = (ref[pl.ds(mine + shift, 1), :] for shift in (-1, 0, 1))
        own.append(here)
        outer.append(jnp.where(bottom, roll(before, -1, 1), roll(after, 1, 1)))
        far.append(jnp.where(bottom, before, after))
    local = stacked(corners(lay, *own))
    dot = functools.partial(jnp.dot, preferred_element_type=F32)
    x_ref[...] += dot(interp_ref[...], local)
    g_ref[...] -= dot(image_ref[...], local)
    h_ref[...] -= dot(image_ref[...], stacked(corners(lay, *outer)))
    edge = dot(edge_ref[...], stacked(corners(lay, *far)))
    low, high = get_rows(h_ref, 0), get_rows(h_ref, N - 1)
    set_rows(h_ref, 0, low - jnp.where(bottom, edge[FACE:], 0.0))
    set_rows(h_ref, N - 1, high - jnp.where(bottom, 0.0, edge[:FACE]))


def pair_kernel(lay, one, coarse, kind, core_ref, chip_ref, g_ref, x_ref, dinv_ref, outer_ref, *refs):
    refs = list(refs)
    high_ref, low_ref, along_ref, edge_high_ref, edge_low_ref = (refs.pop(0) for _ in range(5))
    if coarse:
        loads_ref, image_ref, image_edge_ref = (refs.pop(0) for _ in range(3))
    if coarse or kind == "restrict":
        interp_ref = refs.pop(0)
    if kind != "last":
        extra_ref = refs.pop(0)
    if kind == "last":
        out_ref = refs.pop(0)
    else:
        g_out, x_out = refs.pop(0), refs.pop(0)
        if kind == "restrict":
            send_ref = refs.pop(0)
        core_out, chip_out = refs.pop(0), refs.pop(0)
        if kind == "plain":
            points_out = refs.pop(0)
            points_out[...] = extra_ref[...]
    s_ref, sh_ref, h_ref, u_ref = (refs.pop(0) for _ in range(4))
    if kind == "last":
        g_out, x_out = refs.pop(0), refs.pop(0)

    g_out[...] = g_ref[...]
    x_out[...] = x_ref[...]
    receive_layers(lay, core_ref, chip_ref, h_ref)
    if coarse:
        first_ref, second_ref = refs
        solve_coarse(lay, *coarse, loads_ref, first_ref, second_ref)
        prolong_coarse(
            lay, first_ref, second_ref, interp_ref, image_ref, image_edge_ref, g_out, h_ref, x_out
        )
    assemble_both(lay, g_out, h_ref, s_ref, sh_ref)
    update = (1.0 / THETA) * dinv_ref[...] * s_ref[...]
    u_ref[...] = update
    outer = (1.0 / THETA) * outer_ref[...] * sh_ref[...]
    edge = times3(edge_high_ref[...], edge_low_ref[...], outer)
    _, _, part_z = lane_parts(lay, (FACE, lay.width))
    near = jnp.where(
        part_z == 0, get_rows(h_ref, N - 1) - edge[FACE:], get_rows(h_ref, 0) - edge[:FACE]
    )
    subtract_stiffness(lay, one, u_ref, g_out, high_ref, low_ref, along_ref)
    assemble(lay, g_out, s_ref, near)
    update = u_ref[...]
    following = OLD * update + NEW * dinv_ref[...] * s_ref[...]
    if kind == "last":
        total = (x_out[...] + (update + following)).T
        count, block = out_ref.shape[0], out_ref.shape[1]
        for d in range(count):
            out_ref[d] = total[d * block : (d + 1) * block]
        return
    x_out[...] += update + following
    u_ref[...] = following
    subtract_stiffness(lay, one, u_ref, g_out, high_ref, low_ref, along_ref)
    if kind == "restrict":
        restriction(lay, g_out, dinv_ref, interp_ref, send_ref)
    send_layers(lay, g_out, s_ref, core_out, chip_out)


def unpack_kernel(lay, recv_ref, out_ref, flat_ref):
    for d in range(lay.slabs):
        first = lay.slab_at(d) * lay.depth
        for e2 in range(lay.tiles_y):
            rows = recv_ref[d, pl.ds(e2 * lay.depth, lay.depth), :]
            flat_ref[pl.ds(e2 * EZ + first, lay.depth), :] = rows
    out_ref[...] = flat_ref[...].T


def forces_kernel(tiles_y, local_points, points_ref, out_ref, done_ref):
    shape = (N, tiles_y * EZ)
    lane = lax.broadcasted_iota(jnp.int32, shape, 1)
    first_x, first_y = lax.axis_index("ex"), lax.axis_index("ey") * tiles_y
    elem_x = jnp.broadcast_to(first_x, shape)
    elem_y = first_y + lax.shift_right_logical(lane, log2(EZ))
    elem_z = lane & (EZ - 1)
    half_nodes = column(0.5 * (1.0 + GLL_POINTS), shape)
    out_ref[...] = jnp.zeros(out_ref.shape, F32)
    done_ref[...] = jnp.zeros(done_ref.shape, F32)

    def visit(p, place):
        base, position, force = point_values(points_ref, p, place, GAUSS_NORM)
        low_x, low_y = first_x.astype(F32), first_y.astype(F32)

        @pl.when(
            (base[0] + 2.0 >= low_x)
            & (base[0] - 1.0 <= low_x)
            & (base[1] + 2.0 >= low_y)
            & (base[1] - 1.0 <= low_y + (tiles_y - 1))
        )
        def _():
            x = gauss(elem_x, base[0], position[0], half_nodes)
            y = gauss(elem_y, base[1], position[1], half_nodes)
            z = gauss(elem_z, base[2], position[2], half_nodes)

            def add(along_x, along_y):
                for j in along_y:
                    plane = y[j : j + 1] * z
                    for i in along_x:
                        value = x[i : i + 1] * plane
                        rows = pl.ds((i * N + j) * N, N)
                        for c in range(3):
                            out_ref[c, rows, :] += force[c] * value

            last_y = low_y + (tiles_y - 1)
            in_x = ((base[0] == low_x) | (base[0] + 1.0 == low_x), range(N))
            in_y = ((base[1] + 1.0 >= low_y) & (base[1] <= last_y), range(N))
            for when_x, along_x in (
                in_x,
                (base[0] + 2.0 == low_x, (0,)),
                (base[0] - 1.0 == low_x, (N - 1,)),
            ):
                for when_y, along_y in (
                    in_y,
                    (base[1] + 2.0 == low_y, (0,)),
                    (base[1] - 1.0 == last_y, (N - 1,)),
                ):
                    pl.when(when_x & when_y)(functools.partial(add, along_x, along_y))

    for_points(points_ref, local_points, visit)


def call(kernel, outs, inputs, scratch=(), smem=0, spaces=None, limit=40):
    spaces = spaces or [pltpu.SMEM] * smem + [pltpu.VMEM] * (len(inputs) - smem)
    specs = [pl.BlockSpec(memory_space=space) for space in spaces]
    shapes = [jax.ShapeDtypeStruct(s, F32) for s in outs]
    result = pl.pallas_call(
        kernel,
        out_shape=shapes,
        in_specs=specs,
        out_specs=[pl.BlockSpec(memory_space=pltpu.VMEM)] * len(shapes),
        scratch_shapes=[pltpu.VMEM(s, F32) if isinstance(s, tuple) else s for s in scratch],
        compiler_params=pltpu.CompilerParams(vmem_limit_bytes=limit * 1024 * 1024),
    )(*inputs)
    return result


def shards(source, point_base, point_offset, point_force):
    tiles_x, tiles_y = source.shape[3], source.shape[4] // EZ
    lay = Layout(lax.axis_size("ex"), lax.axis_size("ey"), tiles_x, tiles_y)
    devices = lay.mesh_x * lay.mesh_y
    derivative, weights, interp, stiff_one = build_tables()
    width, fields = lay.width, (N**3, lay.width)

    diag_w = np.diag(weights)
    full = 0.5 * (
        kron3(stiff_one, diag_w, diag_w)
        + kron3(diag_w, stiff_one, diag_w)
        + kron3(diag_w, diag_w, stiff_one)
    )
    edge_rows = np.concatenate([np.arange(FACE) * N, np.arange(FACE) * N + N - 1])
    plane = 0.5 * (np.kron(stiff_one, diag_w) + np.kron(diag_w, stiff_one))
    high, low = (jnp.asarray(t) for t in split_table(np.kron(np.eye(N // 2), plane)))
    along = np.broadcast_to(0.5 * np.kron(weights, weights)[:, None], (FACE, width))
    along = jnp.asarray(along, F32)
    edge_high, edge_low = (jnp.asarray(t) for t in split_table(full[edge_rows]))
    one = (stiff_one, weights)
    interp3 = kron3(interp, interp, interp)
    image3 = full @ interp3
    ratio = (weights[:, None] * derivative**2).sum(axis=0) / weights
    diag = 0.5 * (ratio[:, None, None] + ratio[None, :, None] + ratio[None, None, :])
    diag = diag * weights[:, None, None] * weights[None, :, None] * weights[None, None, :]
    factor = 1.0 / diag
    mass = interp.T @ diag_w @ interp
    stiff = interp.T @ stiff_one @ interp
    restrict3 = jnp.asarray(np.concatenate(split_table(interp3.T), 0))
    prolong3, image3, image_edge = (
        jnp.asarray(stacked_table(t)) for t in (interp3, image3, image3[edge_rows])
    )

    local_points = point_base.shape[1]
    block = lay.block
    (send,) = call(
        functools.partial(pack_kernel, lay),
        [(lay.slabs, block, N**3)],
        [
            pltpu.with_memory_space_constraint(t, pltpu.HBM)
            for t in (
                point_base.T,
                point_offset.T,
                point_force.T,
                source.reshape(N**3, tiles_y * EZ),
            )
        ],
        [
            pltpu.VMEM((local_points, 3), jnp.int32),
            (local_points, 3),
            (local_points, 3),
            (N**3, tiles_y * EZ),
            (tiles_y * EZ, N**3),
            pltpu.SemaphoreType.DMA((4,)),
        ],
        spaces=[pltpu.HBM] * 4,
    )
    recv = lax.all_to_all(send, lay.axis, 0, 0)
    if not lay.joint:
        recv = lax.all_gather(recv, "ex", axis=0, tiled=True)

    def swap(core, chip):
        return (
            lax.ppermute(core, lay.axis, lay.swaps(0)),
            lax.ppermute(chip, lay.axis, lay.swaps(1)),
        )

    def gather(loads):
        return lax.all_to_all(loads, lay.axis, 0, 0)

    face_shape = (FACE, width)
    layer = (N**3 // 2, width)
    loads_shape = (lay.slabs, 2, width)
    table = (devices, -(-9 * N * local_points // 128) * 128)
    g, x, dinv, outer, face, points = call(
        functools.partial(first_kernel, lay, local_points, derivative, one, factor),
        [fields, fields, fields, fields, face_shape, table],
        [recv, high, low, along],
        [fields, face_shape, (width, N**3), pltpu.SMEM(table, F32), pltpu.SemaphoreType.DMA],
    )
    g, x, loads, core, chip = call(
        functools.partial(second_kernel, lay, one),
        [fields, fields, loads_shape, layer, layer],
        [*swap(face, face), g, x, dinv, high, low, along, restrict3],
        [fields, fields],
    )
    coarse = ((mass[0, 0], mass[0, 1]), (stiff[0, 0], stiff[0, 1]))
    stiffness = [high, low, along, edge_high, edge_low]

    for cycle in range(CYCLES):
        core, chip = swap(core, chip)
        last = cycle + 1 == CYCLES
        outs = [fields, fields, layer, layer, table]
        extra = [points]
        scratch = [fields] * 4
        if last:
            extra = []
            outs = [(lay.mesh_x * lay.mesh_y, block, N**3)]
            scratch += [fields, fields]
        outs = call(
            functools.partial(pair_kernel, lay, one, coarse, "last" if last else "plain"),
            outs,
            [core, chip, g, x, dinv, outer, *stiffness, gather(loads), image3, image_edge, prolong3, *extra],
            scratch + [(lay.slabs + 2 * N, width)] * 2,
        )
        if last:
            break
        g, x, core, chip, points = outs
        forces, done = call(
            functools.partial(forces_kernel, tiles_y, local_points),
            [(3, N**3, tiles_y * EZ), (N, 128)],
            [points],
            smem=1,
        )
        g, x, loads, core, chip = call(
            functools.partial(pair_kernel, lay, one, None, "restrict"),
            [fields, fields, loads_shape, layer, layer],
            [*swap(core, chip), g, x, dinv, outer, *stiffness, restrict3, done],
            [fields] * 4,
        )
    (out,) = outs
    if not lay.joint:
        out = lax.dynamic_slice_in_dim(out, lax.axis_index("ex") * lay.mesh_y, lay.mesh_y, 0)
    out = lax.all_to_all(out, lay.axis, 0, 0)
    (pressure,) = call(
        functools.partial(unpack_kernel, lay),
        [(N**3, tiles_y * EZ)],
        [out],
        [(lay.slabs * block, N**3)],
    )
    return (
        pressure.reshape(source.shape),
        forces.reshape((3, *source.shape)),
    )


def solution(mesh):
    in_specs = (
        P(None, None, None, "ex", "ey"),
        P(None, ("ex", "ey")),
        P(None, ("ex", "ey")),
        P(None, ("ex", "ey")),
    )
    out_specs = (P(None, None, None, "ex", "ey"), P(None, None, None, None, "ex", "ey"))
    return jax.shard_map(shards, mesh=mesh, in_specs=in_specs, out_specs=out_specs, check_vma=False)
```

```python
import functools
import math

import jax
import jax.numpy as jnp
import numpy as np
from jax import lax
from jax.experimental import pallas as pl
from jax.experimental.pallas import tpu as pltpu
from jax.sharding import PartitionSpec as P

EZ = 64
CG_STEPS = 4
CYCLES = 2
N = 8
GLL_POINTS = np.array(
    [
        -1.0,
        -0.8717401485096066,
        -0.5917001814331423,
        -0.2092992179024789,
        0.2092992179024789,
        0.5917001814331423,
        0.8717401485096066,
        1.0,
    ]
)
WIDTH_EPS = 0.35
GAUSS_NORM = 1.0 / (math.pi**1.5 * WIDTH_EPS**3)
CHEB_LOW = 1.5
CHEB_HIGH = 12.0
THETA = 0.5 * (CHEB_HIGH + CHEB_LOW)
DELTA = 0.5 * (CHEB_HIGH - CHEB_LOW)
RHO_FIRST = DELTA / THETA
RHO_SECOND = 1.0 / (2.0 * THETA / DELTA - RHO_FIRST)
F32 = jnp.float32
BF16 = jnp.bfloat16
FACE = N * N


def build_tables():
    points = GLL_POINTS
    degree = len(points) - 1
    previous = points * 0.0 + 1.0
    current = points.copy()
    for k in range(1, degree):
        following = ((2 * k + 1) * points * current - k * previous) / (k + 1)
        previous = current
        current = following
    derivative = np.zeros((degree + 1, degree + 1))
    for i in range(degree + 1):
        for j in range(degree + 1):
            if i != j:
                derivative[i, j] = current[i] / (current[j] * (points[i] - points[j]))
    derivative[0, 0] = -degree * (degree + 1) / 4.0
    derivative[degree, degree] = degree * (degree + 1) / 4.0
    weights = 2.0 / (degree * (degree + 1) * current**2)
    interp = np.stack([(1.0 - points) / 2.0, (1.0 + points) / 2.0], axis=1)
    stiff_one = derivative.T @ (weights[:, None] * derivative)
    return derivative, weights, interp, stiff_one


def kron3(a, b, c):
    return np.kron(np.kron(a, b), c)


def log2(n):
    return int(n).bit_length() - 1


class Layout:
    def __init__(self, mesh_x, mesh_y, tiles_x, tiles_y):
        self.mesh_x, self.mesh_y = mesh_x, mesh_y
        self.num_x, self.num_y = tiles_x * mesh_x, tiles_y * mesh_y
        self.tiles_y = tiles_y
        self.joint = EZ % (2 * mesh_x * mesh_y) == 0
        self.axis = ("ex", "ey") if self.joint else "ey"
        self.slabs = mesh_x * mesh_y if self.joint else mesh_y
        self.depth = EZ // self.slabs
        assert self.depth == 2 and tiles_x == 1
        self.width = self.num_x * self.num_y * self.depth
        self.step_y = self.depth
        self.step_x = self.depth * self.num_y
        self.block = tiles_y * self.depth
        slab_of = [self.slab_at(d) for d in range(self.slabs)]
        self.order = [slab_of.index(s) for s in range(self.slabs)]

    def slab_at(self, d):
        if self.joint and self.mesh_x % 2 == 0 and self.mesh_y % 2 == 0:
            high = self.mesh_y // 2
            y = d & 1
            z = (d >> 1) & (high - 1)
            core = (d >> log2(self.mesh_y)) & 1
            x = d >> (log2(self.mesh_y) + 1)
            turn = y ^ (x & 1)
            return ((x * 2 + turn) * high + (z ^ (turn * (high - 1)))) * 2 + core
        if not self.joint and self.mesh_y % 8 == 0:
            return d ^ (((d >> 3) & 1) * 7)
        return d

    def slab(self):
        d = lax.axis_index("ey")
        return self.slab_at(lax.axis_index("ex") * self.mesh_y + d if self.joint else d)

    def swaps(self, first):
        pairs = []
        for s in range(first, self.slabs, 2):
            a, b = self.order[s], self.order[(s + 1) % self.slabs]
            pairs += [(a, b), (b, a)]
        return pairs


def split(x):
    high = x.astype(BF16)
    return high, (x - high.astype(F32)).astype(BF16)


def times3(high, low, x):
    xh, xl = split(x)
    dot = functools.partial(jnp.dot, preferred_element_type=F32)
    return dot(high, xh) + dot(high, xl) + dot(low, xh)


def split_table(x):
    high = x.astype(BF16)
    return high, (x - high.astype(np.float64)).astype(BF16)


def stacked_table(x):
    high, low = split_table(x)
    return np.concatenate([high, high, low, low], 1)


def stacked(x):
    high = x.astype(BF16).astype(F32)
    low = x - high
    return jnp.concatenate([high, low, high, low], 0).astype(BF16)


def subtract_stiffness(lay, one, u_ref, g_ref, high_ref, low_ref, along_ref):
    matrix, weights = one
    dot = functools.partial(jnp.dot, preferred_element_type=F32)
    half = N // 2
    for first in (0, half):
        scaled = [
            float(weights[i]) * u_ref[pl.ds(i * FACE, FACE), :] for i in range(first, first + half)
        ]
        xh, xl = split(jnp.concatenate(scaled, 0))
        both = dot(high_ref[...], jnp.concatenate([xh, xl], 1))
        rows = pl.ds(first * FACE, half * FACE)
        g_ref[rows, :] -= both[:, : lay.width] + both[:, lay.width :] + dot(low_ref[...], xh)
    even = 0.5 * (matrix[:half, :half] + matrix[:half, :half - 1 : -1])
    odd = 0.5 * (matrix[:half, :half] - matrix[:half, :half - 1 : -1])
    for j in range(N):
        values = [u_ref[pl.ds((i * N + j) * N, N), :] for i in range(N)]
        sums = [values[i] + values[N - 1 - i] for i in range(half)]
        gaps = [values[i] - values[N - 1 - i] for i in range(half)]
        along = along_ref[pl.ds(j * N, N), :]
        for i in range(half):
            a = sum(float(even[i, q]) * sums[q] for q in range(half))
            b = sum(float(odd[i, q]) * gaps[q] for q in range(half))
            g_ref[pl.ds((i * N + j) * N, N), :] -= along * (a + b)
            g_ref[pl.ds(((N - 1 - i) * N + j) * N, N), :] -= along * (a - b)


def roll(x, shift, axis):
    size = x.shape[axis]
    return pltpu.roll(x, shift % size, axis)


def lane_parts(lay, shape):
    lane = lax.broadcasted_iota(jnp.int32, shape, len(shape) - 1)
    part_z = lane & (lay.depth - 1)
    part_y = lax.shift_right_logical(lane, log2(lay.step_y)) & (lay.num_y - 1)
    part_x = lax.shift_right_logical(lane, log2(lay.step_x))
    return part_x, part_y, part_z


def get_rows(ref, k):
    if ref.shape[1] == 128:
        return ref[pl.ds(k, FACE, stride=N), :]
    return jnp.concatenate([ref[pl.ds(n * N + k, 1), :] for n in range(FACE)], 0)


def set_rows(ref, k, value):
    if ref.shape[1] == 128:
        ref[pl.ds(k, FACE, stride=N), :] = value
    else:
        for n in range(FACE):
            ref[pl.ds(n * N + k, 1), :] = value[n : n + 1]


def assemble_xy(lay, s_ref):
    last = N - 1
    for j in range(N):
        a, b = pl.ds(j * N, N), pl.ds((last * N + j) * N, N)
        low, high = s_ref[a, :], s_ref[b, :]
        s_ref[a, :] = low + roll(high, lay.step_x, 1)
        s_ref[b, :] = high + roll(low, -lay.step_x, 1)
    for i in range(N):
        a, b = pl.ds(i * N * N, N), pl.ds((i * N + last) * N, N)
        low, high = s_ref[a, :], s_ref[b, :]
        s_ref[a, :] = low + roll(high, lay.step_y, 1)
        s_ref[b, :] = high + roll(low, -lay.step_y, 1)


def assemble(lay, g_ref, s_ref, halo):
    _, _, part_z = lane_parts(lay, halo.shape)
    s_ref[...] = g_ref[...]
    low = get_rows(g_ref, 0)
    high = get_rows(g_ref, N - 1)
    set_rows(s_ref, 0, low + jnp.where(part_z == 0, halo, roll(high, 1, 1)))
    set_rows(s_ref, N - 1, high + jnp.where(part_z == lay.depth - 1, halo, roll(low, -1, 1)))
    assemble_xy(lay, s_ref)


def store_faces(lay, g_ref, face_ref):
    low = get_rows(g_ref, 0)
    high = get_rows(g_ref, N - 1)
    _, _, part_z = lane_parts(lay, low.shape)
    face_ref[...] = jnp.where(part_z == 0, low, high)


def halo_of(lay, core_ref, chip_ref):
    odd = (lay.slab() & 1) == 1
    core, chip = core_ref[...], chip_ref[...]
    below = jnp.where(odd, core, chip)
    above = jnp.where(odd, chip, core)
    _, _, part_z = lane_parts(lay, core.shape)
    return jnp.where(part_z == 0, roll(below, 1 - lay.depth, 1), roll(above, lay.depth - 1, 1))


def assemble_both(lay, g_ref, h_ref, s_ref, sh_ref):
    low, high = get_rows(g_ref, 0), get_rows(g_ref, N - 1)
    out_low, out_high = get_rows(h_ref, 0), get_rows(h_ref, N - 1)
    _, _, part_z = lane_parts(lay, low.shape)
    bottom = part_z == 0
    s_ref[...] = g_ref[...]
    sh_ref[...] = h_ref[...]
    set_rows(s_ref, 0, low + jnp.where(bottom, out_high, roll(high, 1, 1)))
    set_rows(s_ref, N - 1, high + jnp.where(bottom, roll(low, -1, 1), out_low))
    set_rows(sh_ref, N - 1, out_high + jnp.where(bottom, low, 0.0))
    set_rows(sh_ref, 0, out_low + jnp.where(bottom, 0.0, high))
    assemble_xy(lay, s_ref)
    assemble_xy(lay, sh_ref)


def send_layers(lay, g_ref, s_ref, core_ref, chip_ref):
    low, high = get_rows(g_ref, 0), get_rows(g_ref, N - 1)
    _, _, part_z = lane_parts(lay, low.shape)
    s_ref[...] = g_ref[...]
    set_rows(s_ref, N - 1, jnp.where(part_z == 0, high + roll(low, -1, 1), high))
    set_rows(s_ref, 0, jnp.where(part_z == 0, low, low + roll(high, 1, 1)))
    half = N**3 // 2
    a, b = s_ref[:half, :], s_ref[half:, :]
    _, _, part_z = lane_parts(lay, a.shape)
    bottom = part_z == 0
    first = jnp.where(bottom, a, roll(b, 1, 1))
    second = jnp.where(bottom, roll(a, -1, 1), b)
    odd = (lay.slab() & 1) == 1
    core_ref[...] = jnp.where(odd, first, second)
    chip_ref[...] = jnp.where(odd, second, first)


def receive_layers(lay, core_ref, chip_ref, h_ref):
    odd = (lay.slab() & 1) == 1
    core, chip = core_ref[...], chip_ref[...]
    below, above = jnp.where(odd, core, chip), jnp.where(odd, chip, core)
    _, _, part_z = lane_parts(lay, core.shape)
    bottom = part_z == 0
    half = N**3 // 2
    h_ref[:half, :] = jnp.where(bottom, below, roll(above, 1, 1))
    h_ref[half:, :] = jnp.where(bottom, roll(below, -1, 1), above)


def pack_kernel(
    lay,
    base_ref,
    offset_ref,
    force_ref,
    source_ref,
    out_ref,
    base_buf,
    offset_buf,
    force_buf,
    field_ref,
    flat_ref,
    sems,
):
    pairs = (
        (source_ref, field_ref),
        (base_ref, base_buf),
        (offset_ref, offset_buf),
        (force_ref, force_buf),
    )
    copies = [pltpu.make_async_copy(a, b, sems.at[n]) for n, (a, b) in enumerate(pairs)]
    for copy in copies:
        copy.start()
    for copy in copies:
        copy.wait()
    mean = 0.5 * (get_rows(field_ref, N - 1) + roll(get_rows(field_ref, 0), -1, 1))
    set_rows(field_ref, N - 1, mean)
    set_rows(field_ref, 0, roll(mean, 1, 1))
    flat_ref[...] = field_ref[...].T
    shape = (1, N**3)
    lane = lax.broadcasted_iota(jnp.int32, shape, 1)
    points = jnp.zeros(shape, F32)
    for p in range(base_buf.shape[0]):
        for c, ref in enumerate((base_buf, offset_buf, force_buf)):
            for d in range(3):
                value = ref[p : p + 1, d : d + 1].astype(F32)
                points = jnp.where(lane == (p * 9 + c * 3 + d) * N, value, points)
    used = (lane & (N - 1)) == 0
    for d in range(lay.slabs):
        first = lay.slab_at(d) * lay.depth
        for e2 in range(lay.tiles_y):
            rows = flat_ref[pl.ds(e2 * EZ + first, lay.depth), :]
            out_ref[d, pl.ds(e2 * lay.depth, lay.depth), :] = rows
        out_ref[d, 1:2, :] = jnp.where(used, points, out_ref[d, 1:2, :])


def column(values, shape):
    node = lax.broadcasted_iota(jnp.int32, shape, 0)
    out = jnp.full(shape, float(values[0]), F32)
    for n in range(1, N):
        out = jnp.where(node == n, float(values[n]), out)
    return out


def gauss(elem, base, position, half_nodes):
    node = lax.broadcasted_iota(jnp.int32, elem.shape, 0)
    elem = elem.astype(F32)
    away = elem + half_nodes - position
    inside = (
        (elem == base)
        | (elem == base + 1.0)
        | ((elem == base - 1.0) & (node == N - 1))
        | ((elem == base + 2.0) & (node == 0))
    )
    return jnp.where(inside, jnp.exp(-(away * away) / (WIDTH_EPS * WIDTH_EPS)), 0.0)


def point_values(points_ref, row, place, scale):
    base, offset, force = (
        [points_ref[row, (place * 9 + c * 3 + d) * N] for d in range(3)] for c in range(3)
    )
    return base, [b + 1.0 + o for b, o in zip(base, offset)], [scale * f for f in force]


def for_points(points_ref, local_points, visit):
    def row_of(row, _):
        for place in range(local_points):
            visit(row, place)
        return 0

    lax.fori_loop(0, points_ref.shape[0], row_of, 0)


def right_side(lay, local_points, one, points_ref, g_ref, halo_ref):
    derivative, weights = one
    shape = (N, lay.width)
    part_x, part_y, part_z = lane_parts(lay, shape)
    first_z = lay.slab() * lay.depth
    elem_z = first_z + part_z
    elem_halo = jnp.where(part_z == 0, first_z - 1, first_z + lay.depth)
    half_nodes = column(0.5 * (1.0 + GLL_POINTS), shape)
    weight = column(weights, shape)
    columns = [column(derivative[a], shape) for a in range(N)]

    def weighted(elem, base, position):
        plain = weight * gauss(elem, base, position, half_nodes)
        terms = [columns[a] * plain[a : a + 1] for a in range(N)]
        while len(terms) > 1:
            terms = [a + b for a, b in zip(terms[::2], terms[1::2])]
        return plain, terms[0]

    def visit(p, place):
        base, position, force = point_values(points_ref, p, place, 0.25 * GAUSS_NORM)
        first = first_z.astype(F32)

        @pl.when((base[2] + 2.0 >= first - 1.0) & (base[2] - 1.0 <= first + lay.depth))
        def _():
            x0, x1 = weighted(part_x, base[0], position[0])
            y0, y1 = weighted(part_y, base[1], position[1])
            z0, z1 = weighted(elem_z, base[2], position[2])
            h0, h1 = weighted(elem_halo, base[2], position[2])
            pick = part_z[0:1] == 0
            h0 = jnp.where(pick, h0[N - 1 : N], h0[0:1])
            h1 = jnp.where(pick, h1[N - 1 : N], h1[0:1])
            x1 = force[0] * x1
            fz1 = force[2] * z1
            fz0 = force[1] * z0
            for j in range(N):
                first_part = y0[j : j + 1] * z0
                other_part = y1[j : j + 1] * fz0 + y0[j : j + 1] * fz1
                for i in range(N):
                    rows = pl.ds((i * N + j) * N, N)
                    g_ref[rows, :] += x1[i : i + 1] * first_part + x0[i : i + 1] * other_part
            first_part = y0 * h0
            other_part = y1 * (force[1] * h0) + y0 * (force[2] * h1)
            for i in range(N):
                rows = pl.ds(i * N, N)
                halo_ref[rows, :] += x1[i : i + 1] * first_part + x0[i : i + 1] * other_part

    for_points(points_ref, local_points, visit)


def inverse_diagonal(lay, factor, dinv_ref, outer):
    shape = (N, lay.width)
    part_x, part_y, part_z = lane_parts(lay, shape)
    first = lay.slab() * lay.depth
    part_z = jnp.where(part_z == 0, first - 1, first + lay.depth) if outer else first + part_z
    node = lax.broadcasted_iota(jnp.int32, shape, 0)

    def share(low, high):
        return (
            jnp.where(low, 0.0, 0.5),
            jnp.where(high, 0.0, 0.5),
        )

    low_z, high_z = share(part_z == 0, part_z == EZ - 1)
    along_z = jnp.where(node == 0, low_z, jnp.where(node == N - 1, high_z, 1.0))
    if outer:
        along_z = jnp.where((part_z < 0) | (part_z >= EZ), 0.0, along_z)
    along_x = dict(zip((0, N - 1), share(part_x == 0, part_x == lay.num_x - 1)))
    along_y = dict(zip((0, N - 1), share(part_y == 0, part_y == lay.num_y - 1)))
    tables = {}
    for i in range(N // 2):
        for j in range(i + 1):
            tables[i, j] = tables[j, i] = column(factor[i, j], shape) * along_z
    for i in range(N):
        for j in range(N):
            rows = pl.ds((i * N + j) * N, N)
            value = tables[min(i, N - 1 - i), min(j, N - 1 - j)]
            if i in along_x:
                value = value * along_x[i]
            if j in along_y:
                value = value * along_y[j]
            dinv_ref[rows, :] = value


def first_kernel(
    lay,
    local_points,
    derivative,
    one,
    factor,
    recv_ref,
    high_ref,
    low_ref,
    along_ref,
    g_ref,
    x_ref,
    dinv_ref,
    outer_ref,
    face_ref,
    points_ref,
    s_ref,
    halo_ref,
    flat_ref,
    table_ref,
    sem,
):
    count, block = recv_ref.shape[0], recv_ref.shape[1]
    for d in range(count):
        points_ref[pl.ds(d, 1), :] = recv_ref[d, 1:2, : points_ref.shape[1]]
    copy = pltpu.make_async_copy(points_ref, table_ref, sem)
    copy.start()
    for d in range(count):
        flat_ref[pl.ds(d * block, block), :] = recv_ref[d]
    g_ref[...] = flat_ref[...].T
    low, high = get_rows(g_ref, 0), get_rows(g_ref, N - 1)
    _, _, part_z = lane_parts(lay, low.shape)
    set_rows(g_ref, 0, jnp.where(part_z == 0, low, roll(high, 1, 1)))
    halo_ref[...] = jnp.where(part_z == 0, low, high)
    inverse_diagonal(lay, factor, dinv_ref, False)
    inverse_diagonal(lay, factor, outer_ref, True)
    copy.wait()
    right_side(lay, local_points, (derivative, one[1]), table_ref, g_ref, halo_ref)
    assemble(lay, g_ref, s_ref, halo_ref[...])
    x_ref[...] = (1.0 / THETA) * dinv_ref[...] * s_ref[...]
    subtract_stiffness(lay, one, x_ref, g_ref, high_ref, low_ref, along_ref)
    store_faces(lay, g_ref, face_ref)


def restrict_rows(lay, field, interp_ref):
    high, low = split(field)
    both = jnp.dot(
        interp_ref[...], jnp.concatenate([high, low], 1), preferred_element_type=F32
    )
    load = both[:N, : lay.width] + both[:N, lay.width :] + both[N:, : lay.width]
    rows = [load[n : n + 1] for n in range(N)]
    rows = [rows[n] + roll(rows[4 + n], lay.step_x, 1) for n in range(4)]
    return [rows[n] + roll(rows[2 + n], lay.step_y, 1) for n in range(2)]


def send_loads(lay, own, outer, far, send_ref, token_ref):
    _, _, part_z = lane_parts(lay, own[0].shape)
    bottom = part_z == 0
    before = jnp.where(bottom, 0.0, roll(outer[0], 1, 1))
    here = own[0] + jnp.where(bottom, outer[1], roll(own[1], 1, 1))
    after = jnp.where(bottom, roll(own[1], -1, 1) + roll(outer[0], -1, 1), outer[1])
    second = jnp.zeros_like(here)
    if far is not None:
        before = before + jnp.where(bottom, far[0], roll(far[1], 1, 1))
        after = after + jnp.where(bottom, 0.0, far[0])
        second = jnp.where(bottom, roll(far[1], -1, 1), 0.0)
    rows = jnp.concatenate([before, here, after, second] * 2, 0)
    for d in range(send_ref.shape[0]):
        send_ref[d] = rows
    token_ref[...] = jnp.zeros(token_ref.shape, F32)


def embed_faces(lay, u_ref, out_ref):
    low, high = get_rows(u_ref, 0), get_rows(u_ref, N - 1)
    _, _, part_z = lane_parts(lay, low.shape)
    out_ref[...] = jnp.zeros(out_ref.shape, F32)
    set_rows(out_ref, N - 1, jnp.where(part_z == 0, low, 0.0))
    set_rows(out_ref, 0, jnp.where(part_z == 0, 0.0, high))


OLD = RHO_SECOND * RHO_FIRST
NEW = 2.0 * RHO_SECOND / DELTA


def first_response(
    lay, one, g_ref, x_ref, dinv_ref, high_ref, low_ref, along_ref, interp_ref, send_ref, token_ref, s_ref, u_ref, t_ref
):
    tile = (high_ref, low_ref, along_ref)
    assemble(lay, g_ref, s_ref, jnp.zeros((FACE, lay.width), F32))
    update = NEW * dinv_ref[...] * s_ref[...]
    s_ref[...] = update
    u_ref[...] = OLD * x_ref[...] + update
    t_ref[...] = g_ref[...]
    subtract_stiffness(lay, one, u_ref, t_ref, *tile)
    own = restrict_rows(lay, t_ref[...], interp_ref)
    embed_faces(lay, s_ref, u_ref)
    t_ref[...] = jnp.zeros(t_ref.shape, F32)
    subtract_stiffness(lay, one, u_ref, t_ref, *tile)
    outer = restrict_rows(lay, t_ref[...], interp_ref)
    send_loads(lay, own, outer, None, send_ref, token_ref)


def pair_response(
    lay,
    one,
    g_ref,
    dinv_ref,
    outer_ref,
    high_ref,
    low_ref,
    along_ref,
    interp_ref,
    send_ref,
    token_ref,
    s_ref,
    sh_ref,
    u_ref,
    v_ref,
    t_ref,
    h_ref,
):
    tile = (high_ref, low_ref, along_ref)
    assemble(lay, g_ref, s_ref, jnp.zeros((FACE, lay.width), F32))
    u_ref[...] = (1.0 / THETA) * dinv_ref[...] * s_ref[...]
    t_ref[...] = g_ref[...]
    subtract_stiffness(lay, one, u_ref, t_ref, *tile)
    embed_faces(lay, u_ref, v_ref)
    h_ref[...] = jnp.zeros(h_ref.shape, F32)
    subtract_stiffness(lay, one, v_ref, h_ref, *tile)
    assemble_both(lay, t_ref, h_ref, s_ref, sh_ref)
    u_ref[...] = OLD * u_ref[...] + NEW * dinv_ref[...] * s_ref[...]
    v_ref[...] = OLD * v_ref[...] + NEW * outer_ref[...] * sh_ref[...]
    subtract_stiffness(lay, one, u_ref, t_ref, *tile)
    own = restrict_rows(lay, t_ref[...], interp_ref)
    subtract_stiffness(lay, one, v_ref, h_ref, *tile)
    outer = restrict_rows(lay, h_ref[...], interp_ref)
    embed_faces(lay, v_ref, u_ref)
    t_ref[...] = jnp.zeros(t_ref.shape, F32)
    subtract_stiffness(lay, one, u_ref, t_ref, *tile)
    far = restrict_rows(lay, t_ref[...], interp_ref)
    send_loads(lay, own, outer, far, send_ref, token_ref)


def second_kernel(
    lay,
    one,
    core_ref,
    chip_ref,
    g_ref,
    x_ref,
    dinv_ref,
    high_ref,
    low_ref,
    along_ref,
    token_ref,
    g_out,
    x_out,
    core_out,
    chip_out,
    s_ref,
    u_ref,
):
    assemble(lay, g_ref, s_ref, halo_of(lay, core_ref, chip_ref))
    update = OLD * x_ref[...] + NEW * dinv_ref[...] * s_ref[...]
    u_ref[...] = update
    x_out[...] = x_ref[...] + update
    g_out[...] = g_ref[...]
    subtract_stiffness(lay, one, u_ref, g_out, high_ref, low_ref, along_ref)
    send_layers(lay, g_out, s_ref, core_out, chip_out)


def solve_coarse(lay, mass, stiff, loads_ref, rows_ref, first_ref, second_ref):
    count = 4
    for s in range(lay.slabs):
        rows_ref[pl.ds(s * count, count), :] = loads_ref[lay.order[s], :count]

    def part(n):
        if lay.width == 128:
            return rows_ref[pl.ds(n, lay.slabs, stride=count), :]
        return jnp.concatenate(
            [rows_ref[pl.ds(s * count + n, 1), :] for s in range(lay.slabs)], 0
        )

    shape = (lay.slabs, lay.width)
    part_x, part_y, part_z = lane_parts(lay, shape)
    row = lax.broadcasted_iota(jnp.int32, shape, 0)
    keep = ((part_x > 0) & (part_y > 0) & ((part_z > 0) | (row > 0))).astype(F32)
    bottom = part_z == 0

    def around_z(v):
        return jnp.where(bottom, roll(v + roll(v, 1, 0), -1, 1), roll(v + roll(v, -1, 0), 1, 1))

    def above(v):
        return jnp.where(bottom, roll(v, -1, 1), roll(roll(v, -1, 0), 1, 1))

    def neighbours(v, step):
        return roll(v, step, 1) + roll(v, -step, 1)

    def mix(pair, v, around):
        return (2.0 * pair[0]) * v + pair[1] * around

    def operate(v):
        around = around_z(v)
        mass_z, stiff_z = mix(mass, v, around), mix(stiff, v, around)
        around = neighbours(mass_z, lay.step_y)
        both = mix(mass, mass_z, around)
        rest = mix(stiff, mass_z, around) + mix(mass, stiff_z, neighbours(stiff_z, lay.step_y))
        out = mix(stiff, both, neighbours(both, lay.step_x)) + mix(
            mass, rest, neighbours(rest, lay.step_x)
        )
        return (0.5 * keep) * out

    def inner(a, b):
        return jnp.sum(jnp.sum(a * b, axis=1, keepdims=True), axis=0, keepdims=True)

    residual = keep * (part(1) + roll(part(0), -1, 0) + roll(part(2), 1, 0) + roll(part(3), 2, 0))
    image = operate(residual)
    total = jnp.zeros(shape, F32)
    for step in range(CG_STEPS):
        last = step + 1 == CG_STEPS
        norm, curv = inner(residual, residual), inner(image, residual)
        if not last:
            second = operate(image)
        if step == 0:
            alpha = norm / curv
            direction, moved = residual, image
            if not last:
                moved_image = second
        else:
            beta = norm / norm_old
            alpha = norm / (curv - beta * norm / alpha)
            direction = residual + beta * direction
            if not last:
                moved, moved_image = image + beta * moved, second + beta * moved_image
        norm_old = norm
        total = total + alpha * direction
        if not last:
            residual, image = residual - alpha * moved, image - alpha * moved_image
    here = pl.ds(N, lay.slabs)
    for ref, value in ((first_ref, total), (second_ref, above(total))):
        ref[...] = jnp.zeros(ref.shape, F32)
        ref[here, :] = value


def corners(lay, low, high):
    rows = [low, high]
    rows = rows + [roll(r, -lay.step_y, 1) for r in rows]
    rows = rows + [roll(r, -lay.step_x, 1) for r in rows]
    corner = lax.broadcasted_iota(jnp.int32, (N, lay.width), 0)
    local = jnp.broadcast_to(rows[0], (N, lay.width))
    for n in range(1, N):
        local = jnp.where(corner == n, rows[n], local)
    return local


def prolong_coarse(lay, first_ref, second_ref, interp_ref, image_ref, edge_ref, g_ref, h_ref, x_ref):
    mine = lay.slab() + N
    _, _, part_z = lane_parts(lay, (1, lay.width))
    bottom = part_z == 0
    own, outer, far = [], [], []
    for ref in (first_ref, second_ref):
        before, here, after = (ref[pl.ds(mine + shift, 1), :] for shift in (-1, 0, 1))
        own.append(here)
        outer.append(jnp.where(bottom, roll(before, -1, 1), roll(after, 1, 1)))
        far.append(jnp.where(bottom, before, after))
    local = stacked(corners(lay, *own))
    dot = functools.partial(jnp.dot, preferred_element_type=F32)
    x_ref[...] += dot(interp_ref[...], local)
    g_ref[...] -= dot(image_ref[...], local)
    h_ref[...] -= dot(image_ref[...], stacked(corners(lay, *outer)))
    edge = dot(edge_ref[...], stacked(corners(lay, *far)))
    low, high = get_rows(h_ref, 0), get_rows(h_ref, N - 1)
    set_rows(h_ref, 0, low - jnp.where(bottom, edge[FACE:], 0.0))
    set_rows(h_ref, N - 1, high - jnp.where(bottom, 0.0, edge[:FACE]))


def pair_kernel(lay, one, coarse, kind, core_ref, chip_ref, g_ref, x_ref, dinv_ref, outer_ref, *refs):
    refs = list(refs)
    high_ref, low_ref, along_ref, edge_high_ref, edge_low_ref = (refs.pop(0) for _ in range(5))
    if coarse:
        loads_ref, image_ref, image_edge_ref = (refs.pop(0) for _ in range(3))
        interp_ref = refs.pop(0)
    if kind == "inner":
        token_ref, points_ref = refs.pop(0), refs.pop(0)
    if kind == "last":
        token_ref = refs.pop(0)
    if kind == "last":
        out_ref = refs.pop(0)
    else:
        g_out, x_out = refs.pop(0), refs.pop(0)
        core_out, chip_out = refs.pop(0), refs.pop(0)
        if kind == "inner":
            points_out = refs.pop(0)
            points_out[...] = points_ref[...]
    s_ref, sh_ref, h_ref, u_ref = (refs.pop(0) for _ in range(4))
    if kind == "last":
        g_out, x_out = refs.pop(0), refs.pop(0)

    g_out[...] = g_ref[...]
    x_out[...] = x_ref[...]
    receive_layers(lay, core_ref, chip_ref, h_ref)
    if coarse:
        rows_ref, first_ref, second_ref = refs
        solve_coarse(lay, *coarse, loads_ref, rows_ref, first_ref, second_ref)
        prolong_coarse(
            lay, first_ref, second_ref, interp_ref, image_ref, image_edge_ref, g_out, h_ref, x_out
        )
    assemble_both(lay, g_out, h_ref, s_ref, sh_ref)
    update = (1.0 / THETA) * dinv_ref[...] * s_ref[...]
    u_ref[...] = update
    outer = (1.0 / THETA) * outer_ref[...] * sh_ref[...]
    edge = times3(edge_high_ref[...], edge_low_ref[...], outer)
    _, _, part_z = lane_parts(lay, (FACE, lay.width))
    near = jnp.where(
        part_z == 0, get_rows(h_ref, N - 1) - edge[FACE:], get_rows(h_ref, 0) - edge[:FACE]
    )
    subtract_stiffness(lay, one, u_ref, g_out, high_ref, low_ref, along_ref)
    assemble(lay, g_out, s_ref, near)
    update = u_ref[...]
    following = OLD * update + NEW * dinv_ref[...] * s_ref[...]
    if kind == "last":
        total = (x_out[...] + (update + following)).T
        count, block = out_ref.shape[0], out_ref.shape[1]
        for d in range(count):
            out_ref[d] = total[d * block : (d + 1) * block]
        return
    x_out[...] += update + following
    u_ref[...] = following
    subtract_stiffness(lay, one, u_ref, g_out, high_ref, low_ref, along_ref)
    send_layers(lay, g_out, s_ref, core_out, chip_out)


def unpack_kernel(lay, recv_ref, out_ref, flat_ref):
    for d in range(lay.slabs):
        first = lay.slab_at(d) * lay.depth
        for e2 in range(lay.tiles_y):
            rows = recv_ref[d, pl.ds(e2 * lay.depth, lay.depth), :]
            flat_ref[pl.ds(e2 * EZ + first, lay.depth), :] = rows
    out_ref[...] = flat_ref[...].T


def forces_kernel(tiles_y, local_points, points_ref, out_ref, done_ref):
    shape = (N, tiles_y * EZ)
    lane = lax.broadcasted_iota(jnp.int32, shape, 1)
    first_x, first_y = lax.axis_index("ex"), lax.axis_index("ey") * tiles_y
    elem_x = jnp.broadcast_to(first_x, shape)
    elem_y = first_y + lax.shift_right_logical(lane, log2(EZ))
    elem_z = lane & (EZ - 1)
    half_nodes = column(0.5 * (1.0 + GLL_POINTS), shape)
    out_ref[...] = jnp.zeros(out_ref.shape, F32)
    done_ref[...] = jnp.zeros(done_ref.shape, F32)

    def visit(p, place):
        base, position, force = point_values(points_ref, p, place, GAUSS_NORM)
        low_x, low_y = first_x.astype(F32), first_y.astype(F32)

        @pl.when(
            (base[0] + 2.0 >= low_x)
            & (base[0] - 1.0 <= low_x)
            & (base[1] + 2.0 >= low_y)
            & (base[1] - 1.0 <= low_y + (tiles_y - 1))
        )
        def _():
            x = gauss(elem_x, base[0], position[0], half_nodes)
            y = gauss(elem_y, base[1], position[1], half_nodes)
            z = gauss(elem_z, base[2], position[2], half_nodes)

            def add(along_x, along_y):
                for j in along_y:
                    plane = y[j : j + 1] * z
                    for i in along_x:
                        value = x[i : i + 1] * plane
                        rows = pl.ds((i * N + j) * N, N)
                        for c in range(3):
                            out_ref[c, rows, :] += force[c] * value

            last_y = low_y + (tiles_y - 1)
            in_x = ((base[0] == low_x) | (base[0] + 1.0 == low_x), range(N))
            in_y = ((base[1] + 1.0 >= low_y) & (base[1] <= last_y), range(N))
            for when_x, along_x in (
                in_x,
                (base[0] + 2.0 == low_x, (0,)),
                (base[0] - 1.0 == low_x, (N - 1,)),
            ):
                for when_y, along_y in (
                    in_y,
                    (base[1] + 2.0 == low_y, (0,)),
                    (base[1] - 1.0 == last_y, (N - 1,)),
                ):
                    pl.when(when_x & when_y)(functools.partial(add, along_x, along_y))

    for_points(points_ref, local_points, visit)


def call(kernel, outs, inputs, scratch=(), smem=0, spaces=None, limit=40):
    spaces = spaces or [pltpu.SMEM] * smem + [pltpu.VMEM] * (len(inputs) - smem)
    specs = [pl.BlockSpec(memory_space=space) for space in spaces]
    shapes = [jax.ShapeDtypeStruct(s, F32) for s in outs]
    result = pl.pallas_call(
        kernel,
        out_shape=shapes,
        in_specs=specs,
        out_specs=[pl.BlockSpec(memory_space=pltpu.VMEM)] * len(shapes),
        scratch_shapes=[pltpu.VMEM(s, F32) if isinstance(s, tuple) else s for s in scratch],
        compiler_params=pltpu.CompilerParams(vmem_limit_bytes=limit * 1024 * 1024),
    )(*inputs)
    return result


def shards(source, point_base, point_offset, point_force):
    tiles_x, tiles_y = source.shape[3], source.shape[4] // EZ
    lay = Layout(lax.axis_size("ex"), lax.axis_size("ey"), tiles_x, tiles_y)
    devices = lay.mesh_x * lay.mesh_y
    derivative, weights, interp, stiff_one = build_tables()
    width, fields = lay.width, (N**3, lay.width)

    diag_w = np.diag(weights)
    full = 0.5 * (
        kron3(stiff_one, diag_w, diag_w)
        + kron3(diag_w, stiff_one, diag_w)
        + kron3(diag_w, diag_w, stiff_one)
    )
    edge_rows = np.concatenate([np.arange(FACE) * N, np.arange(FACE) * N + N - 1])
    plane = 0.5 * (np.kron(stiff_one, diag_w) + np.kron(diag_w, stiff_one))
    high, low = (jnp.asarray(t) for t in split_table(np.kron(np.eye(N // 2), plane)))
    along = np.broadcast_to(0.5 * np.kron(weights, weights)[:, None], (FACE, width))
    along = jnp.asarray(along, F32)
    edge_high, edge_low = (jnp.asarray(t) for t in split_table(full[edge_rows]))
    one = (stiff_one, weights)
    interp3 = kron3(interp, interp, interp)
    image3 = full @ interp3
    ratio = (weights[:, None] * derivative**2).sum(axis=0) / weights
    diag = 0.5 * (ratio[:, None, None] + ratio[None, :, None] + ratio[None, None, :])
    diag = diag * weights[:, None, None] * weights[None, :, None] * weights[None, None, :]
    factor = 1.0 / diag
    mass = interp.T @ diag_w @ interp
    stiff = interp.T @ stiff_one @ interp
    restrict3 = jnp.asarray(np.concatenate(split_table(interp3.T), 0))
    prolong3, image3, image_edge = (
        jnp.asarray(stacked_table(t)) for t in (interp3, image3, image3[edge_rows])
    )

    local_points = point_base.shape[1]
    block = lay.block
    (send,) = call(
        functools.partial(pack_kernel, lay),
        [(lay.slabs, block, N**3)],
        [
            pltpu.with_memory_space_constraint(t, pltpu.HBM)
            for t in (
                point_base.T,
                point_offset.T,
                point_force.T,
                source.reshape(N**3, tiles_y * EZ),
            )
        ],
        [
            pltpu.VMEM((local_points, 3), jnp.int32),
            (local_points, 3),
            (local_points, 3),
            (N**3, tiles_y * EZ),
            (tiles_y * EZ, N**3),
            pltpu.SemaphoreType.DMA((4,)),
        ],
        spaces=[pltpu.HBM] * 4,
    )
    recv = lax.all_to_all(send, lay.axis, 0, 0)
    if not lay.joint:
        recv = lax.all_gather(recv, "ex", axis=0, tiled=True)

    def swap(core, chip):
        return (
            lax.ppermute(core, lay.axis, lay.swaps(0)),
            lax.ppermute(chip, lay.axis, lay.swaps(1)),
        )

    def gather(loads):
        return lax.all_to_all(loads, lay.axis, 0, 0)

    face_shape = (FACE, width)
    layer = (N**3 // 2, width)
    loads_shape = (lay.slabs, N, width)
    table = (devices, -(-9 * N * local_points // 128) * 128)
    g, x, dinv, outer, face, points = call(
        functools.partial(first_kernel, lay, local_points, derivative, one, factor),
        [fields, fields, fields, fields, face_shape, table],
        [recv, high, low, along],
        [fields, face_shape, (width, N**3), pltpu.SMEM(table, F32), pltpu.SemaphoreType.DMA],
    )
    faces = swap(face, face)
    loads, token = call(
        functools.partial(first_response, lay, one),
        [loads_shape, (N, 128)],
        [g, x, dinv, high, low, along, restrict3],
        [fields] * 3,
    )
    loads = gather(loads)
    g, x, core, chip = call(
        functools.partial(second_kernel, lay, one),
        [fields, fields, layer, layer],
        [*faces, g, x, dinv, high, low, along, token],
        [fields, fields],
    )
    coarse = ((mass[0, 0], mass[0, 1]), (stiff[0, 0], stiff[0, 1]))
    stiffness = [high, low, along, edge_high, edge_low]

    for cycle in range(CYCLES):
        core, chip = swap(core, chip)
        last = cycle + 1 == CYCLES
        outs = [fields, fields, layer, layer]
        extra = [done] if last else []
        scratch = [fields] * 4
        if last:
            outs = [(lay.mesh_x * lay.mesh_y, block, N**3)]
            scratch += [fields, fields]
        outs = call(
            functools.partial(pair_kernel, lay, one, coarse, "last" if last else "plain"),
            outs,
            [core, chip, g, x, dinv, outer, *stiffness, loads, image3, image_edge, prolong3, *extra],
            scratch + [(lay.slabs * 4, width)] + [(lay.slabs + 2 * N, width)] * 2,
        )
        if last:
            break
        g, x, core, chip = outs
        layers = swap(core, chip)
        loads, token = call(
            functools.partial(pair_response, lay, one),
            [loads_shape, (N, 128)],
            [g, dinv, outer, high, low, along, restrict3],
            [fields] * 6,
        )
        loads = gather(loads)
        g, x, core, chip, points = call(
            functools.partial(pair_kernel, lay, one, None, "inner"),
            [fields, fields, layer, layer, table],
            [*layers, g, x, dinv, outer, *stiffness, token, points],
            [fields] * 4,
        )
        forces, done = call(
            functools.partial(forces_kernel, tiles_y, local_points),
            [(3, N**3, tiles_y * EZ), (N, 128)],
            [points],
            smem=1,
        )
    (out,) = outs
    if not lay.joint:
        out = lax.dynamic_slice_in_dim(out, lax.axis_index("ex") * lay.mesh_y, lay.mesh_y, 0)
    out = lax.all_to_all(out, lay.axis, 0, 0)
    (pressure,) = call(
        functools.partial(unpack_kernel, lay),
        [(N**3, tiles_y * EZ)],
        [out],
        [(lay.slabs * block, N**3)],
    )
    return (
        pressure.reshape(source.shape),
        forces.reshape((3, *source.shape)),
    )


def solution(mesh):
    in_specs = (
        P(None, None, None, "ex", "ey"),
        P(None, ("ex", "ey")),
        P(None, ("ex", "ey")),
        P(None, ("ex", "ey")),
    )
    out_specs = (P(None, None, None, "ex", "ey"), P(None, None, None, None, "ex", "ey"))
    return jax.shard_map(shards, mesh=mesh, in_specs=in_specs, out_specs=out_specs, check_vma=False)
```

```python
import functools
import math

import jax
import jax.numpy as jnp
import numpy as np
from jax import lax
from jax.experimental import pallas as pl
from jax.experimental.pallas import tpu as pltpu
from jax.sharding import PartitionSpec as P

EZ = 64
CG_STEPS = 4
CYCLES = 2
N = 8
GLL_POINTS = np.array(
    [
        -1.0,
        -0.8717401485096066,
        -0.5917001814331423,
        -0.2092992179024789,
        0.2092992179024789,
        0.5917001814331423,
        0.8717401485096066,
        1.0,
    ]
)
WIDTH_EPS = 0.35
GAUSS_NORM = 1.0 / (math.pi**1.5 * WIDTH_EPS**3)
CHEB_LOW = 1.5
CHEB_HIGH = 12.0
THETA = 0.5 * (CHEB_HIGH + CHEB_LOW)
DELTA = 0.5 * (CHEB_HIGH - CHEB_LOW)
RHO_FIRST = DELTA / THETA
RHO_SECOND = 1.0 / (2.0 * THETA / DELTA - RHO_FIRST)
F32 = jnp.float32
BF16 = jnp.bfloat16
FACE = N * N


def build_tables():
    points = GLL_POINTS
    degree = len(points) - 1
    previous = points * 0.0 + 1.0
    current = points.copy()
    for k in range(1, degree):
        following = ((2 * k + 1) * points * current - k * previous) / (k + 1)
        previous = current
        current = following
    derivative = np.zeros((degree + 1, degree + 1))
    for i in range(degree + 1):
        for j in range(degree + 1):
            if i != j:
                derivative[i, j] = current[i] / (current[j] * (points[i] - points[j]))
    derivative[0, 0] = -degree * (degree + 1) / 4.0
    derivative[degree, degree] = degree * (degree + 1) / 4.0
    weights = 2.0 / (degree * (degree + 1) * current**2)
    interp = np.stack([(1.0 - points) / 2.0, (1.0 + points) / 2.0], axis=1)
    stiff_one = derivative.T @ (weights[:, None] * derivative)
    return derivative, weights, interp, stiff_one


def kron3(a, b, c):
    return np.kron(np.kron(a, b), c)


def log2(n):
    return int(n).bit_length() - 1


class Layout:
    def __init__(self, mesh_x, mesh_y, tiles_x, tiles_y):
        self.mesh_x, self.mesh_y = mesh_x, mesh_y
        self.num_x, self.num_y = tiles_x * mesh_x, tiles_y * mesh_y
        self.tiles_y = tiles_y
        self.joint = EZ % (2 * mesh_x * mesh_y) == 0
        self.axis = ("ex", "ey") if self.joint else "ey"
        self.slabs = mesh_x * mesh_y if self.joint else mesh_y
        self.depth = EZ // self.slabs
        assert self.depth == 2 and tiles_x == 1
        self.width = self.num_x * self.num_y * self.depth
        self.step_y = self.depth
        self.step_x = self.depth * self.num_y
        self.block = tiles_y * self.depth
        slab_of = [self.slab_at(d) for d in range(self.slabs)]
        self.order = [slab_of.index(s) for s in range(self.slabs)]

    def slab_at(self, d):
        if self.joint and self.mesh_x % 2 == 0 and self.mesh_y % 2 == 0:
            high = self.mesh_y // 2
            y = d & 1
            z = (d >> 1) & (high - 1)
            core = (d >> log2(self.mesh_y)) & 1
            x = d >> (log2(self.mesh_y) + 1)
            turn = y ^ (x & 1)
            return ((x * 2 + turn) * high + (z ^ (turn * (high - 1)))) * 2 + core
        if not self.joint and self.mesh_y % 8 == 0:
            return d ^ (((d >> 3) & 1) * 7)
        return d

    def slab(self):
        d = lax.axis_index("ey")
        return self.slab_at(lax.axis_index("ex") * self.mesh_y + d if self.joint else d)

    def swaps(self, first):
        pairs = []
        for s in range(first, self.slabs, 2):
            a, b = self.order[s], self.order[(s + 1) % self.slabs]
            pairs += [(a, b), (b, a)]
        return pairs


def split(x):
    high = x.astype(BF16)
    return high, (x - high.astype(F32)).astype(BF16)


def times3(high, low, x):
    xh, xl = split(x)
    dot = functools.partial(jnp.dot, preferred_element_type=F32)
    return dot(high, xh) + dot(high, xl) + dot(low, xh)


def split_table(x):
    high = x.astype(BF16)
    return high, (x - high.astype(np.float64)).astype(BF16)


def stacked_table(x):
    high, low = split_table(x)
    return np.concatenate([high, high, low, low], 1)


def stacked(x):
    high = x.astype(BF16).astype(F32)
    low = x - high
    return jnp.concatenate([high, low, high, low], 0).astype(BF16)


def subtract_stiffness(lay, one, u_ref, g_ref, high_ref, low_ref, along_ref):
    matrix, weights = one
    dot = functools.partial(jnp.dot, preferred_element_type=F32)
    half = N // 2
    for first in (0, half):
        scaled = [
            float(weights[i]) * u_ref[pl.ds(i * FACE, FACE), :] for i in range(first, first + half)
        ]
        xh, xl = split(jnp.concatenate(scaled, 0))
        both = dot(high_ref[...], jnp.concatenate([xh, xl], 1))
        rows = pl.ds(first * FACE, half * FACE)
        g_ref[rows, :] -= both[:, : lay.width] + both[:, lay.width :] + dot(low_ref[...], xh)
    even = 0.5 * (matrix[:half, :half] + matrix[:half, :half - 1 : -1])
    odd = 0.5 * (matrix[:half, :half] - matrix[:half, :half - 1 : -1])
    for j in range(N):
        values = [u_ref[pl.ds((i * N + j) * N, N), :] for i in range(N)]
        sums = [values[i] + values[N - 1 - i] for i in range(half)]
        gaps = [values[i] - values[N - 1 - i] for i in range(half)]
        along = along_ref[pl.ds(j * N, N), :]
        for i in range(half):
            a = sum(float(even[i, q]) * sums[q] for q in range(half))
            b = sum(float(odd[i, q]) * gaps[q] for q in range(half))
            g_ref[pl.ds((i * N + j) * N, N), :] -= along * (a + b)
            g_ref[pl.ds(((N - 1 - i) * N + j) * N, N), :] -= along * (a - b)


def roll(x, shift, axis):
    size = x.shape[axis]
    return pltpu.roll(x, shift % size, axis)


def lane_parts(lay, shape):
    lane = lax.broadcasted_iota(jnp.int32, shape, len(shape) - 1)
    part_z = lane & (lay.depth - 1)
    part_y = lax.shift_right_logical(lane, log2(lay.step_y)) & (lay.num_y - 1)
    part_x = lax.shift_right_logical(lane, log2(lay.step_x))
    return part_x, part_y, part_z


def get_rows(ref, k):
    if ref.shape[1] == 128:
        return ref[pl.ds(k, FACE, stride=N), :]
    return jnp.concatenate([ref[pl.ds(n * N + k, 1), :] for n in range(FACE)], 0)


def set_rows(ref, k, value):
    if ref.shape[1] == 128:
        ref[pl.ds(k, FACE, stride=N), :] = value
    else:
        for n in range(FACE):
            ref[pl.ds(n * N + k, 1), :] = value[n : n + 1]


def assemble_xy(lay, s_ref):
    last = N - 1
    for j in range(N):
        a, b = pl.ds(j * N, N), pl.ds((last * N + j) * N, N)
        low, high = s_ref[a, :], s_ref[b, :]
        s_ref[a, :] = low + roll(high, lay.step_x, 1)
        s_ref[b, :] = high + roll(low, -lay.step_x, 1)
    for i in range(N):
        a, b = pl.ds(i * N * N, N), pl.ds((i * N + last) * N, N)
        low, high = s_ref[a, :], s_ref[b, :]
        s_ref[a, :] = low + roll(high, lay.step_y, 1)
        s_ref[b, :] = high + roll(low, -lay.step_y, 1)


def assemble(lay, g_ref, s_ref, halo):
    _, _, part_z = lane_parts(lay, halo.shape)
    s_ref[...] = g_ref[...]
    low = get_rows(g_ref, 0)
    high = get_rows(g_ref, N - 1)
    set_rows(s_ref, 0, low + jnp.where(part_z == 0, halo, roll(high, 1, 1)))
    set_rows(s_ref, N - 1, high + jnp.where(part_z == lay.depth - 1, halo, roll(low, -1, 1)))
    assemble_xy(lay, s_ref)


def store_faces(lay, g_ref, face_ref):
    low = get_rows(g_ref, 0)
    high = get_rows(g_ref, N - 1)
    _, _, part_z = lane_parts(lay, low.shape)
    face_ref[...] = jnp.zeros(face_ref.shape, F32)
    face_ref[:FACE, :] = jnp.where(part_z == 0, low, high)


def halo_of(lay, core_ref, chip_ref):
    odd = (lay.slab() & 1) == 1
    core, chip = core_ref[:FACE, :], chip_ref[:FACE, :]
    below = jnp.where(odd, core, chip)
    above = jnp.where(odd, chip, core)
    _, _, part_z = lane_parts(lay, core.shape)
    return jnp.where(part_z == 0, roll(below, 1 - lay.depth, 1), roll(above, lay.depth - 1, 1))


def assemble_both(lay, g_ref, h_ref, s_ref, sh_ref):
    low, high = get_rows(g_ref, 0), get_rows(g_ref, N - 1)
    out_low, out_high = get_rows(h_ref, 0), get_rows(h_ref, N - 1)
    _, _, part_z = lane_parts(lay, low.shape)
    bottom = part_z == 0
    s_ref[...] = g_ref[...]
    sh_ref[...] = h_ref[...]
    set_rows(s_ref, 0, low + jnp.where(bottom, out_high, roll(high, 1, 1)))
    set_rows(s_ref, N - 1, high + jnp.where(bottom, roll(low, -1, 1), out_low))
    set_rows(sh_ref, N - 1, out_high + jnp.where(bottom, low, 0.0))
    set_rows(sh_ref, 0, out_low + jnp.where(bottom, 0.0, high))
    assemble_xy(lay, s_ref)
    assemble_xy(lay, sh_ref)


def send_layers(lay, g_ref, s_ref, core_ref, chip_ref):
    low, high = get_rows(g_ref, 0), get_rows(g_ref, N - 1)
    _, _, part_z = lane_parts(lay, low.shape)
    s_ref[...] = g_ref[...]
    set_rows(s_ref, N - 1, jnp.where(part_z == 0, high + roll(low, -1, 1), high))
    set_rows(s_ref, 0, jnp.where(part_z == 0, low, low + roll(high, 1, 1)))
    half = N**3 // 2
    a, b = s_ref[:half, :], s_ref[half:, :]
    _, _, part_z = lane_parts(lay, a.shape)
    bottom = part_z == 0
    first = jnp.where(bottom, a, roll(b, 1, 1))
    second = jnp.where(bottom, roll(a, -1, 1), b)
    odd = (lay.slab() & 1) == 1
    core_ref[...] = jnp.where(odd, first, second)
    chip_ref[...] = jnp.where(odd, second, first)


def receive_layers(lay, core_ref, chip_ref, h_ref):
    odd = (lay.slab() & 1) == 1
    core, chip = core_ref[...], chip_ref[...]
    below, above = jnp.where(odd, core, chip), jnp.where(odd, chip, core)
    _, _, part_z = lane_parts(lay, core.shape)
    bottom = part_z == 0
    half = N**3 // 2
    h_ref[:half, :] = jnp.where(bottom, below, roll(above, 1, 1))
    h_ref[half:, :] = jnp.where(bottom, roll(below, -1, 1), above)


def pack_kernel(
    lay,
    base_ref,
    offset_ref,
    force_ref,
    source_ref,
    out_ref,
    base_buf,
    offset_buf,
    force_buf,
    field_ref,
    flat_ref,
    sems,
):
    pairs = (
        (source_ref, field_ref),
        (base_ref, base_buf),
        (offset_ref, offset_buf),
        (force_ref, force_buf),
    )
    copies = [pltpu.make_async_copy(a, b, sems.at[n]) for n, (a, b) in enumerate(pairs)]
    for copy in copies:
        copy.start()
    for copy in copies:
        copy.wait()
    mean = 0.5 * (get_rows(field_ref, N - 1) + roll(get_rows(field_ref, 0), -1, 1))
    set_rows(field_ref, N - 1, mean)
    set_rows(field_ref, 0, roll(mean, 1, 1))
    flat_ref[...] = field_ref[...].T
    shape = (1, N**3)
    lane = lax.broadcasted_iota(jnp.int32, shape, 1)
    points = jnp.zeros(shape, F32)
    for p in range(base_buf.shape[0]):
        for c, ref in enumerate((base_buf, offset_buf, force_buf)):
            for d in range(3):
                value = ref[p : p + 1, d : d + 1].astype(F32)
                points = jnp.where(lane == (p * 9 + c * 3 + d) * N, value, points)
    used = (lane & (N - 1)) == 0
    for d in range(lay.slabs):
        first = lay.slab_at(d) * lay.depth
        for e2 in range(lay.tiles_y):
            rows = flat_ref[pl.ds(e2 * EZ + first, lay.depth), :]
            out_ref[d, pl.ds(e2 * lay.depth, lay.depth), :] = rows
        out_ref[d, 1:2, :] = jnp.where(used, points, out_ref[d, 1:2, :])


def column(values, shape):
    node = lax.broadcasted_iota(jnp.int32, shape, 0)
    out = jnp.full(shape, float(values[0]), F32)
    for n in range(1, N):
        out = jnp.where(node == n, float(values[n]), out)
    return out


def gauss(elem, base, position, half_nodes):
    node = lax.broadcasted_iota(jnp.int32, elem.shape, 0)
    elem = elem.astype(F32)
    away = elem + half_nodes - position
    inside = (
        (elem == base)
        | (elem == base + 1.0)
        | ((elem == base - 1.0) & (node == N - 1))
        | ((elem == base + 2.0) & (node == 0))
    )
    return jnp.where(inside, jnp.exp(-(away * away) / (WIDTH_EPS * WIDTH_EPS)), 0.0)


def point_values(points_ref, row, place, scale):
    base, offset, force = (
        [points_ref[row, (place * 9 + c * 3 + d) * N] for d in range(3)] for c in range(3)
    )
    return base, [b + 1.0 + o for b, o in zip(base, offset)], [scale * f for f in force]


def for_points(points_ref, local_points, visit):
    def row_of(row, _):
        for place in range(local_points):
            visit(row, place)
        return 0

    lax.fori_loop(0, points_ref.shape[0], row_of, 0)


def right_side(lay, local_points, one, points_ref, g_ref, halo_ref):
    derivative, weights = one
    shape = (N, lay.width)
    part_x, part_y, part_z = lane_parts(lay, shape)
    first_z = lay.slab() * lay.depth
    elem_z = first_z + part_z
    elem_halo = jnp.where(part_z == 0, first_z - 1, first_z + lay.depth)
    half_nodes = column(0.5 * (1.0 + GLL_POINTS), shape)
    weight = column(weights, shape)
    columns = [column(derivative[a], shape) for a in range(N)]

    def weighted(elem, base, position):
        plain = weight * gauss(elem, base, position, half_nodes)
        terms = [columns[a] * plain[a : a + 1] for a in range(N)]
        while len(terms) > 1:
            terms = [a + b for a, b in zip(terms[::2], terms[1::2])]
        return plain, terms[0]

    def visit(p, place):
        base, position, force = point_values(points_ref, p, place, 0.25 * GAUSS_NORM)
        first = first_z.astype(F32)

        @pl.when((base[2] + 2.0 >= first - 1.0) & (base[2] - 1.0 <= first + lay.depth))
        def _():
            x0, x1 = weighted(part_x, base[0], position[0])
            y0, y1 = weighted(part_y, base[1], position[1])
            z0, z1 = weighted(elem_z, base[2], position[2])
            h0, h1 = weighted(elem_halo, base[2], position[2])
            pick = part_z[0:1] == 0
            h0 = jnp.where(pick, h0[N - 1 : N], h0[0:1])
            h1 = jnp.where(pick, h1[N - 1 : N], h1[0:1])
            x1 = force[0] * x1
            fz1 = force[2] * z1
            fz0 = force[1] * z0
            for j in range(N):
                first_part = y0[j : j + 1] * z0
                other_part = y1[j : j + 1] * fz0 + y0[j : j + 1] * fz1
                for i in range(N):
                    rows = pl.ds((i * N + j) * N, N)
                    g_ref[rows, :] += x1[i : i + 1] * first_part + x0[i : i + 1] * other_part
            first_part = y0 * h0
            other_part = y1 * (force[1] * h0) + y0 * (force[2] * h1)
            for i in range(N):
                rows = pl.ds(i * N, N)
                halo_ref[rows, :] += x1[i : i + 1] * first_part + x0[i : i + 1] * other_part

    for_points(points_ref, local_points, visit)


def inverse_diagonal(lay, factor, dinv_ref, outer):
    shape = (N, lay.width)
    part_x, part_y, part_z = lane_parts(lay, shape)
    first = lay.slab() * lay.depth
    part_z = jnp.where(part_z == 0, first - 1, first + lay.depth) if outer else first + part_z
    node = lax.broadcasted_iota(jnp.int32, shape, 0)

    def share(low, high):
        return (
            jnp.where(low, 0.0, 0.5),
            jnp.where(high, 0.0, 0.5),
        )

    low_z, high_z = share(part_z == 0, part_z == EZ - 1)
    along_z = jnp.where(node == 0, low_z, jnp.where(node == N - 1, high_z, 1.0))
    if outer:
        along_z = jnp.where((part_z < 0) | (part_z >= EZ), 0.0, along_z)
    along_x = dict(zip((0, N - 1), share(part_x == 0, part_x == lay.num_x - 1)))
    along_y = dict(zip((0, N - 1), share(part_y == 0, part_y == lay.num_y - 1)))
    tables = {}
    for i in range(N // 2):
        for j in range(i + 1):
            tables[i, j] = tables[j, i] = column(factor[i, j], shape) * along_z
    for i in range(N):
        for j in range(N):
            rows = pl.ds((i * N + j) * N, N)
            value = tables[min(i, N - 1 - i), min(j, N - 1 - j)]
            if i in along_x:
                value = value * along_x[i]
            if j in along_y:
                value = value * along_y[j]
            dinv_ref[rows, :] = value


def first_kernel(
    lay,
    local_points,
    derivative,
    one,
    factor,
    recv_ref,
    high_ref,
    low_ref,
    along_ref,
    g_ref,
    x_ref,
    dinv_ref,
    outer_ref,
    face_ref,
    points_ref,
    s_ref,
    halo_ref,
    flat_ref,
    table_ref,
    sem,
):
    count, block = recv_ref.shape[0], recv_ref.shape[1]
    for d in range(count):
        points_ref[pl.ds(d, 1), :] = recv_ref[d, 1:2, : points_ref.shape[1]]
    copy = pltpu.make_async_copy(points_ref, table_ref, sem)
    copy.start()
    for d in range(count):
        flat_ref[pl.ds(d * block, block), :] = recv_ref[d]
    g_ref[...] = flat_ref[...].T
    low, high = get_rows(g_ref, 0), get_rows(g_ref, N - 1)
    _, _, part_z = lane_parts(lay, low.shape)
    set_rows(g_ref, 0, jnp.where(part_z == 0, low, roll(high, 1, 1)))
    halo_ref[...] = jnp.where(part_z == 0, low, high)
    inverse_diagonal(lay, factor, dinv_ref, False)
    inverse_diagonal(lay, factor, outer_ref, True)
    copy.wait()
    right_side(lay, local_points, (derivative, one[1]), table_ref, g_ref, halo_ref)
    assemble(lay, g_ref, s_ref, halo_ref[...])
    x_ref[...] = (1.0 / THETA) * dinv_ref[...] * s_ref[...]
    subtract_stiffness(lay, one, x_ref, g_ref, high_ref, low_ref, along_ref)
    store_faces(lay, g_ref, face_ref)


def vertex_rows(lay, table_ref, values):
    high, low = split(values)
    both = jnp.dot(table_ref[...], jnp.concatenate([high, low], 1), preferred_element_type=F32)
    load = both[:N, : lay.width] + both[:N, lay.width :] + both[N:, : lay.width]
    rows = [load[n : n + 1] for n in range(N)]
    rows = [rows[n] + roll(rows[4 + n], lay.step_x, 1) for n in range(4)]
    return [rows[n] + roll(rows[2 + n], lay.step_y, 1) for n in range(2)]


def face_values(lay, u_ref):
    low, high = get_rows(u_ref, 0), get_rows(u_ref, N - 1)
    _, _, part_z = lane_parts(lay, low.shape)
    return jnp.where(part_z == 0, low, 0.0), jnp.where(part_z == 0, 0.0, high)


def send_loads(lay, own, outer, far, send_ref, token_ref):
    _, _, part_z = lane_parts(lay, own[0].shape)
    bottom = part_z == 0
    before = jnp.where(bottom, 0.0, roll(outer[0], 1, 1))
    here = own[0] + jnp.where(bottom, outer[1], roll(own[1], 1, 1))
    after = jnp.where(bottom, roll(own[1], -1, 1) + roll(outer[0], -1, 1), outer[1])
    second = jnp.zeros_like(here)
    if far is not None:
        before = before + jnp.where(bottom, far[0], roll(far[1], 1, 1))
        after = after + jnp.where(bottom, 0.0, far[0])
        second = jnp.where(bottom, roll(far[1], -1, 1), 0.0)
    rows = jnp.concatenate([before, here, after, second] * 2, 0)
    for d in range(send_ref.shape[0]):
        send_ref[d] = rows
    token_ref[...] = jnp.zeros(token_ref.shape, F32)


OLD = RHO_SECOND * RHO_FIRST
NEW = 2.0 * RHO_SECOND / DELTA


def first_response(
    lay, g_ref, x_ref, dinv_ref, loads_ref, near_ref, send_ref, token_ref, s_ref
):
    assemble(lay, g_ref, s_ref, jnp.zeros((FACE, lay.width), F32))
    update = NEW * dinv_ref[...] * s_ref[...]
    s_ref[...] = update
    total = OLD * x_ref[...] + update
    own = vertex_rows(lay, loads_ref, jnp.concatenate([g_ref[...], total], 0))
    outer = vertex_rows(lay, near_ref, jnp.concatenate(face_values(lay, s_ref), 0))
    send_loads(lay, own, outer, None, send_ref, token_ref)


def pair_response(
    lay,
    one,
    g_ref,
    dinv_ref,
    outer_ref,
    high_ref,
    low_ref,
    along_ref,
    loads_ref,
    near_ref,
    send_ref,
    token_ref,
    s_ref,
    sh_ref,
    u_ref,
    v_ref,
    t_ref,
    h_ref,
):
    tile = (high_ref, low_ref, along_ref)
    assemble(lay, g_ref, s_ref, jnp.zeros((FACE, lay.width), F32))
    u_ref[...] = (1.0 / THETA) * dinv_ref[...] * s_ref[...]
    t_ref[...] = g_ref[...]
    subtract_stiffness(lay, one, u_ref, t_ref, *tile)
    low, high = face_values(lay, u_ref)
    v_ref[...] = jnp.zeros(v_ref.shape, F32)
    set_rows(v_ref, N - 1, low)
    set_rows(v_ref, 0, high)
    h_ref[...] = jnp.zeros(h_ref.shape, F32)
    subtract_stiffness(lay, one, v_ref, h_ref, *tile)
    assemble_both(lay, t_ref, h_ref, s_ref, sh_ref)
    update = OLD * u_ref[...] + NEW * dinv_ref[...] * s_ref[...]
    own = vertex_rows(lay, loads_ref, jnp.concatenate([t_ref[...], update], 0))
    v_ref[...] = OLD * v_ref[...] + NEW * outer_ref[...] * sh_ref[...]
    outer = vertex_rows(lay, loads_ref, jnp.concatenate([h_ref[...], v_ref[...]], 0))
    far = vertex_rows(lay, near_ref, jnp.concatenate(face_values(lay, v_ref), 0))
    send_loads(lay, own, outer, far, send_ref, token_ref)


def second_kernel(
    lay,
    one,
    core_ref,
    chip_ref,
    g_ref,
    x_ref,
    dinv_ref,
    high_ref,
    low_ref,
    along_ref,
    token_ref,
    g_out,
    x_out,
    core_out,
    chip_out,
    s_ref,
    u_ref,
):
    assemble(lay, g_ref, s_ref, halo_of(lay, core_ref, chip_ref))
    update = OLD * x_ref[...] + NEW * dinv_ref[...] * s_ref[...]
    u_ref[...] = update
    x_out[...] = x_ref[...] + update
    g_out[...] = g_ref[...]
    subtract_stiffness(lay, one, u_ref, g_out, high_ref, low_ref, along_ref)
    send_layers(lay, g_out, s_ref, core_out, chip_out)


def solve_coarse(lay, mass, stiff, loads_ref, rows_ref, first_ref, second_ref):
    count = 4
    for s in range(lay.slabs):
        rows_ref[pl.ds(s * count, count), :] = loads_ref[lay.order[s], :count]

    def part(n):
        if lay.width == 128:
            return rows_ref[pl.ds(n, lay.slabs, stride=count), :]
        return jnp.concatenate(
            [rows_ref[pl.ds(s * count + n, 1), :] for s in range(lay.slabs)], 0
        )

    shape = (lay.slabs, lay.width)
    part_x, part_y, part_z = lane_parts(lay, shape)
    row = lax.broadcasted_iota(jnp.int32, shape, 0)
    keep = ((part_x > 0) & (part_y > 0) & ((part_z > 0) | (row > 0))).astype(F32)
    bottom = part_z == 0

    def around_z(v):
        return jnp.where(bottom, roll(v + roll(v, 1, 0), -1, 1), roll(v + roll(v, -1, 0), 1, 1))

    def above(v):
        return jnp.where(bottom, roll(v, -1, 1), roll(roll(v, -1, 0), 1, 1))

    def neighbours(v, step):
        return roll(v, step, 1) + roll(v, -step, 1)

    def mix(pair, v, around):
        return (2.0 * pair[0]) * v + pair[1] * around

    def operate(v):
        around = around_z(v)
        mass_z, stiff_z = mix(mass, v, around), mix(stiff, v, around)
        around = neighbours(mass_z, lay.step_y)
        both = mix(mass, mass_z, around)
        rest = mix(stiff, mass_z, around) + mix(mass, stiff_z, neighbours(stiff_z, lay.step_y))
        out = mix(stiff, both, neighbours(both, lay.step_x)) + mix(
            mass, rest, neighbours(rest, lay.step_x)
        )
        return (0.5 * keep) * out

    def inner(a, b):
        return jnp.sum(jnp.sum(a * b, axis=1, keepdims=True), axis=0, keepdims=True)

    residual = keep * (part(1) + roll(part(0), -1, 0) + roll(part(2), 1, 0) + roll(part(3), 2, 0))
    image = operate(residual)
    total = jnp.zeros(shape, F32)
    for step in range(CG_STEPS):
        last = step + 1 == CG_STEPS
        norm, curv = inner(residual, residual), inner(image, residual)
        if not last:
            second = operate(image)
        if step == 0:
            alpha = norm / curv
            direction, moved = residual, image
            if not last:
                moved_image = second
        else:
            beta = norm / norm_old
            alpha = norm / (curv - beta * norm / alpha)
            direction = residual + beta * direction
            if not last:
                moved, moved_image = image + beta * moved, second + beta * moved_image
        norm_old = norm
        total = total + alpha * direction
        if not last:
            residual, image = residual - alpha * moved, image - alpha * moved_image
    here = pl.ds(N, lay.slabs)
    for ref, value in ((first_ref, total), (second_ref, above(total))):
        ref[...] = jnp.zeros(ref.shape, F32)
        ref[here, :] = value


def corners(lay, low, high):
    rows = [low, high]
    rows = rows + [roll(r, -lay.step_y, 1) for r in rows]
    rows = rows + [roll(r, -lay.step_x, 1) for r in rows]
    corner = lax.broadcasted_iota(jnp.int32, (N, lay.width), 0)
    local = jnp.broadcast_to(rows[0], (N, lay.width))
    for n in range(1, N):
        local = jnp.where(corner == n, rows[n], local)
    return local


def prolong_coarse(lay, first_ref, second_ref, interp_ref, image_ref, edge_ref, g_ref, h_ref, x_ref):
    mine = lay.slab() + N
    _, _, part_z = lane_parts(lay, (1, lay.width))
    bottom = part_z == 0
    own, outer, far = [], [], []
    for ref in (first_ref, second_ref):
        before, here, after = (ref[pl.ds(mine + shift, 1), :] for shift in (-1, 0, 1))
        own.append(here)
        outer.append(jnp.where(bottom, roll(before, -1, 1), roll(after, 1, 1)))
        far.append(jnp.where(bottom, before, after))
    local = stacked(corners(lay, *own))
    dot = functools.partial(jnp.dot, preferred_element_type=F32)
    x_ref[...] += dot(interp_ref[...], local)
    g_ref[...] -= dot(image_ref[...], local)
    h_ref[...] -= dot(image_ref[...], stacked(corners(lay, *outer)))
    edge = dot(edge_ref[...], stacked(corners(lay, *far)))
    low, high = get_rows(h_ref, 0), get_rows(h_ref, N - 1)
    set_rows(h_ref, 0, low - jnp.where(bottom, edge[FACE:], 0.0))
    set_rows(h_ref, N - 1, high - jnp.where(bottom, 0.0, edge[:FACE]))


def pair_kernel(lay, one, coarse, kind, core_ref, chip_ref, g_ref, x_ref, dinv_ref, outer_ref, *refs):
    refs = list(refs)
    high_ref, low_ref, along_ref, edge_high_ref, edge_low_ref = (refs.pop(0) for _ in range(5))
    if coarse:
        loads_ref, image_ref, image_edge_ref = (refs.pop(0) for _ in range(3))
        interp_ref = refs.pop(0)
    if kind == "inner":
        token_ref, points_ref = refs.pop(0), refs.pop(0)
    if kind == "last":
        token_ref = refs.pop(0)
    if kind == "last":
        out_ref = refs.pop(0)
    else:
        g_out, x_out = refs.pop(0), refs.pop(0)
        core_out, chip_out = refs.pop(0), refs.pop(0)
        if kind == "inner":
            points_out = refs.pop(0)
            points_out[...] = points_ref[...]
    s_ref, sh_ref, h_ref, u_ref = (refs.pop(0) for _ in range(4))
    if kind == "last":
        g_out, x_out = refs.pop(0), refs.pop(0)

    g_out[...] = g_ref[...]
    x_out[...] = x_ref[...]
    receive_layers(lay, core_ref, chip_ref, h_ref)
    if coarse:
        rows_ref, first_ref, second_ref = refs
        solve_coarse(lay, *coarse, loads_ref, rows_ref, first_ref, second_ref)
        prolong_coarse(
            lay, first_ref, second_ref, interp_ref, image_ref, image_edge_ref, g_out, h_ref, x_out
        )
    assemble_both(lay, g_out, h_ref, s_ref, sh_ref)
    update = (1.0 / THETA) * dinv_ref[...] * s_ref[...]
    u_ref[...] = update
    outer = (1.0 / THETA) * outer_ref[...] * sh_ref[...]
    edge = times3(edge_high_ref[...], edge_low_ref[...], outer)
    _, _, part_z = lane_parts(lay, (FACE, lay.width))
    near = jnp.where(
        part_z == 0, get_rows(h_ref, N - 1) - edge[FACE:], get_rows(h_ref, 0) - edge[:FACE]
    )
    subtract_stiffness(lay, one, u_ref, g_out, high_ref, low_ref, along_ref)
    assemble(lay, g_out, s_ref, near)
    update = u_ref[...]
    following = OLD * update + NEW * dinv_ref[...] * s_ref[...]
    if kind == "last":
        total = (x_out[...] + (update + following)).T
        count, block = out_ref.shape[0], out_ref.shape[1]
        for d in range(count):
            out_ref[d] = total[d * block : (d + 1) * block]
        return
    x_out[...] += update + following
    u_ref[...] = following
    subtract_stiffness(lay, one, u_ref, g_out, high_ref, low_ref, along_ref)
    send_layers(lay, g_out, s_ref, core_out, chip_out)


def unpack_kernel(lay, recv_ref, out_ref, flat_ref):
    for d in range(lay.slabs):
        first = lay.slab_at(d) * lay.depth
        for e2 in range(lay.tiles_y):
            rows = recv_ref[d, pl.ds(e2 * lay.depth, lay.depth), :]
            flat_ref[pl.ds(e2 * EZ + first, lay.depth), :] = rows
    out_ref[...] = flat_ref[...].T


def forces_kernel(tiles_y, local_points, points_ref, out_ref, done_ref):
    shape = (N, tiles_y * EZ)
    lane = lax.broadcasted_iota(jnp.int32, shape, 1)
    first_x, first_y = lax.axis_index("ex"), lax.axis_index("ey") * tiles_y
    elem_x = jnp.broadcast_to(first_x, shape)
    elem_y = first_y + lax.shift_right_logical(lane, log2(EZ))
    elem_z = lane & (EZ - 1)
    half_nodes = column(0.5 * (1.0 + GLL_POINTS), shape)
    out_ref[...] = jnp.zeros(out_ref.shape, F32)
    done_ref[...] = jnp.zeros(done_ref.shape, F32)

    def visit(p, place):
        base, position, force = point_values(points_ref, p, place, GAUSS_NORM)
        low_x, low_y = first_x.astype(F32), first_y.astype(F32)

        @pl.when(
            (base[0] + 2.0 >= low_x)
            & (base[0] - 1.0 <= low_x)
            & (base[1] + 2.0 >= low_y)
            & (base[1] - 1.0 <= low_y + (tiles_y - 1))
        )
        def _():
            x = gauss(elem_x, base[0], position[0], half_nodes)
            y = gauss(elem_y, base[1], position[1], half_nodes)
            z = gauss(elem_z, base[2], position[2], half_nodes)

            def add(along_x, along_y):
                for j in along_y:
                    plane = y[j : j + 1] * z
                    for i in along_x:
                        value = x[i : i + 1] * plane
                        rows = pl.ds((i * N + j) * N, N)
                        for c in range(3):
                            out_ref[c, rows, :] += force[c] * value

            last_y = low_y + (tiles_y - 1)
            in_x = ((base[0] == low_x) | (base[0] + 1.0 == low_x), range(N))
            in_y = ((base[1] + 1.0 >= low_y) & (base[1] <= last_y), range(N))
            for when_x, along_x in (
                in_x,
                (base[0] + 2.0 == low_x, (0,)),
                (base[0] - 1.0 == low_x, (N - 1,)),
            ):
                for when_y, along_y in (
                    in_y,
                    (base[1] + 2.0 == low_y, (0,)),
                    (base[1] - 1.0 == last_y, (N - 1,)),
                ):
                    pl.when(when_x & when_y)(functools.partial(add, along_x, along_y))

    for_points(points_ref, local_points, visit)


def call(kernel, outs, inputs, scratch=(), smem=0, spaces=None, limit=40):
    spaces = spaces or [pltpu.SMEM] * smem + [pltpu.VMEM] * (len(inputs) - smem)
    specs = [pl.BlockSpec(memory_space=space) for space in spaces]
    shapes = [jax.ShapeDtypeStruct(s, F32) for s in outs]
    result = pl.pallas_call(
        kernel,
        out_shape=shapes,
        in_specs=specs,
        out_specs=[pl.BlockSpec(memory_space=pltpu.VMEM)] * len(shapes),
        scratch_shapes=[pltpu.VMEM(s, F32) if isinstance(s, tuple) else s for s in scratch],
        compiler_params=pltpu.CompilerParams(vmem_limit_bytes=limit * 1024 * 1024),
    )(*inputs)
    return result


def shards(source, point_base, point_offset, point_force):
    tiles_x, tiles_y = source.shape[3], source.shape[4] // EZ
    lay = Layout(lax.axis_size("ex"), lax.axis_size("ey"), tiles_x, tiles_y)
    devices = lay.mesh_x * lay.mesh_y
    derivative, weights, interp, stiff_one = build_tables()
    width, fields = lay.width, (N**3, lay.width)

    diag_w = np.diag(weights)
    full = 0.5 * (
        kron3(stiff_one, diag_w, diag_w)
        + kron3(diag_w, stiff_one, diag_w)
        + kron3(diag_w, diag_w, stiff_one)
    )
    edge_rows = np.concatenate([np.arange(FACE) * N, np.arange(FACE) * N + N - 1])
    plane = 0.5 * (np.kron(stiff_one, diag_w) + np.kron(diag_w, stiff_one))
    high, low = (jnp.asarray(t) for t in split_table(np.kron(np.eye(N // 2), plane)))
    along = np.broadcast_to(0.5 * np.kron(weights, weights)[:, None], (FACE, width))
    along = jnp.asarray(along, F32)
    edge_high, edge_low = (jnp.asarray(t) for t in split_table(full[edge_rows]))
    one = (stiff_one, weights)
    interp3 = kron3(interp, interp, interp)
    image3 = full @ interp3
    ratio = (weights[:, None] * derivative**2).sum(axis=0) / weights
    diag = 0.5 * (ratio[:, None, None] + ratio[None, :, None] + ratio[None, None, :])
    diag = diag * weights[:, None, None] * weights[None, :, None] * weights[None, None, :]
    factor = 1.0 / diag
    mass = interp.T @ diag_w @ interp
    stiff = interp.T @ stiff_one @ interp
    moved = -interp3.T @ full
    loads_table, near_table = (
        jnp.asarray(np.concatenate(split_table(t), 0))
        for t in (
            np.concatenate([interp3.T, moved], 1),
            np.concatenate([moved[:, edge_rows[FACE:]], moved[:, edge_rows[:FACE]]], 1),
        )
    )
    prolong3, image3, image_edge = (
        jnp.asarray(stacked_table(t)) for t in (interp3, image3, image3[edge_rows])
    )

    local_points = point_base.shape[1]
    block = lay.block
    (send,) = call(
        functools.partial(pack_kernel, lay),
        [(lay.slabs, block, N**3)],
        [
            pltpu.with_memory_space_constraint(t, pltpu.HBM)
            for t in (
                point_base.T,
                point_offset.T,
                point_force.T,
                source.reshape(N**3, tiles_y * EZ),
            )
        ],
        [
            pltpu.VMEM((local_points, 3), jnp.int32),
            (local_points, 3),
            (local_points, 3),
            (N**3, tiles_y * EZ),
            (tiles_y * EZ, N**3),
            pltpu.SemaphoreType.DMA((4,)),
        ],
        spaces=[pltpu.HBM] * 4,
    )
    recv = lax.all_to_all(send, lay.axis, 0, 0)
    if not lay.joint:
        recv = lax.all_gather(recv, "ex", axis=0, tiled=True)

    def swap(core, chip):
        return (
            lax.ppermute(core, lay.axis, lay.swaps(0)),
            lax.ppermute(chip, lay.axis, lay.swaps(1)),
        )

    def gather(loads):
        return lax.all_to_all(loads, lay.axis, 0, 0)

    face_shape = (FACE, width)
    layer = (N**3 // 2, width)
    loads_shape = (lay.slabs, N, width)
    table = (devices, -(-9 * N * local_points // 128) * 128)
    g, x, dinv, outer, face, points = call(
        functools.partial(first_kernel, lay, local_points, derivative, one, factor),
        [fields, fields, fields, fields, (256, width), table],
        [recv, high, low, along],
        [fields, face_shape, (width, N**3), pltpu.SMEM(table, F32), pltpu.SemaphoreType.DMA],
    )
    faces = swap(face, face)
    loads, token = call(
        functools.partial(first_response, lay),
        [loads_shape, (N, 128)],
        [g, x, dinv, loads_table, near_table],
        [fields],
    )
    loads = gather(loads)
    g, x, core, chip = call(
        functools.partial(second_kernel, lay, one),
        [fields, fields, layer, layer],
        [*faces, g, x, dinv, high, low, along, token],
        [fields, fields],
    )
    coarse = ((mass[0, 0], mass[0, 1]), (stiff[0, 0], stiff[0, 1]))
    stiffness = [high, low, along, edge_high, edge_low]

    for cycle in range(CYCLES):
        core, chip = swap(core, chip)
        last = cycle + 1 == CYCLES
        outs = [fields, fields, layer, layer]
        extra = [done] if last else []
        scratch = [fields] * 4
        if last:
            outs = [(lay.mesh_x * lay.mesh_y, block, N**3)]
            scratch += [fields, fields]
        outs = call(
            functools.partial(pair_kernel, lay, one, coarse, "last" if last else "plain"),
            outs,
            [core, chip, g, x, dinv, outer, *stiffness, loads, image3, image_edge, prolong3, *extra],
            scratch + [(lay.slabs * 4, width)] + [(lay.slabs + 2 * N, width)] * 2,
        )
        if last:
            break
        g, x, core, chip = outs
        layers = swap(core, chip)
        loads, token = call(
            functools.partial(pair_response, lay, one),
            [loads_shape, (N, 128)],
            [g, dinv, outer, high, low, along, loads_table, near_table],
            [fields] * 6,
        )
        loads = gather(loads)
        g, x, core, chip, points = call(
            functools.partial(pair_kernel, lay, one, None, "inner"),
            [fields, fields, layer, layer, table],
            [*layers, g, x, dinv, outer, *stiffness, token, points],
            [fields] * 4,
        )
        forces, done = call(
            functools.partial(forces_kernel, tiles_y, local_points),
            [(3, N**3, tiles_y * EZ), (N, 128)],
            [points],
            smem=1,
        )
    (out,) = outs
    if not lay.joint:
        out = lax.dynamic_slice_in_dim(out, lax.axis_index("ex") * lay.mesh_y, lay.mesh_y, 0)
    out = lax.all_to_all(out, lay.axis, 0, 0)
    (pressure,) = call(
        functools.partial(unpack_kernel, lay),
        [(N**3, tiles_y * EZ)],
        [out],
        [(lay.slabs * block, N**3)],
    )
    return (
        pressure.reshape(source.shape),
        forces.reshape((3, *source.shape)),
    )


def solution(mesh):
    in_specs = (
        P(None, None, None, "ex", "ey"),
        P(None, ("ex", "ey")),
        P(None, ("ex", "ey")),
        P(None, ("ex", "ey")),
    )
    out_specs = (P(None, None, None, "ex", "ey"), P(None, None, None, None, "ex", "ey"))
    return jax.shard_map(shards, mesh=mesh, in_specs=in_specs, out_specs=out_specs, check_vma=False)
```

```python
import functools
import math

import jax
import jax.numpy as jnp
import numpy as np
from jax import lax
from jax.experimental import pallas as pl
from jax.experimental.pallas import tpu as pltpu
from jax.sharding import PartitionSpec as P

EZ = 64
CG_STEPS = 4
CYCLES = 2
N = 8
GLL_POINTS = np.array(
    [
        -1.0,
        -0.8717401485096066,
        -0.5917001814331423,
        -0.2092992179024789,
        0.2092992179024789,
        0.5917001814331423,
        0.8717401485096066,
        1.0,
    ]
)
WIDTH_EPS = 0.35
GAUSS_NORM = 1.0 / (math.pi**1.5 * WIDTH_EPS**3)
CHEB_LOW = 1.5
CHEB_HIGH = 12.0
THETA = 0.5 * (CHEB_HIGH + CHEB_LOW)
DELTA = 0.5 * (CHEB_HIGH - CHEB_LOW)
RHO_FIRST = DELTA / THETA
RHO_SECOND = 1.0 / (2.0 * THETA / DELTA - RHO_FIRST)
F32 = jnp.float32
BF16 = jnp.bfloat16
FACE = N * N


def build_tables():
    points = GLL_POINTS
    degree = len(points) - 1
    previous = points * 0.0 + 1.0
    current = points.copy()
    for k in range(1, degree):
        following = ((2 * k + 1) * points * current - k * previous) / (k + 1)
        previous = current
        current = following
    derivative = np.zeros((degree + 1, degree + 1))
    for i in range(degree + 1):
        for j in range(degree + 1):
            if i != j:
                derivative[i, j] = current[i] / (current[j] * (points[i] - points[j]))
    derivative[0, 0] = -degree * (degree + 1) / 4.0
    derivative[degree, degree] = degree * (degree + 1) / 4.0
    weights = 2.0 / (degree * (degree + 1) * current**2)
    interp = np.stack([(1.0 - points) / 2.0, (1.0 + points) / 2.0], axis=1)
    stiff_one = derivative.T @ (weights[:, None] * derivative)
    return derivative, weights, interp, stiff_one


def kron3(a, b, c):
    return np.kron(np.kron(a, b), c)


def log2(n):
    return int(n).bit_length() - 1


class Layout:
    def __init__(self, mesh_x, mesh_y, tiles_x, tiles_y):
        self.mesh_x, self.mesh_y = mesh_x, mesh_y
        self.num_x, self.num_y = tiles_x * mesh_x, tiles_y * mesh_y
        self.tiles_y = tiles_y
        self.joint = EZ % (2 * mesh_x * mesh_y) == 0
        self.axis = ("ex", "ey") if self.joint else "ey"
        self.slabs = mesh_x * mesh_y if self.joint else mesh_y
        self.depth = EZ // self.slabs
        assert self.depth == 2 and tiles_x == 1
        self.width = self.num_x * self.num_y * self.depth
        self.step_y = self.depth
        self.step_x = self.depth * self.num_y
        self.block = tiles_y * self.depth
        slab_of = [self.slab_at(d) for d in range(self.slabs)]
        self.order = [slab_of.index(s) for s in range(self.slabs)]

    def slab_at(self, d):
        if self.joint and self.mesh_x % 2 == 0 and self.mesh_y % 2 == 0:
            high = self.mesh_y // 2
            y = d & 1
            z = (d >> 1) & (high - 1)
            core = (d >> log2(self.mesh_y)) & 1
            x = d >> (log2(self.mesh_y) + 1)
            turn = y ^ (x & 1)
            return ((x * 2 + turn) * high + (z ^ (turn * (high - 1)))) * 2 + core
        if not self.joint and self.mesh_y % 8 == 0:
            return d ^ (((d >> 3) & 1) * 7)
        return d

    def slab(self):
        d = lax.axis_index("ey")
        return self.slab_at(lax.axis_index("ex") * self.mesh_y + d if self.joint else d)

    def swaps(self, first):
        pairs = []
        for s in range(first, self.slabs, 2):
            a, b = self.order[s], self.order[(s + 1) % self.slabs]
            pairs += [(a, b), (b, a)]
        return pairs


def split(x):
    high = x.astype(BF16)
    return high, (x - high.astype(F32)).astype(BF16)


def times3(high, low, x):
    xh, xl = split(x)
    dot = functools.partial(jnp.dot, preferred_element_type=F32)
    return dot(high, xh) + dot(high, xl) + dot(low, xh)


def split_table(x):
    high = x.astype(BF16)
    return high, (x - high.astype(np.float64)).astype(BF16)


def stacked_table(x):
    high, low = split_table(x)
    return np.concatenate([high, high, low, low], 1)


def stacked(x):
    high = x.astype(BF16).astype(F32)
    low = x - high
    return jnp.concatenate([high, low, high, low], 0).astype(BF16)


def subtract_stiffness(lay, one, u_ref, g_ref, high_ref, low_ref, along_ref):
    matrix, weights = one
    dot = functools.partial(jnp.dot, preferred_element_type=F32)
    half = N // 2
    for first in (0, half):
        scaled = [
            float(weights[i]) * u_ref[pl.ds(i * FACE, FACE), :] for i in range(first, first + half)
        ]
        xh, xl = split(jnp.concatenate(scaled, 0))
        both = dot(high_ref[...], jnp.concatenate([xh, xl], 1))
        rows = pl.ds(first * FACE, half * FACE)
        g_ref[rows, :] -= both[:, : lay.width] + both[:, lay.width :] + dot(low_ref[...], xh)
    even = 0.5 * (matrix[:half, :half] + matrix[:half, :half - 1 : -1])
    odd = 0.5 * (matrix[:half, :half] - matrix[:half, :half - 1 : -1])
    for j in range(N):
        values = [u_ref[pl.ds((i * N + j) * N, N), :] for i in range(N)]
        sums = [values[i] + values[N - 1 - i] for i in range(half)]
        gaps = [values[i] - values[N - 1 - i] for i in range(half)]
        along = along_ref[pl.ds(j * N, N), :]
        for i in range(half):
            a = sum(float(even[i, q]) * sums[q] for q in range(half))
            b = sum(float(odd[i, q]) * gaps[q] for q in range(half))
            g_ref[pl.ds((i * N + j) * N, N), :] -= along * (a + b)
            g_ref[pl.ds(((N - 1 - i) * N + j) * N, N), :] -= along * (a - b)


def roll(x, shift, axis):
    size = x.shape[axis]
    return pltpu.roll(x, shift % size, axis)


def lane_parts(lay, shape):
    lane = lax.broadcasted_iota(jnp.int32, shape, len(shape) - 1)
    part_z = lane & (lay.depth - 1)
    part_y = lax.shift_right_logical(lane, log2(lay.step_y)) & (lay.num_y - 1)
    part_x = lax.shift_right_logical(lane, log2(lay.step_x))
    return part_x, part_y, part_z


def get_rows(ref, k):
    if ref.shape[1] == 128:
        return ref[pl.ds(k, FACE, stride=N), :]
    return jnp.concatenate([ref[pl.ds(n * N + k, 1), :] for n in range(FACE)], 0)


def set_rows(ref, k, value):
    if ref.shape[1] == 128:
        ref[pl.ds(k, FACE, stride=N), :] = value
    else:
        for n in range(FACE):
            ref[pl.ds(n * N + k, 1), :] = value[n : n + 1]


def assemble_xy(lay, s_ref):
    last = N - 1
    for j in range(N):
        a, b = pl.ds(j * N, N), pl.ds((last * N + j) * N, N)
        low, high = s_ref[a, :], s_ref[b, :]
        s_ref[a, :] = low + roll(high, lay.step_x, 1)
        s_ref[b, :] = high + roll(low, -lay.step_x, 1)
    for i in range(N):
        a, b = pl.ds(i * N * N, N), pl.ds((i * N + last) * N, N)
        low, high = s_ref[a, :], s_ref[b, :]
        s_ref[a, :] = low + roll(high, lay.step_y, 1)
        s_ref[b, :] = high + roll(low, -lay.step_y, 1)


def assemble(lay, g_ref, s_ref, halo):
    _, _, part_z = lane_parts(lay, halo.shape)
    s_ref[...] = g_ref[...]
    low = get_rows(g_ref, 0)
    high = get_rows(g_ref, N - 1)
    set_rows(s_ref, 0, low + jnp.where(part_z == 0, halo, roll(high, 1, 1)))
    set_rows(s_ref, N - 1, high + jnp.where(part_z == lay.depth - 1, halo, roll(low, -1, 1)))
    assemble_xy(lay, s_ref)


def store_faces(lay, g_ref, face_ref):
    low = get_rows(g_ref, 0)
    high = get_rows(g_ref, N - 1)
    _, _, part_z = lane_parts(lay, low.shape)
    face_ref[...] = jnp.zeros(face_ref.shape, F32)
    face_ref[:FACE, :] = jnp.where(part_z == 0, low, high)


def halo_of(lay, core_ref, chip_ref):
    odd = (lay.slab() & 1) == 1
    core, chip = core_ref[:FACE, :], chip_ref[:FACE, :]
    below = jnp.where(odd, core, chip)
    above = jnp.where(odd, chip, core)
    _, _, part_z = lane_parts(lay, core.shape)
    return jnp.where(part_z == 0, roll(below, 1 - lay.depth, 1), roll(above, lay.depth - 1, 1))


def assemble_both(lay, g_ref, h_ref, s_ref, sh_ref):
    low, high = get_rows(g_ref, 0), get_rows(g_ref, N - 1)
    out_low, out_high = get_rows(h_ref, 0), get_rows(h_ref, N - 1)
    _, _, part_z = lane_parts(lay, low.shape)
    bottom = part_z == 0
    s_ref[...] = g_ref[...]
    sh_ref[...] = h_ref[...]
    set_rows(s_ref, 0, low + jnp.where(bottom, out_high, roll(high, 1, 1)))
    set_rows(s_ref, N - 1, high + jnp.where(bottom, roll(low, -1, 1), out_low))
    set_rows(sh_ref, N - 1, out_high + jnp.where(bottom, low, 0.0))
    set_rows(sh_ref, 0, out_low + jnp.where(bottom, 0.0, high))
    assemble_xy(lay, s_ref)
    assemble_xy(lay, sh_ref)


def send_layers(lay, g_ref, s_ref, core_ref, chip_ref):
    low, high = get_rows(g_ref, 0), get_rows(g_ref, N - 1)
    _, _, part_z = lane_parts(lay, low.shape)
    s_ref[...] = g_ref[...]
    set_rows(s_ref, N - 1, jnp.where(part_z == 0, high + roll(low, -1, 1), high))
    set_rows(s_ref, 0, jnp.where(part_z == 0, low, low + roll(high, 1, 1)))
    half = N**3 // 2
    a, b = s_ref[:half, :], s_ref[half:, :]
    _, _, part_z = lane_parts(lay, a.shape)
    bottom = part_z == 0
    first = jnp.where(bottom, a, roll(b, 1, 1))
    second = jnp.where(bottom, roll(a, -1, 1), b)
    odd = (lay.slab() & 1) == 1
    core_ref[...] = jnp.where(odd, first, second)
    chip_ref[...] = jnp.where(odd, second, first)


def receive_layers(lay, core_ref, chip_ref, h_ref):
    odd = (lay.slab() & 1) == 1
    core, chip = core_ref[...], chip_ref[...]
    below, above = jnp.where(odd, core, chip), jnp.where(odd, chip, core)
    _, _, part_z = lane_parts(lay, core.shape)
    bottom = part_z == 0
    half = N**3 // 2
    h_ref[:half, :] = jnp.where(bottom, below, roll(above, 1, 1))
    h_ref[half:, :] = jnp.where(bottom, roll(below, -1, 1), above)


def pack_kernel(
    lay,
    base_ref,
    offset_ref,
    force_ref,
    source_ref,
    out_ref,
    base_buf,
    offset_buf,
    force_buf,
    field_ref,
    flat_ref,
    sems,
):
    pairs = (
        (source_ref, field_ref),
        (base_ref, base_buf),
        (offset_ref, offset_buf),
        (force_ref, force_buf),
    )
    copies = [pltpu.make_async_copy(a, b, sems.at[n]) for n, (a, b) in enumerate(pairs)]
    for copy in copies:
        copy.start()
    for copy in copies:
        copy.wait()
    mean = 0.5 * (get_rows(field_ref, N - 1) + roll(get_rows(field_ref, 0), -1, 1))
    set_rows(field_ref, N - 1, mean)
    set_rows(field_ref, 0, roll(mean, 1, 1))
    flat_ref[...] = field_ref[...].T
    shape = (1, N**3)
    lane = lax.broadcasted_iota(jnp.int32, shape, 1)
    points = jnp.zeros(shape, F32)
    for p in range(base_buf.shape[0]):
        for c, ref in enumerate((base_buf, offset_buf, force_buf)):
            for d in range(3):
                value = ref[p : p + 1, d : d + 1].astype(F32)
                points = jnp.where(lane == (p * 9 + c * 3 + d) * N, value, points)
    used = (lane & (N - 1)) == 0
    for d in range(lay.slabs):
        first = lay.slab_at(d) * lay.depth
        for e2 in range(lay.tiles_y):
            rows = flat_ref[pl.ds(e2 * EZ + first, lay.depth), :]
            out_ref[d, pl.ds(e2 * lay.depth, lay.depth), :] = rows
        out_ref[d, 1:2, :] = jnp.where(used, points, out_ref[d, 1:2, :])


def column(values, shape):
    node = lax.broadcasted_iota(jnp.int32, shape, 0)
    out = jnp.full(shape, float(values[0]), F32)
    for n in range(1, N):
        out = jnp.where(node == n, float(values[n]), out)
    return out


def gauss(elem, base, position, half_nodes):
    node = lax.broadcasted_iota(jnp.int32, elem.shape, 0)
    elem = elem.astype(F32)
    away = elem + half_nodes - position
    inside = (
        (elem == base)
        | (elem == base + 1.0)
        | ((elem == base - 1.0) & (node == N - 1))
        | ((elem == base + 2.0) & (node == 0))
    )
    return jnp.where(inside, jnp.exp(-(away * away) / (WIDTH_EPS * WIDTH_EPS)), 0.0)


def point_values(points_ref, row, place, scale):
    base, offset, force = (
        [points_ref[row, (place * 9 + c * 3 + d) * N] for d in range(3)] for c in range(3)
    )
    return base, [b + 1.0 + o for b, o in zip(base, offset)], [scale * f for f in force]


def for_points(points_ref, local_points, visit):
    def row_of(row, _):
        for place in range(local_points):
            visit(row, place)
        return 0

    lax.fori_loop(0, points_ref.shape[0], row_of, 0)


def right_side(lay, local_points, one, points_ref, g_ref, halo_ref):
    derivative, weights = one
    shape = (N, lay.width)
    part_x, part_y, part_z = lane_parts(lay, shape)
    first_z = lay.slab() * lay.depth
    elem_z = first_z + part_z
    elem_halo = jnp.where(part_z == 0, first_z - 1, first_z + lay.depth)
    half_nodes = column(0.5 * (1.0 + GLL_POINTS), shape)
    weight = column(weights, shape)
    columns = [column(derivative[a], shape) for a in range(N)]

    def weighted(elem, base, position):
        plain = weight * gauss(elem, base, position, half_nodes)
        terms = [columns[a] * plain[a : a + 1] for a in range(N)]
        while len(terms) > 1:
            terms = [a + b for a, b in zip(terms[::2], terms[1::2])]
        return plain, terms[0]

    def visit(p, place):
        base, position, force = point_values(points_ref, p, place, 0.25 * GAUSS_NORM)
        first = first_z.astype(F32)

        @pl.when((base[2] + 2.0 >= first - 1.0) & (base[2] - 1.0 <= first + lay.depth))
        def _():
            x0, x1 = weighted(part_x, base[0], position[0])
            y0, y1 = weighted(part_y, base[1], position[1])
            z0, z1 = weighted(elem_z, base[2], position[2])
            h0, h1 = weighted(elem_halo, base[2], position[2])
            pick = part_z[0:1] == 0
            h0 = jnp.where(pick, h0[N - 1 : N], h0[0:1])
            h1 = jnp.where(pick, h1[N - 1 : N], h1[0:1])
            x1 = force[0] * x1
            fz1 = force[2] * z1
            fz0 = force[1] * z0
            for j in range(N):
                first_part = y0[j : j + 1] * z0
                other_part = y1[j : j + 1] * fz0 + y0[j : j + 1] * fz1
                for i in range(N):
                    rows = pl.ds((i * N + j) * N, N)
                    g_ref[rows, :] += x1[i : i + 1] * first_part + x0[i : i + 1] * other_part
            first_part = y0 * h0
            other_part = y1 * (force[1] * h0) + y0 * (force[2] * h1)
            for i in range(N):
                rows = pl.ds(i * N, N)
                halo_ref[rows, :] += x1[i : i + 1] * first_part + x0[i : i + 1] * other_part

    for_points(points_ref, local_points, visit)


def inverse_diagonal(lay, factor, dinv_ref, outer):
    shape = (N, lay.width)
    part_x, part_y, part_z = lane_parts(lay, shape)
    first = lay.slab() * lay.depth
    part_z = jnp.where(part_z == 0, first - 1, first + lay.depth) if outer else first + part_z
    node = lax.broadcasted_iota(jnp.int32, shape, 0)

    def share(low, high):
        return (
            jnp.where(low, 0.0, 0.5),
            jnp.where(high, 0.0, 0.5),
        )

    low_z, high_z = share(part_z == 0, part_z == EZ - 1)
    along_z = jnp.where(node == 0, low_z, jnp.where(node == N - 1, high_z, 1.0))
    if outer:
        along_z = jnp.where((part_z < 0) | (part_z >= EZ), 0.0, along_z)
    along_x = dict(zip((0, N - 1), share(part_x == 0, part_x == lay.num_x - 1)))
    along_y = dict(zip((0, N - 1), share(part_y == 0, part_y == lay.num_y - 1)))
    tables = {}
    for i in range(N // 2):
        for j in range(i + 1):
            tables[i, j] = tables[j, i] = column(factor[i, j], shape) * along_z
    for i in range(N):
        for j in range(N):
            rows = pl.ds((i * N + j) * N, N)
            value = tables[min(i, N - 1 - i), min(j, N - 1 - j)]
            if i in along_x:
                value = value * along_x[i]
            if j in along_y:
                value = value * along_y[j]
            dinv_ref[rows, :] = value


def first_kernel(
    lay,
    local_points,
    derivative,
    one,
    factor,
    recv_ref,
    high_ref,
    low_ref,
    along_ref,
    g_ref,
    x_ref,
    dinv_ref,
    outer_ref,
    face_ref,
    points_ref,
    s_ref,
    halo_ref,
    flat_ref,
    table_ref,
    sem,
):
    count, block = recv_ref.shape[0], recv_ref.shape[1]
    for d in range(count):
        points_ref[pl.ds(d, 1), :] = recv_ref[d, 1:2, : points_ref.shape[1]]
    copy = pltpu.make_async_copy(points_ref, table_ref, sem)
    copy.start()
    for d in range(count):
        flat_ref[pl.ds(d * block, block), :] = recv_ref[d]
    g_ref[...] = flat_ref[...].T
    low, high = get_rows(g_ref, 0), get_rows(g_ref, N - 1)
    _, _, part_z = lane_parts(lay, low.shape)
    set_rows(g_ref, 0, jnp.where(part_z == 0, low, roll(high, 1, 1)))
    halo_ref[...] = jnp.where(part_z == 0, low, high)
    inverse_diagonal(lay, factor, dinv_ref, False)
    inverse_diagonal(lay, factor, outer_ref, True)
    copy.wait()
    right_side(lay, local_points, (derivative, one[1]), table_ref, g_ref, halo_ref)
    assemble(lay, g_ref, s_ref, halo_ref[...])
    x_ref[...] = (1.0 / THETA) * dinv_ref[...] * s_ref[...]
    subtract_stiffness(lay, one, x_ref, g_ref, high_ref, low_ref, along_ref)
    store_faces(lay, g_ref, face_ref)


def vertex_rows(lay, table_ref, values):
    high, low = split(values)
    both = jnp.dot(table_ref[...], jnp.concatenate([high, low], 1), preferred_element_type=F32)
    load = both[:N, : lay.width] + both[:N, lay.width :] + both[N:, : lay.width]
    rows = [load[n : n + 1] for n in range(N)]
    rows = [rows[n] + roll(rows[4 + n], lay.step_x, 1) for n in range(4)]
    return [rows[n] + roll(rows[2 + n], lay.step_y, 1) for n in range(2)]


def face_values(lay, u_ref):
    low, high = get_rows(u_ref, 0), get_rows(u_ref, N - 1)
    _, _, part_z = lane_parts(lay, low.shape)
    return jnp.where(part_z == 0, low, 0.0), jnp.where(part_z == 0, 0.0, high)


def send_loads(lay, own, outer, far, send_ref, token_ref):
    _, _, part_z = lane_parts(lay, own[0].shape)
    bottom = part_z == 0
    before = jnp.where(bottom, 0.0, roll(outer[0], 1, 1))
    here = own[0] + jnp.where(bottom, outer[1], roll(own[1], 1, 1))
    after = jnp.where(bottom, roll(own[1], -1, 1) + roll(outer[0], -1, 1), outer[1])
    second = jnp.zeros_like(here)
    if far is not None:
        before = before + jnp.where(bottom, far[0], roll(far[1], 1, 1))
        after = after + jnp.where(bottom, 0.0, far[0])
        second = jnp.where(bottom, roll(far[1], -1, 1), 0.0)
    rows = jnp.concatenate([before, here, after, second] * 2, 0)
    for d in range(send_ref.shape[0]):
        send_ref[d] = rows
    token_ref[...] = jnp.zeros(token_ref.shape, F32)


OLD = RHO_SECOND * RHO_FIRST
NEW = 2.0 * RHO_SECOND / DELTA


def first_response(
    lay, g_ref, x_ref, dinv_ref, loads_ref, near_ref, send_ref, token_ref, s_ref
):
    assemble(lay, g_ref, s_ref, jnp.zeros((FACE, lay.width), F32))
    update = NEW * dinv_ref[...] * s_ref[...]
    s_ref[...] = update
    total = OLD * x_ref[...] + update
    own = vertex_rows(lay, loads_ref, jnp.concatenate([g_ref[...], total], 0))
    outer = vertex_rows(lay, near_ref, jnp.concatenate(face_values(lay, s_ref), 0))
    send_loads(lay, own, outer, None, send_ref, token_ref)


def pair_response(
    lay,
    one,
    g_ref,
    dinv_ref,
    outer_ref,
    high_ref,
    low_ref,
    along_ref,
    loads_ref,
    near_ref,
    send_ref,
    token_ref,
    s_ref,
    sh_ref,
    u_ref,
    v_ref,
    t_ref,
    h_ref,
):
    tile = (high_ref, low_ref, along_ref)
    assemble(lay, g_ref, s_ref, jnp.zeros((FACE, lay.width), F32))
    u_ref[...] = (1.0 / THETA) * dinv_ref[...] * s_ref[...]
    t_ref[...] = g_ref[...]
    subtract_stiffness(lay, one, u_ref, t_ref, *tile)
    low, high = face_values(lay, u_ref)
    v_ref[...] = jnp.zeros(v_ref.shape, F32)
    set_rows(v_ref, N - 1, low)
    set_rows(v_ref, 0, high)
    h_ref[...] = jnp.zeros(h_ref.shape, F32)
    subtract_stiffness(lay, one, v_ref, h_ref, *tile)
    assemble_both(lay, t_ref, h_ref, s_ref, sh_ref)
    update = OLD * u_ref[...] + NEW * dinv_ref[...] * s_ref[...]
    own = vertex_rows(lay, loads_ref, jnp.concatenate([t_ref[...], update], 0))
    v_ref[...] = OLD * v_ref[...] + NEW * outer_ref[...] * sh_ref[...]
    outer = vertex_rows(lay, loads_ref, jnp.concatenate([h_ref[...], v_ref[...]], 0))
    far = vertex_rows(lay, near_ref, jnp.concatenate(face_values(lay, v_ref), 0))
    send_loads(lay, own, outer, far, send_ref, token_ref)


def second_kernel(
    lay,
    one,
    core_ref,
    chip_ref,
    g_ref,
    x_ref,
    dinv_ref,
    high_ref,
    low_ref,
    along_ref,
    token_ref,
    g_out,
    x_out,
    core_out,
    chip_out,
    s_ref,
    u_ref,
):
    assemble(lay, g_ref, s_ref, halo_of(lay, core_ref, chip_ref))
    update = OLD * x_ref[...] + NEW * dinv_ref[...] * s_ref[...]
    u_ref[...] = update
    x_out[...] = x_ref[...] + update
    g_out[...] = g_ref[...]
    subtract_stiffness(lay, one, u_ref, g_out, high_ref, low_ref, along_ref)
    send_layers(lay, g_out, s_ref, core_out, chip_out)


def solve_coarse(lay, mass, stiff, loads_ref, rows_ref, first_ref, second_ref):
    count = 4
    for s in range(lay.slabs):
        rows_ref[pl.ds(s * count, count), :] = loads_ref[lay.order[s], :count]

    def part(n):
        if lay.width == 128:
            return rows_ref[pl.ds(n, lay.slabs, stride=count), :]
        return jnp.concatenate(
            [rows_ref[pl.ds(s * count + n, 1), :] for s in range(lay.slabs)], 0
        )

    shape = (lay.slabs, lay.width)
    part_x, part_y, part_z = lane_parts(lay, shape)
    row = lax.broadcasted_iota(jnp.int32, shape, 0)
    keep = ((part_x > 0) & (part_y > 0) & ((part_z > 0) | (row > 0))).astype(F32)
    bottom = part_z == 0

    def around_z(v):
        return jnp.where(bottom, roll(v + roll(v, 1, 0), -1, 1), roll(v + roll(v, -1, 0), 1, 1))

    def above(v):
        return jnp.where(bottom, roll(v, -1, 1), roll(roll(v, -1, 0), 1, 1))

    def neighbours(v, step):
        return roll(v, step, 1) + roll(v, -step, 1)

    def mix(pair, v, around):
        return (2.0 * pair[0]) * v + pair[1] * around

    def operate(v):
        around = around_z(v)
        mass_z, stiff_z = mix(mass, v, around), mix(stiff, v, around)
        around = neighbours(mass_z, lay.step_y)
        both = mix(mass, mass_z, around)
        rest = mix(stiff, mass_z, around) + mix(mass, stiff_z, neighbours(stiff_z, lay.step_y))
        out = mix(stiff, both, neighbours(both, lay.step_x)) + mix(
            mass, rest, neighbours(rest, lay.step_x)
        )
        return (0.5 * keep) * out

    def inner(a, b):
        return jnp.sum(jnp.sum(a * b, axis=1, keepdims=True), axis=0, keepdims=True)

    residual = keep * (part(1) + roll(part(0), -1, 0) + roll(part(2), 1, 0) + roll(part(3), 2, 0))
    image = operate(residual)
    total = jnp.zeros(shape, F32)
    for step in range(CG_STEPS):
        last = step + 1 == CG_STEPS
        norm, curv = inner(residual, residual), inner(image, residual)
        if not last:
            second = operate(image)
        if step == 0:
            alpha = norm / curv
            direction, moved = residual, image
            if not last:
                moved_image = second
        else:
            beta = norm / norm_old
            alpha = norm / (curv - beta * norm / alpha)
            direction = residual + beta * direction
            if not last:
                moved, moved_image = image + beta * moved, second + beta * moved_image
        norm_old = norm
        total = total + alpha * direction
        if not last:
            residual, image = residual - alpha * moved, image - alpha * moved_image
    here = pl.ds(N, lay.slabs)
    for ref, value in ((first_ref, total), (second_ref, above(total))):
        ref[...] = jnp.zeros(ref.shape, F32)
        ref[here, :] = value


def corners(lay, low, high):
    rows = [low, high]
    rows = rows + [roll(r, -lay.step_y, 1) for r in rows]
    rows = rows + [roll(r, -lay.step_x, 1) for r in rows]
    corner = lax.broadcasted_iota(jnp.int32, (N, lay.width), 0)
    local = jnp.broadcast_to(rows[0], (N, lay.width))
    for n in range(1, N):
        local = jnp.where(corner == n, rows[n], local)
    return local


def prolong_coarse(lay, first_ref, second_ref, interp_ref, image_ref, edge_ref, g_ref, h_ref, x_ref):
    mine = lay.slab() + N
    _, _, part_z = lane_parts(lay, (1, lay.width))
    bottom = part_z == 0
    own, outer, far = [], [], []
    for ref in (first_ref, second_ref):
        before, here, after = (ref[pl.ds(mine + shift, 1), :] for shift in (-1, 0, 1))
        own.append(here)
        outer.append(jnp.where(bottom, roll(before, -1, 1), roll(after, 1, 1)))
        far.append(jnp.where(bottom, before, after))
    local = stacked(corners(lay, *own))
    dot = functools.partial(jnp.dot, preferred_element_type=F32)
    x_ref[...] += dot(interp_ref[...], local)
    g_ref[...] -= dot(image_ref[...], local)
    h_ref[...] -= dot(image_ref[...], stacked(corners(lay, *outer)))
    edge = dot(edge_ref[...], stacked(corners(lay, *far)))
    low, high = get_rows(h_ref, 0), get_rows(h_ref, N - 1)
    set_rows(h_ref, 0, low - jnp.where(bottom, edge[FACE:], 0.0))
    set_rows(h_ref, N - 1, high - jnp.where(bottom, 0.0, edge[:FACE]))


def pair_kernel(lay, one, coarse, kind, core_ref, chip_ref, g_ref, x_ref, dinv_ref, outer_ref, *refs):
    refs = list(refs)
    high_ref, low_ref, along_ref, edge_high_ref, edge_low_ref = (refs.pop(0) for _ in range(5))
    if coarse:
        loads_ref, image_ref, image_edge_ref = (refs.pop(0) for _ in range(3))
        interp_ref = refs.pop(0)
    if kind == "inner":
        token_ref, points_ref = refs.pop(0), refs.pop(0)
    if kind == "last":
        token_ref = refs.pop(0)
    if kind == "last":
        out_ref = refs.pop(0)
    else:
        g_out, x_out = refs.pop(0), refs.pop(0)
        core_out, chip_out = refs.pop(0), refs.pop(0)
        if kind == "inner":
            points_out = refs.pop(0)
            points_out[...] = points_ref[...]
    s_ref, sh_ref, h_ref, u_ref = (refs.pop(0) for _ in range(4))
    if kind == "last":
        g_out, x_out = refs.pop(0), refs.pop(0)

    g_out[...] = g_ref[...]
    x_out[...] = x_ref[...]
    receive_layers(lay, core_ref, chip_ref, h_ref)
    if coarse:
        rows_ref, first_ref, second_ref = refs
        solve_coarse(lay, *coarse, loads_ref, rows_ref, first_ref, second_ref)
        prolong_coarse(
            lay, first_ref, second_ref, interp_ref, image_ref, image_edge_ref, g_out, h_ref, x_out
        )
    assemble_both(lay, g_out, h_ref, s_ref, sh_ref)
    update = (1.0 / THETA) * dinv_ref[...] * s_ref[...]
    u_ref[...] = update
    outer = (1.0 / THETA) * outer_ref[...] * sh_ref[...]
    edge = times3(edge_high_ref[...], edge_low_ref[...], outer)
    _, _, part_z = lane_parts(lay, (FACE, lay.width))
    near = jnp.where(
        part_z == 0, get_rows(h_ref, N - 1) - edge[FACE:], get_rows(h_ref, 0) - edge[:FACE]
    )
    subtract_stiffness(lay, one, u_ref, g_out, high_ref, low_ref, along_ref)
    assemble(lay, g_out, s_ref, near)
    update = u_ref[...]
    following = OLD * update + NEW * dinv_ref[...] * s_ref[...]
    if kind == "last":
        total = (x_out[...] + (update + following)).T
        count, block = out_ref.shape[0], out_ref.shape[1]
        for d in range(count):
            out_ref[d] = total[d * block : (d + 1) * block]
        return
    x_out[...] += update + following
    u_ref[...] = following
    subtract_stiffness(lay, one, u_ref, g_out, high_ref, low_ref, along_ref)
    send_layers(lay, g_out, s_ref, core_out, chip_out)


def unpack_kernel(lay, recv_ref, out_ref, flat_ref):
    for d in range(lay.slabs):
        first = lay.slab_at(d) * lay.depth
        for e2 in range(lay.tiles_y):
            rows = recv_ref[d, pl.ds(e2 * lay.depth, lay.depth), :]
            flat_ref[pl.ds(e2 * EZ + first, lay.depth), :] = rows
    out_ref[...] = flat_ref[...].T


def gauss_at(elem, node, base, position):
    half_nodes = jnp.full(node.shape, 0.5 * (1.0 + GLL_POINTS[0]), F32)
    for n in range(1, N):
        half_nodes = jnp.where(node == n, 0.5 * (1.0 + GLL_POINTS[n]), half_nodes)
    elem = elem.astype(F32)
    away = elem + half_nodes - position
    inside = (
        (elem == base)
        | (elem == base + 1.0)
        | ((elem == base - 1.0) & (node == N - 1))
        | ((elem == base + 2.0) & (node == 0))
    )
    return jnp.where(inside, jnp.exp(-(away * away) / (WIDTH_EPS * WIDTH_EPS)), 0.0)


def forces_kernel(tiles_y, local_points, points_ref, out_ref, done_ref):
    done_ref[...] = jnp.zeros(done_ref.shape, F32)
    count = points_ref.shape[0]
    first_x, first_y = lax.axis_index("ex"), lax.axis_index("ey") * tiles_y
    lane = lax.broadcasted_iota(jnp.int32, (count, 3 * FACE), 1)
    node_x, node_y, part = (lane >> 3) & (N - 1), lane & (N - 1), lane >> 6
    lane_z = lax.broadcasted_iota(jnp.int32, (count, tiles_y * EZ), 1)
    planes, columns = [], []
    for place in range(local_points):

        def value(n):
            at = (place * 9 + n) * N
            return points_ref[:, at : at + 1]

        base = [value(d) for d in range(3)]
        position = [value(d) + 1.0 + value(3 + d) for d in range(3)]
        force = jnp.where(part == 0, value(6), jnp.where(part == 1, value(7), value(8)))
        x = gauss_at(jnp.broadcast_to(first_x, lane.shape), node_x, base[0], position[0])
        scaled = GAUSS_NORM * force * x
        for e2 in range(tiles_y):
            y = gauss_at(jnp.broadcast_to(first_y + e2, lane.shape), node_y, base[1], position[1])
            planes.append(scaled * y)
            columns.append((e2, base[2], position[2]))
    high, low = split(jnp.concatenate(planes, 0))
    plane = jnp.concatenate([high, high, low], 0)
    elem_z, row_z = lane_z & (EZ - 1), lane_z >> log2(EZ)
    for k in range(N):
        node = jnp.full(lane_z.shape, k, jnp.int32)
        along = [
            jnp.where(row_z == e2, gauss_at(elem_z, node, base, position), 0.0)
            for e2, base, position in columns
        ]
        high, low = split(jnp.concatenate(along, 0))
        out_ref[pl.ds(k, 3 * FACE, stride=N), :] = lax.dot_general(
            plane,
            jnp.concatenate([high, low, high], 0),
            (((0,), (0,)), ((), ())),
            preferred_element_type=F32,
        )


def call(kernel, outs, inputs, scratch=(), smem=0, spaces=None, limit=40):
    spaces = spaces or [pltpu.SMEM] * smem + [pltpu.VMEM] * (len(inputs) - smem)
    specs = [pl.BlockSpec(memory_space=space) for space in spaces]
    shapes = [jax.ShapeDtypeStruct(s, F32) for s in outs]
    result = pl.pallas_call(
        kernel,
        out_shape=shapes,
        in_specs=specs,
        out_specs=[pl.BlockSpec(memory_space=pltpu.VMEM)] * len(shapes),
        scratch_shapes=[pltpu.VMEM(s, F32) if isinstance(s, tuple) else s for s in scratch],
        compiler_params=pltpu.CompilerParams(vmem_limit_bytes=limit * 1024 * 1024),
    )(*inputs)
    return result


def shards(source, point_base, point_offset, point_force):
    tiles_x, tiles_y = source.shape[3], source.shape[4] // EZ
    lay = Layout(lax.axis_size("ex"), lax.axis_size("ey"), tiles_x, tiles_y)
    devices = lay.mesh_x * lay.mesh_y
    derivative, weights, interp, stiff_one = build_tables()
    width, fields = lay.width, (N**3, lay.width)

    diag_w = np.diag(weights)
    full = 0.5 * (
        kron3(stiff_one, diag_w, diag_w)
        + kron3(diag_w, stiff_one, diag_w)
        + kron3(diag_w, diag_w, stiff_one)
    )
    edge_rows = np.concatenate([np.arange(FACE) * N, np.arange(FACE) * N + N - 1])
    plane = 0.5 * (np.kron(stiff_one, diag_w) + np.kron(diag_w, stiff_one))
    high, low = (jnp.asarray(t) for t in split_table(np.kron(np.eye(N // 2), plane)))
    along = np.broadcast_to(0.5 * np.kron(weights, weights)[:, None], (FACE, width))
    along = jnp.asarray(along, F32)
    edge_high, edge_low = (jnp.asarray(t) for t in split_table(full[edge_rows]))
    one = (stiff_one, weights)
    interp3 = kron3(interp, interp, interp)
    image3 = full @ interp3
    ratio = (weights[:, None] * derivative**2).sum(axis=0) / weights
    diag = 0.5 * (ratio[:, None, None] + ratio[None, :, None] + ratio[None, None, :])
    diag = diag * weights[:, None, None] * weights[None, :, None] * weights[None, None, :]
    factor = 1.0 / diag
    mass = interp.T @ diag_w @ interp
    stiff = interp.T @ stiff_one @ interp
    moved = -interp3.T @ full
    loads_table, near_table = (
        jnp.asarray(np.concatenate(split_table(t), 0))
        for t in (
            np.concatenate([interp3.T, moved], 1),
            np.concatenate([moved[:, edge_rows[FACE:]], moved[:, edge_rows[:FACE]]], 1),
        )
    )
    prolong3, image3, image_edge = (
        jnp.asarray(stacked_table(t)) for t in (interp3, image3, image3[edge_rows])
    )

    local_points = point_base.shape[1]
    block = lay.block
    (send,) = call(
        functools.partial(pack_kernel, lay),
        [(lay.slabs, block, N**3)],
        [
            pltpu.with_memory_space_constraint(t, pltpu.HBM)
            for t in (
                point_base.T,
                point_offset.T,
                point_force.T,
                source.reshape(N**3, tiles_y * EZ),
            )
        ],
        [
            pltpu.VMEM((local_points, 3), jnp.int32),
            (local_points, 3),
            (local_points, 3),
            (N**3, tiles_y * EZ),
            (tiles_y * EZ, N**3),
            pltpu.SemaphoreType.DMA((4,)),
        ],
        spaces=[pltpu.HBM] * 4,
    )
    recv = lax.all_to_all(send, lay.axis, 0, 0)
    if not lay.joint:
        recv = lax.all_gather(recv, "ex", axis=0, tiled=True)

    def swap(core, chip):
        return (
            lax.ppermute(core, lay.axis, lay.swaps(0)),
            lax.ppermute(chip, lay.axis, lay.swaps(1)),
        )

    def gather(loads):
        return lax.all_to_all(loads, lay.axis, 0, 0)

    face_shape = (FACE, width)
    layer = (N**3 // 2, width)
    loads_shape = (lay.slabs, N, width)
    table = (devices, -(-9 * N * local_points // 128) * 128)
    g, x, dinv, outer, face, points = call(
        functools.partial(first_kernel, lay, local_points, derivative, one, factor),
        [fields, fields, fields, fields, (256, width), table],
        [recv, high, low, along],
        [fields, face_shape, (width, N**3), pltpu.SMEM(table, F32), pltpu.SemaphoreType.DMA],
    )
    faces = swap(face, face)
    loads, token = call(
        functools.partial(first_response, lay),
        [loads_shape, (N, 128)],
        [g, x, dinv, loads_table, near_table],
        [fields],
    )
    loads = gather(loads)
    g, x, core, chip = call(
        functools.partial(second_kernel, lay, one),
        [fields, fields, layer, layer],
        [*faces, g, x, dinv, high, low, along, token],
        [fields, fields],
    )
    coarse = ((mass[0, 0], mass[0, 1]), (stiff[0, 0], stiff[0, 1]))
    stiffness = [high, low, along, edge_high, edge_low]

    for cycle in range(CYCLES):
        core, chip = swap(core, chip)
        last = cycle + 1 == CYCLES
        outs = [fields, fields, layer, layer]
        extra = [done] if last else []
        scratch = [fields] * 4
        if last:
            outs = [(lay.mesh_x * lay.mesh_y, block, N**3)]
            scratch += [fields, fields]
        outs = call(
            functools.partial(pair_kernel, lay, one, coarse, "last" if last else "plain"),
            outs,
            [core, chip, g, x, dinv, outer, *stiffness, loads, image3, image_edge, prolong3, *extra],
            scratch + [(lay.slabs * 4, width)] + [(lay.slabs + 2 * N, width)] * 2,
        )
        if last:
            break
        g, x, core, chip = outs
        layers = swap(core, chip)
        loads, token = call(
            functools.partial(pair_response, lay, one),
            [loads_shape, (N, 128)],
            [g, dinv, outer, high, low, along, loads_table, near_table],
            [fields] * 6,
        )
        loads = gather(loads)
        g, x, core, chip, points = call(
            functools.partial(pair_kernel, lay, one, None, "inner"),
            [fields, fields, layer, layer, table],
            [*layers, g, x, dinv, outer, *stiffness, token, points],
            [fields] * 4,
        )
        forces, done = call(
            functools.partial(forces_kernel, tiles_y, local_points),
            [(3 * N**3, tiles_y * EZ), (N, 128)],
            [points],
        )
    (out,) = outs
    if not lay.joint:
        out = lax.dynamic_slice_in_dim(out, lax.axis_index("ex") * lay.mesh_y, lay.mesh_y, 0)
    out = lax.all_to_all(out, lay.axis, 0, 0)
    (pressure,) = call(
        functools.partial(unpack_kernel, lay),
        [(N**3, tiles_y * EZ)],
        [out],
        [(lay.slabs * block, N**3)],
    )
    return (
        pressure.reshape(source.shape),
        forces.reshape((3, *source.shape)),
    )


def solution(mesh):
    in_specs = (
        P(None, None, None, "ex", "ey"),
        P(None, ("ex", "ey")),
        P(None, ("ex", "ey")),
        P(None, ("ex", "ey")),
    )
    out_specs = (P(None, None, None, "ex", "ey"), P(None, None, None, None, "ex", "ey"))
    return jax.shard_map(shards, mesh=mesh, in_specs=in_specs, out_specs=out_specs, check_vma=False)
```

```python
import functools
import math

import jax
import jax.numpy as jnp
import numpy as np
from jax import lax
from jax.experimental import pallas as pl
from jax.experimental.pallas import tpu as pltpu
from jax.sharding import PartitionSpec as P

EZ = 64
CG_STEPS = 4
CYCLES = 2
N = 8
GLL_POINTS = np.array(
    [
        -1.0,
        -0.8717401485096066,
        -0.5917001814331423,
        -0.2092992179024789,
        0.2092992179024789,
        0.5917001814331423,
        0.8717401485096066,
        1.0,
    ]
)
WIDTH_EPS = 0.35
GAUSS_NORM = 1.0 / (math.pi**1.5 * WIDTH_EPS**3)
CHEB_LOW = 1.5
CHEB_HIGH = 12.0
THETA = 0.5 * (CHEB_HIGH + CHEB_LOW)
DELTA = 0.5 * (CHEB_HIGH - CHEB_LOW)
RHO_FIRST = DELTA / THETA
RHO_SECOND = 1.0 / (2.0 * THETA / DELTA - RHO_FIRST)
F32 = jnp.float32
BF16 = jnp.bfloat16
FACE = N * N


def build_tables():
    points = GLL_POINTS
    degree = len(points) - 1
    previous = points * 0.0 + 1.0
    current = points.copy()
    for k in range(1, degree):
        following = ((2 * k + 1) * points * current - k * previous) / (k + 1)
        previous = current
        current = following
    derivative = np.zeros((degree + 1, degree + 1))
    for i in range(degree + 1):
        for j in range(degree + 1):
            if i != j:
                derivative[i, j] = current[i] / (current[j] * (points[i] - points[j]))
    derivative[0, 0] = -degree * (degree + 1) / 4.0
    derivative[degree, degree] = degree * (degree + 1) / 4.0
    weights = 2.0 / (degree * (degree + 1) * current**2)
    interp = np.stack([(1.0 - points) / 2.0, (1.0 + points) / 2.0], axis=1)
    stiff_one = derivative.T @ (weights[:, None] * derivative)
    return derivative, weights, interp, stiff_one


def kron3(a, b, c):
    return np.kron(np.kron(a, b), c)


def log2(n):
    return int(n).bit_length() - 1


class Layout:
    def __init__(self, mesh_x, mesh_y, tiles_x, tiles_y):
        self.mesh_x, self.mesh_y = mesh_x, mesh_y
        self.num_x, self.num_y = tiles_x * mesh_x, tiles_y * mesh_y
        self.tiles_y = tiles_y
        self.joint = EZ % (2 * mesh_x * mesh_y) == 0
        self.axis = ("ex", "ey") if self.joint else "ey"
        self.slabs = mesh_x * mesh_y if self.joint else mesh_y
        self.depth = EZ // self.slabs
        assert self.depth == 2 and tiles_x == 1
        self.width = self.num_x * self.num_y * self.depth
        self.step_y = self.depth
        self.step_x = self.depth * self.num_y
        self.block = tiles_y * self.depth
        slab_of = [self.slab_at(d) for d in range(self.slabs)]
        self.order = [slab_of.index(s) for s in range(self.slabs)]

    def slab_at(self, d):
        if self.joint and self.mesh_x % 2 == 0 and self.mesh_y % 2 == 0:
            high = self.mesh_y // 2
            y = d & 1
            z = (d >> 1) & (high - 1)
            core = (d >> log2(self.mesh_y)) & 1
            x = d >> (log2(self.mesh_y) + 1)
            turn = y ^ (x & 1)
            return ((x * 2 + turn) * high + (z ^ (turn * (high - 1)))) * 2 + core
        if not self.joint and self.mesh_y % 8 == 0:
            return d ^ (((d >> 3) & 1) * 7)
        return d

    def slab(self):
        d = lax.axis_index("ey")
        return self.slab_at(lax.axis_index("ex") * self.mesh_y + d if self.joint else d)

    def swaps(self, first):
        pairs = []
        for s in range(first, self.slabs, 2):
            a, b = self.order[s], self.order[(s + 1) % self.slabs]
            pairs += [(a, b), (b, a)]
        return pairs


def split(x):
    high = x.astype(BF16)
    return high, (x - high.astype(F32)).astype(BF16)


def times3(high, low, x):
    xh, xl = split(x)
    dot = functools.partial(jnp.dot, preferred_element_type=F32)
    return dot(high, xh) + dot(high, xl) + dot(low, xh)


def split_table(x):
    high = x.astype(BF16)
    return high, (x - high.astype(np.float64)).astype(BF16)


def stacked_table(x):
    high, low = split_table(x)
    return np.concatenate([high, high, low, low], 1)


def stacked(x):
    high = x.astype(BF16).astype(F32)
    low = x - high
    return jnp.concatenate([high, low, high, low], 0).astype(BF16)


def subtract_stiffness(lay, one, u_ref, g_ref, high_ref, low_ref, along_ref):
    matrix, weights = one
    dot = functools.partial(jnp.dot, preferred_element_type=F32)
    half = N // 2
    for first in (0, half):
        scaled = [
            float(weights[i]) * u_ref[pl.ds(i * FACE, FACE), :] for i in range(first, first + half)
        ]
        xh, xl = split(jnp.concatenate(scaled, 0))
        both = dot(high_ref[...], jnp.concatenate([xh, xl], 1))
        rows = pl.ds(first * FACE, half * FACE)
        g_ref[rows, :] -= both[:, : lay.width] + both[:, lay.width :] + dot(low_ref[...], xh)
    even = 0.5 * (matrix[:half, :half] + matrix[:half, :half - 1 : -1])
    odd = 0.5 * (matrix[:half, :half] - matrix[:half, :half - 1 : -1])
    for j in range(N):
        values = [u_ref[pl.ds((i * N + j) * N, N), :] for i in range(N)]
        sums = [values[i] + values[N - 1 - i] for i in range(half)]
        gaps = [values[i] - values[N - 1 - i] for i in range(half)]
        along = along_ref[pl.ds(j * N, N), :]
        for i in range(half):
            a = sum(float(even[i, q]) * sums[q] for q in range(half))
            b = sum(float(odd[i, q]) * gaps[q] for q in range(half))
            g_ref[pl.ds((i * N + j) * N, N), :] -= along * (a + b)
            g_ref[pl.ds(((N - 1 - i) * N + j) * N, N), :] -= along * (a - b)


def roll(x, shift, axis):
    size = x.shape[axis]
    return pltpu.roll(x, shift % size, axis)


def lane_parts(lay, shape):
    lane = lax.broadcasted_iota(jnp.int32, shape, len(shape) - 1)
    part_z = lane & (lay.depth - 1)
    part_y = lax.shift_right_logical(lane, log2(lay.step_y)) & (lay.num_y - 1)
    part_x = lax.shift_right_logical(lane, log2(lay.step_x))
    return part_x, part_y, part_z


def get_rows(ref, k):
    if ref.shape[1] == 128:
        return ref[pl.ds(k, FACE, stride=N), :]
    return jnp.concatenate([ref[pl.ds(n * N + k, 1), :] for n in range(FACE)], 0)


def set_rows(ref, k, value):
    if ref.shape[1] == 128:
        ref[pl.ds(k, FACE, stride=N), :] = value
    else:
        for n in range(FACE):
            ref[pl.ds(n * N + k, 1), :] = value[n : n + 1]


def assemble_xy(lay, s_ref):
    last = N - 1
    for j in range(N):
        a, b = pl.ds(j * N, N), pl.ds((last * N + j) * N, N)
        low, high = s_ref[a, :], s_ref[b, :]
        s_ref[a, :] = low + roll(high, lay.step_x, 1)
        s_ref[b, :] = high + roll(low, -lay.step_x, 1)
    for i in range(N):
        a, b = pl.ds(i * N * N, N), pl.ds((i * N + last) * N, N)
        low, high = s_ref[a, :], s_ref[b, :]
        s_ref[a, :] = low + roll(high, lay.step_y, 1)
        s_ref[b, :] = high + roll(low, -lay.step_y, 1)


def assemble(lay, g_ref, s_ref, halo):
    _, _, part_z = lane_parts(lay, halo.shape)
    s_ref[...] = g_ref[...]
    low = get_rows(g_ref, 0)
    high = get_rows(g_ref, N - 1)
    set_rows(s_ref, 0, low + jnp.where(part_z == 0, halo, roll(high, 1, 1)))
    set_rows(s_ref, N - 1, high + jnp.where(part_z == lay.depth - 1, halo, roll(low, -1, 1)))
    assemble_xy(lay, s_ref)


def store_faces(lay, g_ref, face_ref):
    low = get_rows(g_ref, 0)
    high = get_rows(g_ref, N - 1)
    _, _, part_z = lane_parts(lay, low.shape)
    face_ref[...] = jnp.zeros(face_ref.shape, F32)
    face_ref[:FACE, :] = jnp.where(part_z == 0, low, high)


def halo_of(lay, core_ref, chip_ref):
    odd = (lay.slab() & 1) == 1
    core, chip = core_ref[:FACE, :], chip_ref[:FACE, :]
    below = jnp.where(odd, core, chip)
    above = jnp.where(odd, chip, core)
    _, _, part_z = lane_parts(lay, core.shape)
    return jnp.where(part_z == 0, roll(below, 1 - lay.depth, 1), roll(above, lay.depth - 1, 1))


def assemble_both(lay, g_ref, h_ref, s_ref, sh_ref):
    low, high = get_rows(g_ref, 0), get_rows(g_ref, N - 1)
    out_low, out_high = get_rows(h_ref, 0), get_rows(h_ref, N - 1)
    _, _, part_z = lane_parts(lay, low.shape)
    bottom = part_z == 0
    s_ref[...] = g_ref[...]
    sh_ref[...] = h_ref[...]
    set_rows(s_ref, 0, low + jnp.where(bottom, out_high, roll(high, 1, 1)))
    set_rows(s_ref, N - 1, high + jnp.where(bottom, roll(low, -1, 1), out_low))
    set_rows(sh_ref, N - 1, out_high + jnp.where(bottom, low, 0.0))
    set_rows(sh_ref, 0, out_low + jnp.where(bottom, 0.0, high))
    assemble_xy(lay, s_ref)
    assemble_xy(lay, sh_ref)


def send_layers(lay, g_ref, s_ref, core_ref, chip_ref):
    low, high = get_rows(g_ref, 0), get_rows(g_ref, N - 1)
    _, _, part_z = lane_parts(lay, low.shape)
    s_ref[...] = g_ref[...]
    set_rows(s_ref, N - 1, jnp.where(part_z == 0, high + roll(low, -1, 1), high))
    set_rows(s_ref, 0, jnp.where(part_z == 0, low, low + roll(high, 1, 1)))
    half = N**3 // 2
    a, b = s_ref[:half, :], s_ref[half:, :]
    _, _, part_z = lane_parts(lay, a.shape)
    bottom = part_z == 0
    first = jnp.where(bottom, a, roll(b, 1, 1))
    second = jnp.where(bottom, roll(a, -1, 1), b)
    odd = (lay.slab() & 1) == 1
    core_ref[...] = jnp.where(odd, first, second)
    chip_ref[...] = jnp.where(odd, second, first)


def receive_layers(lay, core_ref, chip_ref, h_ref):
    odd = (lay.slab() & 1) == 1
    core, chip = core_ref[...], chip_ref[...]
    below, above = jnp.where(odd, core, chip), jnp.where(odd, chip, core)
    _, _, part_z = lane_parts(lay, core.shape)
    bottom = part_z == 0
    half = N**3 // 2
    h_ref[:half, :] = jnp.where(bottom, below, roll(above, 1, 1))
    h_ref[half:, :] = jnp.where(bottom, roll(below, -1, 1), above)


def pack_kernel(
    lay,
    base_ref,
    offset_ref,
    force_ref,
    source_ref,
    out_ref,
    base_buf,
    offset_buf,
    force_buf,
    field_ref,
    flat_ref,
    sems,
):
    pairs = (
        (source_ref, field_ref),
        (base_ref, base_buf),
        (offset_ref, offset_buf),
        (force_ref, force_buf),
    )
    copies = [pltpu.make_async_copy(a, b, sems.at[n]) for n, (a, b) in enumerate(pairs)]
    for copy in copies:
        copy.start()
    for copy in copies:
        copy.wait()
    mean = 0.5 * (get_rows(field_ref, N - 1) + roll(get_rows(field_ref, 0), -1, 1))
    set_rows(field_ref, N - 1, mean)
    set_rows(field_ref, 0, roll(mean, 1, 1))
    flat_ref[...] = field_ref[...].T
    shape = (1, N**3)
    lane = lax.broadcasted_iota(jnp.int32, shape, 1)
    points = jnp.zeros(shape, F32)
    for p in range(base_buf.shape[0]):
        for c, ref in enumerate((base_buf, offset_buf, force_buf)):
            for d in range(3):
                value = ref[p : p + 1, d : d + 1].astype(F32)
                points = jnp.where(lane == (p * 9 + c * 3 + d) * N, value, points)
    used = (lane & (N - 1)) == 0
    for d in range(lay.slabs):
        first = lay.slab_at(d) * lay.depth
        for e2 in range(lay.tiles_y):
            rows = flat_ref[pl.ds(e2 * EZ + first, lay.depth), :]
            out_ref[d, pl.ds(e2 * lay.depth, lay.depth), :] = rows
        out_ref[d, 1:2, :] = jnp.where(used, points, out_ref[d, 1:2, :])


def column(values, shape):
    node = lax.broadcasted_iota(jnp.int32, shape, 0)
    out = jnp.full(shape, float(values[0]), F32)
    for n in range(1, N):
        out = jnp.where(node == n, float(values[n]), out)
    return out


def gauss(elem, base, position, half_nodes):
    node = lax.broadcasted_iota(jnp.int32, elem.shape, 0)
    elem = elem.astype(F32)
    away = elem + half_nodes - position
    inside = (
        (elem == base)
        | (elem == base + 1.0)
        | ((elem == base - 1.0) & (node == N - 1))
        | ((elem == base + 2.0) & (node == 0))
    )
    return jnp.where(inside, jnp.exp(-(away * away) / (WIDTH_EPS * WIDTH_EPS)), 0.0)


def point_values(points_ref, row, place, scale):
    base, offset, force = (
        [points_ref[row, (place * 9 + c * 3 + d) * N] for d in range(3)] for c in range(3)
    )
    return base, [b + 1.0 + o for b, o in zip(base, offset)], [scale * f for f in force]


def for_points(points_ref, local_points, visit):
    def row_of(row, _):
        for place in range(local_points):
            visit(row, place)
        return 0

    lax.fori_loop(0, points_ref.shape[0], row_of, 0)


def right_side(lay, local_points, one, points_ref, g_ref, halo_ref):
    derivative, weights = one
    shape = (N, lay.width)
    part_x, part_y, part_z = lane_parts(lay, shape)
    first_z = lay.slab() * lay.depth
    elem_z = first_z + part_z
    elem_halo = jnp.where(part_z == 0, first_z - 1, first_z + lay.depth)
    half_nodes = column(0.5 * (1.0 + GLL_POINTS), shape)
    weight = column(weights, shape)
    columns = [column(derivative[a], shape) for a in range(N)]

    def weighted(elem, base, position):
        plain = weight * gauss(elem, base, position, half_nodes)
        terms = [columns[a] * plain[a : a + 1] for a in range(N)]
        while len(terms) > 1:
            terms = [a + b for a, b in zip(terms[::2], terms[1::2])]
        return plain, terms[0]

    def visit(p, place):
        base, position, force = point_values(points_ref, p, place, 0.25 * GAUSS_NORM)
        first = first_z.astype(F32)

        @pl.when((base[2] + 2.0 >= first - 1.0) & (base[2] - 1.0 <= first + lay.depth))
        def _():
            x0, x1 = weighted(part_x, base[0], position[0])
            y0, y1 = weighted(part_y, base[1], position[1])
            z0, z1 = weighted(elem_z, base[2], position[2])
            h0, h1 = weighted(elem_halo, base[2], position[2])
            pick = part_z[0:1] == 0
            h0 = jnp.where(pick, h0[N - 1 : N], h0[0:1])
            h1 = jnp.where(pick, h1[N - 1 : N], h1[0:1])
            x1 = force[0] * x1
            fz1 = force[2] * z1
            fz0 = force[1] * z0
            for j in range(N):
                first_part = y0[j : j + 1] * z0
                other_part = y1[j : j + 1] * fz0 + y0[j : j + 1] * fz1
                for i in range(N):
                    rows = pl.ds((i * N + j) * N, N)
                    g_ref[rows, :] += x1[i : i + 1] * first_part + x0[i : i + 1] * other_part
            first_part = y0 * h0
            other_part = y1 * (force[1] * h0) + y0 * (force[2] * h1)
            for i in range(N):
                rows = pl.ds(i * N, N)
                halo_ref[rows, :] += x1[i : i + 1] * first_part + x0[i : i + 1] * other_part

    for_points(points_ref, local_points, visit)


def inverse_diagonal(lay, factor, dinv_ref, outer):
    shape = (N, lay.width)
    part_x, part_y, part_z = lane_parts(lay, shape)
    first = lay.slab() * lay.depth
    part_z = jnp.where(part_z == 0, first - 1, first + lay.depth) if outer else first + part_z
    node = lax.broadcasted_iota(jnp.int32, shape, 0)

    def share(low, high):
        return (
            jnp.where(low, 0.0, 0.5),
            jnp.where(high, 0.0, 0.5),
        )

    low_z, high_z = share(part_z == 0, part_z == EZ - 1)
    along_z = jnp.where(node == 0, low_z, jnp.where(node == N - 1, high_z, 1.0))
    if outer:
        along_z = jnp.where((part_z < 0) | (part_z >= EZ), 0.0, along_z)
    along_x = dict(zip((0, N - 1), share(part_x == 0, part_x == lay.num_x - 1)))
    along_y = dict(zip((0, N - 1), share(part_y == 0, part_y == lay.num_y - 1)))
    tables = {}
    for i in range(N // 2):
        for j in range(i + 1):
            tables[i, j] = tables[j, i] = column(factor[i, j], shape) * along_z
    for i in range(N):
        for j in range(N):
            rows = pl.ds((i * N + j) * N, N)
            value = tables[min(i, N - 1 - i), min(j, N - 1 - j)]
            if i in along_x:
                value = value * along_x[i]
            if j in along_y:
                value = value * along_y[j]
            dinv_ref[rows, :] = value


def first_kernel(
    lay,
    local_points,
    derivative,
    one,
    factor,
    recv_ref,
    high_ref,
    low_ref,
    along_ref,
    g_ref,
    x_ref,
    dinv_ref,
    outer_ref,
    face_ref,
    points_ref,
    s_ref,
    halo_ref,
    flat_ref,
    table_ref,
    sem,
):
    count, block = recv_ref.shape[0], recv_ref.shape[1]
    for d in range(count):
        points_ref[pl.ds(d, 1), :] = recv_ref[d, 1:2, : points_ref.shape[1]]
    copy = pltpu.make_async_copy(points_ref, table_ref, sem)
    copy.start()
    for d in range(count):
        flat_ref[pl.ds(d * block, block), :] = recv_ref[d]
    g_ref[...] = flat_ref[...].T
    low, high = get_rows(g_ref, 0), get_rows(g_ref, N - 1)
    _, _, part_z = lane_parts(lay, low.shape)
    set_rows(g_ref, 0, jnp.where(part_z == 0, low, roll(high, 1, 1)))
    halo_ref[...] = jnp.where(part_z == 0, low, high)
    inverse_diagonal(lay, factor, dinv_ref, False)
    inverse_diagonal(lay, factor, outer_ref, True)
    copy.wait()
    right_side(lay, local_points, (derivative, one[1]), table_ref, g_ref, halo_ref)
    assemble(lay, g_ref, s_ref, halo_ref[...])
    x_ref[...] = (1.0 / THETA) * dinv_ref[...] * s_ref[...]
    subtract_stiffness(lay, one, x_ref, g_ref, high_ref, low_ref, along_ref)
    store_faces(lay, g_ref, face_ref)


def vertex_rows(lay, table_ref, values):
    high, low = split(values)
    both = jnp.dot(table_ref[...], jnp.concatenate([high, low], 1), preferred_element_type=F32)
    load = both[:N, : lay.width] + both[:N, lay.width :] + both[N:, : lay.width]
    rows = [load[n : n + 1] for n in range(N)]
    rows = [rows[n] + roll(rows[4 + n], lay.step_x, 1) for n in range(4)]
    return [rows[n] + roll(rows[2 + n], lay.step_y, 1) for n in range(2)]


def face_values(lay, u_ref):
    low, high = get_rows(u_ref, 0), get_rows(u_ref, N - 1)
    _, _, part_z = lane_parts(lay, low.shape)
    return jnp.where(part_z == 0, low, 0.0), jnp.where(part_z == 0, 0.0, high)


def send_loads(lay, own, outer, far, send_ref, token_ref):
    _, _, part_z = lane_parts(lay, own[0].shape)
    bottom = part_z == 0
    before = jnp.where(bottom, 0.0, roll(outer[0], 1, 1))
    here = own[0] + jnp.where(bottom, outer[1], roll(own[1], 1, 1))
    after = jnp.where(bottom, roll(own[1], -1, 1) + roll(outer[0], -1, 1), outer[1])
    second = jnp.zeros_like(here)
    if far is not None:
        before = before + jnp.where(bottom, far[0], roll(far[1], 1, 1))
        after = after + jnp.where(bottom, 0.0, far[0])
        second = jnp.where(bottom, roll(far[1], -1, 1), 0.0)
    rows = jnp.concatenate([before, here, after, second] * 2, 0)
    for d in range(send_ref.shape[0]):
        send_ref[d] = rows
    token_ref[...] = jnp.zeros(token_ref.shape, F32)


OLD = RHO_SECOND * RHO_FIRST
NEW = 2.0 * RHO_SECOND / DELTA


def first_response(
    lay, g_ref, x_ref, dinv_ref, loads_ref, near_ref, send_ref, token_ref, s_ref
):
    assemble(lay, g_ref, s_ref, jnp.zeros((FACE, lay.width), F32))
    update = NEW * dinv_ref[...] * s_ref[...]
    s_ref[...] = update
    total = OLD * x_ref[...] + update
    own = vertex_rows(lay, loads_ref, jnp.concatenate([g_ref[...], total], 0))
    outer = vertex_rows(lay, near_ref, jnp.concatenate(face_values(lay, s_ref), 0))
    send_loads(lay, own, outer, None, send_ref, token_ref)


def pair_response(
    lay,
    one,
    g_ref,
    dinv_ref,
    outer_ref,
    high_ref,
    low_ref,
    along_ref,
    loads_ref,
    near_ref,
    send_ref,
    token_ref,
    s_ref,
    sh_ref,
    u_ref,
    v_ref,
    t_ref,
    h_ref,
):
    tile = (high_ref, low_ref, along_ref)
    assemble(lay, g_ref, s_ref, jnp.zeros((FACE, lay.width), F32))
    u_ref[...] = (1.0 / THETA) * dinv_ref[...] * s_ref[...]
    t_ref[...] = g_ref[...]
    subtract_stiffness(lay, one, u_ref, t_ref, *tile)
    low, high = face_values(lay, u_ref)
    v_ref[...] = jnp.zeros(v_ref.shape, F32)
    set_rows(v_ref, N - 1, low)
    set_rows(v_ref, 0, high)
    h_ref[...] = jnp.zeros(h_ref.shape, F32)
    subtract_stiffness(lay, one, v_ref, h_ref, *tile)
    assemble_both(lay, t_ref, h_ref, s_ref, sh_ref)
    update = OLD * u_ref[...] + NEW * dinv_ref[...] * s_ref[...]
    own = vertex_rows(lay, loads_ref, jnp.concatenate([t_ref[...], update], 0))
    v_ref[...] = OLD * v_ref[...] + NEW * outer_ref[...] * sh_ref[...]
    outer = vertex_rows(lay, loads_ref, jnp.concatenate([h_ref[...], v_ref[...]], 0))
    far = vertex_rows(lay, near_ref, jnp.concatenate(face_values(lay, v_ref), 0))
    send_loads(lay, own, outer, far, send_ref, token_ref)


def second_kernel(
    lay,
    one,
    core_ref,
    chip_ref,
    g_ref,
    x_ref,
    dinv_ref,
    high_ref,
    low_ref,
    along_ref,
    token_ref,
    g_out,
    x_out,
    core_out,
    chip_out,
    s_ref,
    u_ref,
):
    assemble(lay, g_ref, s_ref, halo_of(lay, core_ref, chip_ref))
    update = OLD * x_ref[...] + NEW * dinv_ref[...] * s_ref[...]
    u_ref[...] = update
    x_out[...] = x_ref[...] + update
    g_out[...] = g_ref[...]
    subtract_stiffness(lay, one, u_ref, g_out, high_ref, low_ref, along_ref)
    send_layers(lay, g_out, s_ref, core_out, chip_out)


def solve_coarse(lay, mass, stiff, loads_ref, rows_ref, first_ref, second_ref):
    count = 4
    for s in range(lay.slabs):
        rows_ref[pl.ds(s * count, count), :] = loads_ref[lay.order[s], :count]

    def part(n):
        if lay.width == 128:
            return rows_ref[pl.ds(n, lay.slabs, stride=count), :]
        return jnp.concatenate(
            [rows_ref[pl.ds(s * count + n, 1), :] for s in range(lay.slabs)], 0
        )

    shape = (lay.slabs, lay.width)
    part_x, part_y, part_z = lane_parts(lay, shape)
    row = lax.broadcasted_iota(jnp.int32, shape, 0)
    keep = ((part_x > 0) & (part_y > 0) & ((part_z > 0) | (row > 0))).astype(F32)
    bottom = part_z == 0

    def around_z(v):
        return jnp.where(bottom, roll(v + roll(v, 1, 0), -1, 1), roll(v + roll(v, -1, 0), 1, 1))

    def above(v):
        return jnp.where(bottom, roll(v, -1, 1), roll(roll(v, -1, 0), 1, 1))

    def neighbours(v, step):
        return roll(v, step, 1) + roll(v, -step, 1)

    def mix(pair, v, around):
        return (2.0 * pair[0]) * v + pair[1] * around

    def operate(v):
        around = around_z(v)
        mass_z, stiff_z = mix(mass, v, around), mix(stiff, v, around)
        around = neighbours(mass_z, lay.step_y)
        both = mix(mass, mass_z, around)
        rest = mix(stiff, mass_z, around) + mix(mass, stiff_z, neighbours(stiff_z, lay.step_y))
        out = mix(stiff, both, neighbours(both, lay.step_x)) + mix(
            mass, rest, neighbours(rest, lay.step_x)
        )
        return (0.5 * keep) * out

    def inner(a, b):
        return jnp.sum(jnp.sum(a * b, axis=1, keepdims=True), axis=0, keepdims=True)

    residual = keep * (part(1) + roll(part(0), -1, 0) + roll(part(2), 1, 0) + roll(part(3), 2, 0))
    image = operate(residual)
    total = jnp.zeros(shape, F32)
    for step in range(CG_STEPS):
        last = step + 1 == CG_STEPS
        norm, curv = inner(residual, residual), inner(image, residual)
        if not last:
            second = operate(image)
        if step == 0:
            alpha = norm / curv
            direction, moved = residual, image
            if not last:
                moved_image = second
        else:
            beta = norm / norm_old
            alpha = norm / (curv - beta * norm / alpha)
            direction = residual + beta * direction
            if not last:
                moved, moved_image = image + beta * moved, second + beta * moved_image
        norm_old = norm
        total = total + alpha * direction
        if not last:
            residual, image = residual - alpha * moved, image - alpha * moved_image
    here = pl.ds(N, lay.slabs)
    for ref, value in ((first_ref, total), (second_ref, above(total))):
        ref[...] = jnp.zeros(ref.shape, F32)
        ref[here, :] = value


def corners(lay, low, high):
    rows = [low, high]
    rows = rows + [roll(r, -lay.step_y, 1) for r in rows]
    rows = rows + [roll(r, -lay.step_x, 1) for r in rows]
    corner = lax.broadcasted_iota(jnp.int32, (N, lay.width), 0)
    local = jnp.broadcast_to(rows[0], (N, lay.width))
    for n in range(1, N):
        local = jnp.where(corner == n, rows[n], local)
    return local


def coarse_kernel(
    lay,
    mass,
    stiff,
    loads_ref,
    g_ref,
    x_ref,
    interp_ref,
    image_ref,
    g_out,
    x_out,
    around_ref,
    rows_ref,
    first_ref,
    second_ref,
):
    solve_coarse(lay, mass, stiff, loads_ref, rows_ref, first_ref, second_ref)
    mine = lay.slab() + N
    _, _, part_z = lane_parts(lay, (1, lay.width))
    bottom = part_z == 0
    own, outer, far = [], [], []
    for ref in (first_ref, second_ref):
        before, here, after = (ref[pl.ds(mine + shift, 1), :] for shift in (-1, 0, 1))
        own.append(here)
        outer.append(jnp.where(bottom, roll(before, -1, 1), roll(after, 1, 1)))
        far.append(jnp.where(bottom, before, after))
    local = stacked(corners(lay, *own))
    dot = functools.partial(jnp.dot, preferred_element_type=F32)
    x_out[...] = x_ref[...] + dot(interp_ref[...], local)
    g_out[...] = g_ref[...] - dot(image_ref[...], local)
    around_ref[:N, :] = corners(lay, *outer)
    around_ref[N:, :] = corners(lay, *far)


def correct_layers(lay, around_ref, image_ref, edge_ref, h_ref):
    dot = functools.partial(jnp.dot, preferred_element_type=F32)
    h_ref[...] -= dot(image_ref[...], stacked(around_ref[:N, :]))
    edge = dot(edge_ref[...], stacked(around_ref[N:, :]))
    _, _, part_z = lane_parts(lay, (FACE, lay.width))
    bottom = part_z == 0
    low, high = get_rows(h_ref, 0), get_rows(h_ref, N - 1)
    set_rows(h_ref, 0, low - jnp.where(bottom, edge[FACE:], 0.0))
    set_rows(h_ref, N - 1, high - jnp.where(bottom, 0.0, edge[:FACE]))


def pair_kernel(lay, one, kind, core_ref, chip_ref, g_ref, x_ref, dinv_ref, outer_ref, *refs):
    refs = list(refs)
    high_ref, low_ref, along_ref, edge_high_ref, edge_low_ref = (refs.pop(0) for _ in range(5))
    if kind != "inner":
        around_ref, image_ref, image_edge_ref = (refs.pop(0) for _ in range(3))
    if kind == "inner":
        token_ref, points_ref = refs.pop(0), refs.pop(0)
    if kind == "last":
        token_ref = refs.pop(0)
    if kind == "last":
        out_ref = refs.pop(0)
    else:
        g_out, x_out = refs.pop(0), refs.pop(0)
        core_out, chip_out = refs.pop(0), refs.pop(0)
        if kind == "inner":
            points_out = refs.pop(0)
            points_out[...] = points_ref[...]
    s_ref, sh_ref, h_ref, u_ref = (refs.pop(0) for _ in range(4))
    if kind == "last":
        g_out = refs.pop(0)

    g_out[...] = g_ref[...]
    receive_layers(lay, core_ref, chip_ref, h_ref)
    if kind != "inner":
        correct_layers(lay, around_ref, image_ref, image_edge_ref, h_ref)
    assemble_both(lay, g_out, h_ref, s_ref, sh_ref)
    update = (1.0 / THETA) * dinv_ref[...] * s_ref[...]
    u_ref[...] = update
    outer = (1.0 / THETA) * outer_ref[...] * sh_ref[...]
    edge = times3(edge_high_ref[...], edge_low_ref[...], outer)
    _, _, part_z = lane_parts(lay, (FACE, lay.width))
    near = jnp.where(
        part_z == 0, get_rows(h_ref, N - 1) - edge[FACE:], get_rows(h_ref, 0) - edge[:FACE]
    )
    subtract_stiffness(lay, one, u_ref, g_out, high_ref, low_ref, along_ref)
    assemble(lay, g_out, s_ref, near)
    update = u_ref[...]
    following = OLD * update + NEW * dinv_ref[...] * s_ref[...]
    if kind == "last":
        total = (x_ref[...] + (update + following)).T
        count, block = out_ref.shape[0], out_ref.shape[1]
        for d in range(count):
            out_ref[d] = total[d * block : (d + 1) * block]
        return
    x_out[...] = x_ref[...] + (update + following)
    u_ref[...] = following
    subtract_stiffness(lay, one, u_ref, g_out, high_ref, low_ref, along_ref)
    send_layers(lay, g_out, s_ref, core_out, chip_out)


def unpack_kernel(lay, recv_ref, out_ref, flat_ref):
    for d in range(lay.slabs):
        first = lay.slab_at(d) * lay.depth
        for e2 in range(lay.tiles_y):
            rows = recv_ref[d, pl.ds(e2 * lay.depth, lay.depth), :]
            flat_ref[pl.ds(e2 * EZ + first, lay.depth), :] = rows
    out_ref[...] = flat_ref[...].T


def gauss_at(elem, node, base, position):
    half_nodes = jnp.full(node.shape, 0.5 * (1.0 + GLL_POINTS[0]), F32)
    for n in range(1, N):
        half_nodes = jnp.where(node == n, 0.5 * (1.0 + GLL_POINTS[n]), half_nodes)
    elem = elem.astype(F32)
    away = elem + half_nodes - position
    inside = (
        (elem == base)
        | (elem == base + 1.0)
        | ((elem == base - 1.0) & (node == N - 1))
        | ((elem == base + 2.0) & (node == 0))
    )
    return jnp.where(inside, jnp.exp(-(away * away) / (WIDTH_EPS * WIDTH_EPS)), 0.0)


def forces_kernel(tiles_y, local_points, points_ref, out_ref, done_ref):
    done_ref[...] = jnp.zeros(done_ref.shape, F32)
    count = points_ref.shape[0]
    first_x, first_y = lax.axis_index("ex"), lax.axis_index("ey") * tiles_y
    lane = lax.broadcasted_iota(jnp.int32, (count, 3 * FACE), 1)
    node_x, node_y, part = (lane >> 3) & (N - 1), lane & (N - 1), lane >> 6
    lane_z = lax.broadcasted_iota(jnp.int32, (count, tiles_y * EZ), 1)
    planes, columns = [], []
    for place in range(local_points):

        def value(n):
            at = (place * 9 + n) * N
            return points_ref[:, at : at + 1]

        base = [value(d) for d in range(3)]
        position = [value(d) + 1.0 + value(3 + d) for d in range(3)]
        force = jnp.where(part == 0, value(6), jnp.where(part == 1, value(7), value(8)))
        x = gauss_at(jnp.broadcast_to(first_x, lane.shape), node_x, base[0], position[0])
        scaled = GAUSS_NORM * force * x
        for e2 in range(tiles_y):
            y = gauss_at(jnp.broadcast_to(first_y + e2, lane.shape), node_y, base[1], position[1])
            planes.append(scaled * y)
            columns.append((e2, base[2], position[2]))
    high, low = split(jnp.concatenate(planes, 0))
    plane = jnp.concatenate([high, high, low], 0)
    elem_z, row_z = lane_z & (EZ - 1), lane_z >> log2(EZ)
    for k in range(N):
        node = jnp.full(lane_z.shape, k, jnp.int32)
        along = [
            jnp.where(row_z == e2, gauss_at(elem_z, node, base, position), 0.0)
            for e2, base, position in columns
        ]
        high, low = split(jnp.concatenate(along, 0))
        out_ref[pl.ds(k, 3 * FACE, stride=N), :] = lax.dot_general(
            plane,
            jnp.concatenate([high, low, high], 0),
            (((0,), (0,)), ((), ())),
            preferred_element_type=F32,
        )


def call(kernel, outs, inputs, scratch=(), smem=0, spaces=None, limit=40):
    spaces = spaces or [pltpu.SMEM] * smem + [pltpu.VMEM] * (len(inputs) - smem)
    specs = [pl.BlockSpec(memory_space=space) for space in spaces]
    shapes = [jax.ShapeDtypeStruct(s, F32) for s in outs]
    result = pl.pallas_call(
        kernel,
        out_shape=shapes,
        in_specs=specs,
        out_specs=[pl.BlockSpec(memory_space=pltpu.VMEM)] * len(shapes),
        scratch_shapes=[pltpu.VMEM(s, F32) if isinstance(s, tuple) else s for s in scratch],
        compiler_params=pltpu.CompilerParams(vmem_limit_bytes=limit * 1024 * 1024),
    )(*inputs)
    return result


def shards(source, point_base, point_offset, point_force):
    tiles_x, tiles_y = source.shape[3], source.shape[4] // EZ
    lay = Layout(lax.axis_size("ex"), lax.axis_size("ey"), tiles_x, tiles_y)
    devices = lay.mesh_x * lay.mesh_y
    derivative, weights, interp, stiff_one = build_tables()
    width, fields = lay.width, (N**3, lay.width)

    diag_w = np.diag(weights)
    full = 0.5 * (
        kron3(stiff_one, diag_w, diag_w)
        + kron3(diag_w, stiff_one, diag_w)
        + kron3(diag_w, diag_w, stiff_one)
    )
    edge_rows = np.concatenate([np.arange(FACE) * N, np.arange(FACE) * N + N - 1])
    plane = 0.5 * (np.kron(stiff_one, diag_w) + np.kron(diag_w, stiff_one))
    high, low = (jnp.asarray(t) for t in split_table(np.kron(np.eye(N // 2), plane)))
    along = np.broadcast_to(0.5 * np.kron(weights, weights)[:, None], (FACE, width))
    along = jnp.asarray(along, F32)
    edge_high, edge_low = (jnp.asarray(t) for t in split_table(full[edge_rows]))
    one = (stiff_one, weights)
    interp3 = kron3(interp, interp, interp)
    image3 = full @ interp3
    ratio = (weights[:, None] * derivative**2).sum(axis=0) / weights
    diag = 0.5 * (ratio[:, None, None] + ratio[None, :, None] + ratio[None, None, :])
    diag = diag * weights[:, None, None] * weights[None, :, None] * weights[None, None, :]
    factor = 1.0 / diag
    mass = interp.T @ diag_w @ interp
    stiff = interp.T @ stiff_one @ interp
    moved = -interp3.T @ full
    loads_table, near_table = (
        jnp.asarray(np.concatenate(split_table(t), 0))
        for t in (
            np.concatenate([interp3.T, moved], 1),
            np.concatenate([moved[:, edge_rows[FACE:]], moved[:, edge_rows[:FACE]]], 1),
        )
    )
    prolong3, image3, image_edge = (
        jnp.asarray(stacked_table(t)) for t in (interp3, image3, image3[edge_rows])
    )

    local_points = point_base.shape[1]
    block = lay.block
    (send,) = call(
        functools.partial(pack_kernel, lay),
        [(lay.slabs, block, N**3)],
        [
            pltpu.with_memory_space_constraint(t, pltpu.HBM)
            for t in (
                point_base.T,
                point_offset.T,
                point_force.T,
                source.reshape(N**3, tiles_y * EZ),
            )
        ],
        [
            pltpu.VMEM((local_points, 3), jnp.int32),
            (local_points, 3),
            (local_points, 3),
            (N**3, tiles_y * EZ),
            (tiles_y * EZ, N**3),
            pltpu.SemaphoreType.DMA((4,)),
        ],
        spaces=[pltpu.HBM] * 4,
    )
    recv = lax.all_to_all(send, lay.axis, 0, 0)
    if not lay.joint:
        recv = lax.all_gather(recv, "ex", axis=0, tiled=True)

    def swap(core, chip):
        return (
            lax.ppermute(core, lay.axis, lay.swaps(0)),
            lax.ppermute(chip, lay.axis, lay.swaps(1)),
        )

    def gather(loads):
        return lax.all_to_all(loads, lay.axis, 0, 0)

    face_shape = (FACE, width)
    layer = (N**3 // 2, width)
    loads_shape = (lay.slabs, N, width)
    table = (devices, -(-9 * N * local_points // 128) * 128)
    g, x, dinv, outer, face, points = call(
        functools.partial(first_kernel, lay, local_points, derivative, one, factor),
        [fields, fields, fields, fields, (256, width), table],
        [recv, high, low, along],
        [fields, face_shape, (width, N**3), pltpu.SMEM(table, F32), pltpu.SemaphoreType.DMA],
    )
    faces = swap(face, face)
    loads, token = call(
        functools.partial(first_response, lay),
        [loads_shape, (N, 128)],
        [g, x, dinv, loads_table, near_table],
        [fields],
    )
    loads = gather(loads)
    g, x, core, chip = call(
        functools.partial(second_kernel, lay, one),
        [fields, fields, layer, layer],
        [*faces, g, x, dinv, high, low, along, token],
        [fields, fields],
    )
    coarse = ((mass[0, 0], mass[0, 1]), (stiff[0, 0], stiff[0, 1]))
    stiffness = [high, low, along, edge_high, edge_low]

    for cycle in range(CYCLES):
        core, chip = swap(core, chip)
        last = cycle + 1 == CYCLES
        outs = [fields, fields, layer, layer]
        extra = [done] if last else []
        scratch = [fields] * 4
        if last:
            outs = [(lay.mesh_x * lay.mesh_y, block, N**3)]
            scratch += [fields]
        g, x, around = call(
            functools.partial(coarse_kernel, lay, *coarse),
            [fields, fields, (2 * N, width)],
            [loads, g, x, prolong3, image3],
            [(lay.slabs * 4, width)] + [(lay.slabs + 2 * N, width)] * 2,
        )
        outs = call(
            functools.partial(pair_kernel, lay, one, "last" if last else "plain"),
            outs,
            [core, chip, g, x, dinv, outer, *stiffness, around, image3, image_edge, *extra],
            scratch,
        )
        if last:
            break
        g, x, core, chip = outs
        layers = swap(core, chip)
        loads, token = call(
            functools.partial(pair_response, lay, one),
            [loads_shape, (N, 128)],
            [g, dinv, outer, high, low, along, loads_table, near_table],
            [fields] * 6,
        )
        loads = gather(loads)
        g, x, core, chip, points = call(
            functools.partial(pair_kernel, lay, one, "inner"),
            [fields, fields, layer, layer, table],
            [*layers, g, x, dinv, outer, *stiffness, token, points],
            [fields] * 4,
        )
        forces, done = call(
            functools.partial(forces_kernel, tiles_y, local_points),
            [(3 * N**3, tiles_y * EZ), (N, 128)],
            [points],
        )
    (out,) = outs
    if not lay.joint:
        out = lax.dynamic_slice_in_dim(out, lax.axis_index("ex") * lay.mesh_y, lay.mesh_y, 0)
    out = lax.all_to_all(out, lay.axis, 0, 0)
    (pressure,) = call(
        functools.partial(unpack_kernel, lay),
        [(N**3, tiles_y * EZ)],
        [out],
        [(lay.slabs * block, N**3)],
    )
    return (
        pressure.reshape(source.shape),
        forces.reshape((3, *source.shape)),
    )


def solution(mesh):
    in_specs = (
        P(None, None, None, "ex", "ey"),
        P(None, ("ex", "ey")),
        P(None, ("ex", "ey")),
        P(None, ("ex", "ey")),
    )
    out_specs = (P(None, None, None, "ex", "ey"), P(None, None, None, None, "ex", "ey"))
    return jax.shard_map(shards, mesh=mesh, in_specs=in_specs, out_specs=out_specs, check_vma=False)
```

```python
import functools
import math

import jax
import jax.numpy as jnp
import numpy as np
from jax import lax
from jax.experimental import pallas as pl
from jax.experimental.pallas import tpu as pltpu
from jax.sharding import PartitionSpec as P

EZ = 64
CG_STEPS = 4
CYCLES = 2
N = 8
GLL_POINTS = np.array(
    [
        -1.0,
        -0.8717401485096066,
        -0.5917001814331423,
        -0.2092992179024789,
        0.2092992179024789,
        0.5917001814331423,
        0.8717401485096066,
        1.0,
    ]
)
WIDTH_EPS = 0.35
GAUSS_NORM = 1.0 / (math.pi**1.5 * WIDTH_EPS**3)
CHEB_LOW = 1.5
CHEB_HIGH = 12.0
THETA = 0.5 * (CHEB_HIGH + CHEB_LOW)
DELTA = 0.5 * (CHEB_HIGH - CHEB_LOW)
RHO_FIRST = DELTA / THETA
RHO_SECOND = 1.0 / (2.0 * THETA / DELTA - RHO_FIRST)
F32 = jnp.float32
BF16 = jnp.bfloat16
FACE = N * N


def build_tables():
    points = GLL_POINTS
    degree = len(points) - 1
    previous = points * 0.0 + 1.0
    current = points.copy()
    for k in range(1, degree):
        following = ((2 * k + 1) * points * current - k * previous) / (k + 1)
        previous = current
        current = following
    derivative = np.zeros((degree + 1, degree + 1))
    for i in range(degree + 1):
        for j in range(degree + 1):
            if i != j:
                derivative[i, j] = current[i] / (current[j] * (points[i] - points[j]))
    derivative[0, 0] = -degree * (degree + 1) / 4.0
    derivative[degree, degree] = degree * (degree + 1) / 4.0
    weights = 2.0 / (degree * (degree + 1) * current**2)
    interp = np.stack([(1.0 - points) / 2.0, (1.0 + points) / 2.0], axis=1)
    stiff_one = derivative.T @ (weights[:, None] * derivative)
    return derivative, weights, interp, stiff_one


def kron3(a, b, c):
    return np.kron(np.kron(a, b), c)


def log2(n):
    return int(n).bit_length() - 1


class Layout:
    def __init__(self, mesh_x, mesh_y, tiles_x, tiles_y):
        self.mesh_x, self.mesh_y = mesh_x, mesh_y
        self.num_x, self.num_y = tiles_x * mesh_x, tiles_y * mesh_y
        self.tiles_y = tiles_y
        self.joint = EZ % (2 * mesh_x * mesh_y) == 0
        self.axis = ("ex", "ey") if self.joint else "ey"
        self.slabs = mesh_x * mesh_y if self.joint else mesh_y
        self.depth = EZ // self.slabs
        assert self.depth == 2 and tiles_x == 1
        self.width = self.num_x * self.num_y * self.depth
        self.step_y = self.depth
        self.step_x = self.depth * self.num_y
        self.block = tiles_y * self.depth
        slab_of = [self.slab_at(d) for d in range(self.slabs)]
        self.order = [slab_of.index(s) for s in range(self.slabs)]

    def slab_at(self, d):
        if self.joint and self.mesh_x % 2 == 0 and self.mesh_y % 2 == 0:
            high = self.mesh_y // 2
            y = d & 1
            z = (d >> 1) & (high - 1)
            core = (d >> log2(self.mesh_y)) & 1
            x = d >> (log2(self.mesh_y) + 1)
            turn = y ^ (x & 1)
            return ((x * 2 + turn) * high + (z ^ (turn * (high - 1)))) * 2 + core
        if not self.joint and self.mesh_y % 8 == 0:
            return d ^ (((d >> 3) & 1) * 7)
        return d

    def slab(self):
        d = lax.axis_index("ey")
        return self.slab_at(lax.axis_index("ex") * self.mesh_y + d if self.joint else d)

    def swaps(self, first):
        pairs = []
        for s in range(first, self.slabs, 2):
            a, b = self.order[s], self.order[(s + 1) % self.slabs]
            pairs += [(a, b), (b, a)]
        return pairs


def split(x):
    high = x.astype(BF16)
    return high, (x - high.astype(F32)).astype(BF16)


def times3(high, low, x):
    xh, xl = split(x)
    dot = functools.partial(jnp.dot, preferred_element_type=F32)
    return dot(high, xh) + dot(high, xl) + dot(low, xh)


def split_table(x):
    high = x.astype(BF16)
    return high, (x - high.astype(np.float64)).astype(BF16)


def stacked_table(x):
    high, low = split_table(x)
    return np.concatenate([high, high, low, low], 1)


def stacked(x):
    high = x.astype(BF16).astype(F32)
    low = x - high
    return jnp.concatenate([high, low, high, low], 0).astype(BF16)


def subtract_stiffness(lay, one, u_ref, g_ref, high_ref, low_ref, along_ref):
    matrix, weights = one
    dot = functools.partial(jnp.dot, preferred_element_type=F32)
    half = N // 2
    for first in (0, half):
        scaled = [
            float(weights[i]) * u_ref[pl.ds(i * FACE, FACE), :] for i in range(first, first + half)
        ]
        xh, xl = split(jnp.concatenate(scaled, 0))
        both = dot(high_ref[...], jnp.concatenate([xh, xl], 1))
        rows = pl.ds(first * FACE, half * FACE)
        g_ref[rows, :] -= both[:, : lay.width] + both[:, lay.width :] + dot(low_ref[...], xh)
    even = 0.5 * (matrix[:half, :half] + matrix[:half, :half - 1 : -1])
    odd = 0.5 * (matrix[:half, :half] - matrix[:half, :half - 1 : -1])
    for j in range(N):
        values = [u_ref[pl.ds((i * N + j) * N, N), :] for i in range(N)]
        sums = [values[i] + values[N - 1 - i] for i in range(half)]
        gaps = [values[i] - values[N - 1 - i] for i in range(half)]
        along = along_ref[pl.ds(j * N, N), :]
        for i in range(half):
            a = sum(float(even[i, q]) * sums[q] for q in range(half))
            b = sum(float(odd[i, q]) * gaps[q] for q in range(half))
            g_ref[pl.ds((i * N + j) * N, N), :] -= along * (a + b)
            g_ref[pl.ds(((N - 1 - i) * N + j) * N, N), :] -= along * (a - b)


def roll(x, shift, axis):
    size = x.shape[axis]
    return pltpu.roll(x, shift % size, axis)


def lane_parts(lay, shape):
    lane = lax.broadcasted_iota(jnp.int32, shape, len(shape) - 1)
    part_z = lane & (lay.depth - 1)
    part_y = lax.shift_right_logical(lane, log2(lay.step_y)) & (lay.num_y - 1)
    part_x = lax.shift_right_logical(lane, log2(lay.step_x))
    return part_x, part_y, part_z


def get_rows(ref, k):
    if ref.shape[1] == 128:
        return ref[pl.ds(k, FACE, stride=N), :]
    return jnp.concatenate([ref[pl.ds(n * N + k, 1), :] for n in range(FACE)], 0)


def set_rows(ref, k, value):
    if ref.shape[1] == 128:
        ref[pl.ds(k, FACE, stride=N), :] = value
    else:
        for n in range(FACE):
            ref[pl.ds(n * N + k, 1), :] = value[n : n + 1]


def assemble_xy(lay, s_ref):
    last = N - 1
    for j in range(N):
        a, b = pl.ds(j * N, N), pl.ds((last * N + j) * N, N)
        low, high = s_ref[a, :], s_ref[b, :]
        s_ref[a, :] = low + roll(high, lay.step_x, 1)
        s_ref[b, :] = high + roll(low, -lay.step_x, 1)
    for i in range(N):
        a, b = pl.ds(i * N * N, N), pl.ds((i * N + last) * N, N)
        low, high = s_ref[a, :], s_ref[b, :]
        s_ref[a, :] = low + roll(high, lay.step_y, 1)
        s_ref[b, :] = high + roll(low, -lay.step_y, 1)


def assemble(lay, g_ref, s_ref, halo):
    _, _, part_z = lane_parts(lay, halo.shape)
    s_ref[...] = g_ref[...]
    low = get_rows(g_ref, 0)
    high = get_rows(g_ref, N - 1)
    set_rows(s_ref, 0, low + jnp.where(part_z == 0, halo, roll(high, 1, 1)))
    set_rows(s_ref, N - 1, high + jnp.where(part_z == lay.depth - 1, halo, roll(low, -1, 1)))
    assemble_xy(lay, s_ref)


def store_faces(lay, g_ref, face_ref):
    low = get_rows(g_ref, 0)
    high = get_rows(g_ref, N - 1)
    _, _, part_z = lane_parts(lay, low.shape)
    face_ref[...] = jnp.zeros(face_ref.shape, F32)
    face_ref[:FACE, :] = jnp.where(part_z == 0, low, high)


def halo_of(lay, core_ref, chip_ref):
    odd = (lay.slab() & 1) == 1
    core, chip = core_ref[:FACE, :], chip_ref[:FACE, :]
    below = jnp.where(odd, core, chip)
    above = jnp.where(odd, chip, core)
    _, _, part_z = lane_parts(lay, core.shape)
    return jnp.where(part_z == 0, roll(below, 1 - lay.depth, 1), roll(above, lay.depth - 1, 1))


def assemble_both(lay, g_ref, h_ref, s_ref, sh_ref):
    low, high = get_rows(g_ref, 0), get_rows(g_ref, N - 1)
    out_low, out_high = get_rows(h_ref, 0), get_rows(h_ref, N - 1)
    _, _, part_z = lane_parts(lay, low.shape)
    bottom = part_z == 0
    s_ref[...] = g_ref[...]
    sh_ref[...] = h_ref[...]
    set_rows(s_ref, 0, low + jnp.where(bottom, out_high, roll(high, 1, 1)))
    set_rows(s_ref, N - 1, high + jnp.where(bottom, roll(low, -1, 1), out_low))
    set_rows(sh_ref, N - 1, out_high + jnp.where(bottom, low, 0.0))
    set_rows(sh_ref, 0, out_low + jnp.where(bottom, 0.0, high))
    assemble_xy(lay, s_ref)
    assemble_xy(lay, sh_ref)


def send_layers(lay, g_ref, s_ref, core_ref, chip_ref):
    low, high = get_rows(g_ref, 0), get_rows(g_ref, N - 1)
    _, _, part_z = lane_parts(lay, low.shape)
    s_ref[...] = g_ref[...]
    set_rows(s_ref, N - 1, jnp.where(part_z == 0, high + roll(low, -1, 1), high))
    set_rows(s_ref, 0, jnp.where(part_z == 0, low, low + roll(high, 1, 1)))
    half = N**3 // 2
    a, b = s_ref[:half, :], s_ref[half:, :]
    _, _, part_z = lane_parts(lay, a.shape)
    bottom = part_z == 0
    first = jnp.where(bottom, a, roll(b, 1, 1))
    second = jnp.where(bottom, roll(a, -1, 1), b)
    odd = (lay.slab() & 1) == 1
    core_ref[...] = jnp.where(odd, first, second)
    chip_ref[...] = jnp.where(odd, second, first)


def receive_layers(lay, core_ref, chip_ref, h_ref):
    odd = (lay.slab() & 1) == 1
    core, chip = core_ref[...], chip_ref[...]
    below, above = jnp.where(odd, core, chip), jnp.where(odd, chip, core)
    _, _, part_z = lane_parts(lay, core.shape)
    bottom = part_z == 0
    half = N**3 // 2
    h_ref[:half, :] = jnp.where(bottom, below, roll(above, 1, 1))
    h_ref[half:, :] = jnp.where(bottom, roll(below, -1, 1), above)


def pack_kernel(
    lay,
    base_ref,
    offset_ref,
    force_ref,
    source_ref,
    out_ref,
    base_buf,
    offset_buf,
    force_buf,
    field_ref,
    flat_ref,
    sems,
):
    pairs = (
        (source_ref, field_ref),
        (base_ref, base_buf),
        (offset_ref, offset_buf),
        (force_ref, force_buf),
    )
    copies = [pltpu.make_async_copy(a, b, sems.at[n]) for n, (a, b) in enumerate(pairs)]
    for copy in copies:
        copy.start()
    for copy in copies:
        copy.wait()
    mean = 0.5 * (get_rows(field_ref, N - 1) + roll(get_rows(field_ref, 0), -1, 1))
    set_rows(field_ref, N - 1, mean)
    set_rows(field_ref, 0, roll(mean, 1, 1))
    flat_ref[...] = field_ref[...].T
    shape = (1, N**3)
    lane = lax.broadcasted_iota(jnp.int32, shape, 1)
    points = jnp.zeros(shape, F32)
    for p in range(base_buf.shape[0]):
        for c, ref in enumerate((base_buf, offset_buf, force_buf)):
            for d in range(3):
                value = ref[p : p + 1, d : d + 1].astype(F32)
                points = jnp.where(lane == (p * 9 + c * 3 + d) * N, value, points)
    used = (lane & (N - 1)) == 0
    for d in range(lay.slabs):
        first = lay.slab_at(d) * lay.depth
        for e2 in range(lay.tiles_y):
            rows = flat_ref[pl.ds(e2 * EZ + first, lay.depth), :]
            out_ref[d, pl.ds(e2 * lay.depth, lay.depth), :] = rows
        out_ref[d, 1:2, :] = jnp.where(used, points, out_ref[d, 1:2, :])


def column(values, shape):
    node = lax.broadcasted_iota(jnp.int32, shape, 0)
    out = jnp.full(shape, float(values[0]), F32)
    for n in range(1, N):
        out = jnp.where(node == n, float(values[n]), out)
    return out


def gauss(elem, base, position, half_nodes):
    node = lax.broadcasted_iota(jnp.int32, elem.shape, 0)
    elem = elem.astype(F32)
    away = elem + half_nodes - position
    inside = (
        (elem == base)
        | (elem == base + 1.0)
        | ((elem == base - 1.0) & (node == N - 1))
        | ((elem == base + 2.0) & (node == 0))
    )
    return jnp.where(inside, jnp.exp(-(away * away) / (WIDTH_EPS * WIDTH_EPS)), 0.0)


def point_values(points_ref, row, place, scale):
    base, offset, force = (
        [points_ref[row, (place * 9 + c * 3 + d) * N] for d in range(3)] for c in range(3)
    )
    return base, [b + 1.0 + o for b, o in zip(base, offset)], [scale * f for f in force]


def right_side(lay, local_points, one, points_ref, list_ref, g_ref, halo_ref):
    derivative, weights = one
    shape = (N, lay.width)
    part_x, part_y, part_z = lane_parts(lay, shape)
    first_z = lay.slab() * lay.depth
    elem_z = first_z + part_z
    elem_halo = jnp.where(part_z == 0, first_z - 1, first_z + lay.depth)
    half_nodes = column(0.5 * (1.0 + GLL_POINTS), shape)
    weight = column(weights, shape)
    columns = [column(derivative[a], shape) for a in range(N)]

    def weighted(elem, base, position):
        plain = weight * gauss(elem, base, position, half_nodes)
        terms = [columns[a] * plain[a : a + 1] for a in range(N)]
        while len(terms) > 1:
            terms = [a + b for a, b in zip(terms[::2], terms[1::2])]
        return plain, terms[0]

    def place_of(p):
        return (p, 0) if local_points == 1 else (lax.div(p, local_points), lax.rem(p, local_points))

    first = first_z.astype(F32)

    def collect(p, found):
        row, place = place_of(p)
        base = points_ref[row, (place * 9 + 2) * N]
        list_ref[found] = p
        reached = (base + 2.0 >= first - 1.0) & (base - 1.0 <= first + lay.depth)
        return found + jnp.where(reached, 1, 0)

    found = lax.fori_loop(0, points_ref.shape[0] * local_points, collect, jnp.int32(0))
    pick = part_z[0:1] == 0

    def factors(n):
        row, place = place_of(list_ref[jnp.minimum(n, found - 1)])
        base, position, force = point_values(
            points_ref, row, place, jnp.where(n < found, 0.25 * GAUSS_NORM, 0.0)
        )
        x0, x1 = weighted(part_x, base[0], position[0])
        y0, y1 = weighted(part_y, base[1], position[1])
        z0, z1 = weighted(elem_z, base[2], position[2])
        h0, h1 = weighted(elem_halo, base[2], position[2])
        h0 = jnp.where(pick, h0[N - 1 : N], h0[0:1])
        h1 = jnp.where(pick, h1[N - 1 : N], h1[0:1])
        planes = []
        for j in range(N):
            row0, row1 = y0[j : j + 1], y1[j : j + 1]
            planes.append((row0 * z0, row1 * (force[1] * z0) + row0 * (force[2] * z1)))
        planes.append((y0 * h0, y1 * (force[1] * h0) + y0 * (force[2] * h1)))
        return force[0] * x1, x0, planes

    def two(t, _):
        points = [factors(2 * t), factors(2 * t + 1)]

        def term(i, j):
            parts = [
                x1[i : i + 1] * planes[j][0] + x0[i : i + 1] * planes[j][1] for x1, x0, planes in points
            ]
            return parts[0] + parts[1]

        for i in range(N):
            for j in range(N):
                g_ref[pl.ds((i * N + j) * N, N), :] += term(i, j)
            halo_ref[pl.ds(i * N, N), :] += term(i, N)
        return 0

    lax.fori_loop(0, lax.div(found + 1, 2), two, 0)


def inverse_diagonal(lay, factor, dinv_ref, outer):
    shape = (N, lay.width)
    part_x, part_y, part_z = lane_parts(lay, shape)
    first = lay.slab() * lay.depth
    part_z = jnp.where(part_z == 0, first - 1, first + lay.depth) if outer else first + part_z
    node = lax.broadcasted_iota(jnp.int32, shape, 0)

    def share(low, high):
        return (
            jnp.where(low, 0.0, 0.5),
            jnp.where(high, 0.0, 0.5),
        )

    low_z, high_z = share(part_z == 0, part_z == EZ - 1)
    along_z = jnp.where(node == 0, low_z, jnp.where(node == N - 1, high_z, 1.0))
    if outer:
        along_z = jnp.where((part_z < 0) | (part_z >= EZ), 0.0, along_z)
    along_x = dict(zip((0, N - 1), share(part_x == 0, part_x == lay.num_x - 1)))
    along_y = dict(zip((0, N - 1), share(part_y == 0, part_y == lay.num_y - 1)))
    tables = {}
    for i in range(N // 2):
        for j in range(i + 1):
            tables[i, j] = tables[j, i] = column(factor[i, j], shape) * along_z
    for i in range(N):
        for j in range(N):
            rows = pl.ds((i * N + j) * N, N)
            value = tables[min(i, N - 1 - i), min(j, N - 1 - j)]
            if i in along_x:
                value = value * along_x[i]
            if j in along_y:
                value = value * along_y[j]
            dinv_ref[rows, :] = value


def first_kernel(
    lay,
    local_points,
    derivative,
    one,
    factor,
    recv_ref,
    high_ref,
    low_ref,
    along_ref,
    g_ref,
    x_ref,
    dinv_ref,
    outer_ref,
    face_ref,
    points_ref,
    s_ref,
    halo_ref,
    flat_ref,
    table_ref,
    list_ref,
    sem,
):
    count, block = recv_ref.shape[0], recv_ref.shape[1]
    for d in range(count):
        points_ref[pl.ds(d, 1), :] = recv_ref[d, 1:2, : points_ref.shape[1]]
    copy = pltpu.make_async_copy(points_ref, table_ref, sem)
    copy.start()
    for d in range(count):
        flat_ref[pl.ds(d * block, block), :] = recv_ref[d]
    g_ref[...] = flat_ref[...].T
    low, high = get_rows(g_ref, 0), get_rows(g_ref, N - 1)
    _, _, part_z = lane_parts(lay, low.shape)
    set_rows(g_ref, 0, jnp.where(part_z == 0, low, roll(high, 1, 1)))
    halo_ref[...] = jnp.where(part_z == 0, low, high)
    inverse_diagonal(lay, factor, dinv_ref, False)
    inverse_diagonal(lay, factor, outer_ref, True)
    copy.wait()
    right_side(lay, local_points, (derivative, one[1]), table_ref, list_ref, g_ref, halo_ref)
    assemble(lay, g_ref, s_ref, halo_ref[...])
    x_ref[...] = (1.0 / THETA) * dinv_ref[...] * s_ref[...]
    subtract_stiffness(lay, one, x_ref, g_ref, high_ref, low_ref, along_ref)
    store_faces(lay, g_ref, face_ref)


def vertex_rows(lay, table_ref, values):
    high, low = split(values)
    both = jnp.dot(table_ref[...], jnp.concatenate([high, low], 1), preferred_element_type=F32)
    load = both[:N, : lay.width] + both[:N, lay.width :] + both[N:, : lay.width]
    rows = [load[n : n + 1] for n in range(N)]
    rows = [rows[n] + roll(rows[4 + n], lay.step_x, 1) for n in range(4)]
    return [rows[n] + roll(rows[2 + n], lay.step_y, 1) for n in range(2)]


def face_values(lay, u_ref):
    low, high = get_rows(u_ref, 0), get_rows(u_ref, N - 1)
    _, _, part_z = lane_parts(lay, low.shape)
    return jnp.where(part_z == 0, low, 0.0), jnp.where(part_z == 0, 0.0, high)


def send_loads(lay, own, outer, far, send_ref, token_ref):
    _, _, part_z = lane_parts(lay, own[0].shape)
    bottom = part_z == 0
    before = jnp.where(bottom, 0.0, roll(outer[0], 1, 1))
    here = own[0] + jnp.where(bottom, outer[1], roll(own[1], 1, 1))
    after = jnp.where(bottom, roll(own[1], -1, 1) + roll(outer[0], -1, 1), outer[1])
    second = jnp.zeros_like(here)
    if far is not None:
        before = before + jnp.where(bottom, far[0], roll(far[1], 1, 1))
        after = after + jnp.where(bottom, 0.0, far[0])
        second = jnp.where(bottom, roll(far[1], -1, 1), 0.0)
    rows = jnp.concatenate([before, here, after, second] * 2, 0)
    for d in range(send_ref.shape[0]):
        send_ref[d] = rows
    token_ref[...] = jnp.zeros(token_ref.shape, F32)


OLD = RHO_SECOND * RHO_FIRST
NEW = 2.0 * RHO_SECOND / DELTA


def first_response(
    lay, g_ref, x_ref, dinv_ref, loads_ref, near_ref, send_ref, token_ref, s_ref
):
    assemble(lay, g_ref, s_ref, jnp.zeros((FACE, lay.width), F32))
    update = NEW * dinv_ref[...] * s_ref[...]
    s_ref[...] = update
    total = OLD * x_ref[...] + update
    own = vertex_rows(lay, loads_ref, jnp.concatenate([g_ref[...], total], 0))
    outer = vertex_rows(lay, near_ref, jnp.concatenate(face_values(lay, s_ref), 0))
    send_loads(lay, own, outer, None, send_ref, token_ref)


def pair_response(
    lay,
    one,
    g_ref,
    dinv_ref,
    outer_ref,
    high_ref,
    low_ref,
    along_ref,
    loads_ref,
    near_ref,
    send_ref,
    token_ref,
    s_ref,
    sh_ref,
    u_ref,
    v_ref,
    t_ref,
    h_ref,
):
    tile = (high_ref, low_ref, along_ref)
    assemble(lay, g_ref, s_ref, jnp.zeros((FACE, lay.width), F32))
    u_ref[...] = (1.0 / THETA) * dinv_ref[...] * s_ref[...]
    t_ref[...] = g_ref[...]
    subtract_stiffness(lay, one, u_ref, t_ref, *tile)
    low, high = face_values(lay, u_ref)
    v_ref[...] = jnp.zeros(v_ref.shape, F32)
    set_rows(v_ref, N - 1, low)
    set_rows(v_ref, 0, high)
    h_ref[...] = jnp.zeros(h_ref.shape, F32)
    subtract_stiffness(lay, one, v_ref, h_ref, *tile)
    assemble_both(lay, t_ref, h_ref, s_ref, sh_ref)
    update = OLD * u_ref[...] + NEW * dinv_ref[...] * s_ref[...]
    own = vertex_rows(lay, loads_ref, jnp.concatenate([t_ref[...], update], 0))
    v_ref[...] = OLD * v_ref[...] + NEW * outer_ref[...] * sh_ref[...]
    outer = vertex_rows(lay, loads_ref, jnp.concatenate([h_ref[...], v_ref[...]], 0))
    far = vertex_rows(lay, near_ref, jnp.concatenate(face_values(lay, v_ref), 0))
    send_loads(lay, own, outer, far, send_ref, token_ref)


def second_kernel(
    lay,
    one,
    core_ref,
    chip_ref,
    g_ref,
    x_ref,
    dinv_ref,
    high_ref,
    low_ref,
    along_ref,
    token_ref,
    g_out,
    x_out,
    core_out,
    chip_out,
    s_ref,
    u_ref,
):
    assemble(lay, g_ref, s_ref, halo_of(lay, core_ref, chip_ref))
    update = OLD * x_ref[...] + NEW * dinv_ref[...] * s_ref[...]
    u_ref[...] = update
    x_out[...] = x_ref[...] + update
    g_out[...] = g_ref[...]
    subtract_stiffness(lay, one, u_ref, g_out, high_ref, low_ref, along_ref)
    send_layers(lay, g_out, s_ref, core_out, chip_out)


def solve_coarse(lay, mass, stiff, loads_ref, rows_ref, first_ref, second_ref):
    count = 4
    for s in range(lay.slabs):
        rows_ref[pl.ds(s * count, count), :] = loads_ref[lay.order[s], :count]

    def part(n):
        if lay.width == 128:
            return rows_ref[pl.ds(n, lay.slabs, stride=count), :]
        return jnp.concatenate(
            [rows_ref[pl.ds(s * count + n, 1), :] for s in range(lay.slabs)], 0
        )

    shape = (lay.slabs, lay.width)
    part_x, part_y, part_z = lane_parts(lay, shape)
    row = lax.broadcasted_iota(jnp.int32, shape, 0)
    keep = ((part_x > 0) & (part_y > 0) & ((part_z > 0) | (row > 0))).astype(F32)
    bottom = part_z == 0

    def around_z(v):
        return jnp.where(bottom, roll(v + roll(v, 1, 0), -1, 1), roll(v + roll(v, -1, 0), 1, 1))

    def above(v):
        return jnp.where(bottom, roll(v, -1, 1), roll(roll(v, -1, 0), 1, 1))

    def neighbours(v, step):
        return roll(v, step, 1) + roll(v, -step, 1)

    def mix(pair, v, around):
        return (2.0 * pair[0]) * v + pair[1] * around

    def operate(v):
        around = around_z(v)
        mass_z, stiff_z = mix(mass, v, around), mix(stiff, v, around)
        around = neighbours(mass_z, lay.step_y)
        both = mix(mass, mass_z, around)
        rest = mix(stiff, mass_z, around) + mix(mass, stiff_z, neighbours(stiff_z, lay.step_y))
        out = mix(stiff, both, neighbours(both, lay.step_x)) + mix(
            mass, rest, neighbours(rest, lay.step_x)
        )
        return (0.5 * keep) * out

    def inner(a, b):
        return jnp.sum(jnp.sum(a * b, axis=1, keepdims=True), axis=0, keepdims=True)

    residual = keep * (part(1) + roll(part(0), -1, 0) + roll(part(2), 1, 0) + roll(part(3), 2, 0))
    image = operate(residual)
    total = jnp.zeros(shape, F32)
    for step in range(CG_STEPS):
        last = step + 1 == CG_STEPS
        norm, curv = inner(residual, residual), inner(image, residual)
        if not last:
            second = operate(image)
        if step == 0:
            alpha = norm / curv
            direction, moved = residual, image
            if not last:
                moved_image = second
        else:
            beta = norm / norm_old
            alpha = norm / (curv - beta * norm / alpha)
            direction = residual + beta * direction
            if not last:
                moved, moved_image = image + beta * moved, second + beta * moved_image
        norm_old = norm
        total = total + alpha * direction
        if not last:
            residual, image = residual - alpha * moved, image - alpha * moved_image
    here = pl.ds(N, lay.slabs)
    for ref, value in ((first_ref, total), (second_ref, above(total))):
        ref[...] = jnp.zeros(ref.shape, F32)
        ref[here, :] = value


def corners(lay, low, high):
    rows = [low, high]
    rows = rows + [roll(r, -lay.step_y, 1) for r in rows]
    rows = rows + [roll(r, -lay.step_x, 1) for r in rows]
    corner = lax.broadcasted_iota(jnp.int32, (N, lay.width), 0)
    local = jnp.broadcast_to(rows[0], (N, lay.width))
    for n in range(1, N):
        local = jnp.where(corner == n, rows[n], local)
    return local


def coarse_kernel(
    lay,
    mass,
    stiff,
    loads_ref,
    g_ref,
    x_ref,
    interp_ref,
    image_ref,
    g_out,
    x_out,
    around_ref,
    rows_ref,
    first_ref,
    second_ref,
):
    solve_coarse(lay, mass, stiff, loads_ref, rows_ref, first_ref, second_ref)
    mine = lay.slab() + N
    _, _, part_z = lane_parts(lay, (1, lay.width))
    bottom = part_z == 0
    own, outer, far = [], [], []
    for ref in (first_ref, second_ref):
        before, here, after = (ref[pl.ds(mine + shift, 1), :] for shift in (-1, 0, 1))
        own.append(here)
        outer.append(jnp.where(bottom, roll(before, -1, 1), roll(after, 1, 1)))
        far.append(jnp.where(bottom, before, after))
    local = stacked(corners(lay, *own))
    dot = functools.partial(jnp.dot, preferred_element_type=F32)
    x_out[...] = x_ref[...] + dot(interp_ref[...], local)
    g_out[...] = g_ref[...] - dot(image_ref[...], local)
    around_ref[:N, :] = corners(lay, *outer)
    around_ref[N:, :] = corners(lay, *far)


def correct_layers(lay, around_ref, image_ref, edge_ref, h_ref):
    dot = functools.partial(jnp.dot, preferred_element_type=F32)
    h_ref[...] -= dot(image_ref[...], stacked(around_ref[:N, :]))
    edge = dot(edge_ref[...], stacked(around_ref[N:, :]))
    _, _, part_z = lane_parts(lay, (FACE, lay.width))
    bottom = part_z == 0
    low, high = get_rows(h_ref, 0), get_rows(h_ref, N - 1)
    set_rows(h_ref, 0, low - jnp.where(bottom, edge[FACE:], 0.0))
    set_rows(h_ref, N - 1, high - jnp.where(bottom, 0.0, edge[:FACE]))


def pair_kernel(lay, one, kind, core_ref, chip_ref, g_ref, x_ref, dinv_ref, outer_ref, *refs):
    refs = list(refs)
    high_ref, low_ref, along_ref, edge_high_ref, edge_low_ref = (refs.pop(0) for _ in range(5))
    if kind != "inner":
        around_ref, image_ref, image_edge_ref = (refs.pop(0) for _ in range(3))
    if kind == "inner":
        token_ref, points_ref = refs.pop(0), refs.pop(0)
    if kind == "last":
        token_ref = refs.pop(0)
    if kind == "last":
        out_ref = refs.pop(0)
    else:
        g_out, x_out = refs.pop(0), refs.pop(0)
        core_out, chip_out = refs.pop(0), refs.pop(0)
        if kind == "inner":
            points_out = refs.pop(0)
            points_out[...] = points_ref[...]
    s_ref, sh_ref, h_ref, u_ref = (refs.pop(0) for _ in range(4))
    if kind == "last":
        g_out = refs.pop(0)

    g_out[...] = g_ref[...]
    receive_layers(lay, core_ref, chip_ref, h_ref)
    if kind != "inner":
        correct_layers(lay, around_ref, image_ref, image_edge_ref, h_ref)
    assemble_both(lay, g_out, h_ref, s_ref, sh_ref)
    update = (1.0 / THETA) * dinv_ref[...] * s_ref[...]
    u_ref[...] = update
    outer = (1.0 / THETA) * outer_ref[...] * sh_ref[...]
    edge = times3(edge_high_ref[...], edge_low_ref[...], outer)
    _, _, part_z = lane_parts(lay, (FACE, lay.width))
    near = jnp.where(
        part_z == 0, get_rows(h_ref, N - 1) - edge[FACE:], get_rows(h_ref, 0) - edge[:FACE]
    )
    subtract_stiffness(lay, one, u_ref, g_out, high_ref, low_ref, along_ref)
    assemble(lay, g_out, s_ref, near)
    update = u_ref[...]
    following = OLD * update + NEW * dinv_ref[...] * s_ref[...]
    if kind == "last":
        total = (x_ref[...] + (update + following)).T
        count, block = out_ref.shape[0], out_ref.shape[1]
        for d in range(count):
            out_ref[d] = total[d * block : (d + 1) * block]
        return
    x_out[...] = x_ref[...] + (update + following)
    u_ref[...] = following
    subtract_stiffness(lay, one, u_ref, g_out, high_ref, low_ref, along_ref)
    send_layers(lay, g_out, s_ref, core_out, chip_out)


def unpack_kernel(lay, recv_ref, out_ref, flat_ref):
    for d in range(lay.slabs):
        first = lay.slab_at(d) * lay.depth
        for e2 in range(lay.tiles_y):
            rows = recv_ref[d, pl.ds(e2 * lay.depth, lay.depth), :]
            flat_ref[pl.ds(e2 * EZ + first, lay.depth), :] = rows
    out_ref[...] = flat_ref[...].T


def gauss_at(elem, node, base, position):
    half_nodes = jnp.full(node.shape, 0.5 * (1.0 + GLL_POINTS[0]), F32)
    for n in range(1, N):
        half_nodes = jnp.where(node == n, 0.5 * (1.0 + GLL_POINTS[n]), half_nodes)
    elem = elem.astype(F32)
    away = elem + half_nodes - position
    inside = (
        (elem == base)
        | (elem == base + 1.0)
        | ((elem == base - 1.0) & (node == N - 1))
        | ((elem == base + 2.0) & (node == 0))
    )
    return jnp.where(inside, jnp.exp(-(away * away) / (WIDTH_EPS * WIDTH_EPS)), 0.0)


def forces_kernel(tiles_y, local_points, points_ref, out_ref, done_ref):
    done_ref[...] = jnp.zeros(done_ref.shape, F32)
    count = points_ref.shape[0]
    first_x, first_y = lax.axis_index("ex"), lax.axis_index("ey") * tiles_y
    lane = lax.broadcasted_iota(jnp.int32, (count, 3 * FACE), 1)
    node_x, node_y, part = (lane >> 3) & (N - 1), lane & (N - 1), lane >> 6
    lane_z = lax.broadcasted_iota(jnp.int32, (count, tiles_y * EZ), 1)
    planes, columns = [], []
    for place in range(local_points):

        def value(n):
            at = (place * 9 + n) * N
            return points_ref[:, at : at + 1]

        base = [value(d) for d in range(3)]
        position = [value(d) + 1.0 + value(3 + d) for d in range(3)]
        force = jnp.where(part == 0, value(6), jnp.where(part == 1, value(7), value(8)))
        x = gauss_at(jnp.broadcast_to(first_x, lane.shape), node_x, base[0], position[0])
        scaled = GAUSS_NORM * force * x
        for e2 in range(tiles_y):
            y = gauss_at(jnp.broadcast_to(first_y + e2, lane.shape), node_y, base[1], position[1])
            planes.append(scaled * y)
            columns.append((e2, base[2], position[2]))
    high, low = split(jnp.concatenate(planes, 0))
    plane = jnp.concatenate([high, high, low], 0)
    elem_z, row_z = lane_z & (EZ - 1), lane_z >> log2(EZ)
    for k in range(N):
        node = jnp.full(lane_z.shape, k, jnp.int32)
        along = [
            jnp.where(row_z == e2, gauss_at(elem_z, node, base, position), 0.0)
            for e2, base, position in columns
        ]
        high, low = split(jnp.concatenate(along, 0))
        out_ref[pl.ds(k, 3 * FACE, stride=N), :] = lax.dot_general(
            plane,
            jnp.concatenate([high, low, high], 0),
            (((0,), (0,)), ((), ())),
            preferred_element_type=F32,
        )


def call(kernel, outs, inputs, scratch=(), smem=0, spaces=None, limit=40):
    spaces = spaces or [pltpu.SMEM] * smem + [pltpu.VMEM] * (len(inputs) - smem)
    specs = [pl.BlockSpec(memory_space=space) for space in spaces]
    shapes = [jax.ShapeDtypeStruct(s, F32) for s in outs]
    result = pl.pallas_call(
        kernel,
        out_shape=shapes,
        in_specs=specs,
        out_specs=[pl.BlockSpec(memory_space=pltpu.VMEM)] * len(shapes),
        scratch_shapes=[pltpu.VMEM(s, F32) if isinstance(s, tuple) else s for s in scratch],
        compiler_params=pltpu.CompilerParams(vmem_limit_bytes=limit * 1024 * 1024),
    )(*inputs)
    return result


def shards(source, point_base, point_offset, point_force):
    tiles_x, tiles_y = source.shape[3], source.shape[4] // EZ
    lay = Layout(lax.axis_size("ex"), lax.axis_size("ey"), tiles_x, tiles_y)
    devices = lay.mesh_x * lay.mesh_y
    derivative, weights, interp, stiff_one = build_tables()
    width, fields = lay.width, (N**3, lay.width)

    diag_w = np.diag(weights)
    full = 0.5 * (
        kron3(stiff_one, diag_w, diag_w)
        + kron3(diag_w, stiff_one, diag_w)
        + kron3(diag_w, diag_w, stiff_one)
    )
    edge_rows = np.concatenate([np.arange(FACE) * N, np.arange(FACE) * N + N - 1])
    plane = 0.5 * (np.kron(stiff_one, diag_w) + np.kron(diag_w, stiff_one))
    high, low = (jnp.asarray(t) for t in split_table(np.kron(np.eye(N // 2), plane)))
    along = np.broadcast_to(0.5 * np.kron(weights, weights)[:, None], (FACE, width))
    along = jnp.asarray(along, F32)
    edge_high, edge_low = (jnp.asarray(t) for t in split_table(full[edge_rows]))
    one = (stiff_one, weights)
    interp3 = kron3(interp, interp, interp)
    image3 = full @ interp3
    ratio = (weights[:, None] * derivative**2).sum(axis=0) / weights
    diag = 0.5 * (ratio[:, None, None] + ratio[None, :, None] + ratio[None, None, :])
    diag = diag * weights[:, None, None] * weights[None, :, None] * weights[None, None, :]
    factor = 1.0 / diag
    mass = interp.T @ diag_w @ interp
    stiff = interp.T @ stiff_one @ interp
    moved = -interp3.T @ full
    loads_table, near_table = (
        jnp.asarray(np.concatenate(split_table(t), 0))
        for t in (
            np.concatenate([interp3.T, moved], 1),
            np.concatenate([moved[:, edge_rows[FACE:]], moved[:, edge_rows[:FACE]]], 1),
        )
    )
    prolong3, image3, image_edge = (
        jnp.asarray(stacked_table(t)) for t in (interp3, image3, image3[edge_rows])
    )

    local_points = point_base.shape[1]
    block = lay.block
    (send,) = call(
        functools.partial(pack_kernel, lay),
        [(lay.slabs, block, N**3)],
        [
            pltpu.with_memory_space_constraint(t, pltpu.HBM)
            for t in (
                point_base.T,
                point_offset.T,
                point_force.T,
                source.reshape(N**3, tiles_y * EZ),
            )
        ],
        [
            pltpu.VMEM((local_points, 3), jnp.int32),
            (local_points, 3),
            (local_points, 3),
            (N**3, tiles_y * EZ),
            (tiles_y * EZ, N**3),
            pltpu.SemaphoreType.DMA((4,)),
        ],
        spaces=[pltpu.HBM] * 4,
    )
    recv = lax.all_to_all(send, lay.axis, 0, 0)
    if not lay.joint:
        recv = lax.all_gather(recv, "ex", axis=0, tiled=True)

    def swap(core, chip):
        return (
            lax.ppermute(core, lay.axis, lay.swaps(0)),
            lax.ppermute(chip, lay.axis, lay.swaps(1)),
        )

    def gather(loads):
        return lax.all_to_all(loads, lay.axis, 0, 0)

    face_shape = (FACE, width)
    layer = (N**3 // 2, width)
    loads_shape = (lay.slabs, N, width)
    table = (devices, -(-9 * N * local_points // 128) * 128)
    g, x, dinv, outer, face, points = call(
        functools.partial(first_kernel, lay, local_points, derivative, one, factor),
        [fields, fields, fields, fields, (256, width), table],
        [recv, high, low, along],
        [
            fields,
            face_shape,
            (width, N**3),
            pltpu.SMEM(table, F32),
            pltpu.SMEM((devices * local_points,), jnp.int32),
            pltpu.SemaphoreType.DMA,
        ],
    )
    faces = swap(face, face)
    loads, token = call(
        functools.partial(first_response, lay),
        [loads_shape, (N, 128)],
        [g, x, dinv, loads_table, near_table],
        [fields],
    )
    loads = gather(loads)
    g, x, core, chip = call(
        functools.partial(second_kernel, lay, one),
        [fields, fields, layer, layer],
        [*faces, g, x, dinv, high, low, along, token],
        [fields, fields],
    )
    coarse = ((mass[0, 0], mass[0, 1]), (stiff[0, 0], stiff[0, 1]))
    stiffness = [high, low, along, edge_high, edge_low]

    for cycle in range(CYCLES):
        core, chip = swap(core, chip)
        last = cycle + 1 == CYCLES
        outs = [fields, fields, layer, layer]
        extra = [done] if last else []
        scratch = [fields] * 4
        if last:
            outs = [(lay.mesh_x * lay.mesh_y, block, N**3)]
            scratch += [fields]
        g, x, around = call(
            functools.partial(coarse_kernel, lay, *coarse),
            [fields, fields, (2 * N, width)],
            [loads, g, x, prolong3, image3],
            [(lay.slabs * 4, width)] + [(lay.slabs + 2 * N, width)] * 2,
        )
        outs = call(
            functools.partial(pair_kernel, lay, one, "last" if last else "plain"),
            outs,
            [core, chip, g, x, dinv, outer, *stiffness, around, image3, image_edge, *extra],
            scratch,
        )
        if last:
            break
        g, x, core, chip = outs
        layers = swap(core, chip)
        loads, token = call(
            functools.partial(pair_response, lay, one),
            [loads_shape, (N, 128)],
            [g, dinv, outer, high, low, along, loads_table, near_table],
            [fields] * 6,
        )
        loads = gather(loads)
        g, x, core, chip, points = call(
            functools.partial(pair_kernel, lay, one, "inner"),
            [fields, fields, layer, layer, table],
            [*layers, g, x, dinv, outer, *stiffness, token, points],
            [fields] * 4,
        )
        forces, done = call(
            functools.partial(forces_kernel, tiles_y, local_points),
            [(3 * N**3, tiles_y * EZ), (N, 128)],
            [points],
        )
    (out,) = outs
    if not lay.joint:
        out = lax.dynamic_slice_in_dim(out, lax.axis_index("ex") * lay.mesh_y, lay.mesh_y, 0)
    out = lax.all_to_all(out, lay.axis, 0, 0)
    (pressure,) = call(
        functools.partial(unpack_kernel, lay),
        [(N**3, tiles_y * EZ)],
        [out],
        [(lay.slabs * block, N**3)],
    )
    return (
        pressure.reshape(source.shape),
        forces.reshape((3, *source.shape)),
    )


def solution(mesh):
    in_specs = (
        P(None, None, None, "ex", "ey"),
        P(None, ("ex", "ey")),
        P(None, ("ex", "ey")),
        P(None, ("ex", "ey")),
    )
    out_specs = (P(None, None, None, "ex", "ey"), P(None, None, None, None, "ex", "ey"))
    return jax.shard_map(shards, mesh=mesh, in_specs=in_specs, out_specs=out_specs, check_vma=False)
```

```python
import functools
import math

import jax
import jax.numpy as jnp
import numpy as np
from jax import lax
from jax.experimental import pallas as pl
from jax.experimental.pallas import tpu as pltpu
from jax.sharding import PartitionSpec as P

EZ = 64
CG_STEPS = 4
CYCLES = 2
N = 8
GLL_POINTS = np.array(
    [
        -1.0,
        -0.8717401485096066,
        -0.5917001814331423,
        -0.2092992179024789,
        0.2092992179024789,
        0.5917001814331423,
        0.8717401485096066,
        1.0,
    ]
)
WIDTH_EPS = 0.35
GAUSS_NORM = 1.0 / (math.pi**1.5 * WIDTH_EPS**3)
CHEB_LOW = 1.5
CHEB_HIGH = 12.0
THETA = 0.5 * (CHEB_HIGH + CHEB_LOW)
DELTA = 0.5 * (CHEB_HIGH - CHEB_LOW)
RHO_FIRST = DELTA / THETA
RHO_SECOND = 1.0 / (2.0 * THETA / DELTA - RHO_FIRST)
F32 = jnp.float32
BF16 = jnp.bfloat16
FACE = N * N


def build_tables():
    points = GLL_POINTS
    degree = len(points) - 1
    previous = points * 0.0 + 1.0
    current = points.copy()
    for k in range(1, degree):
        following = ((2 * k + 1) * points * current - k * previous) / (k + 1)
        previous = current
        current = following
    derivative = np.zeros((degree + 1, degree + 1))
    for i in range(degree + 1):
        for j in range(degree + 1):
            if i != j:
                derivative[i, j] = current[i] / (current[j] * (points[i] - points[j]))
    derivative[0, 0] = -degree * (degree + 1) / 4.0
    derivative[degree, degree] = degree * (degree + 1) / 4.0
    weights = 2.0 / (degree * (degree + 1) * current**2)
    interp = np.stack([(1.0 - points) / 2.0, (1.0 + points) / 2.0], axis=1)
    stiff_one = derivative.T @ (weights[:, None] * derivative)
    return derivative, weights, interp, stiff_one


def kron3(a, b, c):
    return np.kron(np.kron(a, b), c)


def log2(n):
    return int(n).bit_length() - 1


class Layout:
    def __init__(self, mesh_x, mesh_y, tiles_x, tiles_y):
        self.mesh_x, self.mesh_y = mesh_x, mesh_y
        self.num_x, self.num_y = tiles_x * mesh_x, tiles_y * mesh_y
        self.tiles_y = tiles_y
        self.joint = EZ % (2 * mesh_x * mesh_y) == 0
        self.axis = ("ex", "ey") if self.joint else "ey"
        self.slabs = mesh_x * mesh_y if self.joint else mesh_y
        self.depth = EZ // self.slabs
        assert self.depth == 2 and tiles_x == 1
        self.width = self.num_x * self.num_y * self.depth
        self.step_y = self.depth
        self.step_x = self.depth * self.num_y
        self.block = tiles_y * self.depth
        slab_of = [self.slab_at(d) for d in range(self.slabs)]
        self.order = [slab_of.index(s) for s in range(self.slabs)]

    def slab_at(self, d):
        if self.joint and self.mesh_x % 2 == 0 and self.mesh_y % 2 == 0:
            high = self.mesh_y // 2
            y = d & 1
            z = (d >> 1) & (high - 1)
            core = (d >> log2(self.mesh_y)) & 1
            x = d >> (log2(self.mesh_y) + 1)
            turn = y ^ (x & 1)
            return ((x * 2 + turn) * high + (z ^ (turn * (high - 1)))) * 2 + core
        if not self.joint and self.mesh_y % 8 == 0:
            return d ^ (((d >> 3) & 1) * 7)
        return d

    def slab(self):
        d = lax.axis_index("ey")
        return self.slab_at(lax.axis_index("ex") * self.mesh_y + d if self.joint else d)

    def swaps(self, first):
        pairs = []
        for s in range(first, self.slabs, 2):
            a, b = self.order[s], self.order[(s + 1) % self.slabs]
            pairs += [(a, b), (b, a)]
        return pairs


def split(x):
    high = x.astype(BF16)
    return high, (x - high.astype(F32)).astype(BF16)


def times3(high, low, x):
    xh, xl = split(x)
    dot = functools.partial(jnp.dot, preferred_element_type=F32)
    return dot(high, xh) + dot(high, xl) + dot(low, xh)


def split_table(x):
    high = x.astype(BF16)
    return high, (x - high.astype(np.float64)).astype(BF16)


def stacked_table(x):
    high, low = split_table(x)
    return np.concatenate([high, high, low, low], 1)


def stacked(x):
    high = x.astype(BF16).astype(F32)
    low = x - high
    return jnp.concatenate([high, low, high, low], 0).astype(BF16)


def subtract_stiffness(lay, one, u_ref, g_ref, high_ref, low_ref, along_ref):
    matrix, weights = one
    dot = functools.partial(jnp.dot, preferred_element_type=F32)
    half = N // 2
    for first in (0, half):
        scaled = [
            float(weights[i]) * u_ref[pl.ds(i * FACE, FACE), :] for i in range(first, first + half)
        ]
        xh, xl = split(jnp.concatenate(scaled, 0))
        both = dot(high_ref[...], jnp.concatenate([xh, xl], 1))
        rows = pl.ds(first * FACE, half * FACE)
        g_ref[rows, :] -= both[:, : lay.width] + both[:, lay.width :] + dot(low_ref[...], xh)
    even = 0.5 * (matrix[:half, :half] + matrix[:half, :half - 1 : -1])
    odd = 0.5 * (matrix[:half, :half] - matrix[:half, :half - 1 : -1])
    for j in range(N):
        values = [u_ref[pl.ds((i * N + j) * N, N), :] for i in range(N)]
        sums = [values[i] + values[N - 1 - i] for i in range(half)]
        gaps = [values[i] - values[N - 1 - i] for i in range(half)]
        along = along_ref[pl.ds(j * N, N), :]
        for i in range(half):
            a = sum(float(even[i, q]) * sums[q] for q in range(half))
            b = sum(float(odd[i, q]) * gaps[q] for q in range(half))
            g_ref[pl.ds((i * N + j) * N, N), :] -= along * (a + b)
            g_ref[pl.ds(((N - 1 - i) * N + j) * N, N), :] -= along * (a - b)


def roll(x, shift, axis):
    size = x.shape[axis]
    return pltpu.roll(x, shift % size, axis)


def lane_parts(lay, shape):
    lane = lax.broadcasted_iota(jnp.int32, shape, len(shape) - 1)
    part_z = lane & (lay.depth - 1)
    part_y = lax.shift_right_logical(lane, log2(lay.step_y)) & (lay.num_y - 1)
    part_x = lax.shift_right_logical(lane, log2(lay.step_x))
    return part_x, part_y, part_z


def get_rows(ref, k):
    if ref.shape[1] == 128:
        return ref[pl.ds(k, FACE, stride=N), :]
    return jnp.concatenate([ref[pl.ds(n * N + k, 1), :] for n in range(FACE)], 0)


def set_rows(ref, k, value):
    if ref.shape[1] == 128:
        ref[pl.ds(k, FACE, stride=N), :] = value
    else:
        for n in range(FACE):
            ref[pl.ds(n * N + k, 1), :] = value[n : n + 1]


def assemble_xy(lay, s_ref):
    last = N - 1
    for j in range(N):
        a, b = pl.ds(j * N, N), pl.ds((last * N + j) * N, N)
        low, high = s_ref[a, :], s_ref[b, :]
        s_ref[a, :] = low + roll(high, lay.step_x, 1)
        s_ref[b, :] = high + roll(low, -lay.step_x, 1)
    for i in range(N):
        a, b = pl.ds(i * N * N, N), pl.ds((i * N + last) * N, N)
        low, high = s_ref[a, :], s_ref[b, :]
        s_ref[a, :] = low + roll(high, lay.step_y, 1)
        s_ref[b, :] = high + roll(low, -lay.step_y, 1)


def assemble(lay, g_ref, s_ref, halo):
    _, _, part_z = lane_parts(lay, halo.shape)
    s_ref[...] = g_ref[...]
    low = get_rows(g_ref, 0)
    high = get_rows(g_ref, N - 1)
    set_rows(s_ref, 0, low + jnp.where(part_z == 0, halo, roll(high, 1, 1)))
    set_rows(s_ref, N - 1, high + jnp.where(part_z == lay.depth - 1, halo, roll(low, -1, 1)))
    assemble_xy(lay, s_ref)


def store_faces(lay, g_ref, face_ref):
    low = get_rows(g_ref, 0)
    high = get_rows(g_ref, N - 1)
    _, _, part_z = lane_parts(lay, low.shape)
    face_ref[...] = jnp.zeros(face_ref.shape, F32)
    face_ref[:FACE, :] = jnp.where(part_z == 0, low, high)


def halo_of(lay, core_ref, chip_ref):
    odd = (lay.slab() & 1) == 1
    core, chip = core_ref[:FACE, :], chip_ref[:FACE, :]
    below = jnp.where(odd, core, chip)
    above = jnp.where(odd, chip, core)
    _, _, part_z = lane_parts(lay, core.shape)
    return jnp.where(part_z == 0, roll(below, 1 - lay.depth, 1), roll(above, lay.depth - 1, 1))


def assemble_both(lay, g_ref, h_ref, s_ref, sh_ref):
    low, high = get_rows(g_ref, 0), get_rows(g_ref, N - 1)
    out_low, out_high = get_rows(h_ref, 0), get_rows(h_ref, N - 1)
    _, _, part_z = lane_parts(lay, low.shape)
    bottom = part_z == 0
    s_ref[...] = g_ref[...]
    sh_ref[...] = h_ref[...]
    set_rows(s_ref, 0, low + jnp.where(bottom, out_high, roll(high, 1, 1)))
    set_rows(s_ref, N - 1, high + jnp.where(bottom, roll(low, -1, 1), out_low))
    set_rows(sh_ref, N - 1, out_high + jnp.where(bottom, low, 0.0))
    set_rows(sh_ref, 0, out_low + jnp.where(bottom, 0.0, high))
    assemble_xy(lay, s_ref)
    assemble_xy(lay, sh_ref)


def send_layers(lay, g_ref, s_ref, core_ref, chip_ref):
    low, high = get_rows(g_ref, 0), get_rows(g_ref, N - 1)
    _, _, part_z = lane_parts(lay, low.shape)
    s_ref[...] = g_ref[...]
    set_rows(s_ref, N - 1, jnp.where(part_z == 0, high + roll(low, -1, 1), high))
    set_rows(s_ref, 0, jnp.where(part_z == 0, low, low + roll(high, 1, 1)))
    half = N**3 // 2
    a, b = s_ref[:half, :], s_ref[half:, :]
    _, _, part_z = lane_parts(lay, a.shape)
    bottom = part_z == 0
    first = jnp.where(bottom, a, roll(b, 1, 1))
    second = jnp.where(bottom, roll(a, -1, 1), b)
    odd = (lay.slab() & 1) == 1
    core_ref[...] = jnp.where(odd, first, second)
    chip_ref[...] = jnp.where(odd, second, first)


def receive_layers(lay, core_ref, chip_ref, h_ref):
    odd = (lay.slab() & 1) == 1
    core, chip = core_ref[...], chip_ref[...]
    below, above = jnp.where(odd, core, chip), jnp.where(odd, chip, core)
    _, _, part_z = lane_parts(lay, core.shape)
    bottom = part_z == 0
    half = N**3 // 2
    h_ref[:half, :] = jnp.where(bottom, below, roll(above, 1, 1))
    h_ref[half:, :] = jnp.where(bottom, roll(below, -1, 1), above)


def pack_kernel(
    lay,
    base_ref,
    offset_ref,
    force_ref,
    source_ref,
    out_ref,
    base_buf,
    offset_buf,
    force_buf,
    field_ref,
    flat_ref,
    sems,
):
    pairs = (
        (source_ref, field_ref),
        (base_ref, base_buf),
        (offset_ref, offset_buf),
        (force_ref, force_buf),
    )
    copies = [pltpu.make_async_copy(a, b, sems.at[n]) for n, (a, b) in enumerate(pairs)]
    for copy in copies:
        copy.start()
    for copy in copies:
        copy.wait()
    mean = 0.5 * (get_rows(field_ref, N - 1) + roll(get_rows(field_ref, 0), -1, 1))
    set_rows(field_ref, N - 1, mean)
    set_rows(field_ref, 0, roll(mean, 1, 1))
    flat_ref[...] = field_ref[...].T
    shape = (1, N**3)
    lane = lax.broadcasted_iota(jnp.int32, shape, 1)
    points = jnp.zeros(shape, F32)
    for p in range(base_buf.shape[0]):
        for c, ref in enumerate((base_buf, offset_buf, force_buf)):
            for d in range(3):
                value = ref[p : p + 1, d : d + 1].astype(F32)
                points = jnp.where(lane == (p * 9 + c * 3 + d) * N, value, points)
    used = (lane & (N - 1)) == 0
    for d in range(lay.slabs):
        first = lay.slab_at(d) * lay.depth
        for e2 in range(lay.tiles_y):
            rows = flat_ref[pl.ds(e2 * EZ + first, lay.depth), :]
            out_ref[d, pl.ds(e2 * lay.depth, lay.depth), :] = rows
        out_ref[d, 1:2, :] = jnp.where(used, points, out_ref[d, 1:2, :])


def column(values, shape):
    node = lax.broadcasted_iota(jnp.int32, shape, 0)
    out = jnp.full(shape, float(values[0]), F32)
    for n in range(1, N):
        out = jnp.where(node == n, float(values[n]), out)
    return out


def gauss(elem, base, position, half_nodes):
    node = lax.broadcasted_iota(jnp.int32, elem.shape, 0)
    elem = elem.astype(F32)
    away = elem + half_nodes - position
    inside = (
        (elem == base)
        | (elem == base + 1.0)
        | ((elem == base - 1.0) & (node == N - 1))
        | ((elem == base + 2.0) & (node == 0))
    )
    return jnp.where(inside, jnp.exp(-(away * away) / (WIDTH_EPS * WIDTH_EPS)), 0.0)


def point_values(points_ref, row, place, scale):
    base, offset, force = (
        [points_ref[row, (place * 9 + c * 3 + d) * N] for d in range(3)] for c in range(3)
    )
    return base, [b + 1.0 + o for b, o in zip(base, offset)], [scale * f for f in force]


def right_side(lay, local_points, one, points_ref, list_ref, g_ref, halo_ref):
    derivative, weights = one
    shape = (N, lay.width)
    part_x, part_y, part_z = lane_parts(lay, shape)
    first_z = lay.slab() * lay.depth
    elem_z = first_z + part_z
    elem_halo = jnp.where(part_z == 0, first_z - 1, first_z + lay.depth)
    half_nodes = column(0.5 * (1.0 + GLL_POINTS), shape)
    weight = column(weights, shape)
    columns = [column(derivative[a], shape) for a in range(N)]

    def weighted(elem, base, position):
        plain = weight * gauss(elem, base, position, half_nodes)
        terms = [columns[a] * plain[a : a + 1] for a in range(N)]
        while len(terms) > 1:
            terms = [a + b for a, b in zip(terms[::2], terms[1::2])]
        return plain, terms[0]

    def place_of(p):
        return (p, 0) if local_points == 1 else (lax.div(p, local_points), lax.rem(p, local_points))

    first = first_z.astype(F32)

    def collect(p, found):
        row, place = place_of(p)
        base = points_ref[row, (place * 9 + 2) * N]
        list_ref[found] = p
        reached = (base + 2.0 >= first - 1.0) & (base - 1.0 <= first + lay.depth)
        return found + jnp.where(reached, 1, 0)

    found = lax.fori_loop(0, points_ref.shape[0] * local_points, collect, jnp.int32(0))
    pick = part_z[0:1] == 0

    def factors(n):
        row, place = place_of(list_ref[jnp.minimum(n, found - 1)])
        base, position, force = point_values(
            points_ref, row, place, jnp.where(n < found, 0.25 * GAUSS_NORM, 0.0)
        )
        x0, x1 = weighted(part_x, base[0], position[0])
        y0, y1 = weighted(part_y, base[1], position[1])
        z0, z1 = weighted(elem_z, base[2], position[2])
        h0, h1 = weighted(elem_halo, base[2], position[2])
        h0 = jnp.where(pick, h0[N - 1 : N], h0[0:1])
        h1 = jnp.where(pick, h1[N - 1 : N], h1[0:1])
        planes = []
        for j in range(N):
            row0, row1 = y0[j : j + 1], y1[j : j + 1]
            planes.append((row0 * z0, row1 * (force[1] * z0) + row0 * (force[2] * z1)))
        planes.append((y0 * h0, y1 * (force[1] * h0) + y0 * (force[2] * h1)))
        return force[0] * x1, x0, planes

    def two(t, _):
        points = [factors(2 * t), factors(2 * t + 1)]

        def term(i, j):
            parts = [
                x1[i : i + 1] * planes[j][0] + x0[i : i + 1] * planes[j][1] for x1, x0, planes in points
            ]
            return parts[0] + parts[1]

        for i in range(N):
            for j in range(N):
                g_ref[pl.ds((i * N + j) * N, N), :] += term(i, j)
            halo_ref[pl.ds(i * N, N), :] += term(i, N)
        return 0

    lax.fori_loop(0, lax.div(found + 1, 2), two, 0)


def inverse_diagonal(lay, factor, dinv_ref, outer):
    shape = (N, lay.width)
    part_x, part_y, part_z = lane_parts(lay, shape)
    first = lay.slab() * lay.depth
    part_z = jnp.where(part_z == 0, first - 1, first + lay.depth) if outer else first + part_z
    node = lax.broadcasted_iota(jnp.int32, shape, 0)

    def share(low, high):
        return (
            jnp.where(low, 0.0, 0.5),
            jnp.where(high, 0.0, 0.5),
        )

    low_z, high_z = share(part_z == 0, part_z == EZ - 1)
    along_z = jnp.where(node == 0, low_z, jnp.where(node == N - 1, high_z, 1.0))
    if outer:
        along_z = jnp.where((part_z < 0) | (part_z >= EZ), 0.0, along_z)
    along_x = dict(zip((0, N - 1), share(part_x == 0, part_x == lay.num_x - 1)))
    along_y = dict(zip((0, N - 1), share(part_y == 0, part_y == lay.num_y - 1)))
    tables = {}
    for i in range(N // 2):
        for j in range(i + 1):
            tables[i, j] = tables[j, i] = column(factor[i, j], shape) * along_z
    for i in range(N):
        for j in range(N):
            rows = pl.ds((i * N + j) * N, N)
            value = tables[min(i, N - 1 - i), min(j, N - 1 - j)]
            if i in along_x:
                value = value * along_x[i]
            if j in along_y:
                value = value * along_y[j]
            dinv_ref[rows, :] = value


def first_kernel(
    lay,
    local_points,
    derivative,
    one,
    factor,
    recv_ref,
    high_ref,
    low_ref,
    along_ref,
    g_ref,
    x_ref,
    dinv_ref,
    outer_ref,
    face_ref,
    points_ref,
    s_ref,
    halo_ref,
    flat_ref,
    table_ref,
    list_ref,
    sem,
):
    count, block = recv_ref.shape[0], recv_ref.shape[1]
    for d in range(count):
        points_ref[pl.ds(d, 1), :] = recv_ref[d, 1:2, : points_ref.shape[1]]
    copy = pltpu.make_async_copy(points_ref, table_ref, sem)
    copy.start()
    for d in range(count):
        flat_ref[pl.ds(d * block, block), :] = recv_ref[d]
    g_ref[...] = flat_ref[...].T
    low, high = get_rows(g_ref, 0), get_rows(g_ref, N - 1)
    _, _, part_z = lane_parts(lay, low.shape)
    set_rows(g_ref, 0, jnp.where(part_z == 0, low, roll(high, 1, 1)))
    halo_ref[...] = jnp.where(part_z == 0, low, high)
    inverse_diagonal(lay, factor, dinv_ref, False)
    inverse_diagonal(lay, factor, outer_ref, True)
    copy.wait()
    right_side(lay, local_points, (derivative, one[1]), table_ref, list_ref, g_ref, halo_ref)
    assemble(lay, g_ref, s_ref, halo_ref[...])
    x_ref[...] = (1.0 / THETA) * dinv_ref[...] * s_ref[...]
    subtract_stiffness(lay, one, x_ref, g_ref, high_ref, low_ref, along_ref)
    store_faces(lay, g_ref, face_ref)


def vertex_rows(lay, table_ref, values):
    high, low = split(values)
    both = jnp.dot(table_ref[...], jnp.concatenate([high, low], 1), preferred_element_type=F32)
    load = both[:N, : lay.width] + both[:N, lay.width :] + both[N:, : lay.width]
    rows = [load[n : n + 1] for n in range(N)]
    rows = [rows[n] + roll(rows[4 + n], lay.step_x, 1) for n in range(4)]
    return [rows[n] + roll(rows[2 + n], lay.step_y, 1) for n in range(2)]


def face_values(lay, u_ref):
    low, high = get_rows(u_ref, 0), get_rows(u_ref, N - 1)
    _, _, part_z = lane_parts(lay, low.shape)
    return jnp.where(part_z == 0, low, 0.0), jnp.where(part_z == 0, 0.0, high)


def send_loads(lay, own, outer, far, send_ref, token_ref):
    _, _, part_z = lane_parts(lay, own[0].shape)
    bottom = part_z == 0
    before = jnp.where(bottom, 0.0, roll(outer[0], 1, 1))
    here = own[0] + jnp.where(bottom, outer[1], roll(own[1], 1, 1))
    after = jnp.where(bottom, roll(own[1], -1, 1) + roll(outer[0], -1, 1), outer[1])
    second = jnp.zeros_like(here)
    if far is not None:
        before = before + jnp.where(bottom, far[0], roll(far[1], 1, 1))
        after = after + jnp.where(bottom, 0.0, far[0])
        second = jnp.where(bottom, roll(far[1], -1, 1), 0.0)
    rows = jnp.concatenate([before, here, after, second] * 2, 0)
    for d in range(send_ref.shape[0]):
        send_ref[d] = rows
    token_ref[...] = jnp.zeros(token_ref.shape, F32)


OLD = RHO_SECOND * RHO_FIRST
NEW = 2.0 * RHO_SECOND / DELTA


def first_response(
    lay, g_ref, x_ref, dinv_ref, loads_ref, near_ref, send_ref, token_ref, s_ref
):
    assemble(lay, g_ref, s_ref, jnp.zeros((FACE, lay.width), F32))
    update = NEW * dinv_ref[...] * s_ref[...]
    s_ref[...] = update
    total = OLD * x_ref[...] + update
    own = vertex_rows(lay, loads_ref, jnp.concatenate([g_ref[...], total], 0))
    outer = vertex_rows(lay, near_ref, jnp.concatenate(face_values(lay, s_ref), 0))
    send_loads(lay, own, outer, None, send_ref, token_ref)


def pair_response(
    lay,
    one,
    g_ref,
    dinv_ref,
    outer_ref,
    high_ref,
    low_ref,
    along_ref,
    loads_ref,
    near_ref,
    send_ref,
    token_ref,
    s_ref,
    sh_ref,
    u_ref,
    v_ref,
    t_ref,
    h_ref,
):
    tile = (high_ref, low_ref, along_ref)
    assemble(lay, g_ref, s_ref, jnp.zeros((FACE, lay.width), F32))
    u_ref[...] = (1.0 / THETA) * dinv_ref[...] * s_ref[...]
    t_ref[...] = g_ref[...]
    subtract_stiffness(lay, one, u_ref, t_ref, *tile)
    low, high = face_values(lay, u_ref)
    v_ref[...] = jnp.zeros(v_ref.shape, F32)
    set_rows(v_ref, N - 1, low)
    set_rows(v_ref, 0, high)
    h_ref[...] = jnp.zeros(h_ref.shape, F32)
    subtract_stiffness(lay, one, v_ref, h_ref, *tile)
    assemble_both(lay, t_ref, h_ref, s_ref, sh_ref)
    update = OLD * u_ref[...] + NEW * dinv_ref[...] * s_ref[...]
    own = vertex_rows(lay, loads_ref, jnp.concatenate([t_ref[...], update], 0))
    v_ref[...] = OLD * v_ref[...] + NEW * outer_ref[...] * sh_ref[...]
    outer = vertex_rows(lay, loads_ref, jnp.concatenate([h_ref[...], v_ref[...]], 0))
    far = vertex_rows(lay, near_ref, jnp.concatenate(face_values(lay, v_ref), 0))
    send_loads(lay, own, outer, far, send_ref, token_ref)


def second_kernel(
    lay,
    one,
    core_ref,
    chip_ref,
    g_ref,
    x_ref,
    dinv_ref,
    high_ref,
    low_ref,
    along_ref,
    token_ref,
    points_ref,
    g_out,
    x_out,
    core_out,
    chip_out,
    points_out,
    s_ref,
    u_ref,
):
    points_out[...] = points_ref[...]
    assemble(lay, g_ref, s_ref, halo_of(lay, core_ref, chip_ref))
    update = OLD * x_ref[...] + NEW * dinv_ref[...] * s_ref[...]
    u_ref[...] = update
    x_out[...] = x_ref[...] + update
    g_out[...] = g_ref[...]
    subtract_stiffness(lay, one, u_ref, g_out, high_ref, low_ref, along_ref)
    send_layers(lay, g_out, s_ref, core_out, chip_out)


def solve_coarse(lay, mass, stiff, loads_ref, rows_ref, first_ref, second_ref):
    count = 4
    for s in range(lay.slabs):
        rows_ref[pl.ds(s * count, count), :] = loads_ref[lay.order[s], :count]

    def part(n):
        if lay.width == 128:
            return rows_ref[pl.ds(n, lay.slabs, stride=count), :]
        return jnp.concatenate(
            [rows_ref[pl.ds(s * count + n, 1), :] for s in range(lay.slabs)], 0
        )

    shape = (lay.slabs, lay.width)
    part_x, part_y, part_z = lane_parts(lay, shape)
    row = lax.broadcasted_iota(jnp.int32, shape, 0)
    keep = ((part_x > 0) & (part_y > 0) & ((part_z > 0) | (row > 0))).astype(F32)
    bottom = part_z == 0

    def around_z(v):
        return jnp.where(bottom, roll(v + roll(v, 1, 0), -1, 1), roll(v + roll(v, -1, 0), 1, 1))

    def above(v):
        return jnp.where(bottom, roll(v, -1, 1), roll(roll(v, -1, 0), 1, 1))

    def neighbours(v, step):
        return roll(v, step, 1) + roll(v, -step, 1)

    def mix(pair, v, around):
        return (2.0 * pair[0]) * v + pair[1] * around

    def operate(v):
        around = around_z(v)
        mass_z, stiff_z = mix(mass, v, around), mix(stiff, v, around)
        around = neighbours(mass_z, lay.step_y)
        both = mix(mass, mass_z, around)
        rest = mix(stiff, mass_z, around) + mix(mass, stiff_z, neighbours(stiff_z, lay.step_y))
        out = mix(stiff, both, neighbours(both, lay.step_x)) + mix(
            mass, rest, neighbours(rest, lay.step_x)
        )
        return (0.5 * keep) * out

    def inner(a, b):
        return jnp.sum(jnp.sum(a * b, axis=1, keepdims=True), axis=0, keepdims=True)

    residual = keep * (part(1) + roll(part(0), -1, 0) + roll(part(2), 1, 0) + roll(part(3), 2, 0))
    image = operate(residual)
    total = jnp.zeros(shape, F32)
    for step in range(CG_STEPS):
        last = step + 1 == CG_STEPS
        norm, curv = inner(residual, residual), inner(image, residual)
        if not last:
            second = operate(image)
        if step == 0:
            alpha = norm / curv
            direction, moved = residual, image
            if not last:
                moved_image = second
        else:
            beta = norm / norm_old
            alpha = norm / (curv - beta * norm / alpha)
            direction = residual + beta * direction
            if not last:
                moved, moved_image = image + beta * moved, second + beta * moved_image
        norm_old = norm
        total = total + alpha * direction
        if not last:
            residual, image = residual - alpha * moved, image - alpha * moved_image
    here = pl.ds(N, lay.slabs)
    for ref, value in ((first_ref, total), (second_ref, above(total))):
        ref[...] = jnp.zeros(ref.shape, F32)
        ref[here, :] = value


def corners(lay, low, high):
    rows = [low, high]
    rows = rows + [roll(r, -lay.step_y, 1) for r in rows]
    rows = rows + [roll(r, -lay.step_x, 1) for r in rows]
    corner = lax.broadcasted_iota(jnp.int32, (N, lay.width), 0)
    local = jnp.broadcast_to(rows[0], (N, lay.width))
    for n in range(1, N):
        local = jnp.where(corner == n, rows[n], local)
    return local


def coarse_kernel(
    lay,
    mass,
    stiff,
    loads_ref,
    g_ref,
    x_ref,
    interp_ref,
    image_ref,
    done_ref,
    g_out,
    x_out,
    around_ref,
    rows_ref,
    first_ref,
    second_ref,
):
    solve_coarse(lay, mass, stiff, loads_ref, rows_ref, first_ref, second_ref)
    mine = lay.slab() + N
    _, _, part_z = lane_parts(lay, (1, lay.width))
    bottom = part_z == 0
    own, outer, far = [], [], []
    for ref in (first_ref, second_ref):
        before, here, after = (ref[pl.ds(mine + shift, 1), :] for shift in (-1, 0, 1))
        own.append(here)
        outer.append(jnp.where(bottom, roll(before, -1, 1), roll(after, 1, 1)))
        far.append(jnp.where(bottom, before, after))
    local = stacked(corners(lay, *own))
    dot = functools.partial(jnp.dot, preferred_element_type=F32)
    x_out[...] = x_ref[...] + dot(interp_ref[...], local)
    g_out[...] = g_ref[...] - dot(image_ref[...], local)
    around_ref[:N, :] = corners(lay, *outer)
    around_ref[N:, :] = corners(lay, *far)


def correct_layers(lay, around_ref, image_ref, edge_ref, h_ref):
    dot = functools.partial(jnp.dot, preferred_element_type=F32)
    h_ref[...] -= dot(image_ref[...], stacked(around_ref[:N, :]))
    edge = dot(edge_ref[...], stacked(around_ref[N:, :]))
    _, _, part_z = lane_parts(lay, (FACE, lay.width))
    bottom = part_z == 0
    low, high = get_rows(h_ref, 0), get_rows(h_ref, N - 1)
    set_rows(h_ref, 0, low - jnp.where(bottom, edge[FACE:], 0.0))
    set_rows(h_ref, N - 1, high - jnp.where(bottom, 0.0, edge[:FACE]))


def pair_kernel(lay, one, kind, core_ref, chip_ref, g_ref, x_ref, dinv_ref, outer_ref, *refs):
    refs = list(refs)
    high_ref, low_ref, along_ref, edge_high_ref, edge_low_ref = (refs.pop(0) for _ in range(5))
    if kind != "inner":
        around_ref, image_ref, image_edge_ref = (refs.pop(0) for _ in range(3))
    if kind == "inner":
        token_ref = refs.pop(0)
    if kind == "last":
        out_ref = refs.pop(0)
    else:
        g_out, x_out = refs.pop(0), refs.pop(0)
        core_out, chip_out = refs.pop(0), refs.pop(0)
    s_ref, sh_ref, h_ref, u_ref = (refs.pop(0) for _ in range(4))
    if kind == "last":
        g_out = refs.pop(0)

    g_out[...] = g_ref[...]
    receive_layers(lay, core_ref, chip_ref, h_ref)
    if kind != "inner":
        correct_layers(lay, around_ref, image_ref, image_edge_ref, h_ref)
    assemble_both(lay, g_out, h_ref, s_ref, sh_ref)
    update = (1.0 / THETA) * dinv_ref[...] * s_ref[...]
    u_ref[...] = update
    outer = (1.0 / THETA) * outer_ref[...] * sh_ref[...]
    edge = times3(edge_high_ref[...], edge_low_ref[...], outer)
    _, _, part_z = lane_parts(lay, (FACE, lay.width))
    near = jnp.where(
        part_z == 0, get_rows(h_ref, N - 1) - edge[FACE:], get_rows(h_ref, 0) - edge[:FACE]
    )
    subtract_stiffness(lay, one, u_ref, g_out, high_ref, low_ref, along_ref)
    assemble(lay, g_out, s_ref, near)
    update = u_ref[...]
    following = OLD * update + NEW * dinv_ref[...] * s_ref[...]
    if kind == "last":
        total = (x_ref[...] + (update + following)).T
        count, block = out_ref.shape[0], out_ref.shape[1]
        for d in range(count):
            out_ref[d] = total[d * block : (d + 1) * block]
        return
    x_out[...] = x_ref[...] + (update + following)
    u_ref[...] = following
    subtract_stiffness(lay, one, u_ref, g_out, high_ref, low_ref, along_ref)
    send_layers(lay, g_out, s_ref, core_out, chip_out)


def unpack_kernel(lay, recv_ref, out_ref, flat_ref):
    for d in range(lay.slabs):
        first = lay.slab_at(d) * lay.depth
        for e2 in range(lay.tiles_y):
            rows = recv_ref[d, pl.ds(e2 * lay.depth, lay.depth), :]
            flat_ref[pl.ds(e2 * EZ + first, lay.depth), :] = rows
    out_ref[...] = flat_ref[...].T


def gauss_at(elem, node, base, position):
    half_nodes = jnp.full(node.shape, 0.5 * (1.0 + GLL_POINTS[0]), F32)
    for n in range(1, N):
        half_nodes = jnp.where(node == n, 0.5 * (1.0 + GLL_POINTS[n]), half_nodes)
    elem = elem.astype(F32)
    away = elem + half_nodes - position
    inside = (
        (elem == base)
        | (elem == base + 1.0)
        | ((elem == base - 1.0) & (node == N - 1))
        | ((elem == base + 2.0) & (node == 0))
    )
    return jnp.where(inside, jnp.exp(-(away * away) / (WIDTH_EPS * WIDTH_EPS)), 0.0)


def forces_kernel(tiles_y, local_points, points_ref, out_ref, done_ref):
    done_ref[...] = jnp.zeros(done_ref.shape, F32)
    count = points_ref.shape[0]
    first_x, first_y = lax.axis_index("ex"), lax.axis_index("ey") * tiles_y
    lane = lax.broadcasted_iota(jnp.int32, (count, 3 * FACE), 1)
    node_x, node_y, part = (lane >> 3) & (N - 1), lane & (N - 1), lane >> 6
    lane_z = lax.broadcasted_iota(jnp.int32, (count, tiles_y * EZ), 1)
    planes, columns = [], []
    for place in range(local_points):

        def value(n):
            at = (place * 9 + n) * N
            return points_ref[:, at : at + 1]

        base = [value(d) for d in range(3)]
        position = [value(d) + 1.0 + value(3 + d) for d in range(3)]
        force = jnp.where(part == 0, value(6), jnp.where(part == 1, value(7), value(8)))
        x = gauss_at(jnp.broadcast_to(first_x, lane.shape), node_x, base[0], position[0])
        scaled = GAUSS_NORM * force * x
        for e2 in range(tiles_y):
            y = gauss_at(jnp.broadcast_to(first_y + e2, lane.shape), node_y, base[1], position[1])
            planes.append(scaled * y)
            columns.append((e2, base[2], position[2]))
    high, low = split(jnp.concatenate(planes, 0))
    plane = jnp.concatenate([high, high, low], 0)
    elem_z, row_z = lane_z & (EZ - 1), lane_z >> log2(EZ)
    for k in range(N):
        node = jnp.full(lane_z.shape, k, jnp.int32)
        along = [
            jnp.where(row_z == e2, gauss_at(elem_z, node, base, position), 0.0)
            for e2, base, position in columns
        ]
        high, low = split(jnp.concatenate(along, 0))
        out_ref[pl.ds(k, 3 * FACE, stride=N), :] = lax.dot_general(
            plane,
            jnp.concatenate([high, low, high], 0),
            (((0,), (0,)), ((), ())),
            preferred_element_type=F32,
        )


def call(kernel, outs, inputs, scratch=(), smem=0, spaces=None, limit=40):
    spaces = spaces or [pltpu.SMEM] * smem + [pltpu.VMEM] * (len(inputs) - smem)
    specs = [pl.BlockSpec(memory_space=space) for space in spaces]
    shapes = [jax.ShapeDtypeStruct(s, F32) for s in outs]
    result = pl.pallas_call(
        kernel,
        out_shape=shapes,
        in_specs=specs,
        out_specs=[pl.BlockSpec(memory_space=pltpu.VMEM)] * len(shapes),
        scratch_shapes=[pltpu.VMEM(s, F32) if isinstance(s, tuple) else s for s in scratch],
        compiler_params=pltpu.CompilerParams(vmem_limit_bytes=limit * 1024 * 1024),
    )(*inputs)
    return result


def shards(source, point_base, point_offset, point_force):
    tiles_x, tiles_y = source.shape[3], source.shape[4] // EZ
    lay = Layout(lax.axis_size("ex"), lax.axis_size("ey"), tiles_x, tiles_y)
    devices = lay.mesh_x * lay.mesh_y
    derivative, weights, interp, stiff_one = build_tables()
    width, fields = lay.width, (N**3, lay.width)

    diag_w = np.diag(weights)
    full = 0.5 * (
        kron3(stiff_one, diag_w, diag_w)
        + kron3(diag_w, stiff_one, diag_w)
        + kron3(diag_w, diag_w, stiff_one)
    )
    edge_rows = np.concatenate([np.arange(FACE) * N, np.arange(FACE) * N + N - 1])
    plane = 0.5 * (np.kron(stiff_one, diag_w) + np.kron(diag_w, stiff_one))
    high, low = (jnp.asarray(t) for t in split_table(np.kron(np.eye(N // 2), plane)))
    along = np.broadcast_to(0.5 * np.kron(weights, weights)[:, None], (FACE, width))
    along = jnp.asarray(along, F32)
    edge_high, edge_low = (jnp.asarray(t) for t in split_table(full[edge_rows]))
    one = (stiff_one, weights)
    interp3 = kron3(interp, interp, interp)
    image3 = full @ interp3
    ratio = (weights[:, None] * derivative**2).sum(axis=0) / weights
    diag = 0.5 * (ratio[:, None, None] + ratio[None, :, None] + ratio[None, None, :])
    diag = diag * weights[:, None, None] * weights[None, :, None] * weights[None, None, :]
    factor = 1.0 / diag
    mass = interp.T @ diag_w @ interp
    stiff = interp.T @ stiff_one @ interp
    moved = -interp3.T @ full
    loads_table, near_table = (
        jnp.asarray(np.concatenate(split_table(t), 0))
        for t in (
            np.concatenate([interp3.T, moved], 1),
            np.concatenate([moved[:, edge_rows[FACE:]], moved[:, edge_rows[:FACE]]], 1),
        )
    )
    prolong3, image3, image_edge = (
        jnp.asarray(stacked_table(t)) for t in (interp3, image3, image3[edge_rows])
    )

    local_points = point_base.shape[1]
    block = lay.block
    (send,) = call(
        functools.partial(pack_kernel, lay),
        [(lay.slabs, block, N**3)],
        [
            pltpu.with_memory_space_constraint(t, pltpu.HBM)
            for t in (
                point_base.T,
                point_offset.T,
                point_force.T,
                source.reshape(N**3, tiles_y * EZ),
            )
        ],
        [
            pltpu.VMEM((local_points, 3), jnp.int32),
            (local_points, 3),
            (local_points, 3),
            (N**3, tiles_y * EZ),
            (tiles_y * EZ, N**3),
            pltpu.SemaphoreType.DMA((4,)),
        ],
        spaces=[pltpu.HBM] * 4,
    )
    recv = lax.all_to_all(send, lay.axis, 0, 0)
    if not lay.joint:
        recv = lax.all_gather(recv, "ex", axis=0, tiled=True)

    def swap(core, chip):
        return (
            lax.ppermute(core, lay.axis, lay.swaps(0)),
            lax.ppermute(chip, lay.axis, lay.swaps(1)),
        )

    def gather(loads):
        return lax.all_to_all(loads, lay.axis, 0, 0)

    face_shape = (FACE, width)
    layer = (N**3 // 2, width)
    loads_shape = (lay.slabs, N, width)
    table = (devices, -(-9 * N * local_points // 128) * 128)
    g, x, dinv, outer, face, points = call(
        functools.partial(first_kernel, lay, local_points, derivative, one, factor),
        [fields, fields, fields, fields, (256, width), table],
        [recv, high, low, along],
        [
            fields,
            face_shape,
            (width, N**3),
            pltpu.SMEM(table, F32),
            pltpu.SMEM((devices * local_points,), jnp.int32),
            pltpu.SemaphoreType.DMA,
        ],
    )
    faces = swap(face, face)
    loads, token = call(
        functools.partial(first_response, lay),
        [loads_shape, (N, 128)],
        [g, x, dinv, loads_table, near_table],
        [fields],
    )
    loads = gather(loads)
    g, x, core, chip, points = call(
        functools.partial(second_kernel, lay, one),
        [fields, fields, layer, layer, table],
        [*faces, g, x, dinv, high, low, along, token, points],
        [fields, fields],
    )
    forces, done = call(
        functools.partial(forces_kernel, tiles_y, local_points),
        [(3 * N**3, tiles_y * EZ), (N, 128)],
        [points],
    )
    coarse = ((mass[0, 0], mass[0, 1]), (stiff[0, 0], stiff[0, 1]))
    stiffness = [high, low, along, edge_high, edge_low]

    for cycle in range(CYCLES):
        core, chip = swap(core, chip)
        last = cycle + 1 == CYCLES
        outs = [fields, fields, layer, layer]
        scratch = [fields] * 4
        if last:
            outs = [(lay.mesh_x * lay.mesh_y, block, N**3)]
            scratch += [fields]
        g, x, around = call(
            functools.partial(coarse_kernel, lay, *coarse),
            [fields, fields, (2 * N, width)],
            [loads, g, x, prolong3, image3, done],
            [(lay.slabs * 4, width)] + [(lay.slabs + 2 * N, width)] * 2,
        )
        outs = call(
            functools.partial(pair_kernel, lay, one, "last" if last else "plain"),
            outs,
            [core, chip, g, x, dinv, outer, *stiffness, around, image3, image_edge],
            scratch,
        )
        if last:
            break
        g, x, core, chip = outs
        layers = swap(core, chip)
        loads, token = call(
            functools.partial(pair_response, lay, one),
            [loads_shape, (N, 128)],
            [g, dinv, outer, high, low, along, loads_table, near_table],
            [fields] * 6,
        )
        loads = gather(loads)
        g, x, core, chip = call(
            functools.partial(pair_kernel, lay, one, "inner"),
            [fields, fields, layer, layer],
            [*layers, g, x, dinv, outer, *stiffness, token],
            [fields] * 4,
        )
    (out,) = outs
    if not lay.joint:
        out = lax.dynamic_slice_in_dim(out, lax.axis_index("ex") * lay.mesh_y, lay.mesh_y, 0)
    out = lax.all_to_all(out, lay.axis, 0, 0)
    (pressure,) = call(
        functools.partial(unpack_kernel, lay),
        [(N**3, tiles_y * EZ)],
        [out],
        [(lay.slabs * block, N**3)],
    )
    return (
        pressure.reshape(source.shape),
        forces.reshape((3, *source.shape)),
    )


def solution(mesh):
    in_specs = (
        P(None, None, None, "ex", "ey"),
        P(None, ("ex", "ey")),
        P(None, ("ex", "ey")),
        P(None, ("ex", "ey")),
    )
    out_specs = (P(None, None, None, "ex", "ey"), P(None, None, None, None, "ex", "ey"))
    return jax.shard_map(shards, mesh=mesh, in_specs=in_specs, out_specs=out_specs, check_vma=False)
```

```python
import functools
import math

import jax
import jax.numpy as jnp
import numpy as np
from jax import lax
from jax.experimental import pallas as pl
from jax.experimental.pallas import tpu as pltpu
from jax.sharding import PartitionSpec as P

EZ = 64
CG_STEPS = 4
CYCLES = 2
N = 8
GLL_POINTS = np.array(
    [
        -1.0,
        -0.8717401485096066,
        -0.5917001814331423,
        -0.2092992179024789,
        0.2092992179024789,
        0.5917001814331423,
        0.8717401485096066,
        1.0,
    ]
)
WIDTH_EPS = 0.35
GAUSS_NORM = 1.0 / (math.pi**1.5 * WIDTH_EPS**3)
CHEB_LOW = 1.5
CHEB_HIGH = 12.0
THETA = 0.5 * (CHEB_HIGH + CHEB_LOW)
DELTA = 0.5 * (CHEB_HIGH - CHEB_LOW)
RHO_FIRST = DELTA / THETA
RHO_SECOND = 1.0 / (2.0 * THETA / DELTA - RHO_FIRST)
F32 = jnp.float32
BF16 = jnp.bfloat16
FACE = N * N


def build_tables():
    points = GLL_POINTS
    degree = len(points) - 1
    previous = points * 0.0 + 1.0
    current = points.copy()
    for k in range(1, degree):
        following = ((2 * k + 1) * points * current - k * previous) / (k + 1)
        previous = current
        current = following
    derivative = np.zeros((degree + 1, degree + 1))
    for i in range(degree + 1):
        for j in range(degree + 1):
            if i != j:
                derivative[i, j] = current[i] / (current[j] * (points[i] - points[j]))
    derivative[0, 0] = -degree * (degree + 1) / 4.0
    derivative[degree, degree] = degree * (degree + 1) / 4.0
    weights = 2.0 / (degree * (degree + 1) * current**2)
    interp = np.stack([(1.0 - points) / 2.0, (1.0 + points) / 2.0], axis=1)
    stiff_one = derivative.T @ (weights[:, None] * derivative)
    return derivative, weights, interp, stiff_one


def kron3(a, b, c):
    return np.kron(np.kron(a, b), c)


def log2(n):
    return int(n).bit_length() - 1


class Layout:
    def __init__(self, mesh_x, mesh_y, tiles_x, tiles_y):
        self.mesh_x, self.mesh_y = mesh_x, mesh_y
        self.num_x, self.num_y = tiles_x * mesh_x, tiles_y * mesh_y
        self.tiles_y = tiles_y
        self.joint = EZ % (2 * mesh_x * mesh_y) == 0
        self.axis = ("ex", "ey") if self.joint else "ey"
        self.slabs = mesh_x * mesh_y if self.joint else mesh_y
        self.depth = EZ // self.slabs
        assert self.depth == 2 and tiles_x == 1
        self.width = self.num_x * self.num_y * self.depth
        self.step_y = self.depth
        self.step_x = self.depth * self.num_y
        self.block = tiles_y * self.depth
        slab_of = [self.slab_at(d) for d in range(self.slabs)]
        self.order = [slab_of.index(s) for s in range(self.slabs)]

    def slab_at(self, d):
        if self.joint and self.mesh_x % 2 == 0 and self.mesh_y % 2 == 0:
            high = self.mesh_y // 2
            y = d & 1
            z = (d >> 1) & (high - 1)
            core = (d >> log2(self.mesh_y)) & 1
            x = d >> (log2(self.mesh_y) + 1)
            turn = y ^ (x & 1)
            return ((x * 2 + turn) * high + (z ^ (turn * (high - 1)))) * 2 + core
        if not self.joint and self.mesh_y % 8 == 0:
            return d ^ (((d >> 3) & 1) * 7)
        return d

    def slab(self):
        d = lax.axis_index("ey")
        return self.slab_at(lax.axis_index("ex") * self.mesh_y + d if self.joint else d)

    def swaps(self, first):
        pairs = []
        for s in range(first, self.slabs, 2):
            a, b = self.order[s], self.order[(s + 1) % self.slabs]
            pairs += [(a, b), (b, a)]
        return pairs


def split(x):
    high = x.astype(BF16)
    return high, (x - high.astype(F32)).astype(BF16)


def times3(high, low, x):
    xh, xl = split(x)
    dot = functools.partial(jnp.dot, preferred_element_type=F32)
    width = x.shape[1]
    both = dot(high, jnp.concatenate([xh, xl], 1))
    return both[:, :width] + both[:, width:] + dot(low, xh)


def split_table(x):
    high = x.astype(BF16)
    return high, (x - high.astype(np.float64)).astype(BF16)


def stacked_table(x):
    high, low = split_table(x)
    return np.concatenate([high, high, low, low], 1)


def stacked(x):
    high = x.astype(BF16).astype(F32)
    low = x - high
    return jnp.concatenate([high, low, high, low], 0).astype(BF16)


def subtract_stiffness(lay, one, u_ref, g_ref, high_ref, low_ref, along_ref):
    matrix, weights = one
    dot = functools.partial(jnp.dot, preferred_element_type=F32)
    half = N // 2
    for first in (0, half):
        scaled = [
            float(weights[i]) * u_ref[pl.ds(i * FACE, FACE), :] for i in range(first, first + half)
        ]
        xh, xl = split(jnp.concatenate(scaled, 0))
        both = dot(high_ref[...], jnp.concatenate([xh, xl], 1))
        rows = pl.ds(first * FACE, half * FACE)
        g_ref[rows, :] -= both[:, : lay.width] + both[:, lay.width :] + dot(low_ref[...], xh)
    even = 0.5 * (matrix[:half, :half] + matrix[:half, :half - 1 : -1])
    odd = 0.5 * (matrix[:half, :half] - matrix[:half, :half - 1 : -1])
    for j in range(N):
        values = [u_ref[pl.ds((i * N + j) * N, N), :] for i in range(N)]
        sums = [values[i] + values[N - 1 - i] for i in range(half)]
        gaps = [values[i] - values[N - 1 - i] for i in range(half)]
        along = along_ref[pl.ds(j * N, N), :]
        for i in range(half):
            a = sum(float(even[i, q]) * sums[q] for q in range(half))
            b = sum(float(odd[i, q]) * gaps[q] for q in range(half))
            g_ref[pl.ds((i * N + j) * N, N), :] -= along * (a + b)
            g_ref[pl.ds(((N - 1 - i) * N + j) * N, N), :] -= along * (a - b)


def roll(x, shift, axis):
    size = x.shape[axis]
    return pltpu.roll(x, shift % size, axis)


def lane_parts(lay, shape):
    lane = lax.broadcasted_iota(jnp.int32, shape, len(shape) - 1)
    part_z = lane & (lay.depth - 1)
    part_y = lax.shift_right_logical(lane, log2(lay.step_y)) & (lay.num_y - 1)
    part_x = lax.shift_right_logical(lane, log2(lay.step_x))
    return part_x, part_y, part_z


def get_rows(ref, k):
    if ref.shape[1] == 128:
        return ref[pl.ds(k, FACE, stride=N), :]
    return jnp.concatenate([ref[pl.ds(n * N + k, 1), :] for n in range(FACE)], 0)


def set_rows(ref, k, value):
    if ref.shape[1] == 128:
        ref[pl.ds(k, FACE, stride=N), :] = value
    else:
        for n in range(FACE):
            ref[pl.ds(n * N + k, 1), :] = value[n : n + 1]


def assemble_xy(lay, s_ref):
    last = N - 1
    for j in range(N):
        a, b = pl.ds(j * N, N), pl.ds((last * N + j) * N, N)
        low, high = s_ref[a, :], s_ref[b, :]
        s_ref[a, :] = low + roll(high, lay.step_x, 1)
        s_ref[b, :] = high + roll(low, -lay.step_x, 1)
    for i in range(N):
        a, b = pl.ds(i * N * N, N), pl.ds((i * N + last) * N, N)
        low, high = s_ref[a, :], s_ref[b, :]
        s_ref[a, :] = low + roll(high, lay.step_y, 1)
        s_ref[b, :] = high + roll(low, -lay.step_y, 1)


def assemble(lay, g_ref, s_ref, halo):
    _, _, part_z = lane_parts(lay, halo.shape)
    s_ref[...] = g_ref[...]
    low = get_rows(g_ref, 0)
    high = get_rows(g_ref, N - 1)
    set_rows(s_ref, 0, low + jnp.where(part_z == 0, halo, roll(high, 1, 1)))
    set_rows(s_ref, N - 1, high + jnp.where(part_z == lay.depth - 1, halo, roll(low, -1, 1)))
    assemble_xy(lay, s_ref)


def store_faces(lay, g_ref, face_ref):
    low = get_rows(g_ref, 0)
    high = get_rows(g_ref, N - 1)
    _, _, part_z = lane_parts(lay, low.shape)
    face_ref[...] = jnp.zeros(face_ref.shape, F32)
    face_ref[:FACE, :] = jnp.where(part_z == 0, low, high)


def halo_of(lay, core_ref, chip_ref):
    odd = (lay.slab() & 1) == 1
    core, chip = core_ref[:FACE, :], chip_ref[:FACE, :]
    below = jnp.where(odd, core, chip)
    above = jnp.where(odd, chip, core)
    _, _, part_z = lane_parts(lay, core.shape)
    return jnp.where(part_z == 0, roll(below, 1 - lay.depth, 1), roll(above, lay.depth - 1, 1))


def assemble_both(lay, g_ref, h_ref, s_ref, sh_ref):
    low, high = get_rows(g_ref, 0), get_rows(g_ref, N - 1)
    out_low, out_high = get_rows(h_ref, 0), get_rows(h_ref, N - 1)
    _, _, part_z = lane_parts(lay, low.shape)
    bottom = part_z == 0
    s_ref[...] = g_ref[...]
    sh_ref[...] = h_ref[...]
    set_rows(s_ref, 0, low + jnp.where(bottom, out_high, roll(high, 1, 1)))
    set_rows(s_ref, N - 1, high + jnp.where(bottom, roll(low, -1, 1), out_low))
    set_rows(sh_ref, N - 1, out_high + jnp.where(bottom, low, 0.0))
    set_rows(sh_ref, 0, out_low + jnp.where(bottom, 0.0, high))
    assemble_xy(lay, s_ref)
    assemble_xy(lay, sh_ref)


def send_layers(lay, g_ref, s_ref, core_ref, chip_ref):
    low, high = get_rows(g_ref, 0), get_rows(g_ref, N - 1)
    _, _, part_z = lane_parts(lay, low.shape)
    s_ref[...] = g_ref[...]
    set_rows(s_ref, N - 1, jnp.where(part_z == 0, high + roll(low, -1, 1), high))
    set_rows(s_ref, 0, jnp.where(part_z == 0, low, low + roll(high, 1, 1)))
    half = N**3 // 2
    a, b = s_ref[:half, :], s_ref[half:, :]
    _, _, part_z = lane_parts(lay, a.shape)
    bottom = part_z == 0
    first = jnp.where(bottom, a, roll(b, 1, 1))
    second = jnp.where(bottom, roll(a, -1, 1), b)
    odd = (lay.slab() & 1) == 1
    core_ref[...] = jnp.where(odd, first, second)
    chip_ref[...] = jnp.where(odd, second, first)


def receive_layers(lay, core_ref, chip_ref, h_ref):
    odd = (lay.slab() & 1) == 1
    core, chip = core_ref[...], chip_ref[...]
    below, above = jnp.where(odd, core, chip), jnp.where(odd, chip, core)
    _, _, part_z = lane_parts(lay, core.shape)
    bottom = part_z == 0
    half = N**3 // 2
    h_ref[:half, :] = jnp.where(bottom, below, roll(above, 1, 1))
    h_ref[half:, :] = jnp.where(bottom, roll(below, -1, 1), above)


def pack_kernel(
    lay,
    base_ref,
    offset_ref,
    force_ref,
    source_ref,
    out_ref,
    base_buf,
    offset_buf,
    force_buf,
    field_ref,
    flat_ref,
    sems,
):
    pairs = (
        (source_ref, field_ref),
        (base_ref, base_buf),
        (offset_ref, offset_buf),
        (force_ref, force_buf),
    )
    copies = [pltpu.make_async_copy(a, b, sems.at[n]) for n, (a, b) in enumerate(pairs)]
    for copy in copies:
        copy.start()
    for copy in copies:
        copy.wait()
    mean = 0.5 * (get_rows(field_ref, N - 1) + roll(get_rows(field_ref, 0), -1, 1))
    set_rows(field_ref, N - 1, mean)
    set_rows(field_ref, 0, roll(mean, 1, 1))
    flat_ref[...] = field_ref[...].T
    shape = (1, N**3)
    lane = lax.broadcasted_iota(jnp.int32, shape, 1)
    points = jnp.zeros(shape, F32)
    for p in range(base_buf.shape[0]):
        for c, ref in enumerate((base_buf, offset_buf, force_buf)):
            for d in range(3):
                value = ref[p : p + 1, d : d + 1].astype(F32)
                points = jnp.where(lane == (p * 9 + c * 3 + d) * N, value, points)
    used = (lane & (N - 1)) == 0
    for d in range(lay.slabs):
        first = lay.slab_at(d) * lay.depth
        for e2 in range(lay.tiles_y):
            rows = flat_ref[pl.ds(e2 * EZ + first, lay.depth), :]
            out_ref[d, pl.ds(e2 * lay.depth, lay.depth), :] = rows
        out_ref[d, 1:2, :] = jnp.where(used, points, out_ref[d, 1:2, :])


def column(values, shape):
    node = lax.broadcasted_iota(jnp.int32, shape, 0)
    out = jnp.full(shape, float(values[0]), F32)
    for n in range(1, N):
        out = jnp.where(node == n, float(values[n]), out)
    return out


def gauss(elem, base, position, half_nodes):
    node = lax.broadcasted_iota(jnp.int32, elem.shape, 0)
    elem = elem.astype(F32)
    away = elem + half_nodes - position
    inside = (
        (elem == base)
        | (elem == base + 1.0)
        | ((elem == base - 1.0) & (node == N - 1))
        | ((elem == base + 2.0) & (node == 0))
    )
    return jnp.where(inside, jnp.exp(-(away * away) / (WIDTH_EPS * WIDTH_EPS)), 0.0)


def point_values(points_ref, row, place, scale):
    base, offset, force = (
        [points_ref[row, (place * 9 + c * 3 + d) * N] for d in range(3)] for c in range(3)
    )
    return base, [b + 1.0 + o for b, o in zip(base, offset)], [scale * f for f in force]


def right_side(lay, local_points, one, points_ref, list_ref, g_ref, halo_ref):
    derivative, weights = one
    shape = (N, lay.width)
    part_x, part_y, part_z = lane_parts(lay, shape)
    first_z = lay.slab() * lay.depth
    elem_z = first_z + part_z
    elem_halo = jnp.where(part_z == 0, first_z - 1, first_z + lay.depth)
    half_nodes = column(0.5 * (1.0 + GLL_POINTS), shape)
    weight = column(weights, shape)
    columns = [column(derivative[a], shape) for a in range(N)]

    def weighted(elem, base, position):
        plain = weight * gauss(elem, base, position, half_nodes)
        terms = [columns[a] * plain[a : a + 1] for a in range(N)]
        while len(terms) > 1:
            terms = [a + b for a, b in zip(terms[::2], terms[1::2])]
        return plain, terms[0]

    def place_of(p):
        return (p, 0) if local_points == 1 else (lax.div(p, local_points), lax.rem(p, local_points))

    first = first_z.astype(F32)

    def collect(p, found):
        row, place = place_of(p)
        base = points_ref[row, (place * 9 + 2) * N]
        list_ref[found] = p
        reached = (base + 2.0 >= first - 1.0) & (base - 1.0 <= first + lay.depth)
        return found + jnp.where(reached, 1, 0)

    found = lax.fori_loop(0, points_ref.shape[0] * local_points, collect, jnp.int32(0))
    pick = part_z[0:1] == 0

    def factors(n):
        row, place = place_of(list_ref[jnp.minimum(n, found - 1)])
        base, position, force = point_values(
            points_ref, row, place, jnp.where(n < found, 0.25 * GAUSS_NORM, 0.0)
        )
        x0, x1 = weighted(part_x, base[0], position[0])
        y0, y1 = weighted(part_y, base[1], position[1])
        z0, z1 = weighted(elem_z, base[2], position[2])
        h0, h1 = weighted(elem_halo, base[2], position[2])
        h0 = jnp.where(pick, h0[N - 1 : N], h0[0:1])
        h1 = jnp.where(pick, h1[N - 1 : N], h1[0:1])
        planes = []
        for j in range(N):
            row0, row1 = y0[j : j + 1], y1[j : j + 1]
            planes.append((row0 * z0, row1 * (force[1] * z0) + row0 * (force[2] * z1)))
        planes.append((y0 * h0, y1 * (force[1] * h0) + y0 * (force[2] * h1)))
        return force[0] * x1, x0, planes

    def two(t, _):
        points = [factors(2 * t), factors(2 * t + 1)]

        def term(i, j):
            parts = [
                x1[i : i + 1] * planes[j][0] + x0[i : i + 1] * planes[j][1] for x1, x0, planes in points
            ]
            return parts[0] + parts[1]

        for i in range(N):
            for j in range(N):
                g_ref[pl.ds((i * N + j) * N, N), :] += term(i, j)
            halo_ref[pl.ds(i * N, N), :] += term(i, N)
        return 0

    lax.fori_loop(0, lax.div(found + 1, 2), two, 0)


def inverse_diagonal(lay, factor, dinv_ref, outer):
    shape = (N, lay.width)
    part_x, part_y, part_z = lane_parts(lay, shape)
    first = lay.slab() * lay.depth
    part_z = jnp.where(part_z == 0, first - 1, first + lay.depth) if outer else first + part_z
    node = lax.broadcasted_iota(jnp.int32, shape, 0)

    def share(low, high):
        return (
            jnp.where(low, 0.0, 0.5),
            jnp.where(high, 0.0, 0.5),
        )

    low_z, high_z = share(part_z == 0, part_z == EZ - 1)
    along_z = jnp.where(node == 0, low_z, jnp.where(node == N - 1, high_z, 1.0))
    if outer:
        along_z = jnp.where((part_z < 0) | (part_z >= EZ), 0.0, along_z)
    along_x = dict(zip((0, N - 1), share(part_x == 0, part_x == lay.num_x - 1)))
    along_y = dict(zip((0, N - 1), share(part_y == 0, part_y == lay.num_y - 1)))
    tables = {}
    for i in range(N // 2):
        for j in range(i + 1):
            tables[i, j] = tables[j, i] = column(factor[i, j], shape) * along_z
    for i in range(N):
        for j in range(N):
            rows = pl.ds((i * N + j) * N, N)
            value = tables[min(i, N - 1 - i), min(j, N - 1 - j)]
            if i in along_x:
                value = value * along_x[i]
            if j in along_y:
                value = value * along_y[j]
            dinv_ref[rows, :] = value


def first_kernel(
    lay,
    local_points,
    derivative,
    one,
    factor,
    recv_ref,
    high_ref,
    low_ref,
    along_ref,
    g_ref,
    x_ref,
    dinv_ref,
    outer_ref,
    face_ref,
    points_ref,
    s_ref,
    halo_ref,
    flat_ref,
    table_ref,
    list_ref,
    sem,
):
    count, block = recv_ref.shape[0], recv_ref.shape[1]
    for d in range(count):
        points_ref[pl.ds(d, 1), :] = recv_ref[d, 1:2, : points_ref.shape[1]]
    copy = pltpu.make_async_copy(points_ref, table_ref, sem)
    copy.start()
    for d in range(count):
        flat_ref[pl.ds(d * block, block), :] = recv_ref[d]
    g_ref[...] = flat_ref[...].T
    low, high = get_rows(g_ref, 0), get_rows(g_ref, N - 1)
    _, _, part_z = lane_parts(lay, low.shape)
    set_rows(g_ref, 0, jnp.where(part_z == 0, low, roll(high, 1, 1)))
    halo_ref[...] = jnp.where(part_z == 0, low, high)
    inverse_diagonal(lay, factor, dinv_ref, False)
    inverse_diagonal(lay, factor, outer_ref, True)
    copy.wait()
    right_side(lay, local_points, (derivative, one[1]), table_ref, list_ref, g_ref, halo_ref)
    assemble(lay, g_ref, s_ref, halo_ref[...])
    x_ref[...] = (1.0 / THETA) * dinv_ref[...] * s_ref[...]
    subtract_stiffness(lay, one, x_ref, g_ref, high_ref, low_ref, along_ref)
    store_faces(lay, g_ref, face_ref)


def vertex_rows(lay, table_ref, values):
    high, low = split(values)
    both = jnp.dot(table_ref[...], jnp.concatenate([high, low], 1), preferred_element_type=F32)
    load = both[:N, : lay.width] + both[:N, lay.width :] + both[N:, : lay.width]
    rows = [load[n : n + 1] for n in range(N)]
    rows = [rows[n] + roll(rows[4 + n], lay.step_x, 1) for n in range(4)]
    return [rows[n] + roll(rows[2 + n], lay.step_y, 1) for n in range(2)]


def face_values(lay, u_ref):
    low, high = get_rows(u_ref, 0), get_rows(u_ref, N - 1)
    _, _, part_z = lane_parts(lay, low.shape)
    return jnp.where(part_z == 0, low, 0.0), jnp.where(part_z == 0, 0.0, high)


def send_loads(lay, own, outer, far, send_ref, token_ref):
    _, _, part_z = lane_parts(lay, own[0].shape)
    bottom = part_z == 0
    before = jnp.where(bottom, 0.0, roll(outer[0], 1, 1))
    here = own[0] + jnp.where(bottom, outer[1], roll(own[1], 1, 1))
    after = jnp.where(bottom, roll(own[1], -1, 1) + roll(outer[0], -1, 1), outer[1])
    second = jnp.zeros_like(here)
    if far is not None:
        before = before + jnp.where(bottom, far[0], roll(far[1], 1, 1))
        after = after + jnp.where(bottom, 0.0, far[0])
        second = jnp.where(bottom, roll(far[1], -1, 1), 0.0)
    rows = jnp.concatenate([before, here, after, second] * 2, 0)
    for d in range(send_ref.shape[0]):
        send_ref[d] = rows
    token_ref[...] = jnp.zeros(token_ref.shape, F32)


OLD = RHO_SECOND * RHO_FIRST
NEW = 2.0 * RHO_SECOND / DELTA


def first_response(
    lay, g_ref, x_ref, dinv_ref, loads_ref, near_ref, send_ref, token_ref, s_ref
):
    assemble(lay, g_ref, s_ref, jnp.zeros((FACE, lay.width), F32))
    update = NEW * dinv_ref[...] * s_ref[...]
    s_ref[...] = update
    total = OLD * x_ref[...] + update
    own = vertex_rows(lay, loads_ref, jnp.concatenate([g_ref[...], total], 0))
    outer = vertex_rows(lay, near_ref, jnp.concatenate(face_values(lay, s_ref), 0))
    send_loads(lay, own, outer, None, send_ref, token_ref)


def pair_response(
    lay,
    one,
    g_ref,
    dinv_ref,
    outer_ref,
    high_ref,
    low_ref,
    along_ref,
    loads_ref,
    near_ref,
    send_ref,
    token_ref,
    s_ref,
    sh_ref,
    u_ref,
    v_ref,
    t_ref,
    h_ref,
):
    tile = (high_ref, low_ref, along_ref)
    assemble(lay, g_ref, s_ref, jnp.zeros((FACE, lay.width), F32))
    u_ref[...] = (1.0 / THETA) * dinv_ref[...] * s_ref[...]
    t_ref[...] = g_ref[...]
    subtract_stiffness(lay, one, u_ref, t_ref, *tile)
    low, high = face_values(lay, u_ref)
    v_ref[...] = jnp.zeros(v_ref.shape, F32)
    set_rows(v_ref, N - 1, low)
    set_rows(v_ref, 0, high)
    h_ref[...] = jnp.zeros(h_ref.shape, F32)
    subtract_stiffness(lay, one, v_ref, h_ref, *tile)
    assemble_both(lay, t_ref, h_ref, s_ref, sh_ref)
    update = OLD * u_ref[...] + NEW * dinv_ref[...] * s_ref[...]
    own = vertex_rows(lay, loads_ref, jnp.concatenate([t_ref[...], update], 0))
    v_ref[...] = OLD * v_ref[...] + NEW * outer_ref[...] * sh_ref[...]
    outer = vertex_rows(lay, loads_ref, jnp.concatenate([h_ref[...], v_ref[...]], 0))
    far = vertex_rows(lay, near_ref, jnp.concatenate(face_values(lay, v_ref), 0))
    send_loads(lay, own, outer, far, send_ref, token_ref)


def second_kernel(
    lay,
    one,
    core_ref,
    chip_ref,
    g_ref,
    x_ref,
    dinv_ref,
    high_ref,
    low_ref,
    along_ref,
    token_ref,
    points_ref,
    g_out,
    x_out,
    core_out,
    chip_out,
    points_out,
    s_ref,
    u_ref,
):
    points_out[...] = points_ref[...]
    assemble(lay, g_ref, s_ref, halo_of(lay, core_ref, chip_ref))
    update = OLD * x_ref[...] + NEW * dinv_ref[...] * s_ref[...]
    u_ref[...] = update
    x_out[...] = x_ref[...] + update
    g_out[...] = g_ref[...]
    subtract_stiffness(lay, one, u_ref, g_out, high_ref, low_ref, along_ref)
    send_layers(lay, g_out, s_ref, core_out, chip_out)


def solve_coarse(lay, mass, stiff, loads_ref, rows_ref, first_ref, second_ref):
    count = 4
    for s in range(lay.slabs):
        rows_ref[pl.ds(s * count, count), :] = loads_ref[lay.order[s], :count]

    def part(n):
        if lay.width == 128:
            return rows_ref[pl.ds(n, lay.slabs, stride=count), :]
        return jnp.concatenate(
            [rows_ref[pl.ds(s * count + n, 1), :] for s in range(lay.slabs)], 0
        )

    shape = (lay.slabs, lay.width)
    part_x, part_y, part_z = lane_parts(lay, shape)
    row = lax.broadcasted_iota(jnp.int32, shape, 0)
    keep = ((part_x > 0) & (part_y > 0) & ((part_z > 0) | (row > 0))).astype(F32)
    bottom = part_z == 0

    def around_z(v):
        return jnp.where(bottom, roll(v + roll(v, 1, 0), -1, 1), roll(v + roll(v, -1, 0), 1, 1))

    def above(v):
        return jnp.where(bottom, roll(v, -1, 1), roll(roll(v, -1, 0), 1, 1))

    def neighbours(v, step):
        return roll(v, step, 1) + roll(v, -step, 1)

    def mix(pair, v, around):
        return (2.0 * pair[0]) * v + pair[1] * around

    def operate(v):
        around = around_z(v)
        mass_z, stiff_z = mix(mass, v, around), mix(stiff, v, around)
        around = neighbours(mass_z, lay.step_y)
        both = mix(mass, mass_z, around)
        rest = mix(stiff, mass_z, around) + mix(mass, stiff_z, neighbours(stiff_z, lay.step_y))
        out = mix(stiff, both, neighbours(both, lay.step_x)) + mix(
            mass, rest, neighbours(rest, lay.step_x)
        )
        return (0.5 * keep) * out

    def inner(a, b):
        return jnp.sum(jnp.sum(a * b, axis=1, keepdims=True), axis=0, keepdims=True)

    residual = keep * (part(1) + roll(part(0), -1, 0) + roll(part(2), 1, 0) + roll(part(3), 2, 0))
    image = operate(residual)
    total = jnp.zeros(shape, F32)
    for step in range(CG_STEPS):
        last = step + 1 == CG_STEPS
        norm, curv = inner(residual, residual), inner(image, residual)
        if not last:
            second = operate(image)
        if step == 0:
            alpha = norm / curv
            direction, moved = residual, image
            if not last:
                moved_image = second
        else:
            beta = norm / norm_old
            alpha = norm / (curv - beta * norm / alpha)
            direction = residual + beta * direction
            if not last:
                moved, moved_image = image + beta * moved, second + beta * moved_image
        norm_old = norm
        total = total + alpha * direction
        if not last:
            residual, image = residual - alpha * moved, image - alpha * moved_image
    here = pl.ds(N, lay.slabs)
    for ref, value in ((first_ref, total), (second_ref, above(total))):
        ref[...] = jnp.zeros(ref.shape, F32)
        ref[here, :] = value


def corners(lay, low, high):
    rows = [low, high]
    rows = rows + [roll(r, -lay.step_y, 1) for r in rows]
    rows = rows + [roll(r, -lay.step_x, 1) for r in rows]
    corner = lax.broadcasted_iota(jnp.int32, (N, lay.width), 0)
    local = jnp.broadcast_to(rows[0], (N, lay.width))
    for n in range(1, N):
        local = jnp.where(corner == n, rows[n], local)
    return local


def coarse_kernel(
    lay,
    mass,
    stiff,
    loads_ref,
    g_ref,
    x_ref,
    interp_ref,
    image_ref,
    done_ref,
    g_out,
    x_out,
    around_ref,
    rows_ref,
    first_ref,
    second_ref,
):
    solve_coarse(lay, mass, stiff, loads_ref, rows_ref, first_ref, second_ref)
    mine = lay.slab() + N
    _, _, part_z = lane_parts(lay, (1, lay.width))
    bottom = part_z == 0
    own, outer, far = [], [], []
    for ref in (first_ref, second_ref):
        before, here, after = (ref[pl.ds(mine + shift, 1), :] for shift in (-1, 0, 1))
        own.append(here)
        outer.append(jnp.where(bottom, roll(before, -1, 1), roll(after, 1, 1)))
        far.append(jnp.where(bottom, before, after))
    local = stacked(corners(lay, *own))
    dot = functools.partial(jnp.dot, preferred_element_type=F32)
    x_out[...] = x_ref[...] + dot(interp_ref[...], local)
    g_out[...] = g_ref[...] - dot(image_ref[...], local)
    around_ref[:N, :] = corners(lay, *outer)
    around_ref[N:, :] = corners(lay, *far)


def correct_layers(lay, around_ref, image_ref, edge_ref, h_ref):
    dot = functools.partial(jnp.dot, preferred_element_type=F32)
    h_ref[...] -= dot(image_ref[...], stacked(around_ref[:N, :]))
    edge = dot(edge_ref[...], stacked(around_ref[N:, :]))
    _, _, part_z = lane_parts(lay, (FACE, lay.width))
    bottom = part_z == 0
    low, high = get_rows(h_ref, 0), get_rows(h_ref, N - 1)
    set_rows(h_ref, 0, low - jnp.where(bottom, edge[FACE:], 0.0))
    set_rows(h_ref, N - 1, high - jnp.where(bottom, 0.0, edge[:FACE]))


def pair_kernel(lay, one, kind, core_ref, chip_ref, g_ref, x_ref, dinv_ref, outer_ref, *refs):
    refs = list(refs)
    high_ref, low_ref, along_ref, edge_high_ref, edge_low_ref = (refs.pop(0) for _ in range(5))
    if kind != "inner":
        around_ref, image_ref, image_edge_ref = (refs.pop(0) for _ in range(3))
    if kind == "inner":
        token_ref = refs.pop(0)
    if kind == "last":
        out_ref = refs.pop(0)
    else:
        g_out, x_out = refs.pop(0), refs.pop(0)
        core_out, chip_out = refs.pop(0), refs.pop(0)
    s_ref, sh_ref, h_ref, u_ref = (refs.pop(0) for _ in range(4))
    if kind == "last":
        g_out = refs.pop(0)

    g_out[...] = g_ref[...]
    receive_layers(lay, core_ref, chip_ref, h_ref)
    if kind != "inner":
        correct_layers(lay, around_ref, image_ref, image_edge_ref, h_ref)
    assemble_both(lay, g_out, h_ref, s_ref, sh_ref)
    update = (1.0 / THETA) * dinv_ref[...] * s_ref[...]
    u_ref[...] = update
    outer = (1.0 / THETA) * outer_ref[...] * sh_ref[...]
    edge = times3(edge_high_ref[...], edge_low_ref[...], outer)
    _, _, part_z = lane_parts(lay, (FACE, lay.width))
    near = jnp.where(
        part_z == 0, get_rows(h_ref, N - 1) - edge[FACE:], get_rows(h_ref, 0) - edge[:FACE]
    )
    subtract_stiffness(lay, one, u_ref, g_out, high_ref, low_ref, along_ref)
    assemble(lay, g_out, s_ref, near)
    update = u_ref[...]
    following = OLD * update + NEW * dinv_ref[...] * s_ref[...]
    if kind == "last":
        total = (x_ref[...] + (update + following)).T
        count, block = out_ref.shape[0], out_ref.shape[1]
        for d in range(count):
            out_ref[d] = total[d * block : (d + 1) * block]
        return
    x_out[...] = x_ref[...] + (update + following)
    u_ref[...] = following
    subtract_stiffness(lay, one, u_ref, g_out, high_ref, low_ref, along_ref)
    send_layers(lay, g_out, s_ref, core_out, chip_out)


def unpack_kernel(lay, recv_ref, out_ref, flat_ref):
    for d in range(lay.slabs):
        first = lay.slab_at(d) * lay.depth
        for e2 in range(lay.tiles_y):
            rows = recv_ref[d, pl.ds(e2 * lay.depth, lay.depth), :]
            flat_ref[pl.ds(e2 * EZ + first, lay.depth), :] = rows
    out_ref[...] = flat_ref[...].T


def gauss_at(elem, node, base, position):
    half_nodes = jnp.full(node.shape, 0.5 * (1.0 + GLL_POINTS[0]), F32)
    for n in range(1, N):
        half_nodes = jnp.where(node == n, 0.5 * (1.0 + GLL_POINTS[n]), half_nodes)
    elem = elem.astype(F32)
    away = elem + half_nodes - position
    inside = (
        (elem == base)
        | (elem == base + 1.0)
        | ((elem == base - 1.0) & (node == N - 1))
        | ((elem == base + 2.0) & (node == 0))
    )
    return jnp.where(inside, jnp.exp(-(away * away) / (WIDTH_EPS * WIDTH_EPS)), 0.0)


def forces_kernel(tiles_y, local_points, points_ref, out_ref, done_ref):
    done_ref[...] = jnp.zeros(done_ref.shape, F32)
    count = points_ref.shape[0]
    first_x, first_y = lax.axis_index("ex"), lax.axis_index("ey") * tiles_y
    lane = lax.broadcasted_iota(jnp.int32, (count, 3 * FACE), 1)
    node_x, node_y, part = (lane >> 3) & (N - 1), lane & (N - 1), lane >> 6
    lane_z = lax.broadcasted_iota(jnp.int32, (count, tiles_y * EZ), 1)
    planes, columns = [], []
    for place in range(local_points):

        def value(n):
            at = (place * 9 + n) * N
            return points_ref[:, at : at + 1]

        base = [value(d) for d in range(3)]
        position = [value(d) + 1.0 + value(3 + d) for d in range(3)]
        force = jnp.where(part == 0, value(6), jnp.where(part == 1, value(7), value(8)))
        x = gauss_at(jnp.broadcast_to(first_x, lane.shape), node_x, base[0], position[0])
        scaled = GAUSS_NORM * force * x
        for e2 in range(tiles_y):
            y = gauss_at(jnp.broadcast_to(first_y + e2, lane.shape), node_y, base[1], position[1])
            planes.append(scaled * y)
            columns.append((e2, base[2], position[2]))
    high, low = split(jnp.concatenate(planes, 0))
    plane = jnp.concatenate([high, high, low], 0)
    elem_z, row_z = lane_z & (EZ - 1), lane_z >> log2(EZ)
    for k in range(N):
        node = jnp.full(lane_z.shape, k, jnp.int32)
        along = [
            jnp.where(row_z == e2, gauss_at(elem_z, node, base, position), 0.0)
            for e2, base, position in columns
        ]
        high, low = split(jnp.concatenate(along, 0))
        out_ref[pl.ds(k, 3 * FACE, stride=N), :] = lax.dot_general(
            plane,
            jnp.concatenate([high, low, high], 0),
            (((0,), (0,)), ((), ())),
            preferred_element_type=F32,
        )


def call(kernel, outs, inputs, scratch=(), smem=0, spaces=None, limit=40):
    spaces = spaces or [pltpu.SMEM] * smem + [pltpu.VMEM] * (len(inputs) - smem)
    specs = [pl.BlockSpec(memory_space=space) for space in spaces]
    shapes = [jax.ShapeDtypeStruct(s, F32) for s in outs]
    result = pl.pallas_call(
        kernel,
        out_shape=shapes,
        in_specs=specs,
        out_specs=[pl.BlockSpec(memory_space=pltpu.VMEM)] * len(shapes),
        scratch_shapes=[pltpu.VMEM(s, F32) if isinstance(s, tuple) else s for s in scratch],
        compiler_params=pltpu.CompilerParams(vmem_limit_bytes=limit * 1024 * 1024),
    )(*inputs)
    return result


def shards(source, point_base, point_offset, point_force):
    tiles_x, tiles_y = source.shape[3], source.shape[4] // EZ
    lay = Layout(lax.axis_size("ex"), lax.axis_size("ey"), tiles_x, tiles_y)
    devices = lay.mesh_x * lay.mesh_y
    derivative, weights, interp, stiff_one = build_tables()
    width, fields = lay.width, (N**3, lay.width)

    diag_w = np.diag(weights)
    full = 0.5 * (
        kron3(stiff_one, diag_w, diag_w)
        + kron3(diag_w, stiff_one, diag_w)
        + kron3(diag_w, diag_w, stiff_one)
    )
    edge_rows = np.concatenate([np.arange(FACE) * N, np.arange(FACE) * N + N - 1])
    plane = 0.5 * (np.kron(stiff_one, diag_w) + np.kron(diag_w, stiff_one))
    high, low = (jnp.asarray(t) for t in split_table(np.kron(np.eye(N // 2), plane)))
    along = np.broadcast_to(0.5 * np.kron(weights, weights)[:, None], (FACE, width))
    along = jnp.asarray(along, F32)
    edge_high, edge_low = (jnp.asarray(t) for t in split_table(full[edge_rows]))
    one = (stiff_one, weights)
    interp3 = kron3(interp, interp, interp)
    image3 = full @ interp3
    ratio = (weights[:, None] * derivative**2).sum(axis=0) / weights
    diag = 0.5 * (ratio[:, None, None] + ratio[None, :, None] + ratio[None, None, :])
    diag = diag * weights[:, None, None] * weights[None, :, None] * weights[None, None, :]
    factor = 1.0 / diag
    mass = interp.T @ diag_w @ interp
    stiff = interp.T @ stiff_one @ interp
    moved = -interp3.T @ full
    loads_table, near_table = (
        jnp.asarray(np.concatenate(split_table(t), 0))
        for t in (
            np.concatenate([interp3.T, moved], 1),
            np.concatenate([moved[:, edge_rows[FACE:]], moved[:, edge_rows[:FACE]]], 1),
        )
    )
    prolong3, image3, image_edge = (
        jnp.asarray(stacked_table(t)) for t in (interp3, image3, image3[edge_rows])
    )

    local_points = point_base.shape[1]
    block = lay.block
    (send,) = call(
        functools.partial(pack_kernel, lay),
        [(lay.slabs, block, N**3)],
        [
            pltpu.with_memory_space_constraint(t, pltpu.HBM)
            for t in (
                point_base.T,
                point_offset.T,
                point_force.T,
                source.reshape(N**3, tiles_y * EZ),
            )
        ],
        [
            pltpu.VMEM((local_points, 3), jnp.int32),
            (local_points, 3),
            (local_points, 3),
            (N**3, tiles_y * EZ),
            (tiles_y * EZ, N**3),
            pltpu.SemaphoreType.DMA((4,)),
        ],
        spaces=[pltpu.HBM] * 4,
    )
    recv = lax.all_to_all(send, lay.axis, 0, 0)
    if not lay.joint:
        recv = lax.all_gather(recv, "ex", axis=0, tiled=True)

    def swap(core, chip):
        return (
            lax.ppermute(core, lay.axis, lay.swaps(0)),
            lax.ppermute(chip, lay.axis, lay.swaps(1)),
        )

    def gather(loads):
        return lax.all_to_all(loads, lay.axis, 0, 0)

    face_shape = (FACE, width)
    layer = (N**3 // 2, width)
    loads_shape = (lay.slabs, N, width)
    table = (devices, -(-9 * N * local_points // 128) * 128)
    g, x, dinv, outer, face, points = call(
        functools.partial(first_kernel, lay, local_points, derivative, one, factor),
        [fields, fields, fields, fields, (256, width), table],
        [recv, high, low, along],
        [
            fields,
            face_shape,
            (width, N**3),
            pltpu.SMEM(table, F32),
            pltpu.SMEM((devices * local_points,), jnp.int32),
            pltpu.SemaphoreType.DMA,
        ],
    )
    faces = swap(face, face)
    loads, token = call(
        functools.partial(first_response, lay),
        [loads_shape, (N, 128)],
        [g, x, dinv, loads_table, near_table],
        [fields],
    )
    loads = gather(loads)
    g, x, core, chip, points = call(
        functools.partial(second_kernel, lay, one),
        [fields, fields, layer, layer, table],
        [*faces, g, x, dinv, high, low, along, token, points],
        [fields, fields],
    )
    forces, done = call(
        functools.partial(forces_kernel, tiles_y, local_points),
        [(3 * N**3, tiles_y * EZ), (N, 128)],
        [points],
    )
    coarse = ((mass[0, 0], mass[0, 1]), (stiff[0, 0], stiff[0, 1]))
    stiffness = [high, low, along, edge_high, edge_low]

    for cycle in range(CYCLES):
        core, chip = swap(core, chip)
        last = cycle + 1 == CYCLES
        outs = [fields, fields, layer, layer]
        scratch = [fields] * 4
        if last:
            outs = [(lay.mesh_x * lay.mesh_y, block, N**3)]
            scratch += [fields]
        g, x, around = call(
            functools.partial(coarse_kernel, lay, *coarse),
            [fields, fields, (2 * N, width)],
            [loads, g, x, prolong3, image3, done],
            [(lay.slabs * 4, width)] + [(lay.slabs + 2 * N, width)] * 2,
        )
        outs = call(
            functools.partial(pair_kernel, lay, one, "last" if last else "plain"),
            outs,
            [core, chip, g, x, dinv, outer, *stiffness, around, image3, image_edge],
            scratch,
        )
        if last:
            break
        g, x, core, chip = outs
        layers = swap(core, chip)
        loads, token = call(
            functools.partial(pair_response, lay, one),
            [loads_shape, (N, 128)],
            [g, dinv, outer, high, low, along, loads_table, near_table],
            [fields] * 6,
        )
        loads = gather(loads)
        g, x, core, chip = call(
            functools.partial(pair_kernel, lay, one, "inner"),
            [fields, fields, layer, layer],
            [*layers, g, x, dinv, outer, *stiffness, token],
            [fields] * 4,
        )
    (out,) = outs
    if not lay.joint:
        out = lax.dynamic_slice_in_dim(out, lax.axis_index("ex") * lay.mesh_y, lay.mesh_y, 0)
    out = lax.all_to_all(out, lay.axis, 0, 0)
    (pressure,) = call(
        functools.partial(unpack_kernel, lay),
        [(N**3, tiles_y * EZ)],
        [out],
        [(lay.slabs * block, N**3)],
    )
    return (
        pressure.reshape(source.shape),
        forces.reshape((3, *source.shape)),
    )


def solution(mesh):
    in_specs = (
        P(None, None, None, "ex", "ey"),
        P(None, ("ex", "ey")),
        P(None, ("ex", "ey")),
        P(None, ("ex", "ey")),
    )
    out_specs = (P(None, None, None, "ex", "ey"), P(None, None, None, None, "ex", "ey"))
    return jax.shard_map(shards, mesh=mesh, in_specs=in_specs, out_specs=out_specs, check_vma=False)
```
